32 devices in a mesh: batch: 8 (over y, x, core), blk: 4 (over z).
Axes of the slice: x: 2, y: 2, z: 4, core: 2. Of those that a mesh axis runs over, the one named last changes fastest.
Arguments:
- tokens: bfloat16 [8, 2048, 1024], P('batch', 'blk'), may hold values from -6 to 6
- lengths: int32 [8, 4], P('batch'), may hold values from 1 to 2045, as said below
- first_gain: float32 [1024], replicated, may hold values from 0.5 to 1.5
- first_shift: float32 [1024], replicated, may hold values from -4 to 4
- second_gain: float32 [1024], replicated, may hold values from 0.5 to 1.5
- second_shift: float32 [1024], replicated, may hold values from -4 to 4
- joint_weight: bfloat16 [1024, 3072], replicated, may hold values from -0.1875 to 0.1875
- joint_bias: float32 [3072], replicated, may hold values from -6 to 6
- dense_weight: bfloat16 [1024, 1024], replicated, may hold values from -1.5 to 1.5
- dense_bias: float32 [1024], replicated, may hold values from -6 to 6
- expand_weight: bfloat16 [1024, 4096], replicated, may hold values from -0.1875 to 0.1875
- expand_bias: float32 [4096], replicated, may hold values from -6 to 6
- reduce_weight: bfloat16 [4096, 1024], replicated, may hold values from -0.09375 to 0.09375
- reduce_bias: float32 [1024], replicated, may hold values from -6 to 6
- cotangent: bfloat16 [8, 2048, 1024], P('batch', 'blk'), may hold values from -6 to 6
Outputs:
- result: bfloat16 [8, 2048, 1024], P('batch', 'blk')
- tokens_gradient: bfloat16 [8, 2048, 1024], P('batch', 'blk')
- first_gain_gradient: float32 [1024], P(('batch', 'blk'))
- first_shift_gradient: float32 [1024], P(('batch', 'blk'))
- second_gain_gradient: float32 [1024], P(('batch', 'blk'))
- second_shift_gradient: float32 [1024], P(('batch', 'blk'))
- joint_weight_gradient: float32 [1024, 3072], P(('batch', 'blk'))
- joint_bias_gradient: float32 [2048], P(('batch', 'blk'))
- value_bias_gradient: float32 [1024], P(('batch', 'blk'))
- dense_weight_gradient: float32 [1024, 1024], P(('batch', 'blk'))
- dense_bias_gradient: float32 [1024], P(('batch', 'blk'))
- expand_weight_gradient: float32 [1024, 4096], P(('batch', 'blk'))
- expand_bias_gradient: float32 [4096], P(('batch', 'blk'))
- reduce_weight_gradient: float32 [4096, 1024], P(('batch', 'blk'))
- reduce_bias_gradient: float32 [1024], P(('batch', 'blk'))
The draws below stay inside these ranges and needn't reach their ends.
Inputs may be any that keep to these rules, and one draw needn't show every extreme that they name: `lengths`: each row sums to 2048. In every group of 1 row that one index of batch holds, one row drawn from the seed has one document of 2045 tokens and 3 documents of one token, a number of them drawn from the seed before it and the others after it.
All inputs are finite; a program needn't handle non-finite values.
Results may differ from the reference program's by a relative error of at most 0.017.
Values may be sent and summed in bfloat16 or wider, within the bound.
No kernel may reach another device: no remote copies, remote signals or barrier semaphores. Data moves between devices by JAX's collectives and lax.ppermute only.
A program may use at most 320 MiB of HBM per device.

```python
import jax
import jax.numpy as jnp
from jax import lax

D = 1024
HEADS = 16
HEAD = 64
ROTARY = 16
FF = 4096
SEQ_LEN = 2048
DOCS = 4
SEQS = 1
SEQS_ALL = 8


def draw_lengths(key, part):
    key = jax.random.fold_in(key, 7)
    cut_key, pick_key, lead_key = jax.random.split(key, 3)

    def cuts_for(row_key):
        picked = jax.random.permutation(row_key, SEQ_LEN - 1)[:DOCS - 1] + 1
        return jnp.sort(picked.astype(jnp.int32))
    random_cuts = jax.vmap(cuts_for)(jax.random.split(cut_key, SEQS_ALL))
    group_count = SEQS_ALL // SEQS
    chosen = jax.random.randint(pick_key, (group_count,), 0, SEQS).astype(jnp.int32)
    leading = jax.random.randint(lead_key, (group_count,), 0, DOCS).astype(jnp.int32)
    row_ids = jnp.arange(SEQS_ALL, dtype=jnp.int32)
    group_ids = row_ids // SEQS
    is_chosen = row_ids % SEQS == chosen[group_ids]
    cut_ids = jnp.arange(1, DOCS, dtype=jnp.int32)
    lead_rows = leading[group_ids][:, None]
    fixed_cuts = jnp.where(cut_ids[None, :] <= lead_rows, cut_ids[None, :], SEQ_LEN - DOCS + cut_ids[None, :])
    all_cuts = jnp.where(is_chosen[:, None], fixed_cuts, random_cuts)
    bounds = jnp.concatenate([jnp.zeros((SEQS_ALL, 1), jnp.int32), all_cuts, jnp.full((SEQS_ALL, 1), SEQ_LEN, jnp.int32)], axis=1)
    return bounds[:, 1:] - bounds[:, :-1]


def with_spikes(result, stream_key, source, target, shards_of, factor):
    owner, partner = [(jnp.arange(result.shape[position]) // (result.shape[position] // shards_of)).reshape([-1 if axis == position else 1 for axis in range(result.ndim)]) for position in (source, target)]
    chosen = jax.random.permutation(stream_key, shards_of)[partner]
    strong = (owner == chosen) | (owner == (partner + shards_of // 2) % shards_of)
    return jnp.where(strong, factor * result, result)


def block_levels(key, extent, cuts, smallest, top_value):
    def one(dim, parts):
        draws = jax.random.uniform(jax.random.fold_in(jax.random.fold_in(key, 6), dim), (parts,), jnp.float32, smallest / len(cuts), top_value / len(cuts))
        return jnp.repeat(jnp.exp(draws), extent[dim] // parts).reshape((-1,) + (1,) * (len(extent) - dim - 1))

    loudness = one(*cuts[0])
    for cut in cuts[1:]:
        loudness = loudness * one(*cut)
    return loudness


def noise(stream_key, shape, scale, bound, cuts=(), kind=jnp.bfloat16):
    values = scale * jax.random.normal(stream_key, shape, jnp.float32)
    if cuts:
        values = values * block_levels(stream_key, shape, cuts, -0.22, 0.18)
    return jnp.clip(values, -bound, bound).astype(kind)


def bell_draw_with(key, dims, deviation, limit, cuts, heavy, held_as=jnp.bfloat16):
    values = deviation * jax.random.normal(key, dims, jnp.float32)
    if cuts:
        values = values * block_levels(key, dims, cuts, -0.22, 0.18)
    return jnp.clip(with_spikes(values, jax.random.fold_in(key, 3), *heavy), -limit, limit).astype(held_as)


def setup_inputs(seed: int = 0) -> dict:
    key_list = jax.random.split(jax.random.key(seed), 16)
    tokens = noise(key_list[0], (SEQS_ALL, SEQ_LEN, D), 1.0, 6.0, ((0, 8), (1, 4)))
    lengths = draw_lengths(jax.random.fold_in(key_list[15], 71), 0)
    first_gain = jnp.clip(1.0 + 0.1 * jax.random.normal(key_list[2], (D,), jnp.float32), 0.5, 1.5)
    first_shift = noise(key_list[3], (D,), 0.3, 4.0, (), jnp.float32)
    second_gain = jnp.clip(1.0 + 0.1 * jax.random.normal(key_list[4], (D,), jnp.float32), 0.5, 1.5)
    second_shift = noise(key_list[5], (D,), 0.3, 4.0, (), jnp.float32)
    joint_weight = noise(key_list[6], (D, 3 * D), D ** -0.5, 0.1875)
    joint_bias = noise(key_list[7], (3 * D,), 0.5, 6.0, (), jnp.float32)
    dense_weight = noise(key_list[8], (D, D), (D // 64) ** -0.5, 1.5)
    dense_bias = noise(key_list[9], (D,), 0.5, 6.0, (), jnp.float32)
    expand_weight = noise(key_list[10], (D, FF), D ** -0.5, 0.1875)
    expand_bias = noise(key_list[11], (FF,), 0.5, 6.0, (), jnp.float32)
    reduce_weight = noise(key_list[12], (FF, D), FF ** -0.5, 0.09375)
    reduce_bias = noise(key_list[13], (D,), 0.5, 6.0, (), jnp.float32)
    cotangent = bell_draw_with(key_list[14], (SEQS_ALL, SEQ_LEN, D), 1.0, 6.0, ((0, 8), (1, 4)), (1, 2, 4, 2.0))
    return {"tokens": tokens, "lengths": lengths, "first_gain": first_gain, "first_shift": first_shift, "second_gain": second_gain, "second_shift": second_shift, "joint_weight": joint_weight, "joint_bias": joint_bias, "dense_weight": dense_weight, "dense_bias": dense_bias, "expand_weight": expand_weight, "expand_bias": expand_bias, "reduce_weight": reduce_weight, "reduce_bias": reduce_bias, "cotangent": cotangent}


EPSILON = 1e-05
MASKED = -1e+30
HIGHEST = lax.Precision.HIGHEST

@jax.custom_vjp
def low(v):
    return lax.optimization_barrier(v.astype(jnp.bfloat16)).astype(jnp.float32)

@jax.custom_vjp
def low_back(v):
    return v

def low_keep(v):
    return (low(v), None)

def low_pass(kept, grad):
    return (grad,)

def back_keep(v):
    return (v, None)

def back_low(kept, grad):
    return (low(grad),)
low.defvjp(low_keep, low_pass)
low_back.defvjp(back_keep, back_low)

def doc_tables(lengths, positions):
    doc_ends = jnp.cumsum(lengths, axis=-1)
    doc_starts = doc_ends - lengths
    doc_number = lax.optimization_barrier(jnp.sum((positions[None, :, None] >= doc_ends[:, None, :]).astype(jnp.int32), axis=-1))
    matches = doc_number[:, :, None] == jnp.arange(lengths.shape[-1], dtype=jnp.int32)[None, None, :]
    begins = lax.optimization_barrier(jnp.sum(jnp.where(matches, doc_starts[:, None, :], 0), axis=-1))
    return (doc_number, positions[None, :] - begins)

def angles(offsets):
    half_width = ROTARY // 2
    inverse = 10000.0 ** (-2.0 * jnp.arange(half_width, dtype=jnp.float32) / ROTARY)
    phase = offsets.astype(jnp.float32)[..., None] * inverse
    return (jnp.cos(phase), jnp.sin(phase))

def rotate(values, cosine, sine_table):
    half_width = cosine.shape[-1]
    lead_part = values[..., :half_width]
    tail_part = values[..., half_width:2 * half_width]
    cosine = cosine[:, None, :]
    sine_table = sine_table[:, None, :]
    return jnp.concatenate([lead_part * cosine - tail_part * sine_table, tail_part * cosine + lead_part * sine_table, values[..., 2 * half_width:]], axis=-1)

def normalize(values, gain_row, shift_row):
    center = values - lax.optimization_barrier(jnp.mean(values, axis=-1, keepdims=True))
    spread = lax.optimization_barrier(jnp.mean(center * center, axis=-1, keepdims=True))
    return center * lax.rsqrt(spread + EPSILON) * gain_row + shift_row

def attend(queries, key_rows, value_rows, doc_number):
    block_rows = min(512, SEQ_LEN)
    block_count = SEQ_LEN // block_rows
    places = jnp.arange(SEQ_LEN, dtype=jnp.int32)
    factor = HEAD ** (-0.5)

    @jax.checkpoint
    def one_block(block_item):
        query_part, number_part, place_part = block_item
        scores = low_back(jnp.einsum('qhd,khd->hqk', query_part, key_rows, precision=HIGHEST) * factor)
        visible = (number_part[:, None] == doc_number[None, :]) & (places[None, :] <= place_part[:, None])
        scores = jnp.where(visible[None], scores, MASKED)
        row_peak = lax.optimization_barrier(jnp.max(scores, axis=-1, keepdims=True))
        shares = jnp.exp(scores - row_peak)
        softmax_out = shares / lax.optimization_barrier(jnp.sum(shares, axis=-1, keepdims=True))
        return jnp.einsum('hqk,khd->qhd', low(softmax_out), value_rows, precision=HIGHEST)
    pieces = (queries.reshape(block_count, block_rows, HEADS, HEAD), doc_number.reshape(block_count, block_rows), places.reshape(block_count, block_rows))
    return lax.map(one_block, pieces).reshape(SEQ_LEN, HEADS, HEAD)

def forward(inputs, parameters, doc_number, offsets):
    first_gain, first_shift, second_gain, second_shift, joint_weight, joint_bias, dense_weight, dense_bias, expand_weight, expand_bias, reduce_weight, reduce_bias = parameters
    normed = low(normalize(inputs, first_gain, first_shift))
    joint = low_back(jnp.dot(normed, joint_weight, precision=HIGHEST) + joint_bias)
    cosine, sine_table = angles(offsets)
    head_shape = (SEQ_LEN, HEADS, HEAD)
    queries = low(rotate(joint[:, :D].reshape(head_shape), cosine, sine_table))
    key_rows = low(rotate(joint[:, D:2 * D].reshape(head_shape), cosine, sine_table))
    value_rows = low(joint[:, 2 * D:].reshape(head_shape))
    mixed = attend(queries, key_rows, value_rows, doc_number)
    mixed = low(low_back(mixed.reshape(SEQ_LEN, D)))
    attention_out = jnp.dot(mixed, dense_weight, precision=HIGHEST) + dense_bias
    second = low(normalize(inputs, second_gain, second_shift))
    hidden = low_back(jnp.dot(second, expand_weight, precision=HIGHEST) + expand_bias)
    active = low(jax.nn.gelu(hidden, approximate=False))
    feed_out = jnp.dot(active, reduce_weight, precision=HIGHEST) + reduce_bias
    return inputs + attention_out + feed_out

def reference(tokens, lengths, first_gain, first_shift, second_gain, second_shift, joint_weight, joint_bias, dense_weight, dense_bias, expand_weight, expand_bias, reduce_weight, reduce_bias, cotangent):
    parameters = tuple((parameter.astype(jnp.float32) for parameter in (first_gain, first_shift, second_gain, second_shift, joint_weight, joint_bias, dense_weight, dense_bias, expand_weight, expand_bias, reduce_weight, reduce_bias)))
    places = jnp.arange(SEQ_LEN, dtype=jnp.int32)

    def one_sequence(totals, item_tuple):
        inputs, upstream, sizes_row = item_tuple
        doc_number, offsets = doc_tables(sizes_row[None, :], places)

        def run_layer(values, weights):
            return forward(values, weights, doc_number[0], offsets[0])
        output, pullback = jax.vjp(run_layer, inputs.astype(jnp.float32), parameters)
        input_grad, weight_grads = pullback(upstream.astype(jnp.float32))
        totals = tuple((total_part + grad_part for total_part, grad_part in zip(totals, weight_grads)))
        return (totals, (output.astype(jnp.bfloat16), input_grad.astype(jnp.bfloat16)))
    zeros = tuple((jnp.zeros_like(parameter) for parameter in parameters))
    totals, (outputs, input_grads) = lax.scan(one_sequence, zeros, (tokens, cotangent, lengths))
    return (outputs, input_grads, totals[0], totals[1], totals[2], totals[3], totals[4], totals[5][:2 * D], totals[5][2 * D:], totals[6], totals[7], totals[8], totals[9], totals[10], totals[11])
```

```python
from functools import partial

import jax
import jax.numpy as jnp
from jax import lax
from jax.experimental import pallas as pl
from jax.experimental.pallas import tpu as pltpu
from jax.sharding import PartitionSpec as P

HEADS = 16
HEAD = 64
ROTARY = 16


EPSILON = 1e-05
MASKED = -1e30


def doc_tables(lengths, positions):
    doc_ends = jnp.cumsum(lengths, axis=-1)
    doc_starts = doc_ends - lengths
    doc_number = jnp.sum(
        (positions[None, :, None] >= doc_ends[:, None, :]).astype(jnp.int32), axis=-1
    )
    matches = (
        doc_number[:, :, None] == jnp.arange(lengths.shape[-1], dtype=jnp.int32)[None, None, :]
    )
    begins = jnp.sum(jnp.where(matches, doc_starts[:, None, :], 0), axis=-1)
    return (doc_number, positions[None, :] - begins)


def angles(offsets):
    half_width = ROTARY // 2
    inverse = 10000.0 ** (-2.0 * jnp.arange(half_width, dtype=jnp.float32) / ROTARY)
    phase = offsets.astype(jnp.float32)[..., None] * inverse
    return (jnp.cos(phase), jnp.sin(phase))


def rotate(values, cosine, sine_table, direction):
    half_width = cosine.shape[-1]
    lead_part = values[..., :half_width]
    tail_part = values[..., half_width : 2 * half_width]
    cosine = cosine[:, :, None, :]
    sine_table = sine_table[:, :, None, :] * direction
    return jnp.concatenate(
        [
            lead_part * cosine - tail_part * sine_table,
            tail_part * cosine + lead_part * sine_table,
            values[..., 2 * half_width :],
        ],
        axis=-1,
    )


def normalize(values, gain_row, shift_row):
    center = values - jnp.mean(values, axis=-1, keepdims=True)
    spread = jnp.mean(center * center, axis=-1, keepdims=True)
    inverse_root = lax.rsqrt(spread + EPSILON)
    unit_rows = center * inverse_root
    return (unit_rows * gain_row + shift_row, unit_rows, inverse_root)


def normalize_back(upstream, unit_rows, inverse_root, gain_row):
    scaled_back = upstream * gain_row
    input_back = inverse_root * (
        scaled_back
        - jnp.mean(scaled_back, axis=-1, keepdims=True)
        - unit_rows * jnp.mean(scaled_back * unit_rows, axis=-1, keepdims=True)
    )
    return (input_back, jnp.sum(upstream * unit_rows, axis=0), jnp.sum(upstream, axis=0))


def outer(left_rows, right_rows):
    return lax.dot_general(
        left_rows, right_rows, (((0,), (0,)), ((), ())), preferred_element_type=jnp.float32
    )


def against(left_rows, weight_rows):
    return lax.dot_general(
        left_rows, weight_rows, (((1,), (1,)), ((), ())), preferred_element_type=jnp.float32
    )


def over_piece(stepper, running, segment, stride):
    sub_count = segment.shape[1] // stride

    def one_turn(position, current):
        part_rows = lax.dynamic_slice_in_dim(segment, position * stride, stride, 1)
        return stepper(current, part_rows, position * stride)

    return lax.fori_loop(0, sub_count, one_turn, running)


def local(
    tokens,
    lengths,
    first_gain,
    first_shift,
    second_gain,
    second_shift,
    joint_weight,
    joint_bias,
    dense_weight,
    dense_bias,
    expand_weight,
    expand_bias,
    reduce_weight,
    reduce_bias,
    cotangent,
):
    sequences, stride, model_width = tokens.shape
    cycle_size = lax.axis_size("blk")
    seq_total = stride * cycle_size
    rank_here = lax.axis_index("blk")
    row_count = sequences * stride
    factor = HEAD ** (-0.5)
    head_shape = (sequences, stride, HEADS, HEAD)
    places = jnp.arange(seq_total, dtype=jnp.int32)
    number_all, offset_all = doc_tables(lengths, places)
    first_place = rank_here * stride
    query_number = lax.dynamic_slice_in_dim(number_all, first_place, stride, 1)
    query_offset = lax.dynamic_slice_in_dim(offset_all, first_place, stride, 1)
    query_place = first_place + jnp.arange(stride, dtype=jnp.int32)
    last_place = first_place + stride - 1
    cosine, sine_table = angles(query_offset)
    inputs = tokens.reshape(row_count, model_width).astype(jnp.float32)
    first_norm, first_unit, first_scale = normalize(inputs, first_gain, first_shift)
    normed = first_norm.astype(jnp.bfloat16)
    joint_out = jnp.dot(normed, joint_weight, preferred_element_type=jnp.float32) + joint_bias
    queries = rotate(
        joint_out[:, :model_width].reshape(head_shape), cosine, sine_table, 1.0
    ).astype(jnp.bfloat16)
    key_rows = rotate(
        joint_out[:, model_width : 2 * model_width].reshape(head_shape), cosine, sine_table, 1.0
    ).astype(jnp.bfloat16)
    value_rows = joint_out[:, 2 * model_width :].astype(jnp.bfloat16)
    pair_local = jnp.concatenate(
        [
            key_rows.reshape(sequences, stride, model_width),
            value_rows.reshape(sequences, stride, model_width),
        ],
        axis=-1,
    )

    def masked_scores(key_part, begin_row, row_span):
        key_number = lax.dynamic_slice_in_dim(number_all, begin_row, row_span, 1)
        key_place = begin_row + jnp.arange(row_span, dtype=jnp.int32)
        allowed = (query_number[:, :, None] == key_number[:, None, :]) & (
            key_place[None, None, :] <= query_place[None, :, None]
        )
        allowed = allowed[:, None]
        scores = (
            jnp.einsum("sqhd,skhd->shqk", queries, key_part, preferred_element_type=jnp.float32)
            * factor
        )
        return (jnp.where(allowed, scores, MASKED), allowed)

    def split_piece(segment):
        row_span = segment.shape[1]
        key_part = segment[:, :, :model_width].reshape(sequences, row_span, HEADS, HEAD)
        value_part = segment[:, :, model_width:].reshape(sequences, row_span, HEADS, HEAD)
        return (key_part, value_part, row_span)

    def gated(kernel):

        def stepper(running, segment, begin_row):
            return lax.cond(
                begin_row <= last_place,
                lambda current: kernel(current, segment, begin_row),
                lambda current: current,
                running,
            )

        return stepper

    def forward_kernel(running, segment, begin_row):
        row_peak, row_total, weighted = running
        key_part, value_part, row_span = split_piece(segment)
        scores, allowed = masked_scores(key_part, begin_row, row_span)
        new_peak = jnp.maximum(row_peak, jnp.max(scores, axis=-1))
        shares = jnp.where(allowed, jnp.exp(scores - new_peak[..., None]), 0.0)
        decay_factor = jnp.exp(row_peak - new_peak)
        row_total = row_total * decay_factor + jnp.sum(shares, axis=-1)
        update = jnp.einsum(
            "shqk,skhd->sqhd",
            shares.astype(jnp.bfloat16),
            value_part,
            preferred_element_type=jnp.float32,
        )
        weighted = weighted * jnp.transpose(decay_factor, (0, 2, 1))[..., None] + update
        return (new_peak, row_total, weighted)

    forward_step = gated(forward_kernel)
    initial = (
        jnp.full((sequences, HEADS, stride), MASKED, jnp.float32),
        jnp.zeros((sequences, HEADS, stride), jnp.float32),
        jnp.zeros(head_shape, jnp.float32),
    )
    forward_state = over_piece(
        forward_step, initial, lax.all_gather(pair_local, "blk", axis=1, tiled=True), stride
    )
    row_peak, row_total, weighted = forward_state
    mixed_full = weighted / jnp.transpose(row_total, (0, 2, 1))[..., None]
    log_total = row_peak + jnp.log(row_total)
    mixed = mixed_full.reshape(row_count, model_width).astype(jnp.bfloat16)
    attention_out = jnp.dot(mixed, dense_weight, preferred_element_type=jnp.float32) + dense_bias
    second_norm, second_unit, second_scale = normalize(inputs, second_gain, second_shift)
    second = second_norm.astype(jnp.bfloat16)
    hidden = jnp.dot(second, expand_weight, preferred_element_type=jnp.float32) + expand_bias
    active_full, gelu_pull = jax.vjp(partial(jax.nn.gelu, approximate=False), hidden)
    active = active_full.astype(jnp.bfloat16)
    feed_out = jnp.dot(active, reduce_weight, preferred_element_type=jnp.float32) + reduce_bias
    result = (
        (inputs + attention_out + feed_out)
        .astype(jnp.bfloat16)
        .reshape(sequences, stride, model_width)
    )
    upstream = cotangent.reshape(row_count, model_width)
    dense_grad = outer(mixed, upstream)
    bias_total = jnp.sum(upstream, axis=0, dtype=jnp.float32)
    reduce_grad = outer(active, upstream)
    hidden_grad = gelu_pull(against(upstream, reduce_weight))[0].astype(jnp.bfloat16)
    expand_grad = outer(second, hidden_grad)
    hidden_total = jnp.sum(hidden_grad, axis=0, dtype=jnp.float32)
    input_two, gain_second, shift_second = normalize_back(
        against(hidden_grad, expand_weight), second_unit, second_scale, second_gain
    )
    mixed_grad = against(upstream, dense_weight).astype(jnp.bfloat16)
    out_heads = mixed_grad.reshape(head_shape)
    delta_rows = jnp.transpose(jnp.sum(out_heads * mixed_full, axis=-1), (0, 2, 1))

    def backward_kernel(running, segment, begin_row):
        key_part, value_part, row_span = split_piece(segment)
        scores, allowed = masked_scores(key_part, begin_row, row_span)
        weights_now = jnp.where(allowed, jnp.exp(scores - log_total[..., None]), 0.0)
        weight_grad = jnp.einsum(
            "sqhd,skhd->shqk", out_heads, value_part, preferred_element_type=jnp.float32
        )
        score_grad = (weights_now * (weight_grad - delta_rows[..., None])).astype(jnp.bfloat16)
        query_grad = (
            running[0]
            + jnp.einsum(
                "shqk,skhd->sqhd", score_grad, key_part, preferred_element_type=jnp.float32
            )
            * factor
        )
        value_grad = jnp.einsum(
            "shqk,sqhd->skhd",
            weights_now.astype(jnp.bfloat16),
            out_heads,
            preferred_element_type=jnp.float32,
        )
        key_grad = (
            jnp.einsum("shqk,sqhd->skhd", score_grad, queries, preferred_element_type=jnp.float32)
            * factor
        )
        fresh_rows = jnp.concatenate(
            [
                key_grad.reshape(sequences, row_span, model_width),
                value_grad.reshape(sequences, row_span, model_width),
            ],
            axis=-1,
        )
        pair_grad = lax.dynamic_update_slice_in_dim(running[1], fresh_rows, begin_row, 1)
        return (query_grad, pair_grad)

    backward_step = gated(backward_kernel)
    back_initial = (
        jnp.zeros(head_shape, jnp.float32),
        jnp.zeros((sequences, seq_total, 2 * model_width), jnp.float32),
    )
    back_state = over_piece(
        backward_step, back_initial, lax.all_gather(pair_local, "blk", axis=1, tiled=True), stride
    )
    query_grad = back_state[0]
    pair_mine = lax.psum_scatter(back_state[1], "blk", scatter_dimension=1, tiled=True)
    query_back = rotate(query_grad, cosine, sine_table, -1.0).reshape(row_count, model_width)
    key_back = rotate(
        pair_mine[:, :, :model_width].reshape(head_shape), cosine, sine_table, -1.0
    ).reshape(row_count, model_width)
    value_back = pair_mine[:, :, model_width:].reshape(row_count, model_width)
    joint_back = jnp.concatenate([query_back, key_back, value_back], axis=-1).astype(jnp.bfloat16)
    joint_grad = outer(normed, joint_back)
    joint_total = jnp.sum(joint_back, axis=0, dtype=jnp.float32)
    front_total = joint_total[: 2 * model_width]
    value_total = joint_total[2 * model_width :]
    input_one, gain_first, shift_first = normalize_back(
        against(joint_back, joint_weight), first_unit, first_scale, first_gain
    )
    input_total = (
        (upstream.astype(jnp.float32) + input_one + input_two)
        .astype(jnp.bfloat16)
        .reshape(sequences, stride, model_width)
    )
    summed = (
        lax.psum_scatter(gain_first, ("batch", "blk"), scatter_dimension=0, tiled=True),
        lax.psum_scatter(shift_first, ("batch", "blk"), scatter_dimension=0, tiled=True),
        lax.psum_scatter(gain_second, ("batch", "blk"), scatter_dimension=0, tiled=True),
        lax.psum_scatter(shift_second, ("batch", "blk"), scatter_dimension=0, tiled=True),
        lax.psum_scatter(joint_grad, ("batch", "blk"), scatter_dimension=0, tiled=True),
        lax.psum_scatter(front_total, ("batch", "blk"), scatter_dimension=0, tiled=True),
        lax.psum_scatter(value_total, ("batch", "blk"), scatter_dimension=0, tiled=True),
        lax.psum_scatter(dense_grad, ("batch", "blk"), scatter_dimension=0, tiled=True),
        lax.psum_scatter(bias_total, ("batch", "blk"), scatter_dimension=0, tiled=True),
        lax.psum_scatter(expand_grad, ("batch", "blk"), scatter_dimension=0, tiled=True),
        lax.psum_scatter(hidden_total, ("batch", "blk"), scatter_dimension=0, tiled=True),
        lax.psum_scatter(reduce_grad, ("batch", "blk"), scatter_dimension=0, tiled=True),
    )
    return (
        result,
        input_total,
        summed[0],
        summed[1],
        summed[2],
        summed[3],
        summed[4],
        summed[5],
        summed[6],
        summed[7],
        summed[8],
        summed[9],
        summed[10],
        summed[11],
        summed[8],
    )


BQ = 512
TM = 256
VMEM = 56 * 1024 * 1024
NEG = -1e30
NN = (((1,), (0,)), ((), ()))
NT = (((1,), (1,)), ((), ()))
TN = (((0,), (0,)), ((), ()))


def mm(left, right, form=NN):
    return lax.dot_general(left, right, form, preferred_element_type=jnp.float32)


def low(value):
    return value.astype(jnp.bfloat16)


def wide(value):
    return value.astype(jnp.float32)


def gelu_parts(hidden):
    size = jnp.abs(hidden) * (0.5**0.5)
    bell = jnp.exp(-(size * size))
    base = 1.0 + 0.3275911 * size
    guess = pl.reciprocal(base, approx=True)
    t = guess * (2.0 - base * guess)
    series = t * (
        0.5 * 0.254829592
        + t
        * (
            0.5 * -0.284496736
            + t * (0.5 * 1.421413741 + t * (0.5 * -1.453152027 + t * (0.5 * 1.061405429)))
        )
    )
    tail = series * bell
    return (jnp.where(hidden >= 0.0, 1.0 - tail, tail), bell)


def fold_rows(value):
    rows, columns = value.shape
    return jnp.sum(value.reshape(rows // 8, 8, columns), axis=0)


def block_kernel(spot_ref, *refs):
    (x_ref, g_ref, wj_ref, bj_ref, wd_ref, we_ref, be_ref, wr_ref, g1_ref, s1_ref, g2_ref, s2_ref, cos_ref, sin_ref) = refs[:14]
    (qkv_ref, mg_ref, unit_ref, normed_ref, second_ref, active_ref, hg_ref, up_ref, feed_ref, back_ref, sums_ref, hsum_ref) = refs[-12:]
    del spot_ref
    x = wide(x_ref[...])
    center = x - jnp.mean(x, axis=-1, keepdims=True)
    scale = lax.rsqrt(jnp.mean(center * center, axis=-1, keepdims=True) + EPSILON)
    unit = center * scale
    unit_ref[...] = low(unit)
    normed = low(unit * g1_ref[...] + s1_ref[...])
    normed_ref[...] = normed
    second = low(unit * g2_ref[...] + s2_ref[...])
    second_ref[...] = second
    up = g_ref[...]
    up_ref[...] = up
    mg_ref[...] = low(mm(wd_ref[...], up, NT))
    joint = mm(wj_ref[...], normed, NT) + bj_ref[...]
    cosine, sine = cos_ref[...], sin_ref[...]
    half = ROTARY // 2
    part = joint.shape[0] // 3
    for kind in range(3):
        for head in range(part // HEAD):
            top = kind * part + head * HEAD
            rows = joint[top : top + HEAD]
            if kind < 2:
                lead, tail = rows[:half], rows[half : 2 * half]
                rows = jnp.concatenate(
                    [lead * cosine - tail * sine, tail * cosine + lead * sine, rows[2 * half :]], axis=0
                )
            if kind == 0:
                rows = rows * (HEAD**-0.5)
            qkv_ref[top : top + HEAD, :] = low(rows)
    hidden = mm(second, we_ref[...]) + be_ref[...]
    share, bell = gelu_parts(hidden)
    active = low(hidden * share)
    active_ref[...] = active
    hg = mm(up, wr_ref[...], NT) * (share + hidden * bell * 0.3989422804014327)
    hg_low = low(hg)
    hg_ref[...] = hg_low
    feed_ref[...] = low(mm(active, wr_ref[...]))
    back = mm(hg_low, we_ref[...], NT)
    back_ref[...] = low(back * g2_ref[...])

    @pl.when(pl.program_id(0) == 0)
    def _():
        sums_ref[...] = jnp.zeros_like(sums_ref)
        hsum_ref[...] = jnp.zeros_like(hsum_ref)

    sums_ref[0] += fold_rows(back * unit)
    sums_ref[1] += fold_rows(back)
    hsum_ref[...] += fold_rows(wide(hg_low))


def run_block(spot, x, g, weights, tables, before):
    rows, width = x.shape
    total = tables[0].shape[1]
    wj, bj, wd, we, be, wr, g1, s1, g2, s2 = weights
    units = we.shape[1]
    steps = rows // TM

    def whole(array):
        return pl.BlockSpec(array.shape, lambda i, spot: (0,) * array.ndim)

    here = pl.BlockSpec((TM, width), lambda i, spot: (i, 0))
    column = lambda height: pl.BlockSpec((height, TM), lambda i, spot: (0, spot[0] * steps + i))
    placed = lambda size: pl.BlockSpec((TM, size), lambda i, spot: (spot[0] * steps + i, 0))
    in_specs = [here, here] + [whole(w) for w in weights] + [column(ROTARY // 2)] * 2
    out_specs = [
        column(wj.shape[0]),
        column(wd.shape[0]),
        placed(width),
        placed(width),
        placed(width),
        placed(units),
        placed(units),
        placed(width),
        placed(width),
        placed(width),
        pl.BlockSpec((2, 8, width), lambda i, spot: (0, 0, 0)),
        pl.BlockSpec((8, units), lambda i, spot: (0, 0)),
    ]
    shape = lambda *dims: jax.ShapeDtypeStruct(dims, jnp.bfloat16)
    out_shape = [
        shape(wj.shape[0], total),
        shape(wd.shape[0], total),
        shape(total, width),
        shape(total, width),
        shape(total, width),
        shape(total, units),
        shape(total, units),
        shape(total, width),
        shape(total, width),
        shape(total, width),
        jax.ShapeDtypeStruct((2, 8, width), jnp.float32),
        jax.ShapeDtypeStruct((8, units), jnp.float32),
    ]
    operands = [spot, x, g, *weights, *tables]
    aliases = {}
    if before is not None:
        for index, array in enumerate(before):
            aliases[len(operands)] = index
            operands.append(array)
            in_specs.append(pl.BlockSpec(memory_space=pl.ANY))
    products = rows * width * (3 * wd.shape[0] + wd.shape[0] + 4 * units)
    return pl.pallas_call(
        block_kernel,
        grid_spec=pltpu.PrefetchScalarGridSpec(
            num_scalar_prefetch=1, grid=(steps,), in_specs=in_specs, out_specs=out_specs
        ),
        out_shape=out_shape,
        input_output_aliases=aliases,
        compiler_params=pltpu.CompilerParams(vmem_limit_bytes=VMEM),
        cost_estimate=pl.CostEstimate(
            flops=2 * products, bytes_accessed=20 * rows * width, transcendentals=rows * units
        ),
    )(*operands)


def attend_kernel(place, *refs):
    last = place == 0
    count = 8 if place == 3 else 9
    if place == 3:
        qkv_ref, mg_ref, kx_ref, qx_ref, cos_ref, sin_ref = refs[:6]
        acc_in = None
    else:
        qkv_ref, mg_ref, kx_ref, qx_ref, cos_ref, sin_ref, acc_in = refs[:7]
    del count
    scratch = refs[-4:]
    score_ref, share_ref, key_ref, value_ref = scratch
    outs = refs[-7:-4] if not last else refs[-6:-4]
    mixed_ref, jb_ref = outs[0], outs[1]
    acc_out = None if last else outs[2]
    length = (place + 1) * BQ
    here = place * BQ
    key_t = qkv_ref[1, 0]
    value_t = qkv_ref[2, 0]
    query_t = qkv_ref[0, 0, :, here : here + BQ]
    ones = (lax.broadcasted_iota(jnp.int32, (HEAD, length), 0) < 3).astype(jnp.bfloat16)
    key_ref[...] = jnp.concatenate([key_t[:, :length], kx_ref[:, :length]], axis=0).T
    value_ref[...] = jnp.concatenate([value_t[:, :length], ones], axis=0).T
    query_x = jnp.concatenate([query_t, qx_ref[...]], axis=0)
    peak8 = jnp.full((8, BQ), NEG * 2, jnp.float32)
    for j in range(place + 1):
        at = slice(j * BQ, (j + 1) * BQ)
        scores = mm(key_ref[at, :], query_x)
        if j == place:
            key_row = lax.broadcasted_iota(jnp.int32, (BQ, BQ), 0)
            query_column = lax.broadcasted_iota(jnp.int32, (BQ, BQ), 1)
            scores = jnp.where(key_row <= query_column, scores, NEG)
        score_ref[at, :] = scores
        peak8 = jnp.maximum(peak8, jnp.max(scores.reshape(BQ // 8, 8, BQ), axis=0))
    peak = jnp.max(peak8, axis=0, keepdims=True)
    sum8 = jnp.zeros((8, BQ), jnp.float32)
    mixed = jnp.zeros((HEAD, BQ), jnp.float32)
    for j in range(place + 1):
        at = slice(j * BQ, (j + 1) * BQ)
        share = jnp.exp(score_ref[at, :] - peak)
        sum8 = sum8 + jnp.sum(share.reshape(BQ // 8, 8, BQ), axis=0)
        share = low(share)
        share_ref[at, :] = share
        mixed = mixed + mm(value_t[:, at], share)
    inverse = 1.0 / jnp.sum(sum8, axis=0, keepdims=True)
    mixed = mixed * inverse
    mixed_ref[0] = low(mixed)
    mg = low(wide(mg_ref[0]) * inverse)
    delta = -jnp.sum(wide(mg) * mixed, axis=0, keepdims=True)
    first = low(delta)
    rest = delta - wide(first)
    middle = low(rest)
    final = low(rest - wide(middle))
    row = lax.broadcasted_iota(jnp.int32, (HEAD, BQ), 0)
    extra = jnp.where(
        row == 0, wide(first), jnp.where(row == 1, wide(middle), jnp.where(row == 2, wide(final), 0.0))
    )
    blank = jnp.zeros((HEAD, BQ), jnp.bfloat16)
    mg_x = jnp.concatenate([mg, low(extra)], axis=0)
    mg_v = jnp.concatenate([blank, mg], axis=0)
    query_k = jnp.concatenate([query_t, blank], axis=0)
    query_grad = jnp.zeros((HEAD, BQ), jnp.float32)
    for j in range(place + 1):
        at = slice(j * BQ, (j + 1) * BQ)
        share = share_ref[at, :]
        score_grad = low(wide(share) * mm(value_ref[at, :], mg_x))
        pair = mm(share, mg_v, NT) + mm(score_grad, query_k, NT)
        if acc_in is not None:
            pair = pair + acc_in[0, at, :]
        query_grad = query_grad + mm(key_t[:, at], score_grad)
        if j < place:
            acc_out[0, at, :] = pair
        else:
            pair_t = pair.T
    half = ROTARY // 2
    cosine, sine = cos_ref[...], sin_ref[...]

    def turn_back(rows):
        lead, tail = rows[:half], rows[half : 2 * half]
        return low(
            jnp.concatenate([lead * cosine + tail * sine, tail * cosine - lead * sine, rows[2 * half :]], axis=0)
        )

    jb_ref[0, 0] = turn_back(query_grad * (HEAD**-0.5))
    jb_ref[1, 0] = turn_back(pair_t[:HEAD])
    jb_ref[2, 0] = low(pair_t[HEAD:])


def run_attend(place, qkv, mg, kx, qx, tables, acc, before):
    heads, _, total = mg.shape
    length = (place + 1) * BQ
    in_specs = [
        pl.BlockSpec((3, 1, HEAD, total), lambda h: (0, h, 0, 0)),
        pl.BlockSpec((1, HEAD, BQ), lambda h: (h, 0, place)),
        pl.BlockSpec((HEAD, total), lambda h: (0, 0)),
        pl.BlockSpec((HEAD, BQ), lambda h: (0, place)),
        pl.BlockSpec((ROTARY // 2, BQ), lambda h: (0, place)),
        pl.BlockSpec((ROTARY // 2, BQ), lambda h: (0, place)),
    ]
    operands = [qkv, mg, kx, qx, *tables]
    if acc is not None:
        operands.append(acc)
        in_specs.append(pl.BlockSpec((1, length, 2 * HEAD), lambda h: (h, 0, 0)))
    aliases = {}
    if before is not None:
        for index, array in enumerate(before):
            aliases[len(operands)] = index
            operands.append(array)
            in_specs.append(pl.BlockSpec(memory_space=pl.ANY))
    out_specs = [
        pl.BlockSpec((1, HEAD, BQ), lambda h: (h, 0, place)),
        pl.BlockSpec((3, 1, HEAD, BQ), lambda h: (0, h, 0, place)),
    ]
    out_shape = [
        jax.ShapeDtypeStruct((heads, HEAD, total), jnp.bfloat16),
        jax.ShapeDtypeStruct((3, heads, HEAD, total), jnp.bfloat16),
    ]
    if place > 0:
        out_specs.append(pl.BlockSpec((1, place * BQ, 2 * HEAD), lambda h: (h, 0, 0)))
        out_shape.append(jax.ShapeDtypeStruct((heads, place * BQ, 2 * HEAD), jnp.float32))
    got = pl.pallas_call(
        partial(attend_kernel, place),
        grid=(heads,),
        in_specs=in_specs,
        out_specs=out_specs,
        out_shape=out_shape,
        scratch_shapes=[
            pltpu.VMEM((length, BQ), jnp.float32),
            pltpu.VMEM((length, BQ), jnp.bfloat16),
            pltpu.VMEM((length, 2 * HEAD), jnp.bfloat16),
            pltpu.VMEM((length, 2 * HEAD), jnp.bfloat16),
        ],
        input_output_aliases=aliases,
        compiler_params=pltpu.CompilerParams(vmem_limit_bytes=VMEM),
        cost_estimate=pl.CostEstimate(
            flops=2 * 24 * HEAD * heads * length * BQ, bytes_accessed=8 * heads * HEAD * total, transcendentals=heads * length * BQ
        ),
    )(*operands)
    return (got[0], got[1], got[2] if place > 0 else None)


N = 4


def spot_of(core, z):
    return core * N + z


def hop(value, pairs):
    return lax.ppermute(value, ("core", "blk"), [(spot_of(*a), spot_of(*b)) for a, b in pairs])


CORE_SWAP = [((c, z), (1 - c, z)) for c in range(2) for z in range(N)]
FAR_SWAP = [((c, z), (c, z ^ 2)) for c in range(2) for z in range(N)]


def spread(own, main, outer):
    down = [((0, z), (0, z - 1)) for z in (1, 2, 3)]
    up = [((1, z), (1, z + 1)) for z in (0, 1, 2)]
    one = hop(own, down + up)
    side = hop(own, [((0, 0), (0, 1)), ((1, 3), (1, 2))])
    two = hop(one, [((0, 1), (0, 0)), ((0, 2), (0, 1)), ((1, 2), (1, 3)), ((1, 1), (1, 2))])
    three = hop(two, [((0, 1), (0, 0)), ((1, 2), (1, 3))])
    share = [((0, 0), (1, 0)), ((0, 1), (1, 1)), ((1, 2), (0, 2)), ((1, 3), (0, 3))]
    blocks = []
    for mine in (own, one, jnp.where(outer, two, side), jnp.where(outer, three, two)):
        blocks.append(jnp.where(main, mine, hop(mine, share)))
    return blocks


def collect(part, j, core):
    rows = part.shape[0] // 2
    keep = lax.dynamic_slice_in_dim(part, core * rows, rows, 0)
    send = lax.dynamic_slice_in_dim(part, (1 - core) * rows, rows, 0)
    both = low(wide(keep) + wide(hop(send, CORE_SWAP)))
    holders = (0 if j == 0 else 1, 3 if j == 3 else 2)
    pairs = []
    for c in range(2):
        pairs.append(((c, 1 - holders[0]), (c, holders[0])))
        pairs.append(((c, 5 - holders[1]), (c, holders[1])))
    full = low(wide(both) + wide(hop(both, pairs)))
    halves = []
    for c in range(2):
        pairs = [((c, holders[s]), (s, j)) for s in range(2) if (c, holders[s]) != (s, j)]
        half = hop(full, pairs)
        if holders[c] == j:
            half = jnp.where((core == c) & (lax.axis_index("blk") == j), full, half)
        halves.append(half)
    return halves


def pick(value, axis, index):
    return lax.dynamic_index_in_dim(value, index, axis, keepdims=False)


def col_swap(value, bit):
    return lax.ppermute(value, "col", [(i, i ^ bit) for i in range(4)])


def fold_columns(value, col, x_first):
    value = value.reshape((2, 2) + value.shape[1:])
    y, x = col // 2, col % 2
    if x_first:
        value, bits, places = jnp.swapaxes(value, 0, 1), (1, 2), (x, y)
    else:
        bits, places = (2, 1), (y, x)
    for bit, place in zip(bits, places):
        got = col_swap(low(pick(value, 0, 1 - place)), bit)
        value = wide(pick(value, 0, place)) + wide(got)
    return value


def fold_spread(value, core, z):
    rows, width = value.shape
    far, near = z // 2, z % 2
    value = value.reshape(2, 2, 2, rows // 8, width)
    got = hop(low(pick(value, 1, 1 - far)), FAR_SWAP)
    value = low(pick(value, 1, far) + wide(got)).reshape(4, rows // 8, width)
    mine = core * 2 + near
    pieces = []
    for k in range(4):
        dc, dz = k % 2, k // 2
        piece = pick(value, 0, mine ^ (dc * 2 + dz))
        if k:
            piece = hop(piece, [((c, s), (c ^ dc, s ^ dz)) for c in range(2) for s in range(N)])
        pieces.append(piece)
    quarter = 2 * near + core
    stacked = jnp.stack(pieces)
    return jnp.stack([pick(stacked, 0, quarter ^ k) for k in range(4)])


def fold_reduce(value):
    got = hop(low(value), [((c, z), (c, z ^ 2)) for c in range(2) for z in (1, 2)])
    full = low(value + wide(got))
    parts = [
        hop(full[p], [((c, 3 * near), (p, 2 * near + c)) for c in range(2) for near in range(2)]) for p in range(2)
    ]
    return wide(parts[0]) + wide(parts[1])


def fold_dense(value):
    got = hop(low(value), [((c, z), (c, z ^ 2)) for c in range(2) for z in range(N) if z // 2 != c])
    full = low(value + wide(got))
    parts = [
        hop(full[b], [((c, 2 * c + near), (near, 2 * c + b)) for c in range(2) for near in range(2)])
        for b in range(2)
    ]
    return wide(parts[0]) + wide(parts[1])


def split_local(
    tokens,
    lengths,
    first_gain,
    first_shift,
    second_gain,
    second_shift,
    joint_weight,
    joint_bias,
    dense_weight,
    dense_bias,
    expand_weight,
    expand_bias,
    reduce_weight,
    reduce_bias,
    cotangent,
):
    col, core, z = lax.axis_index("col"), lax.axis_index("core"), lax.axis_index("blk")
    far, near = z // 2, z % 2
    quarter = 2 * near + core
    main = core == far
    outer = far == near
    rows, width = tokens.shape[1:]
    total = rows * N
    units = expand_weight.shape[1]
    groups = units // (N * 128)
    heads = HEADS // N
    own_x, own_g = tokens[0], cotangent[0]
    row_of = lambda vector: vector.reshape(1, -1)

    wj = pick(joint_weight.T.reshape(3, heads, N, HEAD, width), 2, quarter).reshape(3 * heads * HEAD, width)
    bj = pick(joint_bias.reshape(3, heads, N, HEAD), 2, quarter).reshape(-1, 1)
    wd = pick(dense_weight.reshape(heads, N, HEAD, width), 1, quarter).reshape(heads * HEAD, width)
    we = pick(expand_weight.reshape(width, groups, N, 128), 2, quarter).reshape(width, groups * 128)
    be = pick(expand_bias.reshape(groups, N, 128), 1, quarter).reshape(1, -1)
    wr = pick(reduce_weight.reshape(groups, N, 128, width), 1, quarter).reshape(groups * 128, width)
    weights = [wj, bj, wd, we, be, wr, row_of(first_gain), row_of(first_shift), row_of(second_gain), row_of(second_shift)]

    sizes = jnp.where(main, lengths, hop(lengths, CORE_SWAP))
    number, offset = doc_tables(sizes, jnp.arange(total, dtype=jnp.int32))
    cosine, sine = angles(offset[0])
    tables = [cosine.T, sine.T]
    docs = lengths.shape[1]
    same = number[0][None, :] == jnp.arange(HEAD, dtype=jnp.int32)[:, None]
    used = jnp.arange(HEAD)[:, None] < docs
    qx = low(jnp.where(same & used, 1.0, 0.0))
    kx = low(jnp.where(used & ~same, NEG, 0.0))

    xs, gs = spread(own_x, main, outer), spread(own_g, main, outer)
    order = jnp.array([[0, 1, 2, 3], [1, 2, 0, 3], [2, 1, 3, 0], [3, 2, 1, 0]], jnp.int32)
    order = pick(order, 0, z)
    before, sums, hsum = None, 0.0, 0.0
    for a in range(N):
        got = run_block(order[a : a + 1], xs[a], gs[a], weights, tables, before)
        before, sums, hsum = got[:10], sums + got[10], hsum + got[11]
    qkv, mg, unit, normed, second, active, hg, ups, feed, back = before

    expand_share = mm(second, hg, TN)
    reduce_share = mm(active, ups, TN)
    expand_mine = fold_spread(fold_columns(expand_share.reshape(4, width // 4, -1), col, True), core, z)
    reduce_mine = fold_reduce(
        fold_columns(reduce_share.reshape(4, groups // 4, 128, width), col, False)
    )

    qkv = qkv.reshape(3, heads, HEAD, total)
    mg = mg.reshape(heads, HEAD, total)
    acc, done = None, None
    outs, backs = [], []
    gain = 0.0
    for place in (3, 2, 1, 0):
        mixed, jb, acc = run_attend(place, qkv, mg, kx, qx, tables, acc, done)
        done = [mixed, jb]
        at = slice(place * rows, (place + 1) * rows)
        mixed_here = mixed[:, :, at].reshape(-1, rows)
        jb_here = jb[:, :, :, at].reshape(-1, rows)
        outs.append(collect(low(mm(mixed_here, wd, TN) + wide(feed[at])), place, core))
        first_back = mm(jb_here, wj, TN)
        gain = gain + jnp.sum(first_back * wide(unit[at]), axis=0)
        backs.append(collect(low(first_back * first_gain + wide(back[at])), place, core))
    mixed, jb = done[0].reshape(-1, total), done[1].reshape(-1, total)
    jb_sum = jnp.sum(wide(jb), axis=1)

    joint_share = mm(normed, jb, (((0,), (1,)), ((), ())))
    dense_share = mm(mixed, ups)
    edge = 2 * heads * HEAD
    front_mine = fold_spread(fold_columns(joint_share[:, :edge].reshape(4, width // 4, edge), col, True), core, z)
    value_mine = fold_spread(
        fold_columns(joint_share[:, edge:].reshape(4, width // 4, edge // 2), col, False), core, z
    )
    dense_mine = fold_dense(fold_columns(dense_share.reshape(4, 2, HEAD // 2, width), col, False))

    parts = 4 * 2 * N
    jb_all = lax.dynamic_update_index_in_dim(
        jnp.zeros((3, heads, N, HEAD), jnp.float32), jb_sum.reshape(3, heads, HEAD), quarter, 2
    ).reshape(-1)
    hidden_all = lax.dynamic_update_index_in_dim(
        jnp.zeros((groups, N, 128), jnp.float32), jnp.sum(hsum, axis=0).reshape(groups, 128), quarter, 1
    ).reshape(-1)
    shift = jnp.dot(jb_sum[None], wide(wj), precision=lax.Precision.HIGHEST)[0]
    vectors = [
        gain,
        shift,
        jnp.sum(sums[0], axis=0),
        jnp.sum(sums[1], axis=0),
        jb_all[: 2 * width],
        jb_all[2 * width :],
        jnp.sum(wide(own_g), axis=0),
        hidden_all,
    ]
    packed = jnp.concatenate([v.reshape(parts, -1) for v in vectors], axis=1)
    packed = lax.psum_scatter(packed, ("col", "core", "blk"), scatter_dimension=0, tiled=True)[0]
    pieces, start = [], 0
    for v in vectors:
        pieces.append(packed[start : start + v.shape[0] // parts])
        start += v.shape[0] // parts

    def own_rows(list_of_halves):
        sides = [sum(wide(halves[c]) for halves in list_of_halves) for c in range(2)]
        return jnp.concatenate(sides, axis=0)

    inputs = wide(own_x)
    result = low(inputs + own_rows(outs) + (dense_bias + reduce_bias))
    _, unit_rows, inverse_root = normalize(inputs, first_gain, first_shift)
    scaled = own_rows(backs)
    input_back = inverse_root * (
        scaled
        - jnp.mean(scaled, axis=-1, keepdims=True)
        - unit_rows * jnp.mean(scaled * unit_rows, axis=-1, keepdims=True)
    )
    tokens_gradient = low(wide(own_g) + input_back)
    joint_mine = jnp.concatenate([front_mine, value_mine], axis=-1).reshape(N, -1, 3, heads, HEAD)
    joint_mine = wide(jnp.transpose(joint_mine, (1, 2, 3, 0, 4))).reshape(-1, 3 * width)
    expand_mine = expand_mine.reshape(N, -1, groups, 128)
    expand_mine = wide(jnp.transpose(expand_mine, (1, 2, 0, 3))).reshape(-1, units)
    return (
        result[None],
        tokens_gradient[None],
        *pieces[:4],
        joint_mine,
        pieces[4],
        pieces[5],
        dense_mine,
        pieces[6],
        expand_mine,
        pieces[7],
        reduce_mine,
        pieces[6],
    )


def solution(mesh):
    count, blocks = mesh.devices.shape
    split = blocks == N and count == 8
    if split:
        mesh = jax.sharding.Mesh(mesh.devices.reshape(count // 2, 2, blocks), ("col", "core", "blk"))
        batch = ("col", "core")
        every = ("col", "core", "blk")
    else:
        batch, every = "batch", ("batch", "blk")
    by_rows = P(batch, "blk", None)
    placed = (by_rows, P(batch, None)) + (P(),) * 12 + (by_rows,)
    vector, matrix = P(every), P(every, None)
    return jax.shard_map(
        split_local if split else local,
        mesh=mesh,
        in_specs=placed,
        out_specs=(
            by_rows,
            by_rows,
            vector,
            vector,
            vector,
            vector,
            matrix,
            vector,
            vector,
            matrix,
            vector,
            matrix,
            vector,
            matrix,
            vector,
        ),
        check_vma=False,
    )
```

```python
from functools import partial

import jax
import jax.numpy as jnp
from jax import lax
from jax.experimental import pallas as pl
from jax.experimental.pallas import tpu as pltpu
from jax.sharding import PartitionSpec as P

HEADS = 16
HEAD = 64
ROTARY = 16


EPSILON = 1e-05
MASKED = -1e30


def doc_tables(lengths, positions):
    doc_ends = jnp.cumsum(lengths, axis=-1)
    doc_starts = doc_ends - lengths
    doc_number = jnp.sum(
        (positions[None, :, None] >= doc_ends[:, None, :]).astype(jnp.int32), axis=-1
    )
    matches = (
        doc_number[:, :, None] == jnp.arange(lengths.shape[-1], dtype=jnp.int32)[None, None, :]
    )
    begins = jnp.sum(jnp.where(matches, doc_starts[:, None, :], 0), axis=-1)
    return (doc_number, positions[None, :] - begins)


def angles(offsets):
    half_width = ROTARY // 2
    inverse = 10000.0 ** (-2.0 * jnp.arange(half_width, dtype=jnp.float32) / ROTARY)
    phase = offsets.astype(jnp.float32)[..., None] * inverse
    return (jnp.cos(phase), jnp.sin(phase))


def rotate(values, cosine, sine_table, direction):
    half_width = cosine.shape[-1]
    lead_part = values[..., :half_width]
    tail_part = values[..., half_width : 2 * half_width]
    cosine = cosine[:, :, None, :]
    sine_table = sine_table[:, :, None, :] * direction
    return jnp.concatenate(
        [
            lead_part * cosine - tail_part * sine_table,
            tail_part * cosine + lead_part * sine_table,
            values[..., 2 * half_width :],
        ],
        axis=-1,
    )


def normalize(values, gain_row, shift_row):
    center = values - jnp.mean(values, axis=-1, keepdims=True)
    spread = jnp.mean(center * center, axis=-1, keepdims=True)
    inverse_root = lax.rsqrt(spread + EPSILON)
    unit_rows = center * inverse_root
    return (unit_rows * gain_row + shift_row, unit_rows, inverse_root)


def normalize_back(upstream, unit_rows, inverse_root, gain_row):
    scaled_back = upstream * gain_row
    input_back = inverse_root * (
        scaled_back
        - jnp.mean(scaled_back, axis=-1, keepdims=True)
        - unit_rows * jnp.mean(scaled_back * unit_rows, axis=-1, keepdims=True)
    )
    return (input_back, jnp.sum(upstream * unit_rows, axis=0), jnp.sum(upstream, axis=0))


def outer(left_rows, right_rows):
    return lax.dot_general(
        left_rows, right_rows, (((0,), (0,)), ((), ())), preferred_element_type=jnp.float32
    )


def against(left_rows, weight_rows):
    return lax.dot_general(
        left_rows, weight_rows, (((1,), (1,)), ((), ())), preferred_element_type=jnp.float32
    )


def over_piece(stepper, running, segment, stride):
    sub_count = segment.shape[1] // stride

    def one_turn(position, current):
        part_rows = lax.dynamic_slice_in_dim(segment, position * stride, stride, 1)
        return stepper(current, part_rows, position * stride)

    return lax.fori_loop(0, sub_count, one_turn, running)


def local(
    tokens,
    lengths,
    first_gain,
    first_shift,
    second_gain,
    second_shift,
    joint_weight,
    joint_bias,
    dense_weight,
    dense_bias,
    expand_weight,
    expand_bias,
    reduce_weight,
    reduce_bias,
    cotangent,
):
    sequences, stride, model_width = tokens.shape
    cycle_size = lax.axis_size("blk")
    seq_total = stride * cycle_size
    rank_here = lax.axis_index("blk")
    row_count = sequences * stride
    factor = HEAD ** (-0.5)
    head_shape = (sequences, stride, HEADS, HEAD)
    places = jnp.arange(seq_total, dtype=jnp.int32)
    number_all, offset_all = doc_tables(lengths, places)
    first_place = rank_here * stride
    query_number = lax.dynamic_slice_in_dim(number_all, first_place, stride, 1)
    query_offset = lax.dynamic_slice_in_dim(offset_all, first_place, stride, 1)
    query_place = first_place + jnp.arange(stride, dtype=jnp.int32)
    last_place = first_place + stride - 1
    cosine, sine_table = angles(query_offset)
    inputs = tokens.reshape(row_count, model_width).astype(jnp.float32)
    first_norm, first_unit, first_scale = normalize(inputs, first_gain, first_shift)
    normed = first_norm.astype(jnp.bfloat16)
    joint_out = jnp.dot(normed, joint_weight, preferred_element_type=jnp.float32) + joint_bias
    queries = rotate(
        joint_out[:, :model_width].reshape(head_shape), cosine, sine_table, 1.0
    ).astype(jnp.bfloat16)
    key_rows = rotate(
        joint_out[:, model_width : 2 * model_width].reshape(head_shape), cosine, sine_table, 1.0
    ).astype(jnp.bfloat16)
    value_rows = joint_out[:, 2 * model_width :].astype(jnp.bfloat16)
    pair_local = jnp.concatenate(
        [
            key_rows.reshape(sequences, stride, model_width),
            value_rows.reshape(sequences, stride, model_width),
        ],
        axis=-1,
    )

    def masked_scores(key_part, begin_row, row_span):
        key_number = lax.dynamic_slice_in_dim(number_all, begin_row, row_span, 1)
        key_place = begin_row + jnp.arange(row_span, dtype=jnp.int32)
        allowed = (query_number[:, :, None] == key_number[:, None, :]) & (
            key_place[None, None, :] <= query_place[None, :, None]
        )
        allowed = allowed[:, None]
        scores = (
            jnp.einsum("sqhd,skhd->shqk", queries, key_part, preferred_element_type=jnp.float32)
            * factor
        )
        return (jnp.where(allowed, scores, MASKED), allowed)

    def split_piece(segment):
        row_span = segment.shape[1]
        key_part = segment[:, :, :model_width].reshape(sequences, row_span, HEADS, HEAD)
        value_part = segment[:, :, model_width:].reshape(sequences, row_span, HEADS, HEAD)
        return (key_part, value_part, row_span)

    def gated(kernel):

        def stepper(running, segment, begin_row):
            return lax.cond(
                begin_row <= last_place,
                lambda current: kernel(current, segment, begin_row),
                lambda current: current,
                running,
            )

        return stepper

    def forward_kernel(running, segment, begin_row):
        row_peak, row_total, weighted = running
        key_part, value_part, row_span = split_piece(segment)
        scores, allowed = masked_scores(key_part, begin_row, row_span)
        new_peak = jnp.maximum(row_peak, jnp.max(scores, axis=-1))
        shares = jnp.where(allowed, jnp.exp(scores - new_peak[..., None]), 0.0)
        decay_factor = jnp.exp(row_peak - new_peak)
        row_total = row_total * decay_factor + jnp.sum(shares, axis=-1)
        update = jnp.einsum(
            "shqk,skhd->sqhd",
            shares.astype(jnp.bfloat16),
            value_part,
            preferred_element_type=jnp.float32,
        )
        weighted = weighted * jnp.transpose(decay_factor, (0, 2, 1))[..., None] + update
        return (new_peak, row_total, weighted)

    forward_step = gated(forward_kernel)
    initial = (
        jnp.full((sequences, HEADS, stride), MASKED, jnp.float32),
        jnp.zeros((sequences, HEADS, stride), jnp.float32),
        jnp.zeros(head_shape, jnp.float32),
    )
    forward_state = over_piece(
        forward_step, initial, lax.all_gather(pair_local, "blk", axis=1, tiled=True), stride
    )
    row_peak, row_total, weighted = forward_state
    mixed_full = weighted / jnp.transpose(row_total, (0, 2, 1))[..., None]
    log_total = row_peak + jnp.log(row_total)
    mixed = mixed_full.reshape(row_count, model_width).astype(jnp.bfloat16)
    attention_out = jnp.dot(mixed, dense_weight, preferred_element_type=jnp.float32) + dense_bias
    second_norm, second_unit, second_scale = normalize(inputs, second_gain, second_shift)
    second = second_norm.astype(jnp.bfloat16)
    hidden = jnp.dot(second, expand_weight, preferred_element_type=jnp.float32) + expand_bias
    active_full, gelu_pull = jax.vjp(partial(jax.nn.gelu, approximate=False), hidden)
    active = active_full.astype(jnp.bfloat16)
    feed_out = jnp.dot(active, reduce_weight, preferred_element_type=jnp.float32) + reduce_bias
    result = (
        (inputs + attention_out + feed_out)
        .astype(jnp.bfloat16)
        .reshape(sequences, stride, model_width)
    )
    upstream = cotangent.reshape(row_count, model_width)
    dense_grad = outer(mixed, upstream)
    bias_total = jnp.sum(upstream, axis=0, dtype=jnp.float32)
    reduce_grad = outer(active, upstream)
    hidden_grad = gelu_pull(against(upstream, reduce_weight))[0].astype(jnp.bfloat16)
    expand_grad = outer(second, hidden_grad)
    hidden_total = jnp.sum(hidden_grad, axis=0, dtype=jnp.float32)
    input_two, gain_second, shift_second = normalize_back(
        against(hidden_grad, expand_weight), second_unit, second_scale, second_gain
    )
    mixed_grad = against(upstream, dense_weight).astype(jnp.bfloat16)
    out_heads = mixed_grad.reshape(head_shape)
    delta_rows = jnp.transpose(jnp.sum(out_heads * mixed_full, axis=-1), (0, 2, 1))

    def backward_kernel(running, segment, begin_row):
        key_part, value_part, row_span = split_piece(segment)
        scores, allowed = masked_scores(key_part, begin_row, row_span)
        weights_now = jnp.where(allowed, jnp.exp(scores - log_total[..., None]), 0.0)
        weight_grad = jnp.einsum(
            "sqhd,skhd->shqk", out_heads, value_part, preferred_element_type=jnp.float32
        )
        score_grad = (weights_now * (weight_grad - delta_rows[..., None])).astype(jnp.bfloat16)
        query_grad = (
            running[0]
            + jnp.einsum(
                "shqk,skhd->sqhd", score_grad, key_part, preferred_element_type=jnp.float32
            )
            * factor
        )
        value_grad = jnp.einsum(
            "shqk,sqhd->skhd",
            weights_now.astype(jnp.bfloat16),
            out_heads,
            preferred_element_type=jnp.float32,
        )
        key_grad = (
            jnp.einsum("shqk,sqhd->skhd", score_grad, queries, preferred_element_type=jnp.float32)
            * factor
        )
        fresh_rows = jnp.concatenate(
            [
                key_grad.reshape(sequences, row_span, model_width),
                value_grad.reshape(sequences, row_span, model_width),
            ],
            axis=-1,
        )
        pair_grad = lax.dynamic_update_slice_in_dim(running[1], fresh_rows, begin_row, 1)
        return (query_grad, pair_grad)

    backward_step = gated(backward_kernel)
    back_initial = (
        jnp.zeros(head_shape, jnp.float32),
        jnp.zeros((sequences, seq_total, 2 * model_width), jnp.float32),
    )
    back_state = over_piece(
        backward_step, back_initial, lax.all_gather(pair_local, "blk", axis=1, tiled=True), stride
    )
    query_grad = back_state[0]
    pair_mine = lax.psum_scatter(back_state[1], "blk", scatter_dimension=1, tiled=True)
    query_back = rotate(query_grad, cosine, sine_table, -1.0).reshape(row_count, model_width)
    key_back = rotate(
        pair_mine[:, :, :model_width].reshape(head_shape), cosine, sine_table, -1.0
    ).reshape(row_count, model_width)
    value_back = pair_mine[:, :, model_width:].reshape(row_count, model_width)
    joint_back = jnp.concatenate([query_back, key_back, value_back], axis=-1).astype(jnp.bfloat16)
    joint_grad = outer(normed, joint_back)
    joint_total = jnp.sum(joint_back, axis=0, dtype=jnp.float32)
    front_total = joint_total[: 2 * model_width]
    value_total = joint_total[2 * model_width :]
    input_one, gain_first, shift_first = normalize_back(
        against(joint_back, joint_weight), first_unit, first_scale, first_gain
    )
    input_total = (
        (upstream.astype(jnp.float32) + input_one + input_two)
        .astype(jnp.bfloat16)
        .reshape(sequences, stride, model_width)
    )
    summed = (
        lax.psum_scatter(gain_first, ("batch", "blk"), scatter_dimension=0, tiled=True),
        lax.psum_scatter(shift_first, ("batch", "blk"), scatter_dimension=0, tiled=True),
        lax.psum_scatter(gain_second, ("batch", "blk"), scatter_dimension=0, tiled=True),
        lax.psum_scatter(shift_second, ("batch", "blk"), scatter_dimension=0, tiled=True),
        lax.psum_scatter(joint_grad, ("batch", "blk"), scatter_dimension=0, tiled=True),
        lax.psum_scatter(front_total, ("batch", "blk"), scatter_dimension=0, tiled=True),
        lax.psum_scatter(value_total, ("batch", "blk"), scatter_dimension=0, tiled=True),
        lax.psum_scatter(dense_grad, ("batch", "blk"), scatter_dimension=0, tiled=True),
        lax.psum_scatter(bias_total, ("batch", "blk"), scatter_dimension=0, tiled=True),
        lax.psum_scatter(expand_grad, ("batch", "blk"), scatter_dimension=0, tiled=True),
        lax.psum_scatter(hidden_total, ("batch", "blk"), scatter_dimension=0, tiled=True),
        lax.psum_scatter(reduce_grad, ("batch", "blk"), scatter_dimension=0, tiled=True),
    )
    return (
        result,
        input_total,
        summed[0],
        summed[1],
        summed[2],
        summed[3],
        summed[4],
        summed[5],
        summed[6],
        summed[7],
        summed[8],
        summed[9],
        summed[10],
        summed[11],
        summed[8],
    )


BQ = 512
N = 4
TM = 256
VMEM = 56 * 1024 * 1024
NEG = -1e30
NN = (((1,), (0,)), ((), ()))
NT = (((1,), (1,)), ((), ()))
TN = (((0,), (0,)), ((), ()))


def mm(left, right, form=NN):
    return lax.dot_general(left, right, form, preferred_element_type=jnp.float32)


def low(value):
    return value.astype(jnp.bfloat16)


def wide(value):
    return value.astype(jnp.float32)


def gelu_parts(hidden):
    size = jnp.abs(hidden) * (0.5**0.5)
    bell = jnp.exp(-(size * size))
    base = 1.0 + 0.3275911 * size
    guess = pl.reciprocal(base, approx=True)
    t = guess * (2.0 - base * guess)
    series = t * (
        0.5 * 0.254829592
        + t
        * (
            0.5 * -0.284496736
            + t * (0.5 * 1.421413741 + t * (0.5 * -1.453152027 + t * (0.5 * 1.061405429)))
        )
    )
    tail = series * bell
    return (jnp.where(hidden >= 0.0, 1.0 - tail, tail), bell)


def fold_rows(value):
    rows, columns = value.shape
    return jnp.sum(value.reshape(rows // 8, 8, columns), axis=0)


def prepare_kernel(spot_ref, wj_ref, wd_ref, we_ref, wr_ref, wj_out, wd_out, we_out, wr_out):
    turned = wj_ref[...].T
    wj_out[...] = jnp.where(lax.rem(spot_ref[0], 2) == 0, turned[:HEAD], turned[HEAD:])
    wd_out[...] = wd_ref[...]
    we_out[...] = we_ref[...]
    wr_out[...] = wr_ref[...]


def prepare(quarter, joint_weight, dense_weight, expand_weight, reduce_weight):
    width, units = expand_weight.shape
    heads = HEADS // N
    groups = units // (N * 128)
    kinds = 3 * heads
    pair = lambda s, spot: (0, (s // heads) * (HEADS // 2) + (s % heads) * (N // 2) + spot[0] // 2)
    row = lambda s: jnp.minimum(s, heads - 1)
    unit = lambda s: jnp.minimum(s, groups - 1)
    group = lambda s, spot: N * unit(s) + lax.rem(spot[0] + 2 * lax.rem(unit(s), 2), N)
    shape = lambda *dims: jax.ShapeDtypeStruct(dims, jnp.bfloat16)
    return pl.pallas_call(
        prepare_kernel,
        grid_spec=pltpu.PrefetchScalarGridSpec(
            num_scalar_prefetch=1,
            grid=(kinds,),
            in_specs=[
                pl.BlockSpec((width, 2 * HEAD), pair),
                pl.BlockSpec((HEAD, width), lambda s, spot: (N * row(s) + spot[0], 0)),
                pl.BlockSpec((width, 128), lambda s, spot: (0, group(s, spot))),
                pl.BlockSpec((128, width), lambda s, spot: (group(s, spot), 0)),
            ],
            out_specs=[
                pl.BlockSpec((HEAD, width), lambda s, spot: (s, 0)),
                pl.BlockSpec((HEAD, width), lambda s, spot: (row(s), 0)),
                pl.BlockSpec((width, 128), lambda s, spot: (0, unit(s))),
                pl.BlockSpec((128, width), lambda s, spot: (unit(s), 0)),
            ],
        ),
        out_shape=[
            shape(kinds * HEAD, width),
            shape(heads * HEAD, width),
            shape(width, groups * 128),
            shape(groups * 128, width),
        ],
        cost_estimate=pl.CostEstimate(flops=0, bytes_accessed=14 * width * width, transcendentals=0),
    )(quarter.reshape(1), joint_weight, dense_weight, expand_weight, reduce_weight)


def block_at(place, j):
    return place * (place + 1) // 2 + j


def forward_kernel(held, qkv_ref, kx_ref, qx_ref, *refs):
    mixed_ref, full_ref, inverse_ref, share_ref, key_ref, *scores = refs[held:]
    key_ref[...] = jnp.concatenate([qkv_ref[1, 0], kx_ref[...]], axis=0).T
    total = kx_ref.shape[1]
    state = {}

    def score(place, j):
        here = slice(place * BQ, (place + 1) * BQ)
        at = slice(j * BQ, (j + 1) * BQ)
        if j == 0:
            query_x = jnp.concatenate([qkv_ref[0, 0, :, here], qx_ref[:, here]], axis=0)
            state[place] = [query_x, jnp.full((8, BQ), NEG * 2, jnp.float32)]
        found = mm(key_ref[at, :], state[place][0])
        if j == place:
            key_row = lax.broadcasted_iota(jnp.int32, (BQ, BQ), 0)
            query_column = lax.broadcasted_iota(jnp.int32, (BQ, BQ), 1)
            found = jnp.where(key_row <= query_column, found, NEG)
        scores[place % 2][at, :] = found
        state[place][1] = jnp.maximum(state[place][1], jnp.max(found.reshape(BQ // 8, 8, BQ), axis=0))

    def weigh(place, j):
        here = slice(place * BQ, (place + 1) * BQ)
        at = slice(j * BQ, (j + 1) * BQ)
        if j == 0:
            peak = jnp.max(state[place][1], axis=0, keepdims=True)
            state[place] = [peak, jnp.zeros((8, BQ), jnp.float32), jnp.zeros((HEAD, BQ), jnp.float32)]
        share = jnp.exp(scores[place % 2][at, :] - state[place][0])
        state[place][1] = state[place][1] + jnp.sum(share.reshape(BQ // 8, 8, BQ), axis=0)
        share = low(share)
        share_ref[0, block_at(place, j)] = share
        state[place][2] = state[place][2] + mm(qkv_ref[2, 0, :, at], share)
        if j == place:
            inverse = 1.0 / jnp.sum(state[place][1], axis=0, keepdims=True)
            mixed = state[place][2] * inverse
            inverse_ref[0, :, here] = inverse
            full_ref[0, :, here] = mixed
            mixed_ref[0, :, here] = low(mixed)

    places = list(range(total // BQ))
    for j in range(places[0] + 1):
        score(places[0], j)
    for n, place in enumerate(places):
        for j in range(places[-1] + 2):
            if n + 1 < len(places) and j <= places[n + 1]:
                score(places[n + 1], j)
            if j <= place:
                weigh(place, j)


def attend_forward(qkv, kx, qx, first, count, before):
    _, heads, _, total = qkv.shape
    places = total // BQ
    blocks = block_at(places, 0)
    head_rows = lambda rows: pl.BlockSpec((1, rows, total), lambda h: (first + h, 0, 0))
    operands = [qkv, kx, qx]
    in_specs = [
        pl.BlockSpec((3, 1, HEAD, total), lambda h: (0, first + h, 0, 0)),
        pl.BlockSpec((HEAD, total), lambda h: (0, 0)),
        pl.BlockSpec((HEAD, total), lambda h: (0, 0)),
    ]
    aliases = {}
    if before is not None:
        for index, array in enumerate(before):
            aliases[len(operands)] = index
            operands.append(array)
            in_specs.append(pl.BlockSpec(memory_space=pl.ANY))
    return pl.pallas_call(
        partial(forward_kernel, len(aliases)),
        grid=(count,),
        in_specs=in_specs,
        out_specs=[
            head_rows(HEAD),
            head_rows(HEAD),
            head_rows(1),
            pl.BlockSpec((1, blocks, BQ, BQ), lambda h: (first + h, 0, 0, 0)),
        ],
        out_shape=[
            jax.ShapeDtypeStruct((heads, HEAD, total), jnp.bfloat16),
            jax.ShapeDtypeStruct((heads, HEAD, total), jnp.float32),
            jax.ShapeDtypeStruct((heads, 1, total), jnp.float32),
            jax.ShapeDtypeStruct((heads, blocks, BQ, BQ), jnp.bfloat16),
        ],
        scratch_shapes=[pltpu.VMEM((total, 2 * HEAD), jnp.bfloat16)] + [pltpu.VMEM((total, BQ), jnp.float32)] * 2,
        input_output_aliases=aliases,
        compiler_params=pltpu.CompilerParams(vmem_limit_bytes=VMEM),
        cost_estimate=pl.CostEstimate(
            flops=16 * HEAD * count * blocks * BQ * BQ,
            bytes_accessed=2 * count * blocks * BQ * BQ,
            transcendentals=count * blocks * BQ * BQ,
        ),
    )(*operands)


def backward_kernel(qkv_ref, mg_ref, full_ref, inverse_ref, share_ref, cos_ref, sin_ref, jb_ref, value_ref, acc_ref):
    total = cos_ref.shape[1]
    ones = (lax.broadcasted_iota(jnp.int32, (HEAD, total), 0) < 3).astype(jnp.bfloat16)
    value_ref[...] = jnp.concatenate([qkv_ref[2, 0], ones], axis=0).T
    half = ROTARY // 2
    blank = jnp.zeros((HEAD, BQ), jnp.bfloat16)
    row = lax.broadcasted_iota(jnp.int32, (HEAD, BQ), 0)

    def turn_back(rows, at):
        lead, tail = rows[:half], rows[half : 2 * half]
        cosine, sine = cos_ref[:, at], sin_ref[:, at]
        return low(
            jnp.concatenate([lead * cosine + tail * sine, tail * cosine - lead * sine, rows[2 * half :]], axis=0)
        )

    for place in reversed(range(total // BQ)):
        here = slice(place * BQ, (place + 1) * BQ)
        query_t = qkv_ref[0, 0, :, here]
        mg = low(wide(mg_ref[0, :, here]) * inverse_ref[0, :, here])
        delta = -jnp.sum(wide(mg) * full_ref[0, :, here], axis=0, keepdims=True)
        first = low(delta)
        rest = delta - wide(first)
        middle = low(rest)
        final = low(rest - wide(middle))
        extra = jnp.where(
            row == 0, wide(first), jnp.where(row == 1, wide(middle), jnp.where(row == 2, wide(final), 0.0))
        )
        mg_x = jnp.concatenate([mg, low(extra)], axis=0)
        mg_v = jnp.concatenate([blank, mg], axis=0)
        query_k = jnp.concatenate([query_t, blank], axis=0)
        query_grad = jnp.zeros((HEAD, BQ), jnp.float32)
        for j in range(place + 1):
            at = slice(j * BQ, (j + 1) * BQ)
            share = share_ref[0, block_at(place, j)]
            score_grad = low(wide(share) * mm(value_ref[at, :], mg_x))
            pair = mm(share, mg_v, NT) + mm(score_grad, query_k, NT)
            query_grad = query_grad + mm(qkv_ref[1, 0, :, at], score_grad)
            if (place + 1) * BQ < total:
                pair = pair + acc_ref[at, :]
            if j < place:
                acc_ref[at, :] = pair
            else:
                pair_t = pair.T
                jb_ref[1, 0, :, at] = turn_back(pair_t[:HEAD], at)
                jb_ref[2, 0, :, at] = low(pair_t[HEAD:])
        jb_ref[0, 0, :, here] = turn_back(query_grad * (HEAD**-0.5), here)


def attend_backward(qkv, mg, full, inverse, shares, tables):
    _, heads, _, total = qkv.shape
    blocks = shares.shape[1]
    head_rows = lambda rows: pl.BlockSpec((1, rows, total), lambda h: (h, 0, 0))
    kinds = pl.BlockSpec((3, 1, HEAD, total), lambda h: (0, h, 0, 0))
    table = pl.BlockSpec((ROTARY // 2, total), lambda h: (0, 0))
    return pl.pallas_call(
        backward_kernel,
        grid=(heads,),
        in_specs=[
            kinds,
            head_rows(HEAD),
            head_rows(HEAD),
            head_rows(1),
            pl.BlockSpec((1, blocks, BQ, BQ), lambda h: (h, 0, 0, 0)),
            table,
            table,
        ],
        out_specs=kinds,
        out_shape=jax.ShapeDtypeStruct((3, heads, HEAD, total), jnp.bfloat16),
        scratch_shapes=[
            pltpu.VMEM((total, 2 * HEAD), jnp.bfloat16),
            pltpu.VMEM((total, 2 * HEAD), jnp.float32),
        ],
        compiler_params=pltpu.CompilerParams(vmem_limit_bytes=VMEM),
        cost_estimate=pl.CostEstimate(
            flops=32 * HEAD * heads * blocks * BQ * BQ,
            bytes_accessed=2 * heads * blocks * BQ * BQ,
            transcendentals=0,
        ),
    )(qkv, mg, full, inverse, shares, *tables)


def token_kernel(count, sub, chunk, spot_ref, *refs):
    a_ref, b_ref = refs[0], refs[count - 1]
    (wj_ref, bj_ref, we_ref, be_ref, wr_ref, g1_ref, s1_ref, g2_ref, s2_ref, cos_ref, sin_ref) = refs[count : count + 11]
    qkv_ref, unit_ref, second_ref, active_ref, slope_ref, feed_ref = refs[-6:]
    step = pl.program_id(0)
    pick_b = spot_ref[pl.num_programs(0) + step] == 1
    rows = a_ref.shape[0]
    half = ROTARY // 2
    part = wj_ref.shape[0] // 3
    for top in range(0, rows, sub):
        at = slice(top, top + sub)
        x = wide(a_ref[at, :] if count == 1 else jnp.where(pick_b, b_ref[at, :], a_ref[at, :]))
        center = x - jnp.mean(x, axis=-1, keepdims=True)
        scale = lax.rsqrt(jnp.mean(center * center, axis=-1, keepdims=True) + EPSILON)
        unit = center * scale
        unit_ref[at, :] = low(unit)
        normed = low(unit * g1_ref[...] + s1_ref[...])
        second = low(unit * g2_ref[...] + s2_ref[...])
        second_ref[at, :] = second
        joint = mm(wj_ref[...], normed, NT) + bj_ref[...]
        cosine, sine = cos_ref[:, at], sin_ref[:, at]
        for kind in range(3):
            for head in range(part // HEAD):
                first = kind * part + head * HEAD
                turned = joint[first : first + HEAD]
                if kind < 2:
                    lead, tail = turned[:half], turned[half : 2 * half]
                    turned = jnp.concatenate(
                        [lead * cosine - tail * sine, tail * cosine + lead * sine, turned[2 * half :]], axis=0
                    )
                if kind == 0:
                    turned = turned * (HEAD**-0.5)
                qkv_ref[first : first + HEAD, at] = low(turned)
        for left in range(0, we_ref.shape[1], chunk):
            over = slice(left, left + chunk)
            hidden = mm(second, we_ref[:, over]) + be_ref[:, over]
            share, bell = gelu_parts(hidden)
            active_ref[at, over] = low(hidden * share)
            slope_ref[at, over] = low(share + hidden * bell * 0.3989422804014327)
    for top in range(0, rows, sub):
        at = slice(top, top + sub)
        feed_ref[at, :] = low(mm(active_ref[at, :], wr_ref[...]))


def run_tokens(slot, spot, a, b, weights, tables, before, sub=256, chunk=256):
    rows, width = a.shape
    total = tables[0].shape[1]
    wj, bj, we, be, wr, g1, s1, g2, s2 = weights
    units = we.shape[1]
    steps = spot.shape[0] // 2

    def whole(array):
        return pl.BlockSpec(array.shape, lambda i, spot: (0,) * array.ndim)

    column = lambda height: pl.BlockSpec((height, rows), lambda i, spot: (0, spot[i]))
    placed = pl.BlockSpec((rows, width), lambda i, spot: (spot[i], 0))
    arrived = lambda size: pl.BlockSpec((rows, size), lambda i, spot: (slot + i, 0))
    data = [a] if a is b else [a, b]
    in_specs = [whole(w) for w in (*data, *weights)] + [column(ROTARY // 2)] * 2
    out_specs = [column(wj.shape[0]), placed, arrived(width), arrived(units), arrived(units), placed]
    shape = lambda *dims: jax.ShapeDtypeStruct(dims, jnp.bfloat16)
    out_shape = [shape(wj.shape[0], total)] + [shape(total, size) for size in (width, width, units, units, width)]
    operands = [spot, *data, *weights, *tables]
    aliases = {}
    if before is not None:
        for index, array in enumerate(before):
            aliases[len(operands)] = index
            operands.append(array)
            in_specs.append(pl.BlockSpec(memory_space=pl.ANY))
    products = steps * rows * width * (wj.shape[0] + 2 * units)
    return pl.pallas_call(
        partial(token_kernel, len(data), sub, chunk),
        grid_spec=pltpu.PrefetchScalarGridSpec(
            num_scalar_prefetch=1, grid=(steps,), in_specs=in_specs, out_specs=out_specs
        ),
        out_shape=out_shape,
        input_output_aliases=aliases,
        compiler_params=pltpu.CompilerParams(vmem_limit_bytes=VMEM),
        cost_estimate=pl.CostEstimate(
            flops=4 * products, bytes_accessed=16 * steps * rows * width, transcendentals=steps * rows * units
        ),
    )(*operands)


def upstream_kernel(chunk, spot_ref, *refs):
    sources = refs[:6]
    (wd_ref, we_ref, wr_ref, g2_ref, unit_ref, slope_ref) = refs[6:12]
    (mg_ref, back_ref, up_ref, hg_ref, sums_ref, hsum_ref) = refs[12:18]
    buffer, sems = refs[18:]
    step = pl.program_id(0)
    steps = pl.num_programs(0)
    slot = lax.rem(step, 2)

    def fetch(which, into):
        for k, source in enumerate(sources):

            @pl.when(spot_ref[steps + which] == k)
            def _():
                pltpu.make_async_copy(source, buffer.at[into], sems.at[into]).start()

    @pl.when(step == 0)
    def _():
        fetch(0, 0)
        sums_ref[...] = jnp.zeros_like(sums_ref)
        hsum_ref[...] = jnp.zeros_like(hsum_ref)

    @pl.when(step + 1 < steps)
    def _():
        fetch(step + 1, 1 - slot)

    pltpu.make_async_copy(sources[0], buffer.at[slot], sems.at[slot]).wait()
    up = buffer[slot]
    up_ref[...] = up
    mg_ref[...] = low(mm(wd_ref[...], up, NT))
    for left in range(0, we_ref.shape[1], chunk):
        over = slice(left, left + chunk)
        piece = low(mm(up, wr_ref[over, :], NT) * wide(slope_ref[:, over]))
        hg_ref[:, over] = piece
        hsum_ref[:, over] += fold_rows(wide(piece))
    for left in range(0, we_ref.shape[0], chunk):
        over = slice(left, left + chunk)
        back = mm(hg_ref[...], we_ref[over, :], NT)
        back_ref[:, over] = low(back * g2_ref[:, over])
        sums_ref[0, :, over] += fold_rows(back * wide(unit_ref[:, over]))
        sums_ref[1, :, over] += fold_rows(back)


def run_upstream(spot, sources, weights, unit, slope, chunk=256):
    rows, width = sources[0].shape
    total = unit.shape[0]
    wd, we, wr, g2 = weights
    units = we.shape[1]
    steps = total // rows

    def whole(array):
        return pl.BlockSpec(array.shape, lambda i, spot: (0,) * array.ndim)

    fixed = lambda *dims: pl.BlockSpec(dims, lambda i, spot: (0,) * len(dims))
    column = lambda height: pl.BlockSpec((height, rows), lambda i, spot: (0, spot[i]))
    placed = pl.BlockSpec((rows, width), lambda i, spot: (spot[i], 0))
    arrived = lambda size: pl.BlockSpec((rows, size), lambda i, spot: (i, 0))
    in_specs = [pl.BlockSpec(memory_space=pl.ANY)] * 6 + [whole(w) for w in weights] + [placed, arrived(units)]
    out_specs = [column(wd.shape[0]), placed, arrived(width), arrived(units), fixed(2, 8, width), fixed(8, units)]
    shape = lambda *dims: jax.ShapeDtypeStruct(dims, jnp.bfloat16)
    out_shape = [
        shape(wd.shape[0], total),
        shape(total, width),
        shape(total, width),
        shape(total, units),
        jax.ShapeDtypeStruct((2, 8, width), jnp.float32),
        jax.ShapeDtypeStruct((8, units), jnp.float32),
    ]
    return pl.pallas_call(
        partial(upstream_kernel, chunk),
        grid_spec=pltpu.PrefetchScalarGridSpec(
            num_scalar_prefetch=1,
            grid=(steps,),
            in_specs=in_specs,
            out_specs=out_specs,
            scratch_shapes=[
                pltpu.VMEM((2, rows, width), jnp.bfloat16),
                pltpu.SemaphoreType.DMA((2,)),
            ],
        ),
        out_shape=out_shape,
        compiler_params=pltpu.CompilerParams(vmem_limit_bytes=VMEM),
        cost_estimate=pl.CostEstimate(
            flops=3 * total * width * (wd.shape[0] + 2 * units), bytes_accessed=12 * total * width, transcendentals=0
        ),
    )(spot, *sources, wd, we, wr, g2, unit, slope)


def weight_kernel(spot_ref, second_ref, hg_ref, active_ref, up_ref, mixed_ref, *refs):
    shares, (expand_sum, reduce_sum, dense_sum) = refs[:4], refs[4:]
    step = pl.program_id(0)
    steps = pl.num_programs(0)

    @pl.when(step == 0)
    def _():
        expand_sum[...] = jnp.zeros_like(expand_sum)
        reduce_sum[...] = jnp.zeros_like(reduce_sum)
        dense_sum[...] = jnp.zeros_like(dense_sum)

    up = up_ref[...]
    dense_sum[...] += mm(mixed_ref[...], up)
    expand_sum[...] += mm(second_ref[...], hg_ref[...], TN)
    reduce_sum[...] += mm(active_ref[...], up, TN)

    @pl.when(step == steps - 1)
    def _():
        col = spot_ref[steps]
        large, small = expand_sum.shape[0] // 4, dense_sum.shape[0] // 4
        for k, share in enumerate(shares):
            i = k + col - 2 * (col & k)
            at = pl.ds(pl.multiple_of(i * large, large), large)
            share[:large] = low(expand_sum[at, :])
            share[large : 2 * large] = low(reduce_sum[at, :])
            share[2 * large :] = low(dense_sum[pl.ds(pl.multiple_of(i * small, small), small), :])


def weight_gradients(spot, second, hg, active, ups, mixed):
    total, width = second.shape
    units = hg.shape[1]
    rows = total // N
    height = mixed.shape[0]
    fixed = lambda *dims: pl.BlockSpec(dims, lambda i, spot: (0,) * len(dims))
    arrived = lambda size: pl.BlockSpec((rows, size), lambda i, spot: (i, 0))
    dims = (width // 4 + units // 4 + height // 4, width)
    return pl.pallas_call(
        weight_kernel,
        grid_spec=pltpu.PrefetchScalarGridSpec(
            num_scalar_prefetch=1,
            grid=(N,),
            in_specs=[
                arrived(width),
                arrived(units),
                arrived(units),
                arrived(width),
                pl.BlockSpec((height, rows), lambda i, spot: (0, spot[i])),
            ],
            out_specs=[fixed(*dims)] * 4,
            scratch_shapes=[
                pltpu.VMEM((width, units), jnp.float32),
                pltpu.VMEM((units, width), jnp.float32),
                pltpu.VMEM((height, width), jnp.float32),
            ],
        ),
        out_shape=[jax.ShapeDtypeStruct(dims, jnp.bfloat16)] * 4,
        compiler_params=pltpu.CompilerParams(vmem_limit_bytes=VMEM),
        cost_estimate=pl.CostEstimate(
            flops=3 * total * width * (height + 2 * units), bytes_accessed=8 * total * width, transcendentals=0
        ),
    )(spot, second, hg, active, ups, mixed)


def deliver_kernel(order_ref, left_ref, weight_ref, add_ref, *refs):
    del order_ref
    send_ref, keep_ref = refs[-2:]
    step = pl.program_id(0)
    value = mm(left_ref[...], weight_ref[...], TN)
    if len(refs) > 2:
        value = value * refs[0][...]
    value = low(value + wide(add_ref[...]))

    @pl.when(step < pl.num_programs(0) // 2)
    def _():
        send_ref[...] = value

    @pl.when(step >= pl.num_programs(0) // 2)
    def _():
        keep_ref[...] = value


def deliver(order, left, weight, add, gain=None):
    depth, total = left.shape
    width = weight.shape[1]
    steps = N
    tile = total // N
    rows = pl.BlockSpec((tile, width), lambda s, order: (order[s], 0))
    in_specs = [
        pl.BlockSpec((depth, tile), lambda s, order: (0, order[s])),
        pl.BlockSpec((depth, width), lambda s, order: (0, 0)),
        rows,
    ]
    operands = [left, weight, add]
    if gain is not None:
        in_specs.append(pl.BlockSpec((1, width), lambda s, order: (0, 0)))
        operands.append(gain)
    return pl.pallas_call(
        deliver_kernel,
        grid_spec=pltpu.PrefetchScalarGridSpec(
            num_scalar_prefetch=1,
            grid=(steps,),
            in_specs=in_specs,
            out_specs=[
                pl.BlockSpec((tile, width), lambda s, order: (jnp.minimum(s, steps // 2 - 1), 0)),
                pl.BlockSpec((tile, width), lambda s, order: (jnp.maximum(s - steps // 2, 0), 0)),
            ],
        ),
        out_shape=[jax.ShapeDtypeStruct((total // 2, width), jnp.bfloat16)] * 2,
        compiler_params=pltpu.CompilerParams(vmem_limit_bytes=VMEM),
        cost_estimate=pl.CostEstimate(
            flops=0, bytes_accessed=0, transcendentals=0
        ),
    )(order, *operands)


def joint_kernel(spot_ref, jb_ref, unit_ref, wj_ref, gain_ref, shift_ref, sums_ref, up_ref, hsum_ref, *refs):
    shares, (vector_ref, total_ref, turned_ref, sum_ref) = refs[:4], refs[4:]
    step = pl.program_id(0)
    jb = jb_ref[...]
    height, tile = jb.shape
    width = unit_ref.shape[1]

    @pl.when(step == 0)
    def _():
        total_ref[...] = jnp.zeros_like(total_ref)
        sum_ref[...] = jnp.zeros_like(sum_ref)

    total_ref[...] += mm(jb, unit_ref[...])
    sum_ref[...] += mm(jb, jnp.ones((tile, 128), jnp.bfloat16))

    @pl.when(step == pl.num_programs(0) - 1)
    def _():
        col, quarter = spot_ref[0], spot_ref[1]
        gain = jnp.sum(total_ref[...] * wide(wj_ref[...]), axis=0, keepdims=True)
        turned_ref[...] = (total_ref[...] * gain_ref[...] + sum_ref[:, :1] * shift_ref[...]).T
        part = width // 4
        for k, share in enumerate(shares):
            i = k + col - 2 * (col & k)
            share[:part] = low(turned_ref[pl.ds(pl.multiple_of(i * part, part), part), :])
        jb_sum = sum_ref[...].T[:1]
        first = low(jb_sum)
        rest = jb_sum - wide(first)
        middle = low(rest)
        final = low(rest - wide(middle))
        shift = mm(jnp.concatenate([first, middle, final], axis=0), wj_ref[...])
        rows = [
            gain,
            jnp.sum(shift, axis=0, keepdims=True),
            jnp.sum(sums_ref[0], axis=0, keepdims=True),
            jnp.sum(sums_ref[1], axis=0, keepdims=True),
            jnp.sum(up_ref[...], axis=0, keepdims=True),
        ]
        jb_sum = jnp.concatenate([jb_sum, jnp.zeros((1, width - height), jnp.float32)], axis=1)
        for whole in (jnp.sum(hsum_ref[...], axis=0, keepdims=True), jb_sum):
            rows += [jnp.where(quarter == i, whole, 0.0) for i in range(N)]
        rows.append(jnp.zeros((3, width), jnp.float32))
        vector = jnp.concatenate(rows, axis=0)
        vector_ref[...] = vector
        coarse = low(vector)
        fine = low(vector - wide(coarse))
        rest = jnp.zeros((16, 2 * height - width), jnp.bfloat16)
        pieces = [coarse[:, :height], fine[:, :height]]
        pieces += [jnp.concatenate([piece[:, height:], rest], axis=1) for piece in (coarse, fine)]
        for share in shares[1:]:
            for n, piece in enumerate(pieces):
                share[part + 16 * n : part + 16 * (n + 1)] = piece


def joint_gradient(spot, jb, unit, wj, gain, shift, sums, up_sum, hsum):
    height, total = jb.shape
    width = unit.shape[1]
    tile = total // N
    fixed = lambda *dims: pl.BlockSpec(dims, lambda s, spot: (0,) * len(dims))
    shapes = [(width // 4, height)] + [(width // 4 + 64, height)] * 3
    return pl.pallas_call(
        joint_kernel,
        grid_spec=pltpu.PrefetchScalarGridSpec(
            num_scalar_prefetch=1,
            grid=(N,),
            in_specs=[
                pl.BlockSpec((height, tile), lambda s, spot: (0, s)),
                pl.BlockSpec((tile, width), lambda s, spot: (s, 0)),
                fixed(height, width),
                fixed(1, width),
                fixed(1, width),
                fixed(2, 8, width),
                fixed(8, width),
                fixed(*hsum.shape),
            ],
            out_specs=[fixed(*dims) for dims in shapes] + [fixed(16, width)],
            scratch_shapes=[
                pltpu.VMEM((height, width), jnp.float32),
                pltpu.VMEM((width, height), jnp.float32),
                pltpu.VMEM((height, 128), jnp.float32),
            ],
        ),
        out_shape=[jax.ShapeDtypeStruct(dims, jnp.bfloat16) for dims in shapes]
        + [jax.ShapeDtypeStruct((16, width), jnp.float32)],
        compiler_params=pltpu.CompilerParams(vmem_limit_bytes=VMEM),
        cost_estimate=pl.CostEstimate(
            flops=0, bytes_accessed=0, transcendentals=0
        ),
    )(spot, jb, unit, wj, gain, shift, sums, up_sum, hsum)


def pack(vector, width):
    coarse = low(vector)
    fine = low(vector - wide(coarse))
    rest = jnp.zeros((vector.shape[0], 2 * width - vector.shape[1]), jnp.bfloat16)
    pieces = [coarse[:, :width], fine[:, :width]]
    pieces += [jnp.concatenate([piece[:, width:], rest], axis=1) for piece in (coarse, fine)]
    return jnp.concatenate(pieces, axis=0)


def unpack(rows, size):
    rows = wide(rows).reshape(4, 16, -1)
    return jnp.concatenate([rows[0] + rows[1], (rows[2] + rows[3])[:, : size - rows.shape[2]]], axis=1)


def hop(value, pairs):
    return lax.ppermute(value, ("core", "blk"), [(a[0] * N + a[1], b[0] * N + b[1]) for a, b in pairs])


PLACES = [(c, z) for c in range(2) for z in range(N)]
MAIN = [(z // 2, z) for z in range(N)]
CORE_SWAP = [((c, z), (1 - c, z)) for c, z in PLACES]
NEAR_SWAP = [((c, z), (c, z ^ 1)) for c, z in PLACES]
FAR_SWAP = [((c, z), (c, z ^ 2)) for c, z in PLACES]
FAR_HOME = [((c, z), (1 - c, z ^ 2)) for c, z in PLACES if c != z // 2]


HOME = [((c, z), (c, z ^ 1)) for c, z in MAIN] + FAR_HOME
OFF_MAIN = [(c, z) for c, z in PLACES if c != z // 2]
FROM_MAIN = [((c, z), (1 - c, z)) for c, z in MAIN]
TO_MAIN = [((c, z), (1 - c, z)) for c, z in OFF_MAIN]
NEAR_OFF = [((c, z), (c, z ^ 1)) for c, z in OFF_MAIN]


def tie(*arrays):
    return lax.optimization_barrier(arrays)


def near_sum(keep, got):
    rows = keep.shape[0] // 2
    return low(wide(keep[rows:]) + wide(got[rows:]))


def home_sum(keep, got, near, got_near, main):
    rows = keep.shape[0] // 2
    return jnp.where(main, near, low(wide(keep[:rows]) + wide(got[:rows]) + wide(got_near)))


def own_sum(keep, got, got_home, main):
    rows = keep.shape[0] // 2
    return jnp.where(main, wide(keep[:rows]) + wide(got[:rows]), 0.0) + wide(got_home)


def pick(value, axis, index):
    return lax.dynamic_index_in_dim(value, index, axis, keepdims=False)


def plane(values):
    return [lax.ppermute(value, "col", [(i, i ^ (k + 1)) for i in range(4)]) for k, value in enumerate(values)]


NEAR = [((c, z), (c, z ^ 1)) for c, z in PLACES]


def first_pieces(value, near):
    return pick(value, 1, 1 - near).reshape(-1, value.shape[-1])


def second_pieces(value, got, core, near):
    got = got.reshape((2,) + value.shape[2:])
    return jnp.concatenate([pick(pick(value, 1, near), 0, 1 - core), pick(got, 0, 1 - core)], axis=0)


def own_pieces(value, got, last, core, near):
    got = got.reshape((2,) + value.shape[2:])
    last = last.reshape((2,) + value.shape[2:])
    return [pick(pick(value, 1, near), 0, core), last[0], pick(got, 0, core), last[1]]


def by_quarter(pieces, quarter, rows):
    stacked = jnp.stack([piece[:rows] for piece in pieces])
    return jnp.stack([pick(stacked, 0, quarter ^ k) for k in range(N)])


def split_local(
    tokens,
    lengths,
    first_gain,
    first_shift,
    second_gain,
    second_shift,
    joint_weight,
    joint_bias,
    dense_weight,
    dense_bias,
    expand_weight,
    expand_bias,
    reduce_weight,
    reduce_bias,
    cotangent,
):
    col, core, z = lax.axis_index("col"), lax.axis_index("core"), lax.axis_index("blk")
    half, near = z // 2, z % 2
    quarter = 2 * near + core
    main = core == half
    flag = main.astype(jnp.int32)
    rows, width = tokens.shape[1:]
    total = rows * N
    units = expand_weight.shape[1]
    groups = units // (N * 128)
    heads = HEADS // N
    own_x, own_g = tokens[0], cotangent[0]
    row_of = lambda vector: vector.reshape(1, -1)

    x_other = hop(own_x, FROM_MAIN)
    x_first = hop(own_x, HOME)

    wj, wd, we, wr = prepare(quarter, joint_weight, dense_weight, expand_weight, reduce_weight)
    bj = pick(joint_bias.reshape(3, heads, N, HEAD), 2, quarter).reshape(-1, 1)
    be = expand_bias.reshape(groups // 2, 2, N, 128)
    be = jnp.stack([pick(be[:, 0], 1, quarter), pick(be[:, 1], 1, quarter ^ 2)], axis=1).reshape(1, -1)
    first_row, second_row = row_of(first_gain), row_of(second_gain)

    weights = [wj, bj, we, be, wr, first_row, row_of(first_shift), second_row, row_of(second_shift)]

    sizes = jnp.where(main, lengths, hop(lengths, CORE_SWAP))
    number, offset = doc_tables(sizes, jnp.arange(total, dtype=jnp.int32))
    inverse = 10000.0 ** (-2.0 * jnp.arange(ROTARY // 2, dtype=jnp.float32) / ROTARY)
    phase = inverse[:, None] * offset.astype(jnp.float32)
    tables = [jnp.cos(phase), jnp.sin(phase)]
    docs = lengths.shape[1]
    same = number == jnp.arange(HEAD, dtype=jnp.int32)[:, None]
    used = jnp.arange(HEAD)[:, None] < docs
    qx = low(jnp.where(same & used, 1.0, 0.0))
    kx = low(jnp.where(used & ~same, NEG, 0.0))

    spots = [z, z ^ (2 - flag), z ^ (1 + flag), z ^ 3]
    zero, one = jnp.int32(0), jnp.int32(1)
    state = run_tokens(0, jnp.stack([spots[0], 1 - flag]), own_x, x_other, weights, tables, None)
    x_first, *state = tie(x_first, *state)
    x_first_other = hop(x_first, CORE_SWAP)
    x_second = hop(x_first, NEAR_OFF)
    state = run_tokens(1, jnp.stack([spots[1], zero]), x_first, x_first, weights, tables, state)
    x_first_other, x_second, own_g_late, *state = tie(x_first_other, x_second, own_g, *state)
    g_first = hop(own_g_late, HOME)
    g_other = hop(own_g_late, FROM_MAIN)
    x_second_other = hop(x_second, TO_MAIN)
    state = run_tokens(2, jnp.stack([spots[2], zero]), x_first_other, x_first_other, weights, tables, state)
    state = run_tokens(3, jnp.stack([spots[3], 1 - flag]), x_second_other, x_second, weights, tables, state)
    qkv, unit, second, active, slope, feed = state
    order = z ^ (jnp.arange(N, dtype=jnp.int32) ^ (2 * flag))
    qkv = qkv.reshape(3, heads, HEAD, total)
    attended = attend_forward(qkv, kx, qx, 0, heads // 2, None)
    g_first, *attended = tie(g_first, *attended)
    g_second = hop(g_first, NEAR_OFF)
    g_first_other = hop(g_first, CORE_SWAP)
    mixed, full, inverse_sum, shares = attend_forward(qkv, kx, qx, heads // 2, heads // 2, attended)
    mixed = mixed.reshape(-1, total)
    out_send, out_keep = deliver(order, mixed, wd, feed)
    g_second, out_send, out_keep = tie(g_second, out_send, out_keep)

    spot = jnp.stack([*spots, 1 - flag, 2 * one, 3 * one, 5 - flag])
    spot, out_send, out_keep = tie(spot, out_send, out_keep)
    g_second_other = hop(g_second, TO_MAIN)
    out_got = hop(out_send, CORE_SWAP)
    gs = (own_g, g_other, g_first, g_first_other, g_second_other, g_second)
    mg, back, ups, hg, sums, hsum = run_upstream(spot, gs, [wd, we, wr, second_row], unit, slope)
    out_near = near_sum(out_keep, out_got)
    out_near, hg = tie(out_near, hg)
    out_got_near = hop(out_near, NEAR_OFF)

    spot = jnp.stack([*spots, col])
    kept_share, *shares_out = weight_gradients(spot, second, hg, active, ups, mixed)
    out_home = home_sum(out_keep, out_got, out_near, out_got_near, main)
    out_home, mg, *shares_out = tie(out_home, mg, *shares_out)
    out_got_home = hop(out_home, HOME)
    shares_got = plane(shares_out)

    jb = attend_backward(qkv, mg.reshape(heads, HEAD, total), full, inverse_sum, shares, tables)
    jb = jb.reshape(-1, total)

    spot = jnp.stack([col, quarter])
    up_sum = jnp.sum(wide(own_g).reshape(-1, 8, width), axis=0)
    kept_joint, *joint_out, vector = joint_gradient(
        spot, jb, unit, wj, first_row, row_of(first_shift), sums, up_sum, hsum
    )
    jb, *joint_out = tie(jb, *joint_out)
    joint_got = plane(joint_out)

    send, keep = deliver(order, jb, wj, back, first_row)

    send, out_got_home, *shares_got = tie(send, out_got_home, *shares_got)
    got = hop(send, CORE_SWAP)
    share = wide(kept_share) + sum(wide(piece) for piece in shares_got)
    kept = near ^ half
    part = width // 4
    expand_part = share[:part].reshape(2, 2, 2, part // 8, units // N)
    reduce_part = share[part : part + units // (4 * N)].reshape(2, -1, width)
    dense_part = share[part + units // (4 * N) :]
    far_send = [pick(expand_part, 1, 1 - half).reshape(part // 2, -1), pick(reduce_part, 0, 1 - kept), dense_part]
    far_send = low(jnp.concatenate(far_send, axis=0))
    far_got = hop(far_send, FAR_SWAP)
    near_part = near_sum(keep, got)
    out = own_sum(out_keep, out_got, out_got_home, main)
    inputs = wide(own_x)
    result = low(inputs + out + (dense_bias + reduce_bias))
    near_part, result = tie(near_part, result)
    got_near = hop(near_part, NEAR_OFF)

    got_near, *joint_got = tie(got_near, *joint_got)
    joint_part = wide(kept_joint) + sum(wide(piece[:part]) for piece in joint_got)
    vector = vector + sum(unpack(piece[part:], width) for piece in joint_got)
    joint_width = joint_part.shape[1]
    joint_part = joint_part.reshape(2, 2, 2, part // 8, joint_width)
    joint_far_send = jnp.concatenate(
        [low(pick(joint_part, 1, 1 - half)).reshape(part // 2, joint_width), pack(vector, joint_width)], axis=0
    )
    far_got = wide(far_got)
    expand_part = low(pick(expand_part, 1, half).reshape(part // 2, -1) + far_got[: part // 2])
    reduce_part = low(pick(reduce_part, 0, kept) + far_got[part // 2 : part // 2 + 128])
    dense_part = low(dense_part + far_got[part // 2 + 128 :]).reshape(2, HEAD // 2, width)
    home = home_sum(keep, got, near_part, got_near, main)
    line = jnp.concatenate(
        [
            expand_part.reshape(2, 2, part // 8, -1),
            jnp.broadcast_to(dense_part[None], (2,) + dense_part.shape),
        ],
        axis=2,
    )
    line_send = first_pieces(line, near)
    home, joint_far_send, line_send, reduce_part = tie(home, joint_far_send, line_send, reduce_part)
    line_got = hop(line_send, NEAR)
    reduce_got = hop(reduce_part, [((c, s), ((s % 2) ^ (s // 2), 2 * (s // 2) + c)) for c, s in PLACES])
    got_home = hop(home, HOME)
    joint_far = hop(joint_far_send, FAR_SWAP)
    line_last = hop(second_pieces(line, line_got, core, near), CORE_SWAP)
    line_mine = own_pieces(line, line_got, line_last, core, near)
    expand_got = by_quarter(line_mine, quarter, part // 8)
    dense_got = pick(jnp.stack([piece[part // 8 :] for piece in line_mine]), 0, 2 * (near ^ core) + (core ^ half))
    expand_mine = expand_got.reshape(2, 2, -1, groups // 2, 2, 128)
    expand_mine = jnp.stack([expand_mine[:, :, :, :, 0], expand_mine[::-1, :, :, :, 1]], axis=4)
    expand_mine = wide(jnp.transpose(expand_mine, (2, 3, 4, 0, 1, 5)).reshape(-1, units))
    reduce_mine = wide(reduce_got)
    dense_mine = wide(dense_got)

    joint_part = low(pick(joint_part, 1, half).reshape(part // 2, joint_width) + wide(joint_far[: part // 2]))
    vector = vector + unpack(joint_far[part // 2 :], width)
    scaled = own_sum(keep, got, got_home, main)
    _, unit_rows, inverse_root = normalize(inputs, first_gain, first_shift)
    input_back = inverse_root * (
        scaled
        - jnp.mean(scaled, axis=-1, keepdims=True)
        - unit_rows * jnp.mean(scaled * unit_rows, axis=-1, keepdims=True)
    )
    tokens_gradient = low(wide(own_g) + input_back)
    joint_part, vector, expand_mine, reduce_mine, dense_mine, tokens_gradient = tie(
        joint_part, vector, expand_mine, reduce_mine, dense_mine, tokens_gradient
    )
    line = joint_part.reshape(2, 2, part // 8, joint_width)
    line_got = hop(jnp.concatenate([first_pieces(line, near), pack(vector, joint_width)], axis=0), NEAR)
    vector = vector + unpack(line_got[part // 4 :], width)
    line_got = line_got[: part // 4]
    line_last = hop(
        jnp.concatenate([second_pieces(line, line_got, core, near), pack(vector, joint_width)], axis=0), CORE_SWAP
    )
    vector = vector + unpack(line_last[part // 4 :], width)
    joint_mine = by_quarter(own_pieces(line, line_got, line_last[: part // 4], core, near), quarter, part // 8)
    joint_mine = joint_mine.reshape(N, -1, 3, heads, HEAD)
    joint_mine = wide(jnp.transpose(joint_mine, (1, 2, 3, 0, 4)).reshape(-1, 3 * width))

    device = (2 * col + core) * N + z
    share = width // (8 * N)
    head_row = lambda head: 5 + N + head % N
    cut = lambda row, start, size: lax.dynamic_slice(vector, (row, start), (1, size))[0]
    pieces = [cut(row, device * share, share) for row in range(5)]
    pieces[4:] = [
        cut(head_row(device % HEADS), (device // HEADS * heads + device % HEADS // N) * HEAD, HEAD),
        cut(head_row(device // 2), (2 * heads + device // 2 // N) * HEAD + device % 2 * share, share),
        pieces[4],
        cut(5 + (z ^ (2 * core)), (2 * col + core) * 128, 128),
    ]

    return (
        result[None],
        tokens_gradient[None],
        *pieces[:4],
        joint_mine,
        pieces[4],
        pieces[5],
        dense_mine,
        pieces[6],
        expand_mine,
        pieces[7],
        reduce_mine,
        pieces[6],
    )


def solution(mesh):
    count, blocks = mesh.devices.shape
    split = blocks == N and count == 8
    if split:
        mesh = jax.sharding.Mesh(mesh.devices.reshape(count // 2, 2, blocks), ("col", "core", "blk"))
        batch = ("col", "core")
        every = ("col", "core", "blk")
    else:
        batch, every = "batch", ("batch", "blk")
    by_rows = P(batch, "blk", None)
    placed = (by_rows, P(batch, None)) + (P(),) * 12 + (by_rows,)
    vector, matrix = P(every), P(every, None)
    return jax.shard_map(
        split_local if split else local,
        mesh=mesh,
        in_specs=placed,
        out_specs=(
            by_rows,
            by_rows,
            vector,
            vector,
            vector,
            vector,
            matrix,
            vector,
            vector,
            matrix,
            vector,
            matrix,
            vector,
            matrix,
            vector,
        ),
        check_vma=False,
    )
```

```python
from functools import partial

import jax
import jax.numpy as jnp
from jax import lax
from jax.experimental import pallas as pl
from jax.experimental.pallas import tpu as pltpu
from jax.sharding import PartitionSpec as P

HEADS = 16
HEAD = 64
ROTARY = 16


EPSILON = 1e-05
MASKED = -1e30


def doc_tables(lengths, positions):
    doc_ends = jnp.cumsum(lengths, axis=-1)
    doc_starts = doc_ends - lengths
    doc_number = jnp.sum(
        (positions[None, :, None] >= doc_ends[:, None, :]).astype(jnp.int32), axis=-1
    )
    matches = (
        doc_number[:, :, None] == jnp.arange(lengths.shape[-1], dtype=jnp.int32)[None, None, :]
    )
    begins = jnp.sum(jnp.where(matches, doc_starts[:, None, :], 0), axis=-1)
    return (doc_number, positions[None, :] - begins)


def angles(offsets):
    half_width = ROTARY // 2
    inverse = 10000.0 ** (-2.0 * jnp.arange(half_width, dtype=jnp.float32) / ROTARY)
    phase = offsets.astype(jnp.float32)[..., None] * inverse
    return (jnp.cos(phase), jnp.sin(phase))


def rotate(values, cosine, sine_table, direction):
    half_width = cosine.shape[-1]
    lead_part = values[..., :half_width]
    tail_part = values[..., half_width : 2 * half_width]
    cosine = cosine[:, :, None, :]
    sine_table = sine_table[:, :, None, :] * direction
    return jnp.concatenate(
        [
            lead_part * cosine - tail_part * sine_table,
            tail_part * cosine + lead_part * sine_table,
            values[..., 2 * half_width :],
        ],
        axis=-1,
    )


def normalize(values, gain_row, shift_row):
    center = values - jnp.mean(values, axis=-1, keepdims=True)
    spread = jnp.mean(center * center, axis=-1, keepdims=True)
    inverse_root = lax.rsqrt(spread + EPSILON)
    unit_rows = center * inverse_root
    return (unit_rows * gain_row + shift_row, unit_rows, inverse_root)


def normalize_back(upstream, unit_rows, inverse_root, gain_row):
    scaled_back = upstream * gain_row
    input_back = inverse_root * (
        scaled_back
        - jnp.mean(scaled_back, axis=-1, keepdims=True)
        - unit_rows * jnp.mean(scaled_back * unit_rows, axis=-1, keepdims=True)
    )
    return (input_back, jnp.sum(upstream * unit_rows, axis=0), jnp.sum(upstream, axis=0))


def outer(left_rows, right_rows):
    return lax.dot_general(
        left_rows, right_rows, (((0,), (0,)), ((), ())), preferred_element_type=jnp.float32
    )


def against(left_rows, weight_rows):
    return lax.dot_general(
        left_rows, weight_rows, (((1,), (1,)), ((), ())), preferred_element_type=jnp.float32
    )


def over_piece(stepper, running, segment, stride):
    sub_count = segment.shape[1] // stride

    def one_turn(position, current):
        part_rows = lax.dynamic_slice_in_dim(segment, position * stride, stride, 1)
        return stepper(current, part_rows, position * stride)

    return lax.fori_loop(0, sub_count, one_turn, running)


def local(
    tokens,
    lengths,
    first_gain,
    first_shift,
    second_gain,
    second_shift,
    joint_weight,
    joint_bias,
    dense_weight,
    dense_bias,
    expand_weight,
    expand_bias,
    reduce_weight,
    reduce_bias,
    cotangent,
):
    sequences, stride, model_width = tokens.shape
    cycle_size = lax.axis_size("blk")
    seq_total = stride * cycle_size
    rank_here = lax.axis_index("blk")
    row_count = sequences * stride
    factor = HEAD ** (-0.5)
    head_shape = (sequences, stride, HEADS, HEAD)
    places = jnp.arange(seq_total, dtype=jnp.int32)
    number_all, offset_all = doc_tables(lengths, places)
    first_place = rank_here * stride
    query_number = lax.dynamic_slice_in_dim(number_all, first_place, stride, 1)
    query_offset = lax.dynamic_slice_in_dim(offset_all, first_place, stride, 1)
    query_place = first_place + jnp.arange(stride, dtype=jnp.int32)
    last_place = first_place + stride - 1
    cosine, sine_table = angles(query_offset)
    inputs = tokens.reshape(row_count, model_width).astype(jnp.float32)
    first_norm, first_unit, first_scale = normalize(inputs, first_gain, first_shift)
    normed = first_norm.astype(jnp.bfloat16)
    joint_out = jnp.dot(normed, joint_weight, preferred_element_type=jnp.float32) + joint_bias
    queries = rotate(
        joint_out[:, :model_width].reshape(head_shape), cosine, sine_table, 1.0
    ).astype(jnp.bfloat16)
    key_rows = rotate(
        joint_out[:, model_width : 2 * model_width].reshape(head_shape), cosine, sine_table, 1.0
    ).astype(jnp.bfloat16)
    value_rows = joint_out[:, 2 * model_width :].astype(jnp.bfloat16)
    pair_local = jnp.concatenate(
        [
            key_rows.reshape(sequences, stride, model_width),
            value_rows.reshape(sequences, stride, model_width),
        ],
        axis=-1,
    )

    def masked_scores(key_part, begin_row, row_span):
        key_number = lax.dynamic_slice_in_dim(number_all, begin_row, row_span, 1)
        key_place = begin_row + jnp.arange(row_span, dtype=jnp.int32)
        allowed = (query_number[:, :, None] == key_number[:, None, :]) & (
            key_place[None, None, :] <= query_place[None, :, None]
        )
        allowed = allowed[:, None]
        scores = (
            jnp.einsum("sqhd,skhd->shqk", queries, key_part, preferred_element_type=jnp.float32)
            * factor
        )
        return (jnp.where(allowed, scores, MASKED), allowed)

    def split_piece(segment):
        row_span = segment.shape[1]
        key_part = segment[:, :, :model_width].reshape(sequences, row_span, HEADS, HEAD)
        value_part = segment[:, :, model_width:].reshape(sequences, row_span, HEADS, HEAD)
        return (key_part, value_part, row_span)

    def gated(kernel):

        def stepper(running, segment, begin_row):
            return lax.cond(
                begin_row <= last_place,
                lambda current: kernel(current, segment, begin_row),
                lambda current: current,
                running,
            )

        return stepper

    def forward_kernel(running, segment, begin_row):
        row_peak, row_total, weighted = running
        key_part, value_part, row_span = split_piece(segment)
        scores, allowed = masked_scores(key_part, begin_row, row_span)
        new_peak = jnp.maximum(row_peak, jnp.max(scores, axis=-1))
        shares = jnp.where(allowed, jnp.exp(scores - new_peak[..., None]), 0.0)
        decay_factor = jnp.exp(row_peak - new_peak)
        row_total = row_total * decay_factor + jnp.sum(shares, axis=-1)
        update = jnp.einsum(
            "shqk,skhd->sqhd",
            shares.astype(jnp.bfloat16),
            value_part,
            preferred_element_type=jnp.float32,
        )
        weighted = weighted * jnp.transpose(decay_factor, (0, 2, 1))[..., None] + update
        return (new_peak, row_total, weighted)

    forward_step = gated(forward_kernel)
    initial = (
        jnp.full((sequences, HEADS, stride), MASKED, jnp.float32),
        jnp.zeros((sequences, HEADS, stride), jnp.float32),
        jnp.zeros(head_shape, jnp.float32),
    )
    forward_state = over_piece(
        forward_step, initial, lax.all_gather(pair_local, "blk", axis=1, tiled=True), stride
    )
    row_peak, row_total, weighted = forward_state
    mixed_full = weighted / jnp.transpose(row_total, (0, 2, 1))[..., None]
    log_total = row_peak + jnp.log(row_total)
    mixed = mixed_full.reshape(row_count, model_width).astype(jnp.bfloat16)
    attention_out = jnp.dot(mixed, dense_weight, preferred_element_type=jnp.float32) + dense_bias
    second_norm, second_unit, second_scale = normalize(inputs, second_gain, second_shift)
    second = second_norm.astype(jnp.bfloat16)
    hidden = jnp.dot(second, expand_weight, preferred_element_type=jnp.float32) + expand_bias
    active_full, gelu_pull = jax.vjp(partial(jax.nn.gelu, approximate=False), hidden)
    active = active_full.astype(jnp.bfloat16)
    feed_out = jnp.dot(active, reduce_weight, preferred_element_type=jnp.float32) + reduce_bias
    result = (
        (inputs + attention_out + feed_out)
        .astype(jnp.bfloat16)
        .reshape(sequences, stride, model_width)
    )
    upstream = cotangent.reshape(row_count, model_width)
    dense_grad = outer(mixed, upstream)
    bias_total = jnp.sum(upstream, axis=0, dtype=jnp.float32)
    reduce_grad = outer(active, upstream)
    hidden_grad = gelu_pull(against(upstream, reduce_weight))[0].astype(jnp.bfloat16)
    expand_grad = outer(second, hidden_grad)
    hidden_total = jnp.sum(hidden_grad, axis=0, dtype=jnp.float32)
    input_two, gain_second, shift_second = normalize_back(
        against(hidden_grad, expand_weight), second_unit, second_scale, second_gain
    )
    mixed_grad = against(upstream, dense_weight).astype(jnp.bfloat16)
    out_heads = mixed_grad.reshape(head_shape)
    delta_rows = jnp.transpose(jnp.sum(out_heads * mixed_full, axis=-1), (0, 2, 1))

    def backward_kernel(running, segment, begin_row):
        key_part, value_part, row_span = split_piece(segment)
        scores, allowed = masked_scores(key_part, begin_row, row_span)
        weights_now = jnp.where(allowed, jnp.exp(scores - log_total[..., None]), 0.0)
        weight_grad = jnp.einsum(
            "sqhd,skhd->shqk", out_heads, value_part, preferred_element_type=jnp.float32
        )
        score_grad = (weights_now * (weight_grad - delta_rows[..., None])).astype(jnp.bfloat16)
        query_grad = (
            running[0]
            + jnp.einsum(
                "shqk,skhd->sqhd", score_grad, key_part, preferred_element_type=jnp.float32
            )
            * factor
        )
        value_grad = jnp.einsum(
            "shqk,sqhd->skhd",
            weights_now.astype(jnp.bfloat16),
            out_heads,
            preferred_element_type=jnp.float32,
        )
        key_grad = (
            jnp.einsum("shqk,sqhd->skhd", score_grad, queries, preferred_element_type=jnp.float32)
            * factor
        )
        fresh_rows = jnp.concatenate(
            [
                key_grad.reshape(sequences, row_span, model_width),
                value_grad.reshape(sequences, row_span, model_width),
            ],
            axis=-1,
        )
        pair_grad = lax.dynamic_update_slice_in_dim(running[1], fresh_rows, begin_row, 1)
        return (query_grad, pair_grad)

    backward_step = gated(backward_kernel)
    back_initial = (
        jnp.zeros(head_shape, jnp.float32),
        jnp.zeros((sequences, seq_total, 2 * model_width), jnp.float32),
    )
    back_state = over_piece(
        backward_step, back_initial, lax.all_gather(pair_local, "blk", axis=1, tiled=True), stride
    )
    query_grad = back_state[0]
    pair_mine = lax.psum_scatter(back_state[1], "blk", scatter_dimension=1, tiled=True)
    query_back = rotate(query_grad, cosine, sine_table, -1.0).reshape(row_count, model_width)
    key_back = rotate(
        pair_mine[:, :, :model_width].reshape(head_shape), cosine, sine_table, -1.0
    ).reshape(row_count, model_width)
    value_back = pair_mine[:, :, model_width:].reshape(row_count, model_width)
    joint_back = jnp.concatenate([query_back, key_back, value_back], axis=-1).astype(jnp.bfloat16)
    joint_grad = outer(normed, joint_back)
    joint_total = jnp.sum(joint_back, axis=0, dtype=jnp.float32)
    front_total = joint_total[: 2 * model_width]
    value_total = joint_total[2 * model_width :]
    input_one, gain_first, shift_first = normalize_back(
        against(joint_back, joint_weight), first_unit, first_scale, first_gain
    )
    input_total = (
        (upstream.astype(jnp.float32) + input_one + input_two)
        .astype(jnp.bfloat16)
        .reshape(sequences, stride, model_width)
    )
    summed = (
        lax.psum_scatter(gain_first, ("batch", "blk"), scatter_dimension=0, tiled=True),
        lax.psum_scatter(shift_first, ("batch", "blk"), scatter_dimension=0, tiled=True),
        lax.psum_scatter(gain_second, ("batch", "blk"), scatter_dimension=0, tiled=True),
        lax.psum_scatter(shift_second, ("batch", "blk"), scatter_dimension=0, tiled=True),
        lax.psum_scatter(joint_grad, ("batch", "blk"), scatter_dimension=0, tiled=True),
        lax.psum_scatter(front_total, ("batch", "blk"), scatter_dimension=0, tiled=True),
        lax.psum_scatter(value_total, ("batch", "blk"), scatter_dimension=0, tiled=True),
        lax.psum_scatter(dense_grad, ("batch", "blk"), scatter_dimension=0, tiled=True),
        lax.psum_scatter(bias_total, ("batch", "blk"), scatter_dimension=0, tiled=True),
        lax.psum_scatter(expand_grad, ("batch", "blk"), scatter_dimension=0, tiled=True),
        lax.psum_scatter(hidden_total, ("batch", "blk"), scatter_dimension=0, tiled=True),
        lax.psum_scatter(reduce_grad, ("batch", "blk"), scatter_dimension=0, tiled=True),
    )
    return (
        result,
        input_total,
        summed[0],
        summed[1],
        summed[2],
        summed[3],
        summed[4],
        summed[5],
        summed[6],
        summed[7],
        summed[8],
        summed[9],
        summed[10],
        summed[11],
        summed[8],
    )


BQ = 512
N = 4
TM = 256
VMEM = 56 * 1024 * 1024
NEG = -1e30
NN = (((1,), (0,)), ((), ()))
NT = (((1,), (1,)), ((), ()))
TN = (((0,), (0,)), ((), ()))


def mm(left, right, form=NN):
    return lax.dot_general(left, right, form, preferred_element_type=jnp.float32)


def low(value):
    return value.astype(jnp.bfloat16)


def wide(value):
    return value.astype(jnp.float32)


def gelu_parts(hidden):
    size = jnp.abs(hidden) * (0.5**0.5)
    bell = jnp.exp(-(size * size))
    base = 1.0 + 0.3275911 * size
    guess = pl.reciprocal(base, approx=True)
    t = guess * (2.0 - base * guess)
    series = t * (
        0.5 * 0.254829592
        + t
        * (
            0.5 * -0.284496736
            + t * (0.5 * 1.421413741 + t * (0.5 * -1.453152027 + t * (0.5 * 1.061405429)))
        )
    )
    tail = series * bell
    return (jnp.where(hidden >= 0.0, 1.0 - tail, tail), bell)


def fold_rows(value):
    rows, columns = value.shape
    return jnp.sum(value.reshape(rows // 8, 8, columns), axis=0)


def prepare_kernel(spot_ref, wj_ref, wd_ref, we_ref, wr_ref, wj_out, wd_out, we_out, wr_out):
    turned = wj_ref[...].T
    wj_out[...] = jnp.where(lax.rem(spot_ref[0], 2) == 0, turned[:HEAD], turned[HEAD:])
    wd_out[...] = wd_ref[...]
    we_out[...] = we_ref[...]
    wr_out[...] = wr_ref[...]


def prepare(quarter, joint_weight, dense_weight, expand_weight, reduce_weight):
    width, units = expand_weight.shape
    heads = HEADS // N
    groups = units // (N * 128)
    kinds = 3 * heads
    pair = lambda s, spot: (0, (s // heads) * (HEADS // 2) + (s % heads) * (N // 2) + spot[0] // 2)
    row = lambda s: jnp.minimum(s, heads - 1)
    unit = lambda s: jnp.minimum(s, groups - 1)
    group = lambda s, spot: N * unit(s) + lax.rem(spot[0] + 2 * lax.rem(unit(s), 2), N)
    shape = lambda *dims: jax.ShapeDtypeStruct(dims, jnp.bfloat16)
    return pl.pallas_call(
        prepare_kernel,
        grid_spec=pltpu.PrefetchScalarGridSpec(
            num_scalar_prefetch=1,
            grid=(kinds,),
            in_specs=[
                pl.BlockSpec((width, 2 * HEAD), pair),
                pl.BlockSpec((HEAD, width), lambda s, spot: (N * row(s) + spot[0], 0)),
                pl.BlockSpec((width, 128), lambda s, spot: (0, group(s, spot))),
                pl.BlockSpec((128, width), lambda s, spot: (group(s, spot), 0)),
            ],
            out_specs=[
                pl.BlockSpec((HEAD, width), lambda s, spot: (s, 0)),
                pl.BlockSpec((HEAD, width), lambda s, spot: (row(s), 0)),
                pl.BlockSpec((width, 128), lambda s, spot: (0, unit(s))),
                pl.BlockSpec((128, width), lambda s, spot: (unit(s), 0)),
            ],
        ),
        out_shape=[
            shape(kinds * HEAD, width),
            shape(heads * HEAD, width),
            shape(width, groups * 128),
            shape(groups * 128, width),
        ],
        cost_estimate=pl.CostEstimate(flops=0, bytes_accessed=14 * width * width, transcendentals=0),
    )(quarter.reshape(1), joint_weight, dense_weight, expand_weight, reduce_weight)


def block_at(place, j):
    return place * (place + 1) // 2 + j


def forward_kernel(held, qkv_ref, kx_ref, qx_ref, *refs):
    mixed_ref, full_ref, inverse_ref, share_ref, key_ref, *scores = refs[held:]
    key_ref[...] = jnp.concatenate([qkv_ref[1, 0], kx_ref[...]], axis=0).T
    total = kx_ref.shape[1]
    state = {}

    def score(place, j):
        here = slice(place * BQ, (place + 1) * BQ)
        at = slice(j * BQ, (j + 1) * BQ)
        if j == 0:
            query_x = jnp.concatenate([qkv_ref[0, 0, :, here], qx_ref[:, here]], axis=0)
            state[place] = [query_x, jnp.full((8, BQ), NEG * 2, jnp.float32)]
        found = mm(key_ref[at, :], state[place][0])
        if j == place:
            key_row = lax.broadcasted_iota(jnp.int32, (BQ, BQ), 0)
            query_column = lax.broadcasted_iota(jnp.int32, (BQ, BQ), 1)
            found = jnp.where(key_row <= query_column, found, NEG)
        scores[place % 2][at, :] = found
        state[place][1] = jnp.maximum(state[place][1], jnp.max(found.reshape(BQ // 8, 8, BQ), axis=0))

    def weigh(place, j):
        here = slice(place * BQ, (place + 1) * BQ)
        at = slice(j * BQ, (j + 1) * BQ)
        if j == 0:
            peak = jnp.max(state[place][1], axis=0, keepdims=True)
            state[place] = [peak, jnp.zeros((8, BQ), jnp.float32), jnp.zeros((HEAD, BQ), jnp.float32)]
        share = jnp.exp(scores[place % 2][at, :] - state[place][0])
        state[place][1] = state[place][1] + jnp.sum(share.reshape(BQ // 8, 8, BQ), axis=0)
        share = low(share)
        share_ref[0, block_at(place, j)] = share
        state[place][2] = state[place][2] + mm(qkv_ref[2, 0, :, at], share)
        if j == place:
            inverse = 1.0 / jnp.sum(state[place][1], axis=0, keepdims=True)
            mixed = state[place][2] * inverse
            inverse_ref[0, :, here] = inverse
            full_ref[0, :, here] = mixed
            mixed_ref[0, :, here] = low(mixed)

    places = list(range(total // BQ))
    for j in range(places[0] + 1):
        score(places[0], j)
    for n, place in enumerate(places):
        for j in range(places[-1] + 2):
            if n + 1 < len(places) and j <= places[n + 1]:
                score(places[n + 1], j)
            if j <= place:
                weigh(place, j)


def attend_forward(qkv, kx, qx, first, count, before):
    _, heads, _, total = qkv.shape
    places = total // BQ
    blocks = block_at(places, 0)
    head_rows = lambda rows: pl.BlockSpec((1, rows, total), lambda h: (first + h, 0, 0))
    operands = [qkv, kx, qx]
    in_specs = [
        pl.BlockSpec((3, 1, HEAD, total), lambda h: (0, first + h, 0, 0)),
        pl.BlockSpec((HEAD, total), lambda h: (0, 0)),
        pl.BlockSpec((HEAD, total), lambda h: (0, 0)),
    ]
    aliases = {}
    if before is not None:
        for index, array in enumerate(before):
            aliases[len(operands)] = index
            operands.append(array)
            in_specs.append(pl.BlockSpec(memory_space=pl.ANY))
    return pl.pallas_call(
        partial(forward_kernel, len(aliases)),
        grid=(count,),
        in_specs=in_specs,
        out_specs=[
            head_rows(HEAD),
            head_rows(HEAD),
            head_rows(1),
            pl.BlockSpec((1, blocks, BQ, BQ), lambda h: (first + h, 0, 0, 0)),
        ],
        out_shape=[
            jax.ShapeDtypeStruct((heads, HEAD, total), jnp.bfloat16),
            jax.ShapeDtypeStruct((heads, HEAD, total), jnp.float32),
            jax.ShapeDtypeStruct((heads, 1, total), jnp.float32),
            jax.ShapeDtypeStruct((heads, blocks, BQ, BQ), jnp.bfloat16),
        ],
        scratch_shapes=[pltpu.VMEM((total, 2 * HEAD), jnp.bfloat16)] + [pltpu.VMEM((total, BQ), jnp.float32)] * 2,
        input_output_aliases=aliases,
        compiler_params=pltpu.CompilerParams(vmem_limit_bytes=VMEM),
        cost_estimate=pl.CostEstimate(
            flops=16 * HEAD * count * blocks * BQ * BQ,
            bytes_accessed=2 * count * blocks * BQ * BQ,
            transcendentals=count * blocks * BQ * BQ,
        ),
    )(*operands)


def backward_kernel(qkv_ref, mg_ref, full_ref, inverse_ref, share_ref, cos_ref, sin_ref, jb_ref, value_ref, acc_ref):
    total = cos_ref.shape[1]
    ones = (lax.broadcasted_iota(jnp.int32, (HEAD, total), 0) < 3).astype(jnp.bfloat16)
    value_ref[...] = jnp.concatenate([qkv_ref[2, 0], ones], axis=0).T
    half = ROTARY // 2
    blank = jnp.zeros((HEAD, BQ), jnp.bfloat16)
    row = lax.broadcasted_iota(jnp.int32, (HEAD, BQ), 0)

    def turn_back(rows, at):
        lead, tail = rows[:half], rows[half : 2 * half]
        cosine, sine = cos_ref[:, at], sin_ref[:, at]
        return low(
            jnp.concatenate([lead * cosine + tail * sine, tail * cosine - lead * sine, rows[2 * half :]], axis=0)
        )

    for place in reversed(range(total // BQ)):
        here = slice(place * BQ, (place + 1) * BQ)
        query_t = qkv_ref[0, 0, :, here]
        mg = low(wide(mg_ref[0, :, here]) * inverse_ref[0, :, here])
        delta = -jnp.sum(wide(mg) * full_ref[0, :, here], axis=0, keepdims=True)
        first = low(delta)
        rest = delta - wide(first)
        middle = low(rest)
        final = low(rest - wide(middle))
        extra = jnp.where(
            row == 0, wide(first), jnp.where(row == 1, wide(middle), jnp.where(row == 2, wide(final), 0.0))
        )
        mg_x = jnp.concatenate([mg, low(extra)], axis=0)
        mg_v = jnp.concatenate([blank, mg], axis=0)
        query_k = jnp.concatenate([query_t, blank], axis=0)
        query_grad = jnp.zeros((HEAD, BQ), jnp.float32)
        for j in range(place + 1):
            at = slice(j * BQ, (j + 1) * BQ)
            share = share_ref[0, block_at(place, j)]
            score_grad = low(wide(share) * mm(value_ref[at, :], mg_x))
            pair = mm(share, mg_v, NT) + mm(score_grad, query_k, NT)
            query_grad = query_grad + mm(qkv_ref[1, 0, :, at], score_grad)
            if (place + 1) * BQ < total:
                pair = pair + acc_ref[at, :]
            if j < place:
                acc_ref[at, :] = pair
            else:
                pair_t = pair.T
                jb_ref[1, 0, :, at] = turn_back(pair_t[:HEAD], at)
                jb_ref[2, 0, :, at] = low(pair_t[HEAD:])
        jb_ref[0, 0, :, here] = turn_back(query_grad * (HEAD**-0.5), here)


def attend_backward(qkv, mg, full, inverse, shares, tables):
    _, heads, _, total = qkv.shape
    blocks = shares.shape[1]
    head_rows = lambda rows: pl.BlockSpec((1, rows, total), lambda h: (h, 0, 0))
    kinds = pl.BlockSpec((3, 1, HEAD, total), lambda h: (0, h, 0, 0))
    table = pl.BlockSpec((ROTARY // 2, total), lambda h: (0, 0))
    return pl.pallas_call(
        backward_kernel,
        grid=(heads,),
        in_specs=[
            kinds,
            head_rows(HEAD),
            head_rows(HEAD),
            head_rows(1),
            pl.BlockSpec((1, blocks, BQ, BQ), lambda h: (h, 0, 0, 0)),
            table,
            table,
        ],
        out_specs=kinds,
        out_shape=jax.ShapeDtypeStruct((3, heads, HEAD, total), jnp.bfloat16),
        scratch_shapes=[
            pltpu.VMEM((total, 2 * HEAD), jnp.bfloat16),
            pltpu.VMEM((total, 2 * HEAD), jnp.float32),
        ],
        compiler_params=pltpu.CompilerParams(vmem_limit_bytes=VMEM),
        cost_estimate=pl.CostEstimate(
            flops=32 * HEAD * heads * blocks * BQ * BQ,
            bytes_accessed=2 * heads * blocks * BQ * BQ,
            transcendentals=0,
        ),
    )(qkv, mg, full, inverse, shares, *tables)


def chosen(index, options):
    value = options[-1]
    for k in reversed(range(len(options) - 1)):
        value = jnp.where(index == k, options[k], value)
    return value


def token_kernel(count, sub, chunk, spot_ref, *refs):
    sources = refs[:count]
    (wj_ref, bj_ref, we_ref, be_ref, wr_ref, g1_ref, s1_ref, g2_ref, s2_ref, cos_ref, sin_ref) = refs[count : count + 11]
    qkv_ref, unit_ref, second_ref, active_ref, slope_ref, feed_ref = refs[-6:]
    choice = spot_ref[pl.num_programs(0) + pl.program_id(0)]
    rows = sources[0].shape[0]
    half = ROTARY // 2
    part = wj_ref.shape[0] // 3
    for top in range(0, rows, sub):
        at = slice(top, top + sub)
        x = wide(chosen(choice, [source[at, :] for source in sources]))
        center = x - jnp.mean(x, axis=-1, keepdims=True)
        scale = lax.rsqrt(jnp.mean(center * center, axis=-1, keepdims=True) + EPSILON)
        unit = center * scale
        unit_ref[at, :] = low(unit)
        normed = low(unit * g1_ref[...] + s1_ref[...])
        second = low(unit * g2_ref[...] + s2_ref[...])
        second_ref[at, :] = second
        joint = mm(wj_ref[...], normed, NT) + bj_ref[...]
        cosine, sine = cos_ref[:, at], sin_ref[:, at]
        for kind in range(3):
            for head in range(part // HEAD):
                first = kind * part + head * HEAD
                turned = joint[first : first + HEAD]
                if kind < 2:
                    lead, tail = turned[:half], turned[half : 2 * half]
                    turned = jnp.concatenate(
                        [lead * cosine - tail * sine, tail * cosine + lead * sine, turned[2 * half :]], axis=0
                    )
                if kind == 0:
                    turned = turned * (HEAD**-0.5)
                qkv_ref[first : first + HEAD, at] = low(turned)
        for left in range(0, we_ref.shape[1], chunk):
            over = slice(left, left + chunk)
            hidden = mm(second, we_ref[:, over]) + be_ref[:, over]
            share, bell = gelu_parts(hidden)
            active_ref[at, over] = low(hidden * share)
            slope_ref[at, over] = low(share + hidden * bell * 0.3989422804014327)
    for top in range(0, rows, sub):
        at = slice(top, top + sub)
        feed_ref[at, :] = low(mm(active_ref[at, :], wr_ref[...]))


def run_tokens(slot, spot, data, weights, tables, before, sub=256, chunk=256):
    rows, width = data[0].shape
    total = tables[0].shape[1]
    wj, bj, we, be, wr, g1, s1, g2, s2 = weights
    units = we.shape[1]
    steps = spot.shape[0] // 2

    def whole(array):
        return pl.BlockSpec(array.shape, lambda i, spot: (0,) * array.ndim)

    column = lambda height: pl.BlockSpec((height, rows), lambda i, spot: (0, spot[i]))
    placed = pl.BlockSpec((rows, width), lambda i, spot: (spot[i], 0))
    arrived = lambda size: pl.BlockSpec((rows, size), lambda i, spot: (slot + i, 0))
    in_specs = [whole(w) for w in (*data, *weights)] + [column(ROTARY // 2)] * 2
    out_specs = [column(wj.shape[0]), placed, arrived(width), arrived(units), arrived(units), placed]
    shape = lambda *dims: jax.ShapeDtypeStruct(dims, jnp.bfloat16)
    out_shape = [shape(wj.shape[0], total)] + [shape(total, size) for size in (width, width, units, units, width)]
    operands = [spot, *data, *weights, *tables]
    aliases = {}
    if before is not None:
        for index, array in enumerate(before):
            aliases[len(operands)] = index
            operands.append(array)
            in_specs.append(pl.BlockSpec(memory_space=pl.ANY))
    return pl.pallas_call(
        partial(token_kernel, len(data), sub, chunk),
        grid_spec=pltpu.PrefetchScalarGridSpec(
            num_scalar_prefetch=1, grid=(steps,), in_specs=in_specs, out_specs=out_specs
        ),
        out_shape=out_shape,
        input_output_aliases=aliases,
        compiler_params=pltpu.CompilerParams(vmem_limit_bytes=VMEM),
        cost_estimate=pl.CostEstimate(flops=0, bytes_accessed=0, transcendentals=0),
    )(*operands)


def upstream_kernel(chunk, spot_ref, *refs):
    sources = refs[:6]
    (wd_ref, we_ref, wr_ref, g2_ref, unit_ref, slope_ref) = refs[6:12]
    (mg_ref, back_ref, up_ref, hg_ref, sums_ref, hsum_ref) = refs[12:18]
    buffer, sems = refs[18:]
    step = pl.program_id(0)
    steps = pl.num_programs(0)
    slot = lax.rem(step, 2)

    def fetch(which, into):
        for k, source in enumerate(sources):

            @pl.when(spot_ref[steps + which] == k)
            def _():
                pltpu.make_async_copy(source, buffer.at[into], sems.at[into]).start()

    @pl.when(step == 0)
    def _():
        fetch(0, 0)
        sums_ref[...] = jnp.zeros_like(sums_ref)
        hsum_ref[...] = jnp.zeros_like(hsum_ref)

    @pl.when(step + 1 < steps)
    def _():
        fetch(step + 1, 1 - slot)

    pltpu.make_async_copy(sources[0], buffer.at[slot], sems.at[slot]).wait()
    up = buffer[slot]
    up_ref[...] = up
    mg_ref[...] = low(mm(wd_ref[...], up, NT))
    for left in range(0, we_ref.shape[1], chunk):
        over = slice(left, left + chunk)
        piece = low(mm(up, wr_ref[over, :], NT) * wide(slope_ref[:, over]))
        hg_ref[:, over] = piece
        hsum_ref[:, over] += fold_rows(wide(piece))
    for left in range(0, we_ref.shape[0], chunk):
        over = slice(left, left + chunk)
        back = mm(hg_ref[...], we_ref[over, :], NT)
        back_ref[:, over] = low(back * g2_ref[:, over])
        sums_ref[0, :, over] += fold_rows(back * wide(unit_ref[:, over]))
        sums_ref[1, :, over] += fold_rows(back)


def run_upstream(spot, sources, weights, unit, slope, chunk=256):
    rows, width = sources[0].shape
    total = unit.shape[0]
    wd, we, wr, g2 = weights
    units = we.shape[1]
    steps = total // rows

    def whole(array):
        return pl.BlockSpec(array.shape, lambda i, spot: (0,) * array.ndim)

    fixed = lambda *dims: pl.BlockSpec(dims, lambda i, spot: (0,) * len(dims))
    column = lambda height: pl.BlockSpec((height, rows), lambda i, spot: (0, spot[i]))
    placed = pl.BlockSpec((rows, width), lambda i, spot: (spot[i], 0))
    arrived = lambda size: pl.BlockSpec((rows, size), lambda i, spot: (i, 0))
    in_specs = [pl.BlockSpec(memory_space=pl.ANY)] * 6 + [whole(w) for w in weights] + [placed, arrived(units)]
    out_specs = [column(wd.shape[0]), placed, arrived(width), arrived(units), fixed(2, 8, width), fixed(8, units)]
    shape = lambda *dims: jax.ShapeDtypeStruct(dims, jnp.bfloat16)
    out_shape = [
        shape(wd.shape[0], total),
        shape(total, width),
        shape(total, width),
        shape(total, units),
        jax.ShapeDtypeStruct((2, 8, width), jnp.float32),
        jax.ShapeDtypeStruct((8, units), jnp.float32),
    ]
    return pl.pallas_call(
        partial(upstream_kernel, chunk),
        grid_spec=pltpu.PrefetchScalarGridSpec(
            num_scalar_prefetch=1,
            grid=(steps,),
            in_specs=in_specs,
            out_specs=out_specs,
            scratch_shapes=[
                pltpu.VMEM((2, rows, width), jnp.bfloat16),
                pltpu.SemaphoreType.DMA((2,)),
            ],
        ),
        out_shape=out_shape,
        compiler_params=pltpu.CompilerParams(vmem_limit_bytes=VMEM),
        cost_estimate=pl.CostEstimate(
            flops=3 * total * width * (wd.shape[0] + 2 * units), bytes_accessed=12 * total * width, transcendentals=0
        ),
    )(spot, *sources, wd, we, wr, g2, unit, slope)


def weight_kernel(spot_ref, second_ref, hg_ref, active_ref, up_ref, mixed_ref, *refs):
    shares, (expand_sum, reduce_sum, dense_sum) = refs[:4], refs[4:]
    step = pl.program_id(0)
    steps = pl.num_programs(0)

    @pl.when(step == 0)
    def _():
        expand_sum[...] = jnp.zeros_like(expand_sum)
        reduce_sum[...] = jnp.zeros_like(reduce_sum)
        dense_sum[...] = jnp.zeros_like(dense_sum)

    up = up_ref[...]
    dense_sum[...] += mm(mixed_ref[...], up)
    expand_sum[...] += mm(second_ref[...], hg_ref[...], TN)
    reduce_sum[...] += mm(active_ref[...], up, TN)

    @pl.when(step == steps - 1)
    def _():
        col = spot_ref[steps]
        large, small = expand_sum.shape[0] // 4, dense_sum.shape[0] // 4
        for k, share in enumerate(shares):
            i = k + col - 2 * (col & k)
            at = pl.ds(pl.multiple_of(i * large, large), large)
            share[:large] = low(expand_sum[at, :])
            share[large : 2 * large] = low(reduce_sum[at, :])
            share[2 * large :] = low(dense_sum[pl.ds(pl.multiple_of(i * small, small), small), :])


def weight_gradients(spot, second, hg, active, ups, mixed):
    total, width = second.shape
    units = hg.shape[1]
    rows = total // N
    height = mixed.shape[0]
    fixed = lambda *dims: pl.BlockSpec(dims, lambda i, spot: (0,) * len(dims))
    arrived = lambda size: pl.BlockSpec((rows, size), lambda i, spot: (i, 0))
    dims = (width // 4 + units // 4 + height // 4, width)
    return pl.pallas_call(
        weight_kernel,
        grid_spec=pltpu.PrefetchScalarGridSpec(
            num_scalar_prefetch=1,
            grid=(N,),
            in_specs=[
                arrived(width),
                arrived(units),
                arrived(units),
                arrived(width),
                pl.BlockSpec((height, rows), lambda i, spot: (0, spot[i])),
            ],
            out_specs=[fixed(*dims)] * 4,
            scratch_shapes=[
                pltpu.VMEM((width, units), jnp.float32),
                pltpu.VMEM((units, width), jnp.float32),
                pltpu.VMEM((height, width), jnp.float32),
            ],
        ),
        out_shape=[jax.ShapeDtypeStruct(dims, jnp.bfloat16)] * 4,
        compiler_params=pltpu.CompilerParams(vmem_limit_bytes=VMEM),
        cost_estimate=pl.CostEstimate(
            flops=3 * total * width * (height + 2 * units), bytes_accessed=8 * total * width, transcendentals=0
        ),
    )(spot, second, hg, active, ups, mixed)


def deliver_kernel(order_ref, left_ref, weight_ref, add_ref, *refs):
    del order_ref
    send_ref, keep_ref = refs[-2:]
    step = pl.program_id(0)
    value = mm(left_ref[...], weight_ref[...], TN)
    if len(refs) > 2:
        value = value * refs[0][...]
    value = low(value + wide(add_ref[...]))

    @pl.when(step < pl.num_programs(0) // 2)
    def _():
        send_ref[...] = value

    @pl.when(step >= pl.num_programs(0) // 2)
    def _():
        keep_ref[...] = value


def deliver(order, left, weight, add, gain=None):
    depth, total = left.shape
    width = weight.shape[1]
    steps = N
    tile = total // N
    rows = pl.BlockSpec((tile, width), lambda s, order: (order[s], 0))
    in_specs = [
        pl.BlockSpec((depth, tile), lambda s, order: (0, order[s])),
        pl.BlockSpec((depth, width), lambda s, order: (0, 0)),
        rows,
    ]
    operands = [left, weight, add]
    if gain is not None:
        in_specs.append(pl.BlockSpec((1, width), lambda s, order: (0, 0)))
        operands.append(gain)
    return pl.pallas_call(
        deliver_kernel,
        grid_spec=pltpu.PrefetchScalarGridSpec(
            num_scalar_prefetch=1,
            grid=(steps,),
            in_specs=in_specs,
            out_specs=[
                pl.BlockSpec((tile, width), lambda s, order: (jnp.minimum(s, steps // 2 - 1), 0)),
                pl.BlockSpec((tile, width), lambda s, order: (jnp.maximum(s - steps // 2, 0), 0)),
            ],
        ),
        out_shape=[jax.ShapeDtypeStruct((total // 2, width), jnp.bfloat16)] * 2,
        compiler_params=pltpu.CompilerParams(vmem_limit_bytes=VMEM),
        cost_estimate=pl.CostEstimate(
            flops=0, bytes_accessed=0, transcendentals=0
        ),
    )(order, *operands)


def joint_kernel(spot_ref, jb_ref, unit_ref, wj_ref, gain_ref, shift_ref, sums_ref, up_ref, hsum_ref, *refs):
    shares, (vector_ref, total_ref, turned_ref, sum_ref) = refs[:4], refs[4:]
    step = pl.program_id(0)
    jb = jb_ref[...]
    height, tile = jb.shape
    width = unit_ref.shape[1]

    @pl.when(step == 0)
    def _():
        total_ref[...] = jnp.zeros_like(total_ref)
        sum_ref[...] = jnp.zeros_like(sum_ref)

    total_ref[...] += mm(jb, unit_ref[...])
    sum_ref[...] += mm(jb, jnp.ones((tile, 128), jnp.bfloat16))

    @pl.when(step == pl.num_programs(0) - 1)
    def _():
        col, quarter = spot_ref[0], spot_ref[1]
        gain = jnp.sum(total_ref[...] * wide(wj_ref[...]), axis=0, keepdims=True)
        turned_ref[...] = (total_ref[...] * gain_ref[...] + sum_ref[:, :1] * shift_ref[...]).T
        part = width // 4
        for k, share in enumerate(shares):
            i = k + col - 2 * (col & k)
            share[:part] = low(turned_ref[pl.ds(pl.multiple_of(i * part, part), part), :])
        jb_sum = sum_ref[...].T[:1]
        first = low(jb_sum)
        rest = jb_sum - wide(first)
        middle = low(rest)
        final = low(rest - wide(middle))
        shift = mm(jnp.concatenate([first, middle, final], axis=0), wj_ref[...])
        rows = [
            gain,
            jnp.sum(shift, axis=0, keepdims=True),
            jnp.sum(sums_ref[0], axis=0, keepdims=True),
            jnp.sum(sums_ref[1], axis=0, keepdims=True),
            jnp.sum(up_ref[...], axis=0, keepdims=True),
        ]
        jb_sum = jnp.concatenate([jb_sum, jnp.zeros((1, width - height), jnp.float32)], axis=1)
        for whole in (jnp.sum(hsum_ref[...], axis=0, keepdims=True), jb_sum):
            rows += [jnp.where(quarter == i, whole, 0.0) for i in range(N)]
        rows.append(jnp.zeros((3, width), jnp.float32))
        vector = jnp.concatenate(rows, axis=0)
        vector_ref[...] = vector
        coarse = low(vector)
        fine = low(vector - wide(coarse))
        rest = jnp.zeros((16, 2 * height - width), jnp.bfloat16)
        pieces = [coarse[:, :height], fine[:, :height]]
        pieces += [jnp.concatenate([piece[:, height:], rest], axis=1) for piece in (coarse, fine)]
        for share in shares[1:]:
            for n, piece in enumerate(pieces):
                share[part + 16 * n : part + 16 * (n + 1)] = piece


def joint_gradient(spot, jb, unit, wj, gain, shift, sums, up_sum, hsum):
    height, total = jb.shape
    width = unit.shape[1]
    tile = total // N
    fixed = lambda *dims: pl.BlockSpec(dims, lambda s, spot: (0,) * len(dims))
    shapes = [(width // 4, height)] + [(width // 4 + 64, height)] * 3
    return pl.pallas_call(
        joint_kernel,
        grid_spec=pltpu.PrefetchScalarGridSpec(
            num_scalar_prefetch=1,
            grid=(N,),
            in_specs=[
                pl.BlockSpec((height, tile), lambda s, spot: (0, s)),
                pl.BlockSpec((tile, width), lambda s, spot: (s, 0)),
                fixed(height, width),
                fixed(1, width),
                fixed(1, width),
                fixed(2, 8, width),
                fixed(8, width),
                fixed(*hsum.shape),
            ],
            out_specs=[fixed(*dims) for dims in shapes] + [fixed(16, width)],
            scratch_shapes=[
                pltpu.VMEM((height, width), jnp.float32),
                pltpu.VMEM((width, height), jnp.float32),
                pltpu.VMEM((height, 128), jnp.float32),
            ],
        ),
        out_shape=[jax.ShapeDtypeStruct(dims, jnp.bfloat16) for dims in shapes]
        + [jax.ShapeDtypeStruct((16, width), jnp.float32)],
        compiler_params=pltpu.CompilerParams(vmem_limit_bytes=VMEM),
        cost_estimate=pl.CostEstimate(
            flops=0, bytes_accessed=0, transcendentals=0
        ),
    )(spot, jb, unit, wj, gain, shift, sums, up_sum, hsum)


def pack(vector, width):
    coarse = low(vector)
    fine = low(vector - wide(coarse))
    rest = jnp.zeros((vector.shape[0], 2 * width - vector.shape[1]), jnp.bfloat16)
    pieces = [coarse[:, :width], fine[:, :width]]
    pieces += [jnp.concatenate([piece[:, width:], rest], axis=1) for piece in (coarse, fine)]
    return jnp.concatenate(pieces, axis=0)


def unpack(rows, size):
    rows = wide(rows).reshape(4, 16, -1)
    return jnp.concatenate([rows[0] + rows[1], (rows[2] + rows[3])[:, : size - rows.shape[2]]], axis=1)


def hop(value, pairs):
    return lax.ppermute(value, ("core", "blk"), [(a[0] * N + a[1], b[0] * N + b[1]) for a, b in pairs])


PLACES = [(c, z) for c in range(2) for z in range(N)]
MAIN = [(z // 2, z) for z in range(N)]
CORE_SWAP = [((c, z), (1 - c, z)) for c, z in PLACES]
NEAR_SWAP = [((c, z), (c, z ^ 1)) for c, z in PLACES]
FAR_SWAP = [((c, z), (c, z ^ 2)) for c, z in PLACES]
FAR_HOME = [((c, z), (1 - c, z ^ 2)) for c, z in PLACES if c != z // 2]


HOME = [((c, z), (c, z ^ 1)) for c, z in MAIN] + FAR_HOME
OFF_MAIN = [(c, z) for c, z in PLACES if c != z // 2]
FROM_MAIN = [((c, z), (1 - c, z)) for c, z in MAIN]
TO_MAIN = [((c, z), (1 - c, z)) for c, z in OFF_MAIN]
NEAR_OFF = [((c, z), (c, z ^ 1)) for c, z in OFF_MAIN]


def tie(*arrays):
    return lax.optimization_barrier(arrays)


def near_sum(keep, got):
    rows = keep.shape[0] // 2
    return low(wide(keep[rows:]) + wide(got[rows:]))


def home_sum(keep, got, near, got_near, main):
    rows = keep.shape[0] // 2
    return jnp.where(main, near, low(wide(keep[:rows]) + wide(got[:rows]) + wide(got_near)))


def own_sum(keep, got, got_home, main):
    rows = keep.shape[0] // 2
    return jnp.where(main, wide(keep[:rows]) + wide(got[:rows]), 0.0) + wide(got_home)


def pick(value, axis, index):
    return lax.dynamic_index_in_dim(value, index, axis, keepdims=False)


def plane(values):
    return [lax.ppermute(value, "col", [(i, i ^ (k + 1)) for i in range(4)]) for k, value in enumerate(values)]


NEAR = [((c, z), (c, z ^ 1)) for c, z in PLACES]


def first_pieces(value, near):
    return pick(value, 1, 1 - near).reshape(-1, value.shape[-1])


def second_pieces(value, got, core, near):
    got = got.reshape((2,) + value.shape[2:])
    return jnp.concatenate([pick(pick(value, 1, near), 0, 1 - core), pick(got, 0, 1 - core)], axis=0)


def quarters(quarter, line, got, last, core, near):
    size = line.shape[2]
    mine = chosen(2 * core + near, [line[0, 0], line[0, 1], line[1, 0], line[1, 1]])
    pieces = [mine, last[:size], jnp.where(core == 0, got[:size], got[size : 2 * size]), last[size : 2 * size]]
    return [chosen(quarter ^ k, pieces) for k in range(N)]


def finish_kernel(spot_ref, line_ref, got_ref, last_ref, reduce_ref, expand_out, dense_out, reduce_out):
    core, near, half = spot_ref[0], spot_ref[1], spot_ref[2]
    pieces = quarters(2 * near + core, wide(line_ref[...]), wide(got_ref[...]), wide(last_ref[...]), core, near)
    rows = expand_out.shape[0]
    for e in range(pieces[0].shape[1] // 128):
        for slot in range(N):
            piece = pieces[slot ^ (2 * (e % 2))]
            to = (N * e + slot) * 128
            expand_out[:, to : to + 128] = piece[:rows, e * 128 : (e + 1) * 128]
    dense_out[...] = chosen(2 * core + half, [piece[rows:] for piece in pieces])
    reduce_out[...] = wide(reduce_ref[...])


def finish(spot, line, got, last, reduced):
    rows, width = line.shape[2] // 2, line.shape[3]
    return pl.pallas_call(
        finish_kernel,
        in_specs=[pl.BlockSpec(memory_space=pltpu.SMEM)] + [pl.BlockSpec(memory_space=pltpu.VMEM)] * 4,
        out_specs=[pl.BlockSpec(memory_space=pltpu.VMEM)] * 3,
        out_shape=[
            jax.ShapeDtypeStruct((rows, N * width), jnp.float32),
            jax.ShapeDtypeStruct((rows, width), jnp.float32),
            jax.ShapeDtypeStruct(reduced.shape, jnp.float32),
        ],
        compiler_params=pltpu.CompilerParams(vmem_limit_bytes=VMEM),
    )(spot, line, got, last, reduced)


def joint_finish_kernel(spot_ref, line_ref, got_ref, last_ref, out_ref):
    core, near = spot_ref[0], spot_ref[1]
    pieces = quarters(2 * near + core, wide(line_ref[...]), wide(got_ref[...]), wide(last_ref[...]), core, near)
    for n in range(pieces[0].shape[1] // (2 * HEAD)):
        for slot in range(0, N, 2):
            for other in range(2):
                at = (2 * n + other) * HEAD
                to = ((2 * n + other) * N + slot) * HEAD
                pair = [piece[:, at : at + HEAD] for piece in pieces[slot : slot + 2]]
                out_ref[:, to : to + 2 * HEAD] = jnp.concatenate(pair, axis=1)


def joint_finish(spot, line, got, last):
    rows, width = line.shape[2:]
    return pl.pallas_call(
        joint_finish_kernel,
        in_specs=[pl.BlockSpec(memory_space=pltpu.SMEM)] + [pl.BlockSpec(memory_space=pltpu.VMEM)] * 3,
        out_specs=pl.BlockSpec(memory_space=pltpu.VMEM),
        out_shape=jax.ShapeDtypeStruct((rows, N * width), jnp.float32),
        compiler_params=pltpu.CompilerParams(vmem_limit_bytes=VMEM),
    )(spot, line, got, last)


def split_local(
    tokens,
    lengths,
    first_gain,
    first_shift,
    second_gain,
    second_shift,
    joint_weight,
    joint_bias,
    dense_weight,
    dense_bias,
    expand_weight,
    expand_bias,
    reduce_weight,
    reduce_bias,
    cotangent,
):
    col, core, z = lax.axis_index("col"), lax.axis_index("core"), lax.axis_index("blk")
    half, near = z // 2, z % 2
    quarter = 2 * near + core
    main = core == half
    flag = main.astype(jnp.int32)
    rows, width = tokens.shape[1:]
    total = rows * N
    units = expand_weight.shape[1]
    groups = units // (N * 128)
    heads = HEADS // N
    own_x, own_g = tokens[0], cotangent[0]
    row_of = lambda vector: vector.reshape(1, -1)

    x_other = hop(own_x, FROM_MAIN)
    x_first = hop(own_x, HOME)

    wj, wd, we, wr = prepare(quarter, joint_weight, dense_weight, expand_weight, reduce_weight)
    bj = pick(joint_bias.reshape(3, heads, N, HEAD), 2, quarter).reshape(-1, 1)
    be = expand_bias.reshape(groups // 2, 2, N, 128)
    be = jnp.stack([pick(be[:, 0], 1, quarter), pick(be[:, 1], 1, quarter ^ 2)], axis=1).reshape(1, -1)
    first_row, second_row = row_of(first_gain), row_of(second_gain)

    weights = [wj, bj, we, be, wr, first_row, row_of(first_shift), second_row, row_of(second_shift)]

    sizes = jnp.where(main, lengths, hop(lengths, CORE_SWAP))
    number, offset = doc_tables(sizes, jnp.arange(total, dtype=jnp.int32))
    inverse = 10000.0 ** (-2.0 * jnp.arange(ROTARY // 2, dtype=jnp.float32) / ROTARY)
    phase = inverse[:, None] * offset.astype(jnp.float32)
    tables = [jnp.cos(phase), jnp.sin(phase)]
    docs = lengths.shape[1]
    same = number == jnp.arange(HEAD, dtype=jnp.int32)[:, None]
    used = jnp.arange(HEAD)[:, None] < docs
    qx = low(jnp.where(same & used, 1.0, 0.0))
    kx = low(jnp.where(used & ~same, NEG, 0.0))

    spots = [z, z ^ (2 - flag), z ^ (1 + flag), z ^ 3]
    zero, one = jnp.int32(0), jnp.int32(1)
    state = run_tokens(0, jnp.stack([spots[0], 1 - flag]), [own_x, x_other], weights, tables, None)
    x_first, *state = tie(x_first, *state)
    x_second = hop(x_first, NEAR_OFF)
    x_first_other = hop(x_first, CORE_SWAP)
    state = run_tokens(1, jnp.stack([spots[1], zero]), [x_first], weights, tables, state)
    x_second, own_g_late, *state = tie(x_second, own_g, *state)
    x_second_other = hop(x_second, TO_MAIN)
    g_first = hop(own_g_late, HOME)
    g_other = hop(own_g_late, FROM_MAIN)
    spot = jnp.stack([spots[2], spots[3], zero, 2 - flag])
    state = run_tokens(2, spot, [x_first_other, x_second_other, x_second], weights, tables, state)
    qkv, unit, second, active, slope, feed = state
    order = z ^ (jnp.arange(N, dtype=jnp.int32) ^ (2 * flag))
    qkv = qkv.reshape(3, heads, HEAD, total)
    attended = attend_forward(qkv, kx, qx, 0, heads // 2, None)
    g_first, *attended = tie(g_first, *attended)
    g_second = hop(g_first, NEAR_OFF)
    g_first_other = hop(g_first, CORE_SWAP)
    mixed, full, inverse_sum, shares = attend_forward(qkv, kx, qx, heads // 2, heads // 2, attended)
    g_second, mixed = tie(g_second, mixed)
    mixed = mixed.reshape(-1, total)
    g_second_other = hop(g_second, TO_MAIN)
    out_send, out_keep = deliver(order, mixed, wd, feed)

    spot = jnp.stack([*spots, 1 - flag, 2 * one, 3 * one, 5 - flag])
    spot, out_send, out_keep = tie(spot, out_send, out_keep)
    out_got = hop(out_send, CORE_SWAP)
    gs = (own_g, g_other, g_first, g_first_other, g_second_other, g_second)
    mg, back, ups, hg, sums, hsum = run_upstream(spot, gs, [wd, we, wr, second_row], unit, slope)
    out_near = near_sum(out_keep, out_got)
    out_near, hg = tie(out_near, hg)
    out_got_near = hop(out_near, NEAR_OFF)

    spot = jnp.stack([*spots, col])
    kept_share, *shares_out = weight_gradients(spot, second, hg, active, ups, mixed)
    out_home = home_sum(out_keep, out_got, out_near, out_got_near, main)
    out_home, mg, *shares_out = tie(out_home, mg, *shares_out)
    out_got_home = hop(out_home, HOME)
    shares_got = plane(shares_out)

    jb = attend_backward(qkv, mg.reshape(heads, HEAD, total), full, inverse_sum, shares, tables)
    jb = jb.reshape(-1, total)

    spot = jnp.stack([col, quarter])
    up_sum = jnp.sum(wide(own_g).reshape(-1, 8, width), axis=0)
    kept_joint, *joint_out, vector = joint_gradient(
        spot, jb, unit, wj, first_row, row_of(first_shift), sums, up_sum, hsum
    )
    jb, *joint_out = tie(jb, *joint_out)
    joint_got = plane(joint_out)

    send, keep = deliver(order, jb, wj, back, first_row)

    send, out_got_home, *shares_got = tie(send, out_got_home, *shares_got)
    share = wide(kept_share) + sum(wide(piece) for piece in shares_got)
    kept = near ^ half
    part = width // 4
    expand_part = share[:part].reshape(2, 2, 2, part // 8, units // N)
    reduce_part = share[part : part + units // (4 * N)].reshape(2, -1, width)
    dense_part = share[part + units // (4 * N) :]
    far_send = [pick(expand_part, 1, 1 - half).reshape(part // 2, -1), pick(reduce_part, 0, 1 - kept), dense_part]
    far_send = low(jnp.concatenate(far_send, axis=0))
    far_send, send = tie(far_send, send)
    got = hop(send, CORE_SWAP)
    far_got = hop(far_send, FAR_SWAP)
    near_part = near_sum(keep, got)
    out = own_sum(out_keep, out_got, out_got_home, main)
    inputs = wide(own_x)
    result = low(inputs + out + (dense_bias + reduce_bias))
    got_near = hop(near_part, NEAR_OFF)

    got_near, *joint_got = tie(got_near, *joint_got)
    joint_part = wide(kept_joint) + sum(wide(piece[:part]) for piece in joint_got)
    vector = vector + sum(unpack(piece[part:], width) for piece in joint_got)
    joint_width = joint_part.shape[1]
    joint_part = joint_part.reshape(2, 2, 2, part // 8, joint_width)
    joint_far_send = jnp.concatenate(
        [low(pick(joint_part, 1, 1 - half)).reshape(part // 2, joint_width), pack(vector, joint_width)], axis=0
    )
    home = home_sum(keep, got, near_part, got_near, main)
    home, joint_far_send, result = tie(home, joint_far_send, result)
    got_home = hop(home, HOME)
    joint_far = hop(joint_far_send, FAR_SWAP)
    home, far_got = tie(home, far_got)
    far_got = wide(far_got)
    expand_part = low(pick(expand_part, 1, half).reshape(part // 2, -1) + far_got[: part // 2])
    reduce_part = low(pick(reduce_part, 0, kept) + far_got[part // 2 : part // 2 + 128])
    dense_part = low(dense_part + far_got[part // 2 + 128 :]).reshape(2, HEAD // 2, width)
    line = jnp.concatenate(
        [
            expand_part.reshape(2, 2, part // 8, -1),
            jnp.broadcast_to(dense_part[None], (2,) + dense_part.shape),
        ],
        axis=2,
    )
    line_send = first_pieces(line, near)
    line_got = hop(line_send, NEAR)
    reduce_got = hop(reduce_part, [((c, s), ((s % 2) ^ (s // 2), 2 * (s // 2) + c)) for c, s in PLACES])
    scaled = own_sum(keep, got, got_home, main)
    _, unit_rows, inverse_root = normalize(inputs, first_gain, first_shift)
    input_back = inverse_root * (
        scaled
        - jnp.mean(scaled, axis=-1, keepdims=True)
        - unit_rows * jnp.mean(scaled * unit_rows, axis=-1, keepdims=True)
    )
    tokens_gradient = low(wide(own_g) + input_back)
    line_got, reduce_got, tokens_gradient = tie(line_got, reduce_got, tokens_gradient)
    line_send = second_pieces(line, line_got, core, near)
    line_last = hop(line_send, CORE_SWAP)
    joint_far, line_send = tie(joint_far, line_send)
    joint_part = low(pick(joint_part, 1, half).reshape(part // 2, joint_width) + wide(joint_far[: part // 2]))
    vector = vector + unpack(joint_far[part // 2 :], width)
    joint_line = joint_part.reshape(2, 2, part // 8, joint_width)
    joint_got = hop(jnp.concatenate([first_pieces(joint_line, near), pack(vector, joint_width)], axis=0), NEAR)
    spot = jnp.stack([core, near, half])
    expand_mine, dense_mine, reduce_mine = finish(spot, line, line_got, line_last, reduce_got)
    joint_got, expand_mine = tie(joint_got, expand_mine)
    vector = vector + unpack(joint_got[part // 4 :], width)
    joint_send = second_pieces(joint_line, joint_got[: part // 4], core, near)
    joint_last = hop(jnp.concatenate([joint_send, pack(vector, joint_width)], axis=0), CORE_SWAP)
    vector = vector + unpack(joint_last[part // 4 :], width)
    joint_mine = joint_finish(spot, joint_line, joint_got, joint_last)

    device = (2 * col + core) * N + z
    share = width // (8 * N)
    head_row = lambda head: 5 + N + head % N
    cut = lambda row, start, size: lax.dynamic_slice(vector, (row, start), (1, size))[0]
    pieces = [cut(row, device * share, share) for row in range(5)]
    pieces[4:] = [
        cut(head_row(device % HEADS), (device // HEADS * heads + device % HEADS // N) * HEAD, HEAD),
        cut(head_row(device // 2), (2 * heads + device // 2 // N) * HEAD + device % 2 * share, share),
        pieces[4],
        cut(5 + (z ^ (2 * core)), (2 * col + core) * 128, 128),
    ]

    return (
        result[None],
        tokens_gradient[None],
        *pieces[:4],
        joint_mine,
        pieces[4],
        pieces[5],
        dense_mine,
        pieces[6],
        expand_mine,
        pieces[7],
        reduce_mine,
        pieces[6],
    )


def solution(mesh):
    count, blocks = mesh.devices.shape
    split = blocks == N and count == 8
    if split:
        mesh = jax.sharding.Mesh(mesh.devices.reshape(count // 2, 2, blocks), ("col", "core", "blk"))
        batch = ("col", "core")
        every = ("col", "core", "blk")
    else:
        batch, every = "batch", ("batch", "blk")
    by_rows = P(batch, "blk", None)
    placed = (by_rows, P(batch, None)) + (P(),) * 12 + (by_rows,)
    vector, matrix = P(every), P(every, None)
    return jax.shard_map(
        split_local if split else local,
        mesh=mesh,
        in_specs=placed,
        out_specs=(
            by_rows,
            by_rows,
            vector,
            vector,
            vector,
            vector,
            matrix,
            vector,
            vector,
            matrix,
            vector,
            matrix,
            vector,
            matrix,
            vector,
        ),
        check_vma=False,
    )
```

```python
from functools import partial

import jax
import jax.numpy as jnp
from jax import lax
from jax.experimental import pallas as pl
from jax.experimental.pallas import tpu as pltpu
from jax.sharding import PartitionSpec as P

HEADS = 16
HEAD = 64
ROTARY = 16


EPSILON = 1e-05
MASKED = -1e30


def doc_tables(lengths, positions):
    doc_ends = jnp.cumsum(lengths, axis=-1)
    doc_starts = doc_ends - lengths
    doc_number = jnp.sum(
        (positions[None, :, None] >= doc_ends[:, None, :]).astype(jnp.int32), axis=-1
    )
    matches = (
        doc_number[:, :, None] == jnp.arange(lengths.shape[-1], dtype=jnp.int32)[None, None, :]
    )
    begins = jnp.sum(jnp.where(matches, doc_starts[:, None, :], 0), axis=-1)
    return (doc_number, positions[None, :] - begins)


def angles(offsets):
    half_width = ROTARY // 2
    inverse = 10000.0 ** (-2.0 * jnp.arange(half_width, dtype=jnp.float32) / ROTARY)
    phase = offsets.astype(jnp.float32)[..., None] * inverse
    return (jnp.cos(phase), jnp.sin(phase))


def rotate(values, cosine, sine_table, direction):
    half_width = cosine.shape[-1]
    lead_part = values[..., :half_width]
    tail_part = values[..., half_width : 2 * half_width]
    cosine = cosine[:, :, None, :]
    sine_table = sine_table[:, :, None, :] * direction
    return jnp.concatenate(
        [
            lead_part * cosine - tail_part * sine_table,
            tail_part * cosine + lead_part * sine_table,
            values[..., 2 * half_width :],
        ],
        axis=-1,
    )


def normalize(values, gain_row, shift_row):
    center = values - jnp.mean(values, axis=-1, keepdims=True)
    spread = jnp.mean(center * center, axis=-1, keepdims=True)
    inverse_root = lax.rsqrt(spread + EPSILON)
    unit_rows = center * inverse_root
    return (unit_rows * gain_row + shift_row, unit_rows, inverse_root)


def normalize_back(upstream, unit_rows, inverse_root, gain_row):
    scaled_back = upstream * gain_row
    input_back = inverse_root * (
        scaled_back
        - jnp.mean(scaled_back, axis=-1, keepdims=True)
        - unit_rows * jnp.mean(scaled_back * unit_rows, axis=-1, keepdims=True)
    )
    return (input_back, jnp.sum(upstream * unit_rows, axis=0), jnp.sum(upstream, axis=0))


def outer(left_rows, right_rows):
    return lax.dot_general(
        left_rows, right_rows, (((0,), (0,)), ((), ())), preferred_element_type=jnp.float32
    )


def against(left_rows, weight_rows):
    return lax.dot_general(
        left_rows, weight_rows, (((1,), (1,)), ((), ())), preferred_element_type=jnp.float32
    )


def over_piece(stepper, running, segment, stride):
    sub_count = segment.shape[1] // stride

    def one_turn(position, current):
        part_rows = lax.dynamic_slice_in_dim(segment, position * stride, stride, 1)
        return stepper(current, part_rows, position * stride)

    return lax.fori_loop(0, sub_count, one_turn, running)


def local(
    tokens,
    lengths,
    first_gain,
    first_shift,
    second_gain,
    second_shift,
    joint_weight,
    joint_bias,
    dense_weight,
    dense_bias,
    expand_weight,
    expand_bias,
    reduce_weight,
    reduce_bias,
    cotangent,
):
    sequences, stride, model_width = tokens.shape
    cycle_size = lax.axis_size("blk")
    seq_total = stride * cycle_size
    rank_here = lax.axis_index("blk")
    row_count = sequences * stride
    factor = HEAD ** (-0.5)
    head_shape = (sequences, stride, HEADS, HEAD)
    places = jnp.arange(seq_total, dtype=jnp.int32)
    number_all, offset_all = doc_tables(lengths, places)
    first_place = rank_here * stride
    query_number = lax.dynamic_slice_in_dim(number_all, first_place, stride, 1)
    query_offset = lax.dynamic_slice_in_dim(offset_all, first_place, stride, 1)
    query_place = first_place + jnp.arange(stride, dtype=jnp.int32)
    last_place = first_place + stride - 1
    cosine, sine_table = angles(query_offset)
    inputs = tokens.reshape(row_count, model_width).astype(jnp.float32)
    first_norm, first_unit, first_scale = normalize(inputs, first_gain, first_shift)
    normed = first_norm.astype(jnp.bfloat16)
    joint_out = jnp.dot(normed, joint_weight, preferred_element_type=jnp.float32) + joint_bias
    queries = rotate(
        joint_out[:, :model_width].reshape(head_shape), cosine, sine_table, 1.0
    ).astype(jnp.bfloat16)
    key_rows = rotate(
        joint_out[:, model_width : 2 * model_width].reshape(head_shape), cosine, sine_table, 1.0
    ).astype(jnp.bfloat16)
    value_rows = joint_out[:, 2 * model_width :].astype(jnp.bfloat16)
    pair_local = jnp.concatenate(
        [
            key_rows.reshape(sequences, stride, model_width),
            value_rows.reshape(sequences, stride, model_width),
        ],
        axis=-1,
    )

    def masked_scores(key_part, begin_row, row_span):
        key_number = lax.dynamic_slice_in_dim(number_all, begin_row, row_span, 1)
        key_place = begin_row + jnp.arange(row_span, dtype=jnp.int32)
        allowed = (query_number[:, :, None] == key_number[:, None, :]) & (
            key_place[None, None, :] <= query_place[None, :, None]
        )
        allowed = allowed[:, None]
        scores = (
            jnp.einsum("sqhd,skhd->shqk", queries, key_part, preferred_element_type=jnp.float32)
            * factor
        )
        return (jnp.where(allowed, scores, MASKED), allowed)

    def split_piece(segment):
        row_span = segment.shape[1]
        key_part = segment[:, :, :model_width].reshape(sequences, row_span, HEADS, HEAD)
        value_part = segment[:, :, model_width:].reshape(sequences, row_span, HEADS, HEAD)
        return (key_part, value_part, row_span)

    def gated(kernel):

        def stepper(running, segment, begin_row):
            return lax.cond(
                begin_row <= last_place,
                lambda current: kernel(current, segment, begin_row),
                lambda current: current,
                running,
            )

        return stepper

    def forward_kernel(running, segment, begin_row):
        row_peak, row_total, weighted = running
        key_part, value_part, row_span = split_piece(segment)
        scores, allowed = masked_scores(key_part, begin_row, row_span)
        new_peak = jnp.maximum(row_peak, jnp.max(scores, axis=-1))
        shares = jnp.where(allowed, jnp.exp(scores - new_peak[..., None]), 0.0)
        decay_factor = jnp.exp(row_peak - new_peak)
        row_total = row_total * decay_factor + jnp.sum(shares, axis=-1)
        update = jnp.einsum(
            "shqk,skhd->sqhd",
            shares.astype(jnp.bfloat16),
            value_part,
            preferred_element_type=jnp.float32,
        )
        weighted = weighted * jnp.transpose(decay_factor, (0, 2, 1))[..., None] + update
        return (new_peak, row_total, weighted)

    forward_step = gated(forward_kernel)
    initial = (
        jnp.full((sequences, HEADS, stride), MASKED, jnp.float32),
        jnp.zeros((sequences, HEADS, stride), jnp.float32),
        jnp.zeros(head_shape, jnp.float32),
    )
    forward_state = over_piece(
        forward_step, initial, lax.all_gather(pair_local, "blk", axis=1, tiled=True), stride
    )
    row_peak, row_total, weighted = forward_state
    mixed_full = weighted / jnp.transpose(row_total, (0, 2, 1))[..., None]
    log_total = row_peak + jnp.log(row_total)
    mixed = mixed_full.reshape(row_count, model_width).astype(jnp.bfloat16)
    attention_out = jnp.dot(mixed, dense_weight, preferred_element_type=jnp.float32) + dense_bias
    second_norm, second_unit, second_scale = normalize(inputs, second_gain, second_shift)
    second = second_norm.astype(jnp.bfloat16)
    hidden = jnp.dot(second, expand_weight, preferred_element_type=jnp.float32) + expand_bias
    active_full, gelu_pull = jax.vjp(partial(jax.nn.gelu, approximate=False), hidden)
    active = active_full.astype(jnp.bfloat16)
    feed_out = jnp.dot(active, reduce_weight, preferred_element_type=jnp.float32) + reduce_bias
    result = (
        (inputs + attention_out + feed_out)
        .astype(jnp.bfloat16)
        .reshape(sequences, stride, model_width)
    )
    upstream = cotangent.reshape(row_count, model_width)
    dense_grad = outer(mixed, upstream)
    bias_total = jnp.sum(upstream, axis=0, dtype=jnp.float32)
    reduce_grad = outer(active, upstream)
    hidden_grad = gelu_pull(against(upstream, reduce_weight))[0].astype(jnp.bfloat16)
    expand_grad = outer(second, hidden_grad)
    hidden_total = jnp.sum(hidden_grad, axis=0, dtype=jnp.float32)
    input_two, gain_second, shift_second = normalize_back(
        against(hidden_grad, expand_weight), second_unit, second_scale, second_gain
    )
    mixed_grad = against(upstream, dense_weight).astype(jnp.bfloat16)
    out_heads = mixed_grad.reshape(head_shape)
    delta_rows = jnp.transpose(jnp.sum(out_heads * mixed_full, axis=-1), (0, 2, 1))

    def backward_kernel(running, segment, begin_row):
        key_part, value_part, row_span = split_piece(segment)
        scores, allowed = masked_scores(key_part, begin_row, row_span)
        weights_now = jnp.where(allowed, jnp.exp(scores - log_total[..., None]), 0.0)
        weight_grad = jnp.einsum(
            "sqhd,skhd->shqk", out_heads, value_part, preferred_element_type=jnp.float32
        )
        score_grad = (weights_now * (weight_grad - delta_rows[..., None])).astype(jnp.bfloat16)
        query_grad = (
            running[0]
            + jnp.einsum(
                "shqk,skhd->sqhd", score_grad, key_part, preferred_element_type=jnp.float32
            )
            * factor
        )
        value_grad = jnp.einsum(
            "shqk,sqhd->skhd",
            weights_now.astype(jnp.bfloat16),
            out_heads,
            preferred_element_type=jnp.float32,
        )
        key_grad = (
            jnp.einsum("shqk,sqhd->skhd", score_grad, queries, preferred_element_type=jnp.float32)
            * factor
        )
        fresh_rows = jnp.concatenate(
            [
                key_grad.reshape(sequences, row_span, model_width),
                value_grad.reshape(sequences, row_span, model_width),
            ],
            axis=-1,
        )
        pair_grad = lax.dynamic_update_slice_in_dim(running[1], fresh_rows, begin_row, 1)
        return (query_grad, pair_grad)

    backward_step = gated(backward_kernel)
    back_initial = (
        jnp.zeros(head_shape, jnp.float32),
        jnp.zeros((sequences, seq_total, 2 * model_width), jnp.float32),
    )
    back_state = over_piece(
        backward_step, back_initial, lax.all_gather(pair_local, "blk", axis=1, tiled=True), stride
    )
    query_grad = back_state[0]
    pair_mine = lax.psum_scatter(back_state[1], "blk", scatter_dimension=1, tiled=True)
    query_back = rotate(query_grad, cosine, sine_table, -1.0).reshape(row_count, model_width)
    key_back = rotate(
        pair_mine[:, :, :model_width].reshape(head_shape), cosine, sine_table, -1.0
    ).reshape(row_count, model_width)
    value_back = pair_mine[:, :, model_width:].reshape(row_count, model_width)
    joint_back = jnp.concatenate([query_back, key_back, value_back], axis=-1).astype(jnp.bfloat16)
    joint_grad = outer(normed, joint_back)
    joint_total = jnp.sum(joint_back, axis=0, dtype=jnp.float32)
    front_total = joint_total[: 2 * model_width]
    value_total = joint_total[2 * model_width :]
    input_one, gain_first, shift_first = normalize_back(
        against(joint_back, joint_weight), first_unit, first_scale, first_gain
    )
    input_total = (
        (upstream.astype(jnp.float32) + input_one + input_two)
        .astype(jnp.bfloat16)
        .reshape(sequences, stride, model_width)
    )
    summed = (
        lax.psum_scatter(gain_first, ("batch", "blk"), scatter_dimension=0, tiled=True),
        lax.psum_scatter(shift_first, ("batch", "blk"), scatter_dimension=0, tiled=True),
        lax.psum_scatter(gain_second, ("batch", "blk"), scatter_dimension=0, tiled=True),
        lax.psum_scatter(shift_second, ("batch", "blk"), scatter_dimension=0, tiled=True),
        lax.psum_scatter(joint_grad, ("batch", "blk"), scatter_dimension=0, tiled=True),
        lax.psum_scatter(front_total, ("batch", "blk"), scatter_dimension=0, tiled=True),
        lax.psum_scatter(value_total, ("batch", "blk"), scatter_dimension=0, tiled=True),
        lax.psum_scatter(dense_grad, ("batch", "blk"), scatter_dimension=0, tiled=True),
        lax.psum_scatter(bias_total, ("batch", "blk"), scatter_dimension=0, tiled=True),
        lax.psum_scatter(expand_grad, ("batch", "blk"), scatter_dimension=0, tiled=True),
        lax.psum_scatter(hidden_total, ("batch", "blk"), scatter_dimension=0, tiled=True),
        lax.psum_scatter(reduce_grad, ("batch", "blk"), scatter_dimension=0, tiled=True),
    )
    return (
        result,
        input_total,
        summed[0],
        summed[1],
        summed[2],
        summed[3],
        summed[4],
        summed[5],
        summed[6],
        summed[7],
        summed[8],
        summed[9],
        summed[10],
        summed[11],
        summed[8],
    )


BQ = 512
N = 4
TM = 256
VMEM = 56 * 1024 * 1024
NEG = -1e30
NN = (((1,), (0,)), ((), ()))
NT = (((1,), (1,)), ((), ()))
TN = (((0,), (0,)), ((), ()))


def mm(left, right, form=NN):
    return lax.dot_general(left, right, form, preferred_element_type=jnp.float32)


def low(value):
    return value.astype(jnp.bfloat16)


def wide(value):
    return value.astype(jnp.float32)


def gelu_parts(hidden):
    size = jnp.abs(hidden) * (0.5**0.5)
    bell = jnp.exp(-(size * size))
    base = 1.0 + 0.3275911 * size
    guess = pl.reciprocal(base, approx=True)
    t = guess * (2.0 - base * guess)
    series = t * (
        0.5 * 0.254829592
        + t
        * (
            0.5 * -0.284496736
            + t * (0.5 * 1.421413741 + t * (0.5 * -1.453152027 + t * (0.5 * 1.061405429)))
        )
    )
    tail = series * bell
    return (jnp.where(hidden >= 0.0, 1.0 - tail, tail), bell)


def fold_rows(value):
    rows, columns = value.shape
    return jnp.sum(value.reshape(rows // 8, 8, columns), axis=0)


def prepare_kernel(spot_ref, wj_ref, wd_ref, we_ref, wr_ref, wj_out, wd_out, we_out, wr_out):
    turned = wj_ref[...].T
    wj_out[...] = jnp.where(lax.rem(spot_ref[0], 2) == 0, turned[:HEAD], turned[HEAD:])
    wd_out[...] = wd_ref[...]
    we_out[...] = we_ref[...]
    wr_out[...] = wr_ref[...]


def prepare(quarter, joint_weight, dense_weight, expand_weight, reduce_weight):
    width, units = expand_weight.shape
    heads = HEADS // N
    groups = units // (N * 128)
    kinds = 3 * heads
    pair = lambda s, spot: (0, (s // heads) * (HEADS // 2) + (s % heads) * (N // 2) + spot[0] // 2)
    row = lambda s: jnp.minimum(s, heads - 1)
    unit = lambda s: jnp.minimum(s, groups - 1)
    group = lambda s, spot: N * unit(s) + lax.rem(spot[0] + 2 * lax.rem(unit(s), 2), N)
    shape = lambda *dims: jax.ShapeDtypeStruct(dims, jnp.bfloat16)
    return pl.pallas_call(
        prepare_kernel,
        grid_spec=pltpu.PrefetchScalarGridSpec(
            num_scalar_prefetch=1,
            grid=(kinds,),
            in_specs=[
                pl.BlockSpec((width, 2 * HEAD), pair),
                pl.BlockSpec((HEAD, width), lambda s, spot: (N * row(s) + spot[0], 0)),
                pl.BlockSpec((width, 128), lambda s, spot: (0, group(s, spot))),
                pl.BlockSpec((128, width), lambda s, spot: (group(s, spot), 0)),
            ],
            out_specs=[
                pl.BlockSpec((HEAD, width), lambda s, spot: (s, 0)),
                pl.BlockSpec((HEAD, width), lambda s, spot: (row(s), 0)),
                pl.BlockSpec((width, 128), lambda s, spot: (0, unit(s))),
                pl.BlockSpec((128, width), lambda s, spot: (unit(s), 0)),
            ],
        ),
        out_shape=[
            shape(kinds * HEAD, width),
            shape(heads * HEAD, width),
            shape(width, groups * 128),
            shape(groups * 128, width),
        ],
        cost_estimate=pl.CostEstimate(flops=0, bytes_accessed=14 * width * width, transcendentals=0),
    )(quarter.reshape(1), joint_weight, dense_weight, expand_weight, reduce_weight)


def block_at(place, j):
    return place * (place + 1) // 2 + j


def forward_kernel(held, qkv_ref, kx_ref, qx_ref, *refs):
    mixed_ref, full_ref, inverse_ref, share_ref, key_ref, *scores = refs[held:]
    key_ref[...] = jnp.concatenate([qkv_ref[1, 0], kx_ref[...]], axis=0).T
    total = kx_ref.shape[1]
    state = {}

    def score(place, j):
        here = slice(place * BQ, (place + 1) * BQ)
        at = slice(j * BQ, (j + 1) * BQ)
        if j == 0:
            query_x = jnp.concatenate([qkv_ref[0, 0, :, here], qx_ref[:, here]], axis=0)
            state[place] = [query_x, jnp.full((8, BQ), NEG * 2, jnp.float32)]
        found = mm(key_ref[at, :], state[place][0])
        if j == place:
            key_row = lax.broadcasted_iota(jnp.int32, (BQ, BQ), 0)
            query_column = lax.broadcasted_iota(jnp.int32, (BQ, BQ), 1)
            found = jnp.where(key_row <= query_column, found, NEG)
        scores[place % 2][at, :] = found
        state[place][1] = jnp.maximum(state[place][1], jnp.max(found.reshape(BQ // 8, 8, BQ), axis=0))

    def weigh(place, j):
        here = slice(place * BQ, (place + 1) * BQ)
        at = slice(j * BQ, (j + 1) * BQ)
        if j == 0:
            peak = jnp.max(state[place][1], axis=0, keepdims=True)
            state[place] = [peak, jnp.zeros((8, BQ), jnp.float32), jnp.zeros((HEAD, BQ), jnp.float32)]
        share = jnp.exp(scores[place % 2][at, :] - state[place][0])
        state[place][1] = state[place][1] + jnp.sum(share.reshape(BQ // 8, 8, BQ), axis=0)
        share = low(share)
        share_ref[0, block_at(place, j)] = share
        state[place][2] = state[place][2] + mm(qkv_ref[2, 0, :, at], share)
        if j == place:
            inverse = 1.0 / jnp.sum(state[place][1], axis=0, keepdims=True)
            mixed = state[place][2] * inverse
            inverse_ref[0, :, here] = inverse
            full_ref[0, :, here] = mixed
            mixed_ref[0, :, here] = low(mixed)

    places = list(range(total // BQ))
    for j in range(places[0] + 1):
        score(places[0], j)
    for n, place in enumerate(places):
        for j in range(places[-1] + 2):
            if n + 1 < len(places) and j <= places[n + 1]:
                score(places[n + 1], j)
            if j <= place:
                weigh(place, j)


def attend_forward(qkv, kx, qx, first, count, before):
    _, heads, _, total = qkv.shape
    places = total // BQ
    blocks = block_at(places, 0)
    head_rows = lambda rows: pl.BlockSpec((1, rows, total), lambda h: (first + h, 0, 0))
    operands = [qkv, kx, qx]
    in_specs = [
        pl.BlockSpec((3, 1, HEAD, total), lambda h: (0, first + h, 0, 0)),
        pl.BlockSpec((HEAD, total), lambda h: (0, 0)),
        pl.BlockSpec((HEAD, total), lambda h: (0, 0)),
    ]
    aliases = {}
    if before is not None:
        for index, array in enumerate(before):
            aliases[len(operands)] = index
            operands.append(array)
            in_specs.append(pl.BlockSpec(memory_space=pl.ANY))
    return pl.pallas_call(
        partial(forward_kernel, len(aliases)),
        grid=(count,),
        in_specs=in_specs,
        out_specs=[
            head_rows(HEAD),
            head_rows(HEAD),
            head_rows(1),
            pl.BlockSpec((1, blocks, BQ, BQ), lambda h: (first + h, 0, 0, 0)),
        ],
        out_shape=[
            jax.ShapeDtypeStruct((heads, HEAD, total), jnp.bfloat16),
            jax.ShapeDtypeStruct((heads, HEAD, total), jnp.float32),
            jax.ShapeDtypeStruct((heads, 1, total), jnp.float32),
            jax.ShapeDtypeStruct((heads, blocks, BQ, BQ), jnp.bfloat16),
        ],
        scratch_shapes=[pltpu.VMEM((total, 2 * HEAD), jnp.bfloat16)] + [pltpu.VMEM((total, BQ), jnp.float32)] * 2,
        input_output_aliases=aliases,
        compiler_params=pltpu.CompilerParams(vmem_limit_bytes=VMEM),
        cost_estimate=pl.CostEstimate(
            flops=16 * HEAD * count * blocks * BQ * BQ,
            bytes_accessed=2 * count * blocks * BQ * BQ,
            transcendentals=count * blocks * BQ * BQ,
        ),
    )(*operands)


def backward_kernel(qkv_ref, mg_ref, full_ref, inverse_ref, share_ref, cos_ref, sin_ref, jb_ref, value_ref, acc_ref):
    total = cos_ref.shape[1]
    ones = (lax.broadcasted_iota(jnp.int32, (HEAD, total), 0) < 3).astype(jnp.bfloat16)
    value_ref[...] = jnp.concatenate([qkv_ref[2, 0], ones], axis=0).T
    half = ROTARY // 2
    blank = jnp.zeros((HEAD, BQ), jnp.bfloat16)
    row = lax.broadcasted_iota(jnp.int32, (HEAD, BQ), 0)

    def turn_back(rows, at):
        lead, tail = rows[:half], rows[half : 2 * half]
        cosine, sine = cos_ref[:, at], sin_ref[:, at]
        return low(
            jnp.concatenate([lead * cosine + tail * sine, tail * cosine - lead * sine, rows[2 * half :]], axis=0)
        )

    for place in reversed(range(total // BQ)):
        here = slice(place * BQ, (place + 1) * BQ)
        query_t = qkv_ref[0, 0, :, here]
        mg = low(wide(mg_ref[0, :, here]) * inverse_ref[0, :, here])
        delta = -jnp.sum(wide(mg) * full_ref[0, :, here], axis=0, keepdims=True)
        first = low(delta)
        rest = delta - wide(first)
        middle = low(rest)
        final = low(rest - wide(middle))
        extra = jnp.where(
            row == 0, wide(first), jnp.where(row == 1, wide(middle), jnp.where(row == 2, wide(final), 0.0))
        )
        mg_x = jnp.concatenate([mg, low(extra)], axis=0)
        mg_v = jnp.concatenate([blank, mg], axis=0)
        query_k = jnp.concatenate([query_t, blank], axis=0)
        query_grad = jnp.zeros((HEAD, BQ), jnp.float32)
        for j in range(place + 1):
            at = slice(j * BQ, (j + 1) * BQ)
            share = share_ref[0, block_at(place, j)]
            score_grad = low(wide(share) * mm(value_ref[at, :], mg_x))
            pair = mm(share, mg_v, NT) + mm(score_grad, query_k, NT)
            query_grad = query_grad + mm(qkv_ref[1, 0, :, at], score_grad)
            if (place + 1) * BQ < total:
                pair = pair + acc_ref[at, :]
            if j < place:
                acc_ref[at, :] = pair
            else:
                pair_t = pair.T
                jb_ref[1, 0, :, at] = turn_back(pair_t[:HEAD], at)
                jb_ref[2, 0, :, at] = low(pair_t[HEAD:])
        jb_ref[0, 0, :, here] = turn_back(query_grad * (HEAD**-0.5), here)


def attend_backward(qkv, mg, full, inverse, shares, tables):
    _, heads, _, total = qkv.shape
    blocks = shares.shape[1]
    head_rows = lambda rows: pl.BlockSpec((1, rows, total), lambda h: (h, 0, 0))
    kinds = pl.BlockSpec((3, 1, HEAD, total), lambda h: (0, h, 0, 0))
    table = pl.BlockSpec((ROTARY // 2, total), lambda h: (0, 0))
    return pl.pallas_call(
        backward_kernel,
        grid=(heads,),
        in_specs=[
            kinds,
            head_rows(HEAD),
            head_rows(HEAD),
            head_rows(1),
            pl.BlockSpec((1, blocks, BQ, BQ), lambda h: (h, 0, 0, 0)),
            table,
            table,
        ],
        out_specs=kinds,
        out_shape=jax.ShapeDtypeStruct((3, heads, HEAD, total), jnp.bfloat16),
        scratch_shapes=[
            pltpu.VMEM((total, 2 * HEAD), jnp.bfloat16),
            pltpu.VMEM((total, 2 * HEAD), jnp.float32),
        ],
        compiler_params=pltpu.CompilerParams(vmem_limit_bytes=VMEM),
        cost_estimate=pl.CostEstimate(
            flops=32 * HEAD * heads * blocks * BQ * BQ,
            bytes_accessed=2 * heads * blocks * BQ * BQ,
            transcendentals=0,
        ),
    )(qkv, mg, full, inverse, shares, *tables)


def chosen(index, options):
    value = options[-1]
    for k in reversed(range(len(options) - 1)):
        value = jnp.where(index == k, options[k], value)
    return value


def token_kernel(count, sub, chunk, spot_ref, *refs):
    sources = refs[:count]
    (wj_ref, bj_ref, we_ref, be_ref, wr_ref, g1_ref, s1_ref, g2_ref, s2_ref, cos_ref, sin_ref) = refs[count : count + 11]
    qkv_ref, unit_ref, second_ref, active_ref, slope_ref, feed_ref = refs[-6:]
    choice = spot_ref[pl.num_programs(0) + pl.program_id(0)]
    rows = sources[0].shape[0]
    half = ROTARY // 2
    part = wj_ref.shape[0] // 3
    for top in range(0, rows, sub):
        at = slice(top, top + sub)
        x = wide(chosen(choice, [source[at, :] for source in sources]))
        center = x - jnp.mean(x, axis=-1, keepdims=True)
        scale = lax.rsqrt(jnp.mean(center * center, axis=-1, keepdims=True) + EPSILON)
        unit = center * scale
        unit_ref[at, :] = low(unit)
        normed = low(unit * g1_ref[...] + s1_ref[...])
        second = low(unit * g2_ref[...] + s2_ref[...])
        second_ref[at, :] = second
        joint = mm(wj_ref[...], normed, NT) + bj_ref[...]
        cosine, sine = cos_ref[:, at], sin_ref[:, at]
        for kind in range(3):
            for head in range(part // HEAD):
                first = kind * part + head * HEAD
                turned = joint[first : first + HEAD]
                if kind < 2:
                    lead, tail = turned[:half], turned[half : 2 * half]
                    turned = jnp.concatenate(
                        [lead * cosine - tail * sine, tail * cosine + lead * sine, turned[2 * half :]], axis=0
                    )
                if kind == 0:
                    turned = turned * (HEAD**-0.5)
                qkv_ref[first : first + HEAD, at] = low(turned)
        for left in range(0, we_ref.shape[1], chunk):
            over = slice(left, left + chunk)
            hidden = mm(second, we_ref[:, over]) + be_ref[:, over]
            share, bell = gelu_parts(hidden)
            active_ref[at, over] = low(hidden * share)
            slope_ref[at, over] = low(share + hidden * bell * 0.3989422804014327)
    for top in range(0, rows, sub):
        at = slice(top, top + sub)
        feed_ref[at, :] = low(mm(active_ref[at, :], wr_ref[...]))


def run_tokens(slot, spot, data, weights, tables, before, sub=256, chunk=256):
    rows, width = data[0].shape
    total = tables[0].shape[1]
    wj, bj, we, be, wr, g1, s1, g2, s2 = weights
    units = we.shape[1]
    steps = spot.shape[0] // 2

    def whole(array):
        return pl.BlockSpec(array.shape, lambda i, spot: (0,) * array.ndim)

    column = lambda height: pl.BlockSpec((height, rows), lambda i, spot: (0, spot[i]))
    placed = pl.BlockSpec((rows, width), lambda i, spot: (spot[i], 0))
    arrived = lambda size: pl.BlockSpec((rows, size), lambda i, spot: (slot + i, 0))
    in_specs = [whole(w) for w in (*data, *weights)] + [column(ROTARY // 2)] * 2
    out_specs = [column(wj.shape[0]), placed, arrived(width), arrived(units), arrived(units), placed]
    shape = lambda *dims: jax.ShapeDtypeStruct(dims, jnp.bfloat16)
    out_shape = [shape(wj.shape[0], total)] + [shape(total, size) for size in (width, width, units, units, width)]
    operands = [spot, *data, *weights, *tables]
    aliases = {}
    if before is not None:
        for index, array in enumerate(before):
            aliases[len(operands)] = index
            operands.append(array)
            in_specs.append(pl.BlockSpec(memory_space=pl.ANY))
    return pl.pallas_call(
        partial(token_kernel, len(data), sub, chunk),
        grid_spec=pltpu.PrefetchScalarGridSpec(
            num_scalar_prefetch=1, grid=(steps,), in_specs=in_specs, out_specs=out_specs
        ),
        out_shape=out_shape,
        input_output_aliases=aliases,
        compiler_params=pltpu.CompilerParams(vmem_limit_bytes=VMEM),
        cost_estimate=pl.CostEstimate(flops=0, bytes_accessed=0, transcendentals=0),
    )(*operands)


def upstream_kernel(chunk, spot_ref, *refs):
    sources, refs = refs[:5], refs[5:]
    (wd_ref, we_ref, wr_ref, g2_ref, unit_ref, slope_ref) = refs[:6]
    (mg_ref, back_ref, up_ref, hg_ref, sums_ref, hsum_ref) = refs[6:12]
    buffer, sems = refs[12:]
    step = pl.program_id(0)
    steps = pl.num_programs(0)
    slot = lax.rem(step, 2)

    def fetch(which, into):
        for k, source in enumerate(sources):

            @pl.when(spot_ref[steps + which] == k)
            def _():
                pltpu.make_async_copy(source, buffer.at[into], sems.at[into]).start()

    @pl.when(step == 0)
    def _():
        fetch(0, 0)
        sums_ref[...] = jnp.zeros_like(sums_ref)
        hsum_ref[...] = jnp.zeros_like(hsum_ref)

    @pl.when(step + 1 < steps)
    def _():
        fetch(step + 1, 1 - slot)

    pltpu.make_async_copy(sources[0], buffer.at[slot], sems.at[slot]).wait()
    up = buffer[slot]
    up_ref[...] = up
    mg_ref[...] = low(mm(wd_ref[...], up, NT))
    for left in range(0, we_ref.shape[1], chunk):
        over = slice(left, left + chunk)
        piece = low(mm(up, wr_ref[over, :], NT) * wide(slope_ref[:, over]))
        hg_ref[:, over] = piece
        hsum_ref[:, over] += fold_rows(wide(piece))
    for left in range(0, we_ref.shape[0], chunk):
        over = slice(left, left + chunk)
        back = mm(hg_ref[...], we_ref[over, :], NT)
        back_ref[:, over] = low(back * g2_ref[:, over])
        sums_ref[0, :, over] += fold_rows(back * wide(unit_ref[:, over]))
        sums_ref[1, :, over] += fold_rows(back)


def run_upstream(spot, sources, weights, unit, slope, chunk=256):
    rows, width = sources[0].shape
    total = unit.shape[0]
    wd, we, wr, g2 = weights
    units = we.shape[1]
    steps = total // rows

    def whole(array):
        return pl.BlockSpec(array.shape, lambda i, spot: (0,) * array.ndim)

    fixed = lambda *dims: pl.BlockSpec(dims, lambda i, spot: (0,) * len(dims))
    column = lambda height: pl.BlockSpec((height, rows), lambda i, spot: (0, spot[i]))
    placed = pl.BlockSpec((rows, width), lambda i, spot: (spot[i], 0))
    arrived = lambda size: pl.BlockSpec((rows, size), lambda i, spot: (i, 0))
    in_specs = [pl.BlockSpec(memory_space=pl.ANY)] * 5 + [whole(w) for w in weights] + [placed, arrived(units)]
    out_specs = [column(wd.shape[0]), placed, arrived(width), arrived(units), fixed(2, 8, width), fixed(8, units)]
    shape = lambda *dims: jax.ShapeDtypeStruct(dims, jnp.bfloat16)
    out_shape = [
        shape(wd.shape[0], total),
        shape(total, width),
        shape(total, width),
        shape(total, units),
        jax.ShapeDtypeStruct((2, 8, width), jnp.float32),
        jax.ShapeDtypeStruct((8, units), jnp.float32),
    ]
    return pl.pallas_call(
        partial(upstream_kernel, chunk),
        grid_spec=pltpu.PrefetchScalarGridSpec(
            num_scalar_prefetch=1,
            grid=(steps,),
            in_specs=in_specs,
            out_specs=out_specs,
            scratch_shapes=[
                pltpu.VMEM((2, rows, width), jnp.bfloat16),
                pltpu.SemaphoreType.DMA((2,)),
            ],
        ),
        out_shape=out_shape,
        compiler_params=pltpu.CompilerParams(vmem_limit_bytes=VMEM),
        cost_estimate=pl.CostEstimate(
            flops=3 * total * width * (wd.shape[0] + 2 * units), bytes_accessed=12 * total * width, transcendentals=0
        ),
    )(spot, *sources, wd, we, wr, g2, unit, slope)


def weight_kernel(spot_ref, second_ref, hg_ref, active_ref, up_ref, mixed_ref, *refs):
    shares, (expand_sum, reduce_sum, dense_sum) = refs[:4], refs[4:]
    step = pl.program_id(0)
    steps = pl.num_programs(0)

    @pl.when(step == 0)
    def _():
        expand_sum[...] = jnp.zeros_like(expand_sum)
        reduce_sum[...] = jnp.zeros_like(reduce_sum)
        dense_sum[...] = jnp.zeros_like(dense_sum)

    up = up_ref[...]
    dense_sum[...] += mm(mixed_ref[...], up)
    expand_sum[...] += mm(second_ref[...], hg_ref[...], TN)
    reduce_sum[...] += mm(active_ref[...], up, TN)

    @pl.when(step == steps - 1)
    def _():
        col = spot_ref[steps]
        large, small = expand_sum.shape[0] // 4, dense_sum.shape[0] // 4
        for k, share in enumerate(shares):
            i = k + col - 2 * (col & k)
            at = pl.ds(pl.multiple_of(i * large, large), large)
            share[:large] = low(expand_sum[at, :])
            share[large : 2 * large] = low(reduce_sum[at, :])
            share[2 * large :] = low(dense_sum[pl.ds(pl.multiple_of(i * small, small), small), :])


def weight_gradients(spot, second, hg, active, ups, mixed):
    total, width = second.shape
    units = hg.shape[1]
    rows = total // N
    height = mixed.shape[0]
    fixed = lambda *dims: pl.BlockSpec(dims, lambda i, spot: (0,) * len(dims))
    arrived = lambda size: pl.BlockSpec((rows, size), lambda i, spot: (i, 0))
    dims = (width // 4 + units // 4 + height // 4, width)
    return pl.pallas_call(
        weight_kernel,
        grid_spec=pltpu.PrefetchScalarGridSpec(
            num_scalar_prefetch=1,
            grid=(N,),
            in_specs=[
                arrived(width),
                arrived(units),
                arrived(units),
                arrived(width),
                pl.BlockSpec((height, rows), lambda i, spot: (0, spot[i])),
            ],
            out_specs=[fixed(*dims)] * 4,
            scratch_shapes=[
                pltpu.VMEM((width, units), jnp.float32),
                pltpu.VMEM((units, width), jnp.float32),
                pltpu.VMEM((height, width), jnp.float32),
            ],
        ),
        out_shape=[jax.ShapeDtypeStruct(dims, jnp.bfloat16)] * 4,
        compiler_params=pltpu.CompilerParams(vmem_limit_bytes=VMEM),
        cost_estimate=pl.CostEstimate(
            flops=3 * total * width * (height + 2 * units), bytes_accessed=8 * total * width, transcendentals=0
        ),
    )(spot, second, hg, active, ups, mixed)


def deliver_kernel(order_ref, left_ref, weight_ref, add_ref, *refs):
    del order_ref
    send_ref, keep_ref = refs[-2:]
    step = pl.program_id(0)
    value = mm(left_ref[...], weight_ref[...], TN)
    if len(refs) > 2:
        value = value * refs[0][...]
    value = low(value + wide(add_ref[...]))

    @pl.when(step < pl.num_programs(0) // 2)
    def _():
        send_ref[...] = value

    @pl.when(step >= pl.num_programs(0) // 2)
    def _():
        keep_ref[...] = value


def deliver(order, left, weight, add, gain=None):
    depth, total = left.shape
    width = weight.shape[1]
    steps = N
    tile = total // N
    rows = pl.BlockSpec((tile, width), lambda s, order: (order[s], 0))
    in_specs = [
        pl.BlockSpec((depth, tile), lambda s, order: (0, order[s])),
        pl.BlockSpec((depth, width), lambda s, order: (0, 0)),
        rows,
    ]
    operands = [left, weight, add]
    if gain is not None:
        in_specs.append(pl.BlockSpec((1, width), lambda s, order: (0, 0)))
        operands.append(gain)
    return pl.pallas_call(
        deliver_kernel,
        grid_spec=pltpu.PrefetchScalarGridSpec(
            num_scalar_prefetch=1,
            grid=(steps,),
            in_specs=in_specs,
            out_specs=[
                pl.BlockSpec((tile, width), lambda s, order: (jnp.minimum(s, steps // 2 - 1), 0)),
                pl.BlockSpec((tile, width), lambda s, order: (jnp.maximum(s - steps // 2, 0), 0)),
            ],
        ),
        out_shape=[jax.ShapeDtypeStruct((total // 2, width), jnp.bfloat16)] * 2,
        compiler_params=pltpu.CompilerParams(vmem_limit_bytes=VMEM),
        cost_estimate=pl.CostEstimate(
            flops=0, bytes_accessed=0, transcendentals=0
        ),
    )(order, *operands)


def joint_kernel(spot_ref, jb_ref, unit_ref, wj_ref, gain_ref, shift_ref, sums_ref, up_ref, hsum_ref, *refs):
    shares, (vector_ref, total_ref, turned_ref, sum_ref) = refs[:4], refs[4:]
    step = pl.program_id(0)
    jb = jb_ref[...]
    height, tile = jb.shape
    width = unit_ref.shape[1]

    @pl.when(step == 0)
    def _():
        total_ref[...] = jnp.zeros_like(total_ref)
        sum_ref[...] = jnp.zeros_like(sum_ref)

    total_ref[...] += mm(jb, unit_ref[...])
    sum_ref[...] += mm(jb, jnp.ones((tile, 128), jnp.bfloat16))

    @pl.when(step == pl.num_programs(0) - 1)
    def _():
        col, quarter = spot_ref[0], spot_ref[1]
        gain = jnp.sum(total_ref[...] * wide(wj_ref[...]), axis=0, keepdims=True)
        turned_ref[...] = (total_ref[...] * gain_ref[...] + sum_ref[:, :1] * shift_ref[...]).T
        part = width // 4
        for k, share in enumerate(shares):
            i = k + col - 2 * (col & k)
            share[:part] = low(turned_ref[pl.ds(pl.multiple_of(i * part, part), part), :])
        jb_sum = sum_ref[...].T[:1]
        first = low(jb_sum)
        rest = jb_sum - wide(first)
        middle = low(rest)
        final = low(rest - wide(middle))
        shift = mm(jnp.concatenate([first, middle, final], axis=0), wj_ref[...])
        rows = [
            gain,
            jnp.sum(shift, axis=0, keepdims=True),
            jnp.sum(sums_ref[0], axis=0, keepdims=True),
            jnp.sum(sums_ref[1], axis=0, keepdims=True),
            jnp.sum(up_ref[...], axis=0, keepdims=True),
        ]
        jb_sum = jnp.concatenate([jb_sum, jnp.zeros((1, width - height), jnp.float32)], axis=1)
        for whole in (jnp.sum(hsum_ref[...], axis=0, keepdims=True), jb_sum):
            rows += [jnp.where(quarter == i, whole, 0.0) for i in range(N)]
        rows.append(jnp.zeros((3, width), jnp.float32))
        vector = jnp.concatenate(rows, axis=0)
        vector_ref[...] = vector
        coarse = low(vector)
        fine = low(vector - wide(coarse))
        rest = jnp.zeros((16, 2 * height - width), jnp.bfloat16)
        pieces = []
        for piece in (coarse, fine):
            pieces += [piece[:, :height], jnp.concatenate([piece[:, height:], rest], axis=1)]
        for share in shares[1:]:
            for n, piece in enumerate(pieces):
                share[part + 16 * n : part + 16 * (n + 1)] = piece


def joint_gradient(spot, jb, unit, wj, gain, shift, sums, up_sum, hsum):
    height, total = jb.shape
    width = unit.shape[1]
    tile = total // N
    fixed = lambda *dims: pl.BlockSpec(dims, lambda s, spot: (0,) * len(dims))
    shapes = [(width // 4, height)] + [(width // 4 + 64, height)] * 3
    return pl.pallas_call(
        joint_kernel,
        grid_spec=pltpu.PrefetchScalarGridSpec(
            num_scalar_prefetch=1,
            grid=(N,),
            in_specs=[
                pl.BlockSpec((height, tile), lambda s, spot: (0, s)),
                pl.BlockSpec((tile, width), lambda s, spot: (s, 0)),
                fixed(height, width),
                fixed(1, width),
                fixed(1, width),
                fixed(2, 8, width),
                fixed(8, width),
                fixed(*hsum.shape),
            ],
            out_specs=[fixed(*dims) for dims in shapes] + [fixed(16, width)],
            scratch_shapes=[
                pltpu.VMEM((height, width), jnp.float32),
                pltpu.VMEM((width, height), jnp.float32),
                pltpu.VMEM((height, 128), jnp.float32),
            ],
        ),
        out_shape=[jax.ShapeDtypeStruct(dims, jnp.bfloat16) for dims in shapes]
        + [jax.ShapeDtypeStruct((16, width), jnp.float32)],
        compiler_params=pltpu.CompilerParams(vmem_limit_bytes=VMEM),
        cost_estimate=pl.CostEstimate(
            flops=0, bytes_accessed=0, transcendentals=0
        ),
    )(spot, jb, unit, wj, gain, shift, sums, up_sum, hsum)


def pack(vector, width):
    rest = jnp.zeros((vector.shape[0], 2 * width - vector.shape[1]), jnp.float32)
    return low(jnp.concatenate([vector[:, :width], jnp.concatenate([vector[:, width:], rest], axis=1)], axis=0))


def unpack(rows, size):
    rows = wide(rows).reshape(-1, 2, 16, rows.shape[1]).sum(0)
    return jnp.concatenate([rows[0], rows[1][:, : size - rows.shape[2]]], axis=1)


def hop(value, pairs):
    return lax.ppermute(value, ("core", "blk"), [(a[0] * N + a[1], b[0] * N + b[1]) for a, b in pairs])


PLACES = [(c, z) for c in range(2) for z in range(N)]
MAIN = [(z // 2, z) for z in range(N)]
CORE_SWAP = [((c, z), (1 - c, z)) for c, z in PLACES]
NEAR_SWAP = [((c, z), (c, z ^ 1)) for c, z in PLACES]
FAR_SWAP = [((c, z), (c, z ^ 2)) for c, z in PLACES]
FAR_HOME = [((c, z), (1 - c, z ^ 2)) for c, z in PLACES if c != z // 2]


HOME = [((c, z), (c, z ^ 1)) for c, z in MAIN] + FAR_HOME
OFF_MAIN = [(c, z) for c, z in PLACES if c != z // 2]
FROM_MAIN = [((c, z), (1 - c, z)) for c, z in MAIN]
TO_MAIN = [((c, z), (1 - c, z)) for c, z in OFF_MAIN]
NEAR_OFF = [((c, z), (c, z ^ 1)) for c, z in OFF_MAIN]


def tie(*arrays):
    return lax.optimization_barrier(arrays)


def near_sum(keep, got):
    rows = keep.shape[0] // 2
    return low(wide(keep[rows:]) + wide(got[rows:]))


def home_sum(keep, got, near, got_near, main):
    rows = keep.shape[0] // 2
    return jnp.where(main, near, low(wide(keep[:rows]) + wide(got[:rows]) + wide(got_near)))


def own_sum(keep, got, got_home, main):
    rows = keep.shape[0] // 2
    return jnp.where(main, wide(keep[:rows]) + wide(got[:rows]), 0.0) + wide(got_home)


def pick(value, axis, index):
    return lax.dynamic_index_in_dim(value, index, axis, keepdims=False)


def plane(values):
    return [lax.ppermute(value, "col", [(i, i ^ (k + 1)) for i in range(4)]) for k, value in enumerate(values)]


NEAR = [((c, z), (c, z ^ 1)) for c, z in PLACES]


def first_pieces(value, near):
    return pick(value, 1, 1 - near).reshape(-1, value.shape[-1])


def second_pieces(value, got, core, near):
    got = got.reshape((2,) + value.shape[2:])
    return jnp.concatenate([pick(pick(value, 1, near), 0, 1 - core), pick(got, 0, 1 - core)], axis=0)


def quarters(quarter, line, got, last, core, near):
    size = line.shape[2]
    mine = chosen(2 * core + near, [line[0, 0], line[0, 1], line[1, 0], line[1, 1]])
    pieces = [mine, last[:size], jnp.where(core == 0, got[:size], got[size : 2 * size]), last[size : 2 * size]]
    return [chosen(quarter ^ k, pieces) for k in range(N)]


def finish_kernel(spot_ref, line_ref, got_ref, last_ref, reduce_ref, expand_out, dense_out, reduce_out):
    core, near, half = spot_ref[0], spot_ref[1], spot_ref[2]
    pieces = quarters(2 * near + core, wide(line_ref[...]), wide(got_ref[...]), wide(last_ref[...]), core, near)
    rows = expand_out.shape[0]
    for e in range(pieces[0].shape[1] // 128):
        for slot in range(N):
            piece = pieces[slot ^ (2 * (e % 2))]
            to = (N * e + slot) * 128
            expand_out[:, to : to + 128] = piece[:rows, e * 128 : (e + 1) * 128]
    dense_out[...] = chosen(2 * core + half, [piece[rows:] for piece in pieces])
    reduce_out[...] = wide(reduce_ref[...])


def finish(spot, line, got, last, reduced):
    rows, width = line.shape[2] // 2, line.shape[3]
    return pl.pallas_call(
        finish_kernel,
        in_specs=[pl.BlockSpec(memory_space=pltpu.SMEM)] + [pl.BlockSpec(memory_space=pltpu.VMEM)] * 4,
        out_specs=[pl.BlockSpec(memory_space=pltpu.VMEM)] * 3,
        out_shape=[
            jax.ShapeDtypeStruct((rows, N * width), jnp.float32),
            jax.ShapeDtypeStruct((rows, width), jnp.float32),
            jax.ShapeDtypeStruct(reduced.shape, jnp.float32),
        ],
        compiler_params=pltpu.CompilerParams(vmem_limit_bytes=VMEM),
    )(spot, line, got, last, reduced)


def joint_finish_kernel(spot_ref, line_ref, other_ref, near_ref, last_ref, out_ref):
    core, near = spot_ref[0], spot_ref[1]
    rows = out_ref.shape[0]
    line = wide(line_ref[...])
    mine = chosen(2 * core + near, [line[0, 0], line[0, 1], line[1, 0], line[1, 1]])
    pieces = [mine] + [wide(ref[:rows]) for ref in (other_ref, near_ref, last_ref)]
    pieces = [chosen((2 * near + core) ^ k, pieces) for k in range(N)]
    for n in range(mine.shape[1] // (2 * HEAD)):
        for slot in range(0, N, 2):
            for other in range(2):
                at = (2 * n + other) * HEAD
                to = ((2 * n + other) * N + slot) * HEAD
                pair = [piece[:, at : at + HEAD] for piece in pieces[slot : slot + 2]]
                out_ref[:, to : to + 2 * HEAD] = jnp.concatenate(pair, axis=1)


def joint_finish(spot, line, got):
    rows, width = line.shape[2:]
    return pl.pallas_call(
        joint_finish_kernel,
        in_specs=[pl.BlockSpec(memory_space=pltpu.SMEM)] + [pl.BlockSpec(memory_space=pltpu.VMEM)] * 4,
        out_specs=pl.BlockSpec(memory_space=pltpu.VMEM),
        out_shape=jax.ShapeDtypeStruct((rows, N * width), jnp.float32),
        compiler_params=pltpu.CompilerParams(vmem_limit_bytes=VMEM),
    )(spot, line, *got)


def split_local(
    tokens,
    lengths,
    first_gain,
    first_shift,
    second_gain,
    second_shift,
    joint_weight,
    joint_bias,
    dense_weight,
    dense_bias,
    expand_weight,
    expand_bias,
    reduce_weight,
    reduce_bias,
    cotangent,
):
    col, core, z = lax.axis_index("col"), lax.axis_index("core"), lax.axis_index("blk")
    half, near = z // 2, z % 2
    quarter = 2 * near + core
    main = core == half
    flag = main.astype(jnp.int32)
    rows, width = tokens.shape[1:]
    total = rows * N
    units = expand_weight.shape[1]
    groups = units // (N * 128)
    heads = HEADS // N
    own_x, own_g = tokens[0], cotangent[0]
    row_of = lambda vector: vector.reshape(1, -1)

    x_other = hop(own_x, FROM_MAIN)
    x_first = hop(own_x, HOME)

    wj, wd, we, wr = prepare(quarter, joint_weight, dense_weight, expand_weight, reduce_weight)
    bj = pick(joint_bias.reshape(3, heads, N, HEAD), 2, quarter).reshape(-1, 1)
    be = expand_bias.reshape(groups // 2, 2, N, 128)
    be = jnp.stack([pick(be[:, 0], 1, quarter), pick(be[:, 1], 1, quarter ^ 2)], axis=1).reshape(1, -1)
    first_row, second_row = row_of(first_gain), row_of(second_gain)

    weights = [wj, bj, we, be, wr, first_row, row_of(first_shift), second_row, row_of(second_shift)]

    sizes = jnp.where(main, lengths, hop(lengths, CORE_SWAP))
    number, offset = doc_tables(sizes, jnp.arange(total, dtype=jnp.int32))
    inverse = 10000.0 ** (-2.0 * jnp.arange(ROTARY // 2, dtype=jnp.float32) / ROTARY)
    phase = inverse[:, None] * offset.astype(jnp.float32)
    tables = [jnp.cos(phase), jnp.sin(phase)]
    docs = lengths.shape[1]
    same = number == jnp.arange(HEAD, dtype=jnp.int32)[:, None]
    used = jnp.arange(HEAD)[:, None] < docs
    qx = low(jnp.where(same & used, 1.0, 0.0))
    kx = low(jnp.where(used & ~same, NEG, 0.0))

    spots = [z, z ^ (2 - flag), z ^ (1 + flag), z ^ 3]
    zero, one = jnp.int32(0), jnp.int32(1)
    state = run_tokens(0, jnp.stack([spots[0], 1 - flag]), [own_x, x_other], weights, tables, None)
    x_first, own_g_late, *state = tie(x_first, own_g, *state)
    g_far = hop(own_g_late, FAR_HOME)
    x_second = hop(x_first, NEAR_OFF)
    x_first_other = hop(x_first, CORE_SWAP)
    state = run_tokens(1, jnp.stack([spots[1], zero]), [x_first], weights, tables, state)
    x_second, *state = tie(x_second, *state)
    x_second_other = hop(x_second, TO_MAIN)
    spot = jnp.stack([spots[2], spots[3], zero, 2 - flag])
    state = run_tokens(2, spot, [x_first_other, x_second_other, x_second], weights, tables, state)
    qkv, unit, second, active, slope, feed = state
    order = z ^ (jnp.arange(N, dtype=jnp.int32) ^ (2 * flag))
    qkv = qkv.reshape(3, heads, HEAD, total)
    g_far, qkv = tie(g_far, qkv)
    g_send = jnp.where(main, own_g, g_far)
    g_send, qkv = tie(g_send, qkv)
    g_near = hop(g_send, NEAR)
    g_other = hop(g_send, CORE_SWAP)
    mixed, full, inverse_sum, shares = attend_forward(qkv, kx, qx, 0, heads, None)
    g_near, mixed = tie(g_near, mixed)
    mixed = mixed.reshape(-1, total)
    g_near_other = hop(g_near, CORE_SWAP)
    out_send, out_keep = deliver(order, mixed, wd, feed)

    spot = jnp.stack([*spots, 1 - flag, 3 - flag, 4 - 3 * flag, 2 + 2 * flag])
    spot, out_send, out_keep = tie(spot, out_send, out_keep)
    out_got = hop(out_send, CORE_SWAP)
    gs = (own_g, g_other, g_near, g_far, g_near_other)
    mg, back, ups, hg, sums, hsum = run_upstream(spot, gs, [wd, we, wr, second_row], unit, slope)
    out_near = near_sum(out_keep, out_got)
    out_near, hg = tie(out_near, hg)
    out_got_near = hop(out_near, NEAR_OFF)

    spot = jnp.stack([*spots, col])
    kept_share, *shares_out = weight_gradients(spot, second, hg, active, ups, mixed)
    out_home = home_sum(out_keep, out_got, out_near, out_got_near, main)
    out_home, mg, *shares_out = tie(out_home, mg, *shares_out)
    out_got_home = hop(out_home, HOME)
    shares_got = plane(shares_out)

    jb = attend_backward(qkv, mg.reshape(heads, HEAD, total), full, inverse_sum, shares, tables)
    jb = jb.reshape(-1, total)

    spot = jnp.stack([col, quarter])
    up_sum = jnp.sum(wide(own_g).reshape(-1, 8, width), axis=0)
    kept_joint, *joint_out, vector = joint_gradient(
        spot, jb, unit, wj, first_row, row_of(first_shift), sums, up_sum, hsum
    )
    jb, *joint_out = tie(jb, *joint_out)
    joint_got = plane(joint_out)

    send, keep = deliver(order, jb, wj, back, first_row)

    send, out_got_home, *shares_got = tie(send, out_got_home, *shares_got)
    share = wide(kept_share) + sum(wide(piece) for piece in shares_got)
    kept = near ^ half
    part = width // 4
    expand_part = share[:part].reshape(2, 2, 2, part // 8, units // N)
    reduce_part = share[part : part + units // (4 * N)].reshape(2, -1, width)
    dense_part = share[part + units // (4 * N) :]
    far_send = [pick(expand_part, 1, 1 - half).reshape(part // 2, -1), pick(reduce_part, 0, 1 - kept), dense_part]
    far_send = low(jnp.concatenate(far_send, axis=0))
    far_send, send = tie(far_send, send)
    got = hop(send, CORE_SWAP)
    far_got = hop(far_send, FAR_SWAP)
    near_part = near_sum(keep, got)
    out = own_sum(out_keep, out_got, out_got_home, main)
    inputs = wide(own_x)
    result = low(inputs + out + (dense_bias + reduce_bias))
    got_near = hop(near_part, NEAR_OFF)

    got_near, *joint_got = tie(got_near, *joint_got)
    joint_part = wide(kept_joint) + sum(wide(piece[:part]) for piece in joint_got)
    vector = vector + sum(unpack(piece[part:], width) for piece in joint_got)
    joint_width = joint_part.shape[1]
    joint_part = joint_part.reshape(2, 2, 2, part // 8, joint_width)
    joint_far_send = jnp.concatenate(
        [low(pick(joint_part, 1, 1 - half)).reshape(part // 2, joint_width), pack(vector, joint_width)], axis=0
    )
    home = home_sum(keep, got, near_part, got_near, main)
    home, joint_far_send, result = tie(home, joint_far_send, result)
    got_home = hop(home, HOME)
    joint_far = hop(joint_far_send, FAR_SWAP)
    home, far_got = tie(home, far_got)
    far_got = wide(far_got)
    expand_part = low(pick(expand_part, 1, half).reshape(part // 2, -1) + far_got[: part // 2])
    reduce_part = low(pick(reduce_part, 0, kept) + far_got[part // 2 : part // 2 + 128])
    dense_part = low(dense_part + far_got[part // 2 + 128 :]).reshape(2, HEAD // 2, width)
    line = jnp.concatenate(
        [
            expand_part.reshape(2, 2, part // 8, -1),
            jnp.broadcast_to(dense_part[None], (2,) + dense_part.shape),
        ],
        axis=2,
    )
    line_send = first_pieces(line, near)
    line_got = hop(line_send, NEAR)
    reduce_got = hop(reduce_part, [((c, s), ((s % 2) ^ (s // 2), 2 * (s // 2) + c)) for c, s in PLACES])
    scaled = own_sum(keep, got, got_home, main)
    _, unit_rows, inverse_root = normalize(inputs, first_gain, first_shift)
    input_back = inverse_root * (
        scaled
        - jnp.mean(scaled, axis=-1, keepdims=True)
        - unit_rows * jnp.mean(scaled * unit_rows, axis=-1, keepdims=True)
    )
    tokens_gradient = low(wide(own_g) + input_back)
    line_got, tokens_gradient = tie(line_got, tokens_gradient)
    line_send = second_pieces(line, line_got, core, near)
    line_last = hop(line_send, CORE_SWAP)
    joint_far, line_send = tie(joint_far, line_send)
    joint_part = low(pick(joint_part, 1, half).reshape(part // 2, joint_width) + wide(joint_far[: part // 2]))
    vector = vector + unpack(joint_far[part // 2 :], width)
    joint_line = joint_part.reshape(2, 2, part // 8, joint_width)
    vector_rows = pack(vector, joint_width)
    joint_got = []
    for dz, dc in ((0, 1), (1, 0), (1, 1)):
        piece = pick(pick(joint_line, 1, near ^ dz), 0, core ^ dc)
        piece = jnp.concatenate([piece, vector_rows], axis=0)
        joint_got.append(hop(piece, [((c, p), (c ^ dc, p ^ dz)) for c, p in PLACES]))
    spot = jnp.stack([core, near, half])
    expand_mine, dense_mine, reduce_mine = finish(spot, line, line_got, line_last, reduce_got)
    expand_mine, *joint_got = tie(expand_mine, *joint_got)
    vector = vector + sum(unpack(piece[part // 8 :], width) for piece in joint_got)
    joint_mine = joint_finish(spot, joint_line, joint_got)

    device = (2 * col + core) * N + z
    share = width // (8 * N)
    head_row = lambda head: 5 + N + head % N
    cut = lambda row, start, size: lax.dynamic_slice(vector, (row, start), (1, size))[0]
    pieces = [cut(row, device * share, share) for row in range(5)]
    pieces[4:] = [
        cut(head_row(device % HEADS), (device // HEADS * heads + device % HEADS // N) * HEAD, HEAD),
        cut(head_row(device // 2), (2 * heads + device // 2 // N) * HEAD + device % 2 * share, share),
        pieces[4],
        cut(5 + (z ^ (2 * core)), (2 * col + core) * 128, 128),
    ]

    return (
        result[None],
        tokens_gradient[None],
        *pieces[:4],
        joint_mine,
        pieces[4],
        pieces[5],
        dense_mine,
        pieces[6],
        expand_mine,
        pieces[7],
        reduce_mine,
        pieces[6],
    )


def solution(mesh):
    count, blocks = mesh.devices.shape
    split = blocks == N and count == 8
    if split:
        mesh = jax.sharding.Mesh(mesh.devices.reshape(count // 2, 2, blocks), ("col", "core", "blk"))
        batch = ("col", "core")
        every = ("col", "core", "blk")
    else:
        batch, every = "batch", ("batch", "blk")
    by_rows = P(batch, "blk", None)
    placed = (by_rows, P(batch, None)) + (P(),) * 12 + (by_rows,)
    vector, matrix = P(every), P(every, None)
    return jax.shard_map(
        split_local if split else local,
        mesh=mesh,
        in_specs=placed,
        out_specs=(
            by_rows,
            by_rows,
            vector,
            vector,
            vector,
            vector,
            matrix,
            vector,
            vector,
            matrix,
            vector,
            matrix,
            vector,
            matrix,
            vector,
        ),
        check_vma=False,
    )
```

```python
from functools import partial

import jax
import jax.numpy as jnp
from jax import lax
from jax.experimental import pallas as pl
from jax.experimental.pallas import tpu as pltpu
from jax.sharding import PartitionSpec as P

HEADS = 16
HEAD = 64
ROTARY = 16


EPSILON = 1e-05
MASKED = -1e30


def doc_tables(lengths, positions):
    doc_ends = jnp.cumsum(lengths, axis=-1)
    doc_starts = doc_ends - lengths
    doc_number = jnp.sum(
        (positions[None, :, None] >= doc_ends[:, None, :]).astype(jnp.int32), axis=-1
    )
    matches = (
        doc_number[:, :, None] == jnp.arange(lengths.shape[-1], dtype=jnp.int32)[None, None, :]
    )
    begins = jnp.sum(jnp.where(matches, doc_starts[:, None, :], 0), axis=-1)
    return (doc_number, positions[None, :] - begins)


def angles(offsets):
    half_width = ROTARY // 2
    inverse = 10000.0 ** (-2.0 * jnp.arange(half_width, dtype=jnp.float32) / ROTARY)
    phase = offsets.astype(jnp.float32)[..., None] * inverse
    return (jnp.cos(phase), jnp.sin(phase))


def rotate(values, cosine, sine_table, direction):
    half_width = cosine.shape[-1]
    lead_part = values[..., :half_width]
    tail_part = values[..., half_width : 2 * half_width]
    cosine = cosine[:, :, None, :]
    sine_table = sine_table[:, :, None, :] * direction
    return jnp.concatenate(
        [
            lead_part * cosine - tail_part * sine_table,
            tail_part * cosine + lead_part * sine_table,
            values[..., 2 * half_width :],
        ],
        axis=-1,
    )


def normalize(values, gain_row, shift_row):
    center = values - jnp.mean(values, axis=-1, keepdims=True)
    spread = jnp.mean(center * center, axis=-1, keepdims=True)
    inverse_root = lax.rsqrt(spread + EPSILON)
    unit_rows = center * inverse_root
    return (unit_rows * gain_row + shift_row, unit_rows, inverse_root)


def normalize_back(upstream, unit_rows, inverse_root, gain_row):
    scaled_back = upstream * gain_row
    input_back = inverse_root * (
        scaled_back
        - jnp.mean(scaled_back, axis=-1, keepdims=True)
        - unit_rows * jnp.mean(scaled_back * unit_rows, axis=-1, keepdims=True)
    )
    return (input_back, jnp.sum(upstream * unit_rows, axis=0), jnp.sum(upstream, axis=0))


def outer(left_rows, right_rows):
    return lax.dot_general(
        left_rows, right_rows, (((0,), (0,)), ((), ())), preferred_element_type=jnp.float32
    )


def against(left_rows, weight_rows):
    return lax.dot_general(
        left_rows, weight_rows, (((1,), (1,)), ((), ())), preferred_element_type=jnp.float32
    )


def over_piece(stepper, running, segment, stride):
    sub_count = segment.shape[1] // stride

    def one_turn(position, current):
        part_rows = lax.dynamic_slice_in_dim(segment, position * stride, stride, 1)
        return stepper(current, part_rows, position * stride)

    return lax.fori_loop(0, sub_count, one_turn, running)


def local(
    tokens,
    lengths,
    first_gain,
    first_shift,
    second_gain,
    second_shift,
    joint_weight,
    joint_bias,
    dense_weight,
    dense_bias,
    expand_weight,
    expand_bias,
    reduce_weight,
    reduce_bias,
    cotangent,
):
    sequences, stride, model_width = tokens.shape
    cycle_size = lax.axis_size("blk")
    seq_total = stride * cycle_size
    rank_here = lax.axis_index("blk")
    row_count = sequences * stride
    factor = HEAD ** (-0.5)
    head_shape = (sequences, stride, HEADS, HEAD)
    places = jnp.arange(seq_total, dtype=jnp.int32)
    number_all, offset_all = doc_tables(lengths, places)
    first_place = rank_here * stride
    query_number = lax.dynamic_slice_in_dim(number_all, first_place, stride, 1)
    query_offset = lax.dynamic_slice_in_dim(offset_all, first_place, stride, 1)
    query_place = first_place + jnp.arange(stride, dtype=jnp.int32)
    last_place = first_place + stride - 1
    cosine, sine_table = angles(query_offset)
    inputs = tokens.reshape(row_count, model_width).astype(jnp.float32)
    first_norm, first_unit, first_scale = normalize(inputs, first_gain, first_shift)
    normed = first_norm.astype(jnp.bfloat16)
    joint_out = jnp.dot(normed, joint_weight, preferred_element_type=jnp.float32) + joint_bias
    queries = rotate(
        joint_out[:, :model_width].reshape(head_shape), cosine, sine_table, 1.0
    ).astype(jnp.bfloat16)
    key_rows = rotate(
        joint_out[:, model_width : 2 * model_width].reshape(head_shape), cosine, sine_table, 1.0
    ).astype(jnp.bfloat16)
    value_rows = joint_out[:, 2 * model_width :].astype(jnp.bfloat16)
    pair_local = jnp.concatenate(
        [
            key_rows.reshape(sequences, stride, model_width),
            value_rows.reshape(sequences, stride, model_width),
        ],
        axis=-1,
    )

    def masked_scores(key_part, begin_row, row_span):
        key_number = lax.dynamic_slice_in_dim(number_all, begin_row, row_span, 1)
        key_place = begin_row + jnp.arange(row_span, dtype=jnp.int32)
        allowed = (query_number[:, :, None] == key_number[:, None, :]) & (
            key_place[None, None, :] <= query_place[None, :, None]
        )
        allowed = allowed[:, None]
        scores = (
            jnp.einsum("sqhd,skhd->shqk", queries, key_part, preferred_element_type=jnp.float32)
            * factor
        )
        return (jnp.where(allowed, scores, MASKED), allowed)

    def split_piece(segment):
        row_span = segment.shape[1]
        key_part = segment[:, :, :model_width].reshape(sequences, row_span, HEADS, HEAD)
        value_part = segment[:, :, model_width:].reshape(sequences, row_span, HEADS, HEAD)
        return (key_part, value_part, row_span)

    def gated(kernel):

        def stepper(running, segment, begin_row):
            return lax.cond(
                begin_row <= last_place,
                lambda current: kernel(current, segment, begin_row),
                lambda current: current,
                running,
            )

        return stepper

    def forward_kernel(running, segment, begin_row):
        row_peak, row_total, weighted = running
        key_part, value_part, row_span = split_piece(segment)
        scores, allowed = masked_scores(key_part, begin_row, row_span)
        new_peak = jnp.maximum(row_peak, jnp.max(scores, axis=-1))
        shares = jnp.where(allowed, jnp.exp(scores - new_peak[..., None]), 0.0)
        decay_factor = jnp.exp(row_peak - new_peak)
        row_total = row_total * decay_factor + jnp.sum(shares, axis=-1)
        update = jnp.einsum(
            "shqk,skhd->sqhd",
            shares.astype(jnp.bfloat16),
            value_part,
            preferred_element_type=jnp.float32,
        )
        weighted = weighted * jnp.transpose(decay_factor, (0, 2, 1))[..., None] + update
        return (new_peak, row_total, weighted)

    forward_step = gated(forward_kernel)
    initial = (
        jnp.full((sequences, HEADS, stride), MASKED, jnp.float32),
        jnp.zeros((sequences, HEADS, stride), jnp.float32),
        jnp.zeros(head_shape, jnp.float32),
    )
    forward_state = over_piece(
        forward_step, initial, lax.all_gather(pair_local, "blk", axis=1, tiled=True), stride
    )
    row_peak, row_total, weighted = forward_state
    mixed_full = weighted / jnp.transpose(row_total, (0, 2, 1))[..., None]
    log_total = row_peak + jnp.log(row_total)
    mixed = mixed_full.reshape(row_count, model_width).astype(jnp.bfloat16)
    attention_out = jnp.dot(mixed, dense_weight, preferred_element_type=jnp.float32) + dense_bias
    second_norm, second_unit, second_scale = normalize(inputs, second_gain, second_shift)
    second = second_norm.astype(jnp.bfloat16)
    hidden = jnp.dot(second, expand_weight, preferred_element_type=jnp.float32) + expand_bias
    active_full, gelu_pull = jax.vjp(partial(jax.nn.gelu, approximate=False), hidden)
    active = active_full.astype(jnp.bfloat16)
    feed_out = jnp.dot(active, reduce_weight, preferred_element_type=jnp.float32) + reduce_bias
    result = (
        (inputs + attention_out + feed_out)
        .astype(jnp.bfloat16)
        .reshape(sequences, stride, model_width)
    )
    upstream = cotangent.reshape(row_count, model_width)
    dense_grad = outer(mixed, upstream)
    bias_total = jnp.sum(upstream, axis=0, dtype=jnp.float32)
    reduce_grad = outer(active, upstream)
    hidden_grad = gelu_pull(against(upstream, reduce_weight))[0].astype(jnp.bfloat16)
    expand_grad = outer(second, hidden_grad)
    hidden_total = jnp.sum(hidden_grad, axis=0, dtype=jnp.float32)
    input_two, gain_second, shift_second = normalize_back(
        against(hidden_grad, expand_weight), second_unit, second_scale, second_gain
    )
    mixed_grad = against(upstream, dense_weight).astype(jnp.bfloat16)
    out_heads = mixed_grad.reshape(head_shape)
    delta_rows = jnp.transpose(jnp.sum(out_heads * mixed_full, axis=-1), (0, 2, 1))

    def backward_kernel(running, segment, begin_row):
        key_part, value_part, row_span = split_piece(segment)
        scores, allowed = masked_scores(key_part, begin_row, row_span)
        weights_now = jnp.where(allowed, jnp.exp(scores - log_total[..., None]), 0.0)
        weight_grad = jnp.einsum(
            "sqhd,skhd->shqk", out_heads, value_part, preferred_element_type=jnp.float32
        )
        score_grad = (weights_now * (weight_grad - delta_rows[..., None])).astype(jnp.bfloat16)
        query_grad = (
            running[0]
            + jnp.einsum(
                "shqk,skhd->sqhd", score_grad, key_part, preferred_element_type=jnp.float32
            )
            * factor
        )
        value_grad = jnp.einsum(
            "shqk,sqhd->skhd",
            weights_now.astype(jnp.bfloat16),
            out_heads,
            preferred_element_type=jnp.float32,
        )
        key_grad = (
            jnp.einsum("shqk,sqhd->skhd", score_grad, queries, preferred_element_type=jnp.float32)
            * factor
        )
        fresh_rows = jnp.concatenate(
            [
                key_grad.reshape(sequences, row_span, model_width),
                value_grad.reshape(sequences, row_span, model_width),
            ],
            axis=-1,
        )
        pair_grad = lax.dynamic_update_slice_in_dim(running[1], fresh_rows, begin_row, 1)
        return (query_grad, pair_grad)

    backward_step = gated(backward_kernel)
    back_initial = (
        jnp.zeros(head_shape, jnp.float32),
        jnp.zeros((sequences, seq_total, 2 * model_width), jnp.float32),
    )
    back_state = over_piece(
        backward_step, back_initial, lax.all_gather(pair_local, "blk", axis=1, tiled=True), stride
    )
    query_grad = back_state[0]
    pair_mine = lax.psum_scatter(back_state[1], "blk", scatter_dimension=1, tiled=True)
    query_back = rotate(query_grad, cosine, sine_table, -1.0).reshape(row_count, model_width)
    key_back = rotate(
        pair_mine[:, :, :model_width].reshape(head_shape), cosine, sine_table, -1.0
    ).reshape(row_count, model_width)
    value_back = pair_mine[:, :, model_width:].reshape(row_count, model_width)
    joint_back = jnp.concatenate([query_back, key_back, value_back], axis=-1).astype(jnp.bfloat16)
    joint_grad = outer(normed, joint_back)
    joint_total = jnp.sum(joint_back, axis=0, dtype=jnp.float32)
    front_total = joint_total[: 2 * model_width]
    value_total = joint_total[2 * model_width :]
    input_one, gain_first, shift_first = normalize_back(
        against(joint_back, joint_weight), first_unit, first_scale, first_gain
    )
    input_total = (
        (upstream.astype(jnp.float32) + input_one + input_two)
        .astype(jnp.bfloat16)
        .reshape(sequences, stride, model_width)
    )
    summed = (
        lax.psum_scatter(gain_first, ("batch", "blk"), scatter_dimension=0, tiled=True),
        lax.psum_scatter(shift_first, ("batch", "blk"), scatter_dimension=0, tiled=True),
        lax.psum_scatter(gain_second, ("batch", "blk"), scatter_dimension=0, tiled=True),
        lax.psum_scatter(shift_second, ("batch", "blk"), scatter_dimension=0, tiled=True),
        lax.psum_scatter(joint_grad, ("batch", "blk"), scatter_dimension=0, tiled=True),
        lax.psum_scatter(front_total, ("batch", "blk"), scatter_dimension=0, tiled=True),
        lax.psum_scatter(value_total, ("batch", "blk"), scatter_dimension=0, tiled=True),
        lax.psum_scatter(dense_grad, ("batch", "blk"), scatter_dimension=0, tiled=True),
        lax.psum_scatter(bias_total, ("batch", "blk"), scatter_dimension=0, tiled=True),
        lax.psum_scatter(expand_grad, ("batch", "blk"), scatter_dimension=0, tiled=True),
        lax.psum_scatter(hidden_total, ("batch", "blk"), scatter_dimension=0, tiled=True),
        lax.psum_scatter(reduce_grad, ("batch", "blk"), scatter_dimension=0, tiled=True),
    )
    return (
        result,
        input_total,
        summed[0],
        summed[1],
        summed[2],
        summed[3],
        summed[4],
        summed[5],
        summed[6],
        summed[7],
        summed[8],
        summed[9],
        summed[10],
        summed[11],
        summed[8],
    )


BQ = 512
N = 4
TM = 256
VMEM = 56 * 1024 * 1024
NEG = -1e30
NN = (((1,), (0,)), ((), ()))
NT = (((1,), (1,)), ((), ()))
TN = (((0,), (0,)), ((), ()))


def mm(left, right, form=NN):
    return lax.dot_general(left, right, form, preferred_element_type=jnp.float32)


def low(value):
    return value.astype(jnp.bfloat16)


def wide(value):
    return value.astype(jnp.float32)


def gelu_parts(hidden):
    size = jnp.abs(hidden) * (0.5**0.5)
    bell = jnp.exp(-(size * size))
    base = 1.0 + 0.3275911 * size
    guess = pl.reciprocal(base, approx=True)
    t = guess * (2.0 - base * guess)
    series = t * (
        0.5 * 0.254829592
        + t
        * (
            0.5 * -0.284496736
            + t * (0.5 * 1.421413741 + t * (0.5 * -1.453152027 + t * (0.5 * 1.061405429)))
        )
    )
    tail = series * bell
    return (jnp.where(hidden >= 0.0, 1.0 - tail, tail), bell)


def fold_rows(value):
    rows, columns = value.shape
    return jnp.sum(value.reshape(rows // 8, 8, columns), axis=0)


def prepare_kernel(spot_ref, wj_ref, wd_ref, we_ref, wr_ref, wj_out, wd_out, we_out, wr_out):
    turned = wj_ref[...].T
    wj_out[...] = jnp.where(lax.rem(spot_ref[0], 2) == 0, turned[:HEAD], turned[HEAD:])
    wd_out[...] = wd_ref[...]
    we_out[...] = we_ref[...]
    wr_out[...] = wr_ref[...]


def prepare(quarter, joint_weight, dense_weight, expand_weight, reduce_weight):
    width, units = expand_weight.shape
    heads = HEADS // N
    groups = units // (N * 128)
    kinds = 3 * heads
    pair = lambda s, spot: (0, (s // heads) * (HEADS // 2) + (s % heads) * (N // 2) + spot[0] // 2)
    row = lambda s: jnp.minimum(s, heads - 1)
    unit = lambda s: jnp.minimum(s, groups - 1)
    group = lambda s, spot: N * unit(s) + lax.rem(spot[0] + 2 * lax.rem(unit(s), 2), N)
    shape = lambda *dims: jax.ShapeDtypeStruct(dims, jnp.bfloat16)
    return pl.pallas_call(
        prepare_kernel,
        grid_spec=pltpu.PrefetchScalarGridSpec(
            num_scalar_prefetch=1,
            grid=(kinds,),
            in_specs=[
                pl.BlockSpec((width, 2 * HEAD), pair),
                pl.BlockSpec((HEAD, width), lambda s, spot: (N * row(s) + spot[0], 0)),
                pl.BlockSpec((width, 128), lambda s, spot: (0, group(s, spot))),
                pl.BlockSpec((128, width), lambda s, spot: (group(s, spot), 0)),
            ],
            out_specs=[
                pl.BlockSpec((HEAD, width), lambda s, spot: (s, 0)),
                pl.BlockSpec((HEAD, width), lambda s, spot: (row(s), 0)),
                pl.BlockSpec((width, 128), lambda s, spot: (0, unit(s))),
                pl.BlockSpec((128, width), lambda s, spot: (unit(s), 0)),
            ],
        ),
        out_shape=[
            shape(kinds * HEAD, width),
            shape(heads * HEAD, width),
            shape(width, groups * 128),
            shape(groups * 128, width),
        ],
        cost_estimate=pl.CostEstimate(flops=0, bytes_accessed=14 * width * width, transcendentals=0),
    )(quarter.reshape(1), joint_weight, dense_weight, expand_weight, reduce_weight)


def block_at(place, j):
    return place * (place + 1) // 2 + j


def forward_kernel(held, qkv_ref, kx_ref, qx_ref, *refs):
    mixed_ref, full_ref, inverse_ref, share_ref, key_ref, *scores = refs[held:]
    key_ref[...] = jnp.concatenate([qkv_ref[1, 0], kx_ref[...]], axis=0).T
    total = kx_ref.shape[1]
    state = {}

    def score(place, j):
        here = slice(place * BQ, (place + 1) * BQ)
        at = slice(j * BQ, (j + 1) * BQ)
        if j == 0:
            query_x = jnp.concatenate([qkv_ref[0, 0, :, here], qx_ref[:, here]], axis=0)
            state[place] = [query_x, jnp.full((8, BQ), NEG * 2, jnp.float32)]
        found = mm(key_ref[at, :], state[place][0])
        if j == place:
            key_row = lax.broadcasted_iota(jnp.int32, (BQ, BQ), 0)
            query_column = lax.broadcasted_iota(jnp.int32, (BQ, BQ), 1)
            found = jnp.where(key_row <= query_column, found, NEG)
        scores[place % 2][at, :] = found
        state[place][1] = jnp.maximum(state[place][1], jnp.max(found.reshape(BQ // 8, 8, BQ), axis=0))

    def weigh(place, j):
        here = slice(place * BQ, (place + 1) * BQ)
        at = slice(j * BQ, (j + 1) * BQ)
        if j == 0:
            peak = jnp.max(state[place][1], axis=0, keepdims=True)
            state[place] = [peak, jnp.zeros((8, BQ), jnp.float32), jnp.zeros((HEAD, BQ), jnp.float32)]
        share = jnp.exp(scores[place % 2][at, :] - state[place][0])
        state[place][1] = state[place][1] + jnp.sum(share.reshape(BQ // 8, 8, BQ), axis=0)
        share = low(share)
        share_ref[0, block_at(place, j)] = share
        state[place][2] = state[place][2] + mm(qkv_ref[2, 0, :, at], share)
        if j == place:
            inverse = 1.0 / jnp.sum(state[place][1], axis=0, keepdims=True)
            mixed = state[place][2] * inverse
            inverse_ref[0, :, here] = inverse
            full_ref[0, :, here] = mixed
            mixed_ref[0, :, here] = low(mixed)

    places = list(range(total // BQ))
    for j in range(places[0] + 1):
        score(places[0], j)
    for n, place in enumerate(places):
        for j in range(places[-1] + 2):
            if n + 1 < len(places) and j <= places[n + 1]:
                score(places[n + 1], j)
            if j <= place:
                weigh(place, j)


def attend_forward(qkv, kx, qx, first, count, before):
    _, heads, _, total = qkv.shape
    places = total // BQ
    blocks = block_at(places, 0)
    head_rows = lambda rows: pl.BlockSpec((1, rows, total), lambda h: (first + h, 0, 0))
    operands = [qkv, kx, qx]
    in_specs = [
        pl.BlockSpec((3, 1, HEAD, total), lambda h: (0, first + h, 0, 0)),
        pl.BlockSpec((HEAD, total), lambda h: (0, 0)),
        pl.BlockSpec((HEAD, total), lambda h: (0, 0)),
    ]
    aliases = {}
    if before is not None:
        for index, array in enumerate(before):
            aliases[len(operands)] = index
            operands.append(array)
            in_specs.append(pl.BlockSpec(memory_space=pl.ANY))
    return pl.pallas_call(
        partial(forward_kernel, len(aliases)),
        grid=(count,),
        in_specs=in_specs,
        out_specs=[
            head_rows(HEAD),
            head_rows(HEAD),
            head_rows(1),
            pl.BlockSpec((1, blocks, BQ, BQ), lambda h: (first + h, 0, 0, 0)),
        ],
        out_shape=[
            jax.ShapeDtypeStruct((heads, HEAD, total), jnp.bfloat16),
            jax.ShapeDtypeStruct((heads, HEAD, total), jnp.float32),
            jax.ShapeDtypeStruct((heads, 1, total), jnp.float32),
            jax.ShapeDtypeStruct((heads, blocks, BQ, BQ), jnp.bfloat16),
        ],
        scratch_shapes=[pltpu.VMEM((total, 2 * HEAD), jnp.bfloat16)] + [pltpu.VMEM((total, BQ), jnp.float32)] * 2,
        input_output_aliases=aliases,
        compiler_params=pltpu.CompilerParams(vmem_limit_bytes=VMEM),
        cost_estimate=pl.CostEstimate(
            flops=16 * HEAD * count * blocks * BQ * BQ,
            bytes_accessed=2 * count * blocks * BQ * BQ,
            transcendentals=count * blocks * BQ * BQ,
        ),
    )(*operands)


def backward_kernel(qkv_ref, mg_ref, full_ref, inverse_ref, share_ref, cos_ref, sin_ref, jb_ref, value_ref, acc_ref):
    total = cos_ref.shape[1]
    ones = (lax.broadcasted_iota(jnp.int32, (HEAD, total), 0) < 3).astype(jnp.bfloat16)
    value_ref[...] = jnp.concatenate([qkv_ref[2, 0], ones], axis=0).T
    half = ROTARY // 2
    blank = jnp.zeros((HEAD, BQ), jnp.bfloat16)
    row = lax.broadcasted_iota(jnp.int32, (HEAD, BQ), 0)

    def turn_back(rows, at):
        lead, tail = rows[:half], rows[half : 2 * half]
        cosine, sine = cos_ref[:, at], sin_ref[:, at]
        return low(
            jnp.concatenate([lead * cosine + tail * sine, tail * cosine - lead * sine, rows[2 * half :]], axis=0)
        )

    for place in reversed(range(total // BQ)):
        here = slice(place * BQ, (place + 1) * BQ)
        query_t = qkv_ref[0, 0, :, here]
        mg = low(wide(mg_ref[0, :, here]) * inverse_ref[0, :, here])
        delta = -jnp.sum(wide(mg) * full_ref[0, :, here], axis=0, keepdims=True)
        first = low(delta)
        rest = delta - wide(first)
        middle = low(rest)
        final = low(rest - wide(middle))
        extra = jnp.where(
            row == 0, wide(first), jnp.where(row == 1, wide(middle), jnp.where(row == 2, wide(final), 0.0))
        )
        mg_x = jnp.concatenate([mg, low(extra)], axis=0)
        mg_v = jnp.concatenate([blank, mg], axis=0)
        query_k = jnp.concatenate([query_t, blank], axis=0)
        query_grad = jnp.zeros((HEAD, BQ), jnp.float32)
        for j in range(place + 1):
            at = slice(j * BQ, (j + 1) * BQ)
            share = share_ref[0, block_at(place, j)]
            score_grad = low(wide(share) * mm(value_ref[at, :], mg_x))
            pair = mm(share, mg_v, NT) + mm(score_grad, query_k, NT)
            query_grad = query_grad + mm(qkv_ref[1, 0, :, at], score_grad)
            if (place + 1) * BQ < total:
                pair = pair + acc_ref[at, :]
            if j < place:
                acc_ref[at, :] = pair
            else:
                pair_t = pair.T
                jb_ref[1, 0, :, at] = turn_back(pair_t[:HEAD], at)
                jb_ref[2, 0, :, at] = low(pair_t[HEAD:])
        jb_ref[0, 0, :, here] = turn_back(query_grad * (HEAD**-0.5), here)


def attend_backward(qkv, mg, full, inverse, shares, tables):
    _, heads, _, total = qkv.shape
    blocks = shares.shape[1]
    head_rows = lambda rows: pl.BlockSpec((1, rows, total), lambda h: (h, 0, 0))
    kinds = pl.BlockSpec((3, 1, HEAD, total), lambda h: (0, h, 0, 0))
    table = pl.BlockSpec((ROTARY // 2, total), lambda h: (0, 0))
    return pl.pallas_call(
        backward_kernel,
        grid=(heads,),
        in_specs=[
            kinds,
            head_rows(HEAD),
            head_rows(HEAD),
            head_rows(1),
            pl.BlockSpec((1, blocks, BQ, BQ), lambda h: (h, 0, 0, 0)),
            table,
            table,
        ],
        out_specs=kinds,
        out_shape=jax.ShapeDtypeStruct((3, heads, HEAD, total), jnp.bfloat16),
        scratch_shapes=[
            pltpu.VMEM((total, 2 * HEAD), jnp.bfloat16),
            pltpu.VMEM((total, 2 * HEAD), jnp.float32),
        ],
        compiler_params=pltpu.CompilerParams(vmem_limit_bytes=VMEM),
        cost_estimate=pl.CostEstimate(
            flops=32 * HEAD * heads * blocks * BQ * BQ,
            bytes_accessed=2 * heads * blocks * BQ * BQ,
            transcendentals=0,
        ),
    )(qkv, mg, full, inverse, shares, *tables)


def chosen(index, options):
    value = options[-1]
    for k in reversed(range(len(options) - 1)):
        value = jnp.where(index == k, options[k], value)
    return value


def token_kernel(count, sub, chunk, spot_ref, *refs):
    sources = refs[:count]
    (wj_ref, bj_ref, we_ref, be_ref, wr_ref, g1_ref, s1_ref, g2_ref, s2_ref, cos_ref, sin_ref) = refs[count : count + 11]
    qkv_ref, unit_ref, second_ref, active_ref, slope_ref, feed_ref = refs[-6:]
    choice = spot_ref[pl.num_programs(0) + pl.program_id(0)]
    rows = sources[0].shape[0]
    half = ROTARY // 2
    part = wj_ref.shape[0] // 3
    for top in range(0, rows, sub):
        at = slice(top, top + sub)
        x = wide(chosen(choice, [source[at, :] for source in sources]))
        center = x - jnp.mean(x, axis=-1, keepdims=True)
        scale = lax.rsqrt(jnp.mean(center * center, axis=-1, keepdims=True) + EPSILON)
        unit = center * scale
        unit_ref[at, :] = low(unit)
        normed = low(unit * g1_ref[...] + s1_ref[...])
        second = low(unit * g2_ref[...] + s2_ref[...])
        second_ref[at, :] = second
        joint = mm(wj_ref[...], normed, NT) + bj_ref[...]
        cosine, sine = cos_ref[:, at], sin_ref[:, at]
        for kind in range(3):
            for head in range(part // HEAD):
                first = kind * part + head * HEAD
                turned = joint[first : first + HEAD]
                if kind < 2:
                    lead, tail = turned[:half], turned[half : 2 * half]
                    turned = jnp.concatenate(
                        [lead * cosine - tail * sine, tail * cosine + lead * sine, turned[2 * half :]], axis=0
                    )
                if kind == 0:
                    turned = turned * (HEAD**-0.5)
                qkv_ref[first : first + HEAD, at] = low(turned)
        for left in range(0, we_ref.shape[1], chunk):
            over = slice(left, left + chunk)
            hidden = mm(second, we_ref[:, over]) + be_ref[:, over]
            share, bell = gelu_parts(hidden)
            active_ref[at, over] = low(hidden * share)
            slope_ref[at, over] = low(share + hidden * bell * 0.3989422804014327)
    for top in range(0, rows, sub):
        at = slice(top, top + sub)
        feed_ref[at, :] = low(mm(active_ref[at, :], wr_ref[...]))


def run_tokens(slot, spot, data, weights, tables, before, sub=256, chunk=256):
    rows, width = data[0].shape
    total = tables[0].shape[1]
    wj, bj, we, be, wr, g1, s1, g2, s2 = weights
    units = we.shape[1]
    steps = spot.shape[0] // 2

    def whole(array):
        return pl.BlockSpec(array.shape, lambda i, spot: (0,) * array.ndim)

    column = lambda height: pl.BlockSpec((height, rows), lambda i, spot: (0, spot[i]))
    placed = pl.BlockSpec((rows, width), lambda i, spot: (spot[i], 0))
    arrived = lambda size: pl.BlockSpec((rows, size), lambda i, spot: (slot + i, 0))
    in_specs = [whole(w) for w in (*data, *weights)] + [column(ROTARY // 2)] * 2
    out_specs = [column(wj.shape[0]), placed, arrived(width), arrived(units), arrived(units), placed]
    shape = lambda *dims: jax.ShapeDtypeStruct(dims, jnp.bfloat16)
    out_shape = [shape(wj.shape[0], total)] + [shape(total, size) for size in (width, width, units, units, width)]
    operands = [spot, *data, *weights, *tables]
    aliases = {}
    if before is not None:
        for index, array in enumerate(before):
            aliases[len(operands)] = index
            operands.append(array)
            in_specs.append(pl.BlockSpec(memory_space=pl.ANY))
    return pl.pallas_call(
        partial(token_kernel, len(data), sub, chunk),
        grid_spec=pltpu.PrefetchScalarGridSpec(
            num_scalar_prefetch=1, grid=(steps,), in_specs=in_specs, out_specs=out_specs
        ),
        out_shape=out_shape,
        input_output_aliases=aliases,
        compiler_params=pltpu.CompilerParams(vmem_limit_bytes=VMEM),
        cost_estimate=pl.CostEstimate(flops=0, bytes_accessed=0, transcendentals=0),
    )(*operands)


def upstream_kernel(chunk, spot_ref, *refs):
    sources, refs = refs[:5], refs[5:]
    (wd_ref, we_ref, wr_ref, g2_ref, unit_ref, slope_ref) = refs[:6]
    (mg_ref, back_ref, up_ref, hg_ref, sums_ref, hsum_ref) = refs[6:12]
    buffer, sems = refs[12:]
    step = pl.program_id(0)
    steps = pl.num_programs(0)
    slot = lax.rem(step, 2)

    def fetch(which, into):
        for k, source in enumerate(sources):

            @pl.when(spot_ref[steps + which] == k)
            def _():
                pltpu.make_async_copy(source, buffer.at[into], sems.at[into]).start()

    @pl.when(step == 0)
    def _():
        fetch(0, 0)
        sums_ref[...] = jnp.zeros_like(sums_ref)
        hsum_ref[...] = jnp.zeros_like(hsum_ref)

    @pl.when(step + 1 < steps)
    def _():
        fetch(step + 1, 1 - slot)

    pltpu.make_async_copy(sources[0], buffer.at[slot], sems.at[slot]).wait()
    up = buffer[slot]
    up_ref[...] = up
    mg_ref[...] = low(mm(wd_ref[...], up, NT))
    for left in range(0, we_ref.shape[1], chunk):
        over = slice(left, left + chunk)
        piece = low(mm(up, wr_ref[over, :], NT) * wide(slope_ref[:, over]))
        hg_ref[:, over] = piece
        hsum_ref[:, over] += fold_rows(wide(piece))
    for left in range(0, we_ref.shape[0], chunk):
        over = slice(left, left + chunk)
        back = mm(hg_ref[...], we_ref[over, :], NT)
        back_ref[:, over] = low(back * g2_ref[:, over])
        sums_ref[0, :, over] += fold_rows(back * wide(unit_ref[:, over]))
        sums_ref[1, :, over] += fold_rows(back)


def run_upstream(spot, sources, weights, unit, slope, chunk=256):
    rows, width = sources[0].shape
    total = unit.shape[0]
    wd, we, wr, g2 = weights
    units = we.shape[1]
    steps = total // rows

    def whole(array):
        return pl.BlockSpec(array.shape, lambda i, spot: (0,) * array.ndim)

    fixed = lambda *dims: pl.BlockSpec(dims, lambda i, spot: (0,) * len(dims))
    column = lambda height: pl.BlockSpec((height, rows), lambda i, spot: (0, spot[i]))
    placed = pl.BlockSpec((rows, width), lambda i, spot: (spot[i], 0))
    arrived = lambda size: pl.BlockSpec((rows, size), lambda i, spot: (i, 0))
    in_specs = [pl.BlockSpec(memory_space=pl.ANY)] * 5 + [whole(w) for w in weights] + [placed, arrived(units)]
    out_specs = [column(wd.shape[0]), placed, arrived(width), arrived(units), fixed(2, 8, width), fixed(8, units)]
    shape = lambda *dims: jax.ShapeDtypeStruct(dims, jnp.bfloat16)
    out_shape = [
        shape(wd.shape[0], total),
        shape(total, width),
        shape(total, width),
        shape(total, units),
        jax.ShapeDtypeStruct((2, 8, width), jnp.float32),
        jax.ShapeDtypeStruct((8, units), jnp.float32),
    ]
    return pl.pallas_call(
        partial(upstream_kernel, chunk),
        grid_spec=pltpu.PrefetchScalarGridSpec(
            num_scalar_prefetch=1,
            grid=(steps,),
            in_specs=in_specs,
            out_specs=out_specs,
            scratch_shapes=[
                pltpu.VMEM((2, rows, width), jnp.bfloat16),
                pltpu.SemaphoreType.DMA((2,)),
            ],
        ),
        out_shape=out_shape,
        compiler_params=pltpu.CompilerParams(vmem_limit_bytes=VMEM),
        cost_estimate=pl.CostEstimate(
            flops=3 * total * width * (wd.shape[0] + 2 * units), bytes_accessed=12 * total * width, transcendentals=0
        ),
    )(spot, *sources, wd, we, wr, g2, unit, slope)


def weight_kernel(spot_ref, second_ref, hg_ref, active_ref, up_ref, mixed_ref, *refs):
    shares, (expand_sum, reduce_sum, dense_sum) = refs[:4], refs[4:]
    step = pl.program_id(0)
    steps = pl.num_programs(0)

    @pl.when(step == 0)
    def _():
        expand_sum[...] = jnp.zeros_like(expand_sum)
        reduce_sum[...] = jnp.zeros_like(reduce_sum)
        dense_sum[...] = jnp.zeros_like(dense_sum)

    up = up_ref[...]
    dense_sum[...] += mm(mixed_ref[...], up)
    expand_sum[...] += mm(second_ref[...], hg_ref[...], TN)
    reduce_sum[...] += mm(active_ref[...], up, TN)

    @pl.when(step == steps - 1)
    def _():
        col = spot_ref[steps]
        large, small = expand_sum.shape[0] // 4, dense_sum.shape[0] // 4
        for k, share in enumerate(shares):
            i = k + col - 2 * (col & k)
            at = pl.ds(pl.multiple_of(i * large, large), large)
            share[:large] = low(expand_sum[at, :])
            share[large : 2 * large] = low(reduce_sum[at, :])
            share[2 * large :] = low(dense_sum[pl.ds(pl.multiple_of(i * small, small), small), :])


def weight_gradients(spot, second, hg, active, ups, mixed):
    total, width = second.shape
    units = hg.shape[1]
    rows = total // N
    height = mixed.shape[0]
    fixed = lambda *dims: pl.BlockSpec(dims, lambda i, spot: (0,) * len(dims))
    arrived = lambda size: pl.BlockSpec((rows, size), lambda i, spot: (i, 0))
    dims = (width // 4 + units // 4 + height // 4, width)
    return pl.pallas_call(
        weight_kernel,
        grid_spec=pltpu.PrefetchScalarGridSpec(
            num_scalar_prefetch=1,
            grid=(N,),
            in_specs=[
                arrived(width),
                arrived(units),
                arrived(units),
                arrived(width),
                pl.BlockSpec((height, rows), lambda i, spot: (0, spot[i])),
            ],
            out_specs=[fixed(*dims)] * 4,
            scratch_shapes=[
                pltpu.VMEM((width, units), jnp.float32),
                pltpu.VMEM((units, width), jnp.float32),
                pltpu.VMEM((height, width), jnp.float32),
            ],
        ),
        out_shape=[jax.ShapeDtypeStruct(dims, jnp.bfloat16)] * 4,
        compiler_params=pltpu.CompilerParams(vmem_limit_bytes=VMEM),
        cost_estimate=pl.CostEstimate(
            flops=3 * total * width * (height + 2 * units), bytes_accessed=8 * total * width, transcendentals=0
        ),
    )(spot, second, hg, active, ups, mixed)


def deliver_kernel(order_ref, left_ref, weight_ref, add_ref, *refs):
    del order_ref
    send_ref, keep_ref = refs[-2:]
    step = pl.program_id(0)
    value = mm(left_ref[...], weight_ref[...], TN)
    if len(refs) > 2:
        value = value * refs[0][...]
    value = low(value + wide(add_ref[...]))

    @pl.when(step < pl.num_programs(0) // 2)
    def _():
        send_ref[...] = value

    @pl.when(step >= pl.num_programs(0) // 2)
    def _():
        keep_ref[...] = value


def deliver(order, left, weight, add, gain=None):
    depth, total = left.shape
    width = weight.shape[1]
    steps = N
    tile = total // N
    rows = pl.BlockSpec((tile, width), lambda s, order: (order[s], 0))
    in_specs = [
        pl.BlockSpec((depth, tile), lambda s, order: (0, order[s])),
        pl.BlockSpec((depth, width), lambda s, order: (0, 0)),
        rows,
    ]
    operands = [left, weight, add]
    if gain is not None:
        in_specs.append(pl.BlockSpec((1, width), lambda s, order: (0, 0)))
        operands.append(gain)
    return pl.pallas_call(
        deliver_kernel,
        grid_spec=pltpu.PrefetchScalarGridSpec(
            num_scalar_prefetch=1,
            grid=(steps,),
            in_specs=in_specs,
            out_specs=[
                pl.BlockSpec((tile, width), lambda s, order: (jnp.minimum(s, steps // 2 - 1), 0)),
                pl.BlockSpec((tile, width), lambda s, order: (jnp.maximum(s - steps // 2, 0), 0)),
            ],
        ),
        out_shape=[jax.ShapeDtypeStruct((total // 2, width), jnp.bfloat16)] * 2,
        compiler_params=pltpu.CompilerParams(vmem_limit_bytes=VMEM),
        cost_estimate=pl.CostEstimate(
            flops=0, bytes_accessed=0, transcendentals=0
        ),
    )(order, *operands)


def joint_kernel(spot_ref, jb_ref, unit_ref, wj_ref, gain_ref, shift_ref, sums_ref, up_ref, hsum_ref, *refs):
    shares, (vector_ref, total_ref, turned_ref, sum_ref) = refs[:4], refs[4:]
    step = pl.program_id(0)
    jb = jb_ref[...]
    height, tile = jb.shape
    width = unit_ref.shape[1]

    @pl.when(step == 0)
    def _():
        total_ref[...] = jnp.zeros_like(total_ref)
        sum_ref[...] = jnp.zeros_like(sum_ref)

    total_ref[...] += mm(jb, unit_ref[...])
    sum_ref[...] += mm(jb, jnp.ones((tile, 128), jnp.bfloat16))

    @pl.when(step == pl.num_programs(0) - 1)
    def _():
        col, quarter = spot_ref[0], spot_ref[1]
        gain = jnp.sum(total_ref[...] * wide(wj_ref[...]), axis=0, keepdims=True)
        turned_ref[...] = (total_ref[...] * gain_ref[...] + sum_ref[:, :1] * shift_ref[...]).T
        part = width // 4
        for k, share in enumerate(shares):
            i = k + col - 2 * (col & k)
            share[:part] = low(turned_ref[pl.ds(pl.multiple_of(i * part, part), part), :])
        jb_sum = sum_ref[...].T[:1]
        first = low(jb_sum)
        rest = jb_sum - wide(first)
        middle = low(rest)
        final = low(rest - wide(middle))
        shift = mm(jnp.concatenate([first, middle, final], axis=0), wj_ref[...])
        rows = [
            gain,
            jnp.sum(shift, axis=0, keepdims=True),
            jnp.sum(sums_ref[0], axis=0, keepdims=True),
            jnp.sum(sums_ref[1], axis=0, keepdims=True),
            jnp.sum(up_ref[...], axis=0, keepdims=True),
        ]
        jb_sum = jnp.concatenate([jb_sum, jnp.zeros((1, width - height), jnp.float32)], axis=1)
        for whole in (jnp.sum(hsum_ref[...], axis=0, keepdims=True), jb_sum):
            rows += [jnp.where(quarter == i, whole, 0.0) for i in range(N)]
        rows.append(jnp.zeros((3, width), jnp.float32))
        vector = jnp.concatenate(rows, axis=0)
        vector_ref[...] = vector
        coarse = low(vector)
        fine = low(vector - wide(coarse))
        rest = jnp.zeros((16, 2 * height - width), jnp.bfloat16)
        pieces = []
        for piece in (coarse, fine):
            pieces += [piece[:, :height], jnp.concatenate([piece[:, height:], rest], axis=1)]
        for share in shares[1:]:
            for n, piece in enumerate(pieces):
                share[part + 16 * n : part + 16 * (n + 1)] = piece


def joint_gradient(spot, jb, unit, wj, gain, shift, sums, up_sum, hsum):
    height, total = jb.shape
    width = unit.shape[1]
    tile = total // N
    fixed = lambda *dims: pl.BlockSpec(dims, lambda s, spot: (0,) * len(dims))
    shapes = [(width // 4, height)] + [(width // 4 + 64, height)] * 3
    return pl.pallas_call(
        joint_kernel,
        grid_spec=pltpu.PrefetchScalarGridSpec(
            num_scalar_prefetch=1,
            grid=(N,),
            in_specs=[
                pl.BlockSpec((height, tile), lambda s, spot: (0, s)),
                pl.BlockSpec((tile, width), lambda s, spot: (s, 0)),
                fixed(height, width),
                fixed(1, width),
                fixed(1, width),
                fixed(2, 8, width),
                fixed(8, width),
                fixed(*hsum.shape),
            ],
            out_specs=[fixed(*dims) for dims in shapes] + [fixed(16, width)],
            scratch_shapes=[
                pltpu.VMEM((height, width), jnp.float32),
                pltpu.VMEM((width, height), jnp.float32),
                pltpu.VMEM((height, 128), jnp.float32),
            ],
        ),
        out_shape=[jax.ShapeDtypeStruct(dims, jnp.bfloat16) for dims in shapes]
        + [jax.ShapeDtypeStruct((16, width), jnp.float32)],
        compiler_params=pltpu.CompilerParams(vmem_limit_bytes=VMEM),
        cost_estimate=pl.CostEstimate(
            flops=0, bytes_accessed=0, transcendentals=0
        ),
    )(spot, jb, unit, wj, gain, shift, sums, up_sum, hsum)


def pack(vector, width):
    rest = jnp.zeros((vector.shape[0], 2 * width - vector.shape[1]), jnp.float32)
    return low(jnp.concatenate([vector[:, :width], jnp.concatenate([vector[:, width:], rest], axis=1)], axis=0))


def unpack(rows, size):
    rows = wide(rows).reshape(-1, 2, 16, rows.shape[1]).sum(0)
    return jnp.concatenate([rows[0], rows[1][:, : size - rows.shape[2]]], axis=1)


def hop(value, pairs):
    return lax.ppermute(value, ("core", "blk"), [(a[0] * N + a[1], b[0] * N + b[1]) for a, b in pairs])


PLACES = [(c, z) for c in range(2) for z in range(N)]
MAIN = [(z // 2, z) for z in range(N)]
CORE_SWAP = [((c, z), (1 - c, z)) for c, z in PLACES]
NEAR_SWAP = [((c, z), (c, z ^ 1)) for c, z in PLACES]
FAR_SWAP = [((c, z), (c, z ^ 2)) for c, z in PLACES]
FAR_HOME = [((c, z), (1 - c, z ^ 2)) for c, z in PLACES if c != z // 2]


HOME = [((c, z), (c, z ^ 1)) for c, z in MAIN] + FAR_HOME
OFF_MAIN = [(c, z) for c, z in PLACES if c != z // 2]
NEAR_OFF = [((c, z), (c, z ^ 1)) for c, z in OFF_MAIN]
STAY = [(place, place) for place in MAIN]


def tie(*arrays):
    return lax.optimization_barrier(arrays)


def near_sum(keep, got):
    rows = keep.shape[0] // 2
    return low(wide(keep[rows:]) + wide(got[rows:]))


def home_sum(keep, got, near, got_near, main):
    rows = keep.shape[0] // 2
    return jnp.where(main, near, low(wide(keep[:rows]) + wide(got[:rows]) + wide(got_near)))


def own_sum(keep, got, got_home, main):
    rows = keep.shape[0] // 2
    return jnp.where(main, wide(keep[:rows]) + wide(got[:rows]), 0.0) + wide(got_home)


def pick(value, axis, index):
    return lax.dynamic_index_in_dim(value, index, axis, keepdims=False)


def plane(values):
    return [lax.ppermute(value, "col", [(i, i ^ (k + 1)) for i in range(4)]) for k, value in enumerate(values)]


NEAR = [((c, z), (c, z ^ 1)) for c, z in PLACES]


def first_pieces(value, near):
    return pick(value, 1, 1 - near).reshape(-1, value.shape[-1])


def second_pieces(value, got, core, near):
    got = got.reshape((2,) + value.shape[2:])
    return jnp.concatenate([pick(pick(value, 1, near), 0, 1 - core), pick(got, 0, 1 - core)], axis=0)


def quarters(quarter, line, got, last, core, near):
    size = line.shape[2]
    mine = chosen(2 * core + near, [line[0, 0], line[0, 1], line[1, 0], line[1, 1]])
    pieces = [mine, last[:size], jnp.where(core == 0, got[:size], got[size : 2 * size]), last[size : 2 * size]]
    return [chosen(quarter ^ k, pieces) for k in range(N)]


def finish_kernel(spot_ref, line_ref, got_ref, last_ref, reduce_ref, expand_out, dense_out, reduce_out):
    core, near, half = spot_ref[0], spot_ref[1], spot_ref[2]
    pieces = quarters(2 * near + core, wide(line_ref[...]), wide(got_ref[...]), wide(last_ref[...]), core, near)
    rows = expand_out.shape[0]
    for e in range(pieces[0].shape[1] // 128):
        for slot in range(N):
            piece = pieces[slot ^ (2 * (e % 2))]
            to = (N * e + slot) * 128
            expand_out[:, to : to + 128] = piece[:rows, e * 128 : (e + 1) * 128]
    dense_out[...] = chosen(2 * core + half, [piece[rows:] for piece in pieces])
    reduce_out[...] = wide(reduce_ref[...])


def finish(spot, line, got, last, reduced):
    rows, width = line.shape[2] // 2, line.shape[3]
    return pl.pallas_call(
        finish_kernel,
        in_specs=[pl.BlockSpec(memory_space=pltpu.SMEM)] + [pl.BlockSpec(memory_space=pltpu.VMEM)] * 4,
        out_specs=[pl.BlockSpec(memory_space=pltpu.VMEM)] * 3,
        out_shape=[
            jax.ShapeDtypeStruct((rows, N * width), jnp.float32),
            jax.ShapeDtypeStruct((rows, width), jnp.float32),
            jax.ShapeDtypeStruct(reduced.shape, jnp.float32),
        ],
        compiler_params=pltpu.CompilerParams(vmem_limit_bytes=VMEM),
    )(spot, line, got, last, reduced)


def joint_finish_kernel(spot_ref, line_ref, other_ref, near_ref, last_ref, out_ref):
    core, near = spot_ref[0], spot_ref[1]
    rows = out_ref.shape[0]
    line = wide(line_ref[...])
    mine = chosen(2 * core + near, [line[0, 0], line[0, 1], line[1, 0], line[1, 1]])
    pieces = [mine] + [wide(ref[:rows]) for ref in (other_ref, near_ref, last_ref)]
    pieces = [chosen((2 * near + core) ^ k, pieces) for k in range(N)]
    for n in range(mine.shape[1] // (2 * HEAD)):
        for slot in range(0, N, 2):
            for other in range(2):
                at = (2 * n + other) * HEAD
                to = ((2 * n + other) * N + slot) * HEAD
                pair = [piece[:, at : at + HEAD] for piece in pieces[slot : slot + 2]]
                out_ref[:, to : to + 2 * HEAD] = jnp.concatenate(pair, axis=1)


def joint_finish(spot, line, got):
    rows, width = line.shape[2:]
    return pl.pallas_call(
        joint_finish_kernel,
        in_specs=[pl.BlockSpec(memory_space=pltpu.SMEM)] + [pl.BlockSpec(memory_space=pltpu.VMEM)] * 4,
        out_specs=pl.BlockSpec(memory_space=pltpu.VMEM),
        out_shape=jax.ShapeDtypeStruct((rows, N * width), jnp.float32),
        compiler_params=pltpu.CompilerParams(vmem_limit_bytes=VMEM),
    )(spot, line, *got)


def split_local(
    tokens,
    lengths,
    first_gain,
    first_shift,
    second_gain,
    second_shift,
    joint_weight,
    joint_bias,
    dense_weight,
    dense_bias,
    expand_weight,
    expand_bias,
    reduce_weight,
    reduce_bias,
    cotangent,
):
    col, core, z = lax.axis_index("col"), lax.axis_index("core"), lax.axis_index("blk")
    half, near = z // 2, z % 2
    quarter = 2 * near + core
    main = core == half
    flag = main.astype(jnp.int32)
    rows, width = tokens.shape[1:]
    total = rows * N
    units = expand_weight.shape[1]
    groups = units // (N * 128)
    heads = HEADS // N
    own_x, own_g = tokens[0], cotangent[0]
    row_of = lambda vector: vector.reshape(1, -1)

    x_other = hop(own_x, CORE_SWAP)
    x_first = hop(own_x, HOME)

    wj, wd, we, wr = prepare(quarter, joint_weight, dense_weight, expand_weight, reduce_weight)
    bj = pick(joint_bias.reshape(3, heads, N, HEAD), 2, quarter).reshape(-1, 1)
    be = expand_bias.reshape(groups // 2, 2, N, 128)
    be = jnp.stack([pick(be[:, 0], 1, quarter), pick(be[:, 1], 1, quarter ^ 2)], axis=1).reshape(1, -1)
    first_row, second_row = row_of(first_gain), row_of(second_gain)

    weights = [wj, bj, we, be, wr, first_row, row_of(first_shift), second_row, row_of(second_shift)]

    sizes = jnp.where(main, lengths, hop(lengths, CORE_SWAP))
    number, offset = doc_tables(sizes, jnp.arange(total, dtype=jnp.int32))
    inverse = 10000.0 ** (-2.0 * jnp.arange(ROTARY // 2, dtype=jnp.float32) / ROTARY)
    phase = inverse[:, None] * offset.astype(jnp.float32)
    tables = [jnp.cos(phase), jnp.sin(phase)]
    docs = lengths.shape[1]
    same = number == jnp.arange(HEAD, dtype=jnp.int32)[:, None]
    used = jnp.arange(HEAD)[:, None] < docs
    qx = low(jnp.where(same & used, 1.0, 0.0))
    kx = low(jnp.where(used & ~same, NEG, 0.0))

    spots = [z, z ^ (2 - flag), z ^ (1 + flag), z ^ 3]
    zero, one = jnp.int32(0), jnp.int32(1)
    state = run_tokens(0, jnp.stack([spots[0], 1 - flag]), [own_x, x_other], weights, tables, None)
    x_first, own_g_late, *state = tie(x_first, own_g, *state)
    g_far = hop(own_g_late, FAR_HOME + STAY)
    x_second = hop(x_first, NEAR_OFF + STAY)
    x_first_other = hop(x_first, CORE_SWAP)
    state = run_tokens(1, jnp.stack([spots[1], zero]), [x_first], weights, tables, state)
    x_second, *state = tie(x_second, *state)
    x_second_other = hop(x_second, CORE_SWAP)
    spot = jnp.stack([spots[2], spots[3], zero, 2 - flag])
    state = run_tokens(2, spot, [x_first_other, x_second_other, x_second], weights, tables, state)
    qkv, unit, second, active, slope, feed = state
    order = z ^ (jnp.arange(N, dtype=jnp.int32) ^ (2 * flag))
    qkv = qkv.reshape(3, heads, HEAD, total)
    g_far, qkv = tie(g_far, qkv)
    g_near = hop(g_far, NEAR)
    g_other = hop(g_far, CORE_SWAP)
    mixed, full, inverse_sum, shares = attend_forward(qkv, kx, qx, 0, heads, None)
    g_near, mixed = tie(g_near, mixed)
    mixed = mixed.reshape(-1, total)
    g_near_other = hop(g_near, CORE_SWAP)
    out_send, out_keep = deliver(order, mixed, wd, feed)

    spot = jnp.stack([*spots, 1 - flag, 3 - flag, 4 - 3 * flag, 2 + 2 * flag])
    spot, out_send, out_keep = tie(spot, out_send, out_keep)
    out_got = hop(out_send, CORE_SWAP)
    gs = (own_g, g_other, g_near, g_far, g_near_other)
    mg, back, ups, hg, sums, hsum = run_upstream(spot, gs, [wd, we, wr, second_row], unit, slope)
    out_near = near_sum(out_keep, out_got)
    out_near, hg = tie(out_near, hg)
    out_got_near = hop(out_near, NEAR_OFF)

    spot = jnp.stack([*spots, col])
    kept_share, *shares_out = weight_gradients(spot, second, hg, active, ups, mixed)
    out_home = home_sum(out_keep, out_got, out_near, out_got_near, main)
    out_home, mg, *shares_out = tie(out_home, mg, *shares_out)
    out_got_home = hop(out_home, HOME)
    shares_got = plane(shares_out)

    jb = attend_backward(qkv, mg.reshape(heads, HEAD, total), full, inverse_sum, shares, tables)
    jb = jb.reshape(-1, total)

    spot = jnp.stack([col, quarter])
    up_sum = jnp.sum(wide(own_g).reshape(-1, 8, width), axis=0)
    kept_joint, *joint_out, vector = joint_gradient(
        spot, jb, unit, wj, first_row, row_of(first_shift), sums, up_sum, hsum
    )
    jb, *joint_out = tie(jb, *joint_out)
    joint_got = plane(joint_out)

    send, keep = deliver(order, jb, wj, back, first_row)

    send, out_got_home, *shares_got = tie(send, out_got_home, *shares_got)
    share = wide(kept_share) + sum(wide(piece) for piece in shares_got)
    kept = near ^ half
    part = width // 4
    expand_part = share[:part].reshape(2, 2, 2, part // 8, units // N)
    reduce_part = share[part : part + units // (4 * N)].reshape(2, -1, width)
    dense_part = share[part + units // (4 * N) :]
    far_send = [pick(expand_part, 1, 1 - half).reshape(part // 2, -1), pick(reduce_part, 0, 1 - kept), dense_part]
    far_send = low(jnp.concatenate(far_send, axis=0))
    far_send, send = tie(far_send, send)
    got = hop(send, CORE_SWAP)
    far_got = hop(far_send, FAR_SWAP)
    near_part = near_sum(keep, got)
    out = own_sum(out_keep, out_got, out_got_home, main)
    inputs = wide(own_x)
    result = low(inputs + out + (dense_bias + reduce_bias))
    got_near = hop(near_part, NEAR_OFF)

    got_near, *joint_got = tie(got_near, *joint_got)
    joint_part = wide(kept_joint) + sum(wide(piece[:part]) for piece in joint_got)
    vector = vector + sum(unpack(piece[part:], width) for piece in joint_got)
    joint_width = joint_part.shape[1]
    joint_part = joint_part.reshape(2, 2, 2, part // 8, joint_width)
    joint_far_send = jnp.concatenate(
        [low(pick(joint_part, 1, 1 - half)).reshape(part // 2, joint_width), pack(vector, joint_width)], axis=0
    )
    home = home_sum(keep, got, near_part, got_near, main)
    home, joint_far_send, result = tie(home, joint_far_send, result)
    got_home = hop(home, HOME)
    joint_far = hop(joint_far_send, FAR_SWAP)
    home, far_got = tie(home, far_got)
    far_got = wide(far_got)
    expand_part = low(pick(expand_part, 1, half).reshape(part // 2, -1) + far_got[: part // 2])
    reduce_part = low(pick(reduce_part, 0, kept) + far_got[part // 2 : part // 2 + 128])
    dense_part = low(dense_part + far_got[part // 2 + 128 :]).reshape(2, HEAD // 2, width)
    line = jnp.concatenate(
        [
            expand_part.reshape(2, 2, part // 8, -1),
            jnp.broadcast_to(dense_part[None], (2,) + dense_part.shape),
        ],
        axis=2,
    )
    line_send = first_pieces(line, near)
    line_got = hop(line_send, NEAR)
    reduce_got = hop(reduce_part, [((c, s), ((s % 2) ^ (s // 2), 2 * (s // 2) + c)) for c, s in PLACES])
    scaled = own_sum(keep, got, got_home, main)
    _, unit_rows, inverse_root = normalize(inputs, first_gain, first_shift)
    input_back = inverse_root * (
        scaled
        - jnp.mean(scaled, axis=-1, keepdims=True)
        - unit_rows * jnp.mean(scaled * unit_rows, axis=-1, keepdims=True)
    )
    tokens_gradient = low(wide(own_g) + input_back)
    line_got, tokens_gradient = tie(line_got, tokens_gradient)
    line_send = second_pieces(line, line_got, core, near)
    line_last = hop(line_send, CORE_SWAP)
    joint_far, line_send = tie(joint_far, line_send)
    joint_part = low(pick(joint_part, 1, half).reshape(part // 2, joint_width) + wide(joint_far[: part // 2]))
    vector = vector + unpack(joint_far[part // 2 :], width)
    joint_line = joint_part.reshape(2, 2, part // 8, joint_width)
    vector_rows = pack(vector, joint_width)
    joint_got = []
    for dz, dc in ((0, 1), (1, 0), (1, 1)):
        piece = pick(pick(joint_line, 1, near ^ dz), 0, core ^ dc)
        piece = jnp.concatenate([piece, vector_rows], axis=0)
        joint_got.append(hop(piece, [((c, p), (c ^ dc, p ^ dz)) for c, p in PLACES]))
    spot = jnp.stack([core, near, half])
    expand_mine, dense_mine, reduce_mine = finish(spot, line, line_got, line_last, reduce_got)
    expand_mine, *joint_got = tie(expand_mine, *joint_got)
    vector = vector + sum(unpack(piece[part // 8 :], width) for piece in joint_got)
    joint_mine = joint_finish(spot, joint_line, joint_got)

    device = (2 * col + core) * N + z
    share = width // (8 * N)
    head_row = lambda head: 5 + N + head % N
    cut = lambda row, start, size: lax.dynamic_slice(vector, (row, start), (1, size))[0]
    pieces = [cut(row, device * share, share) for row in range(5)]
    pieces[4:] = [
        cut(head_row(device % HEADS), (device // HEADS * heads + device % HEADS // N) * HEAD, HEAD),
        cut(head_row(device // 2), (2 * heads + device // 2 // N) * HEAD + device % 2 * share, share),
        pieces[4],
        cut(5 + (z ^ (2 * core)), (2 * col + core) * 128, 128),
    ]

    return (
        result[None],
        tokens_gradient[None],
        *pieces[:4],
        joint_mine,
        pieces[4],
        pieces[5],
        dense_mine,
        pieces[6],
        expand_mine,
        pieces[7],
        reduce_mine,
        pieces[6],
    )


def solution(mesh):
    count, blocks = mesh.devices.shape
    split = blocks == N and count == 8
    if split:
        mesh = jax.sharding.Mesh(mesh.devices.reshape(count // 2, 2, blocks), ("col", "core", "blk"))
        batch = ("col", "core")
        every = ("col", "core", "blk")
    else:
        batch, every = "batch", ("batch", "blk")
    by_rows = P(batch, "blk", None)
    placed = (by_rows, P(batch, None)) + (P(),) * 12 + (by_rows,)
    vector, matrix = P(every), P(every, None)
    return jax.shard_map(
        split_local if split else local,
        mesh=mesh,
        in_specs=placed,
        out_specs=(
            by_rows,
            by_rows,
            vector,
            vector,
            vector,
            vector,
            matrix,
            vector,
            vector,
            matrix,
            vector,
            matrix,
            vector,
            matrix,
            vector,
        ),
        check_vma=False,
    )
```

```python
from functools import partial

import jax
import jax.numpy as jnp
from jax import lax
from jax.experimental import pallas as pl
from jax.experimental.pallas import tpu as pltpu
from jax.sharding import PartitionSpec as P

HEADS = 16
HEAD = 64
ROTARY = 16


EPSILON = 1e-05
MASKED = -1e30


def doc_tables(lengths, positions):
    doc_ends = jnp.cumsum(lengths, axis=-1)
    doc_starts = doc_ends - lengths
    doc_number = jnp.sum(
        (positions[None, :, None] >= doc_ends[:, None, :]).astype(jnp.int32), axis=-1
    )
    matches = (
        doc_number[:, :, None] == jnp.arange(lengths.shape[-1], dtype=jnp.int32)[None, None, :]
    )
    begins = jnp.sum(jnp.where(matches, doc_starts[:, None, :], 0), axis=-1)
    return (doc_number, positions[None, :] - begins)


def angles(offsets):
    half_width = ROTARY // 2
    inverse = 10000.0 ** (-2.0 * jnp.arange(half_width, dtype=jnp.float32) / ROTARY)
    phase = offsets.astype(jnp.float32)[..., None] * inverse
    return (jnp.cos(phase), jnp.sin(phase))


def rotate(values, cosine, sine_table, direction):
    half_width = cosine.shape[-1]
    lead_part = values[..., :half_width]
    tail_part = values[..., half_width : 2 * half_width]
    cosine = cosine[:, :, None, :]
    sine_table = sine_table[:, :, None, :] * direction
    return jnp.concatenate(
        [
            lead_part * cosine - tail_part * sine_table,
            tail_part * cosine + lead_part * sine_table,
            values[..., 2 * half_width :],
        ],
        axis=-1,
    )


def normalize(values, gain_row, shift_row):
    center = values - jnp.mean(values, axis=-1, keepdims=True)
    spread = jnp.mean(center * center, axis=-1, keepdims=True)
    inverse_root = lax.rsqrt(spread + EPSILON)
    unit_rows = center * inverse_root
    return (unit_rows * gain_row + shift_row, unit_rows, inverse_root)


def normalize_back(upstream, unit_rows, inverse_root, gain_row):
    scaled_back = upstream * gain_row
    input_back = inverse_root * (
        scaled_back
        - jnp.mean(scaled_back, axis=-1, keepdims=True)
        - unit_rows * jnp.mean(scaled_back * unit_rows, axis=-1, keepdims=True)
    )
    return (input_back, jnp.sum(upstream * unit_rows, axis=0), jnp.sum(upstream, axis=0))


def outer(left_rows, right_rows):
    return lax.dot_general(
        left_rows, right_rows, (((0,), (0,)), ((), ())), preferred_element_type=jnp.float32
    )


def against(left_rows, weight_rows):
    return lax.dot_general(
        left_rows, weight_rows, (((1,), (1,)), ((), ())), preferred_element_type=jnp.float32
    )


def over_piece(stepper, running, segment, stride):
    sub_count = segment.shape[1] // stride

    def one_turn(position, current):
        part_rows = lax.dynamic_slice_in_dim(segment, position * stride, stride, 1)
        return stepper(current, part_rows, position * stride)

    return lax.fori_loop(0, sub_count, one_turn, running)


def local(
    tokens,
    lengths,
    first_gain,
    first_shift,
    second_gain,
    second_shift,
    joint_weight,
    joint_bias,
    dense_weight,
    dense_bias,
    expand_weight,
    expand_bias,
    reduce_weight,
    reduce_bias,
    cotangent,
):
    sequences, stride, model_width = tokens.shape
    cycle_size = lax.axis_size("blk")
    seq_total = stride * cycle_size
    rank_here = lax.axis_index("blk")
    row_count = sequences * stride
    factor = HEAD ** (-0.5)
    head_shape = (sequences, stride, HEADS, HEAD)
    places = jnp.arange(seq_total, dtype=jnp.int32)
    number_all, offset_all = doc_tables(lengths, places)
    first_place = rank_here * stride
    query_number = lax.dynamic_slice_in_dim(number_all, first_place, stride, 1)
    query_offset = lax.dynamic_slice_in_dim(offset_all, first_place, stride, 1)
    query_place = first_place + jnp.arange(stride, dtype=jnp.int32)
    last_place = first_place + stride - 1
    cosine, sine_table = angles(query_offset)
    inputs = tokens.reshape(row_count, model_width).astype(jnp.float32)
    first_norm, first_unit, first_scale = normalize(inputs, first_gain, first_shift)
    normed = first_norm.astype(jnp.bfloat16)
    joint_out = jnp.dot(normed, joint_weight, preferred_element_type=jnp.float32) + joint_bias
    queries = rotate(
        joint_out[:, :model_width].reshape(head_shape), cosine, sine_table, 1.0
    ).astype(jnp.bfloat16)
    key_rows = rotate(
        joint_out[:, model_width : 2 * model_width].reshape(head_shape), cosine, sine_table, 1.0
    ).astype(jnp.bfloat16)
    value_rows = joint_out[:, 2 * model_width :].astype(jnp.bfloat16)
    pair_local = jnp.concatenate(
        [
            key_rows.reshape(sequences, stride, model_width),
            value_rows.reshape(sequences, stride, model_width),
        ],
        axis=-1,
    )

    def masked_scores(key_part, begin_row, row_span):
        key_number = lax.dynamic_slice_in_dim(number_all, begin_row, row_span, 1)
        key_place = begin_row + jnp.arange(row_span, dtype=jnp.int32)
        allowed = (query_number[:, :, None] == key_number[:, None, :]) & (
            key_place[None, None, :] <= query_place[None, :, None]
        )
        allowed = allowed[:, None]
        scores = (
            jnp.einsum("sqhd,skhd->shqk", queries, key_part, preferred_element_type=jnp.float32)
            * factor
        )
        return (jnp.where(allowed, scores, MASKED), allowed)

    def split_piece(segment):
        row_span = segment.shape[1]
        key_part = segment[:, :, :model_width].reshape(sequences, row_span, HEADS, HEAD)
        value_part = segment[:, :, model_width:].reshape(sequences, row_span, HEADS, HEAD)
        return (key_part, value_part, row_span)

    def gated(kernel):

        def stepper(running, segment, begin_row):
            return lax.cond(
                begin_row <= last_place,
                lambda current: kernel(current, segment, begin_row),
                lambda current: current,
                running,
            )

        return stepper

    def forward_kernel(running, segment, begin_row):
        row_peak, row_total, weighted = running
        key_part, value_part, row_span = split_piece(segment)
        scores, allowed = masked_scores(key_part, begin_row, row_span)
        new_peak = jnp.maximum(row_peak, jnp.max(scores, axis=-1))
        shares = jnp.where(allowed, jnp.exp(scores - new_peak[..., None]), 0.0)
        decay_factor = jnp.exp(row_peak - new_peak)
        row_total = row_total * decay_factor + jnp.sum(shares, axis=-1)
        update = jnp.einsum(
            "shqk,skhd->sqhd",
            shares.astype(jnp.bfloat16),
            value_part,
            preferred_element_type=jnp.float32,
        )
        weighted = weighted * jnp.transpose(decay_factor, (0, 2, 1))[..., None] + update
        return (new_peak, row_total, weighted)

    forward_step = gated(forward_kernel)
    initial = (
        jnp.full((sequences, HEADS, stride), MASKED, jnp.float32),
        jnp.zeros((sequences, HEADS, stride), jnp.float32),
        jnp.zeros(head_shape, jnp.float32),
    )
    forward_state = over_piece(
        forward_step, initial, lax.all_gather(pair_local, "blk", axis=1, tiled=True), stride
    )
    row_peak, row_total, weighted = forward_state
    mixed_full = weighted / jnp.transpose(row_total, (0, 2, 1))[..., None]
    log_total = row_peak + jnp.log(row_total)
    mixed = mixed_full.reshape(row_count, model_width).astype(jnp.bfloat16)
    attention_out = jnp.dot(mixed, dense_weight, preferred_element_type=jnp.float32) + dense_bias
    second_norm, second_unit, second_scale = normalize(inputs, second_gain, second_shift)
    second = second_norm.astype(jnp.bfloat16)
    hidden = jnp.dot(second, expand_weight, preferred_element_type=jnp.float32) + expand_bias
    active_full, gelu_pull = jax.vjp(partial(jax.nn.gelu, approximate=False), hidden)
    active = active_full.astype(jnp.bfloat16)
    feed_out = jnp.dot(active, reduce_weight, preferred_element_type=jnp.float32) + reduce_bias
    result = (
        (inputs + attention_out + feed_out)
        .astype(jnp.bfloat16)
        .reshape(sequences, stride, model_width)
    )
    upstream = cotangent.reshape(row_count, model_width)
    dense_grad = outer(mixed, upstream)
    bias_total = jnp.sum(upstream, axis=0, dtype=jnp.float32)
    reduce_grad = outer(active, upstream)
    hidden_grad = gelu_pull(against(upstream, reduce_weight))[0].astype(jnp.bfloat16)
    expand_grad = outer(second, hidden_grad)
    hidden_total = jnp.sum(hidden_grad, axis=0, dtype=jnp.float32)
    input_two, gain_second, shift_second = normalize_back(
        against(hidden_grad, expand_weight), second_unit, second_scale, second_gain
    )
    mixed_grad = against(upstream, dense_weight).astype(jnp.bfloat16)
    out_heads = mixed_grad.reshape(head_shape)
    delta_rows = jnp.transpose(jnp.sum(out_heads * mixed_full, axis=-1), (0, 2, 1))

    def backward_kernel(running, segment, begin_row):
        key_part, value_part, row_span = split_piece(segment)
        scores, allowed = masked_scores(key_part, begin_row, row_span)
        weights_now = jnp.where(allowed, jnp.exp(scores - log_total[..., None]), 0.0)
        weight_grad = jnp.einsum(
            "sqhd,skhd->shqk", out_heads, value_part, preferred_element_type=jnp.float32
        )
        score_grad = (weights_now * (weight_grad - delta_rows[..., None])).astype(jnp.bfloat16)
        query_grad = (
            running[0]
            + jnp.einsum(
                "shqk,skhd->sqhd", score_grad, key_part, preferred_element_type=jnp.float32
            )
            * factor
        )
        value_grad = jnp.einsum(
            "shqk,sqhd->skhd",
            weights_now.astype(jnp.bfloat16),
            out_heads,
            preferred_element_type=jnp.float32,
        )
        key_grad = (
            jnp.einsum("shqk,sqhd->skhd", score_grad, queries, preferred_element_type=jnp.float32)
            * factor
        )
        fresh_rows = jnp.concatenate(
            [
                key_grad.reshape(sequences, row_span, model_width),
                value_grad.reshape(sequences, row_span, model_width),
            ],
            axis=-1,
        )
        pair_grad = lax.dynamic_update_slice_in_dim(running[1], fresh_rows, begin_row, 1)
        return (query_grad, pair_grad)

    backward_step = gated(backward_kernel)
    back_initial = (
        jnp.zeros(head_shape, jnp.float32),
        jnp.zeros((sequences, seq_total, 2 * model_width), jnp.float32),
    )
    back_state = over_piece(
        backward_step, back_initial, lax.all_gather(pair_local, "blk", axis=1, tiled=True), stride
    )
    query_grad = back_state[0]
    pair_mine = lax.psum_scatter(back_state[1], "blk", scatter_dimension=1, tiled=True)
    query_back = rotate(query_grad, cosine, sine_table, -1.0).reshape(row_count, model_width)
    key_back = rotate(
        pair_mine[:, :, :model_width].reshape(head_shape), cosine, sine_table, -1.0
    ).reshape(row_count, model_width)
    value_back = pair_mine[:, :, model_width:].reshape(row_count, model_width)
    joint_back = jnp.concatenate([query_back, key_back, value_back], axis=-1).astype(jnp.bfloat16)
    joint_grad = outer(normed, joint_back)
    joint_total = jnp.sum(joint_back, axis=0, dtype=jnp.float32)
    front_total = joint_total[: 2 * model_width]
    value_total = joint_total[2 * model_width :]
    input_one, gain_first, shift_first = normalize_back(
        against(joint_back, joint_weight), first_unit, first_scale, first_gain
    )
    input_total = (
        (upstream.astype(jnp.float32) + input_one + input_two)
        .astype(jnp.bfloat16)
        .reshape(sequences, stride, model_width)
    )
    summed = (
        lax.psum_scatter(gain_first, ("batch", "blk"), scatter_dimension=0, tiled=True),
        lax.psum_scatter(shift_first, ("batch", "blk"), scatter_dimension=0, tiled=True),
        lax.psum_scatter(gain_second, ("batch", "blk"), scatter_dimension=0, tiled=True),
        lax.psum_scatter(shift_second, ("batch", "blk"), scatter_dimension=0, tiled=True),
        lax.psum_scatter(joint_grad, ("batch", "blk"), scatter_dimension=0, tiled=True),
        lax.psum_scatter(front_total, ("batch", "blk"), scatter_dimension=0, tiled=True),
        lax.psum_scatter(value_total, ("batch", "blk"), scatter_dimension=0, tiled=True),
        lax.psum_scatter(dense_grad, ("batch", "blk"), scatter_dimension=0, tiled=True),
        lax.psum_scatter(bias_total, ("batch", "blk"), scatter_dimension=0, tiled=True),
        lax.psum_scatter(expand_grad, ("batch", "blk"), scatter_dimension=0, tiled=True),
        lax.psum_scatter(hidden_total, ("batch", "blk"), scatter_dimension=0, tiled=True),
        lax.psum_scatter(reduce_grad, ("batch", "blk"), scatter_dimension=0, tiled=True),
    )
    return (
        result,
        input_total,
        summed[0],
        summed[1],
        summed[2],
        summed[3],
        summed[4],
        summed[5],
        summed[6],
        summed[7],
        summed[8],
        summed[9],
        summed[10],
        summed[11],
        summed[8],
    )


BQ = 512
N = 4
TM = 256
VMEM = 56 * 1024 * 1024
NEG = -1e30
NN = (((1,), (0,)), ((), ()))
NT = (((1,), (1,)), ((), ()))
TN = (((0,), (0,)), ((), ()))


def mm(left, right, form=NN):
    return lax.dot_general(left, right, form, preferred_element_type=jnp.float32)


def low(value):
    return value.astype(jnp.bfloat16)


def wide(value):
    return value.astype(jnp.float32)


def gelu_parts(hidden):
    size = jnp.abs(hidden) * (0.5**0.5)
    bell = jnp.exp(-(size * size))
    base = 1.0 + 0.3275911 * size
    guess = pl.reciprocal(base, approx=True)
    t = guess * (2.0 - base * guess)
    series = t * (
        0.5 * 0.254829592
        + t
        * (
            0.5 * -0.284496736
            + t * (0.5 * 1.421413741 + t * (0.5 * -1.453152027 + t * (0.5 * 1.061405429)))
        )
    )
    tail = series * bell
    return (jnp.where(hidden >= 0.0, 1.0 - tail, tail), bell)


def fold_rows(value):
    rows, columns = value.shape
    return jnp.sum(value.reshape(rows // 8, 8, columns), axis=0)


def prepare_kernel(spot_ref, wj_ref, wd_ref, we_ref, wr_ref, wj_out, wd_out, we_out, wr_out):
    turned = wj_ref[...].T
    wj_out[...] = jnp.where(lax.rem(spot_ref[0], 2) == 0, turned[:HEAD], turned[HEAD:])
    wd_out[...] = wd_ref[...]
    we_out[...] = we_ref[...]
    wr_out[...] = wr_ref[...]


def prepare(quarter, joint_weight, dense_weight, expand_weight, reduce_weight):
    width, units = expand_weight.shape
    heads = HEADS // N
    groups = units // (N * 128)
    kinds = 3 * heads
    pair = lambda s, spot: (0, (s // heads) * (HEADS // 2) + (s % heads) * (N // 2) + spot[0] // 2)
    row = lambda s: jnp.minimum(s, heads - 1)
    unit = lambda s: jnp.minimum(s, groups - 1)
    group = lambda s, spot: N * unit(s) + lax.rem(spot[0] + 2 * lax.rem(unit(s), 2), N)
    shape = lambda *dims: jax.ShapeDtypeStruct(dims, jnp.bfloat16)
    return pl.pallas_call(
        prepare_kernel,
        grid_spec=pltpu.PrefetchScalarGridSpec(
            num_scalar_prefetch=1,
            grid=(kinds,),
            in_specs=[
                pl.BlockSpec((width, 2 * HEAD), pair),
                pl.BlockSpec((HEAD, width), lambda s, spot: (N * row(s) + spot[0], 0)),
                pl.BlockSpec((width, 128), lambda s, spot: (0, group(s, spot))),
                pl.BlockSpec((128, width), lambda s, spot: (group(s, spot), 0)),
            ],
            out_specs=[
                pl.BlockSpec((HEAD, width), lambda s, spot: (s, 0)),
                pl.BlockSpec((HEAD, width), lambda s, spot: (row(s), 0)),
                pl.BlockSpec((width, 128), lambda s, spot: (0, unit(s))),
                pl.BlockSpec((128, width), lambda s, spot: (unit(s), 0)),
            ],
        ),
        out_shape=[
            shape(kinds * HEAD, width),
            shape(heads * HEAD, width),
            shape(width, groups * 128),
            shape(groups * 128, width),
        ],
        cost_estimate=pl.CostEstimate(flops=0, bytes_accessed=14 * width * width, transcendentals=0),
    )(quarter.reshape(1), joint_weight, dense_weight, expand_weight, reduce_weight)


def parts(diagonal):
    whole, half = slice(0, BQ), slice(BQ // 2, BQ)
    return [(slice(0, BQ // 2), whole), (half, half)] if diagonal else [(whole, whole)]


def beside(value, last, columns):
    return jnp.concatenate([value[:, : columns.start], last], axis=1) if columns.start else last


COLUMN, LINE, ORDER, CHOICES = 8, 10, 13, 17


def block_at(place, j):
    return place * (place + 1) // 2 + j


def forward_kernel(held, qkv_ref, kx_ref, qx_ref, *refs):
    mixed_ref, full_ref, inverse_ref, share_ref, key_ref, *scores = refs[held:]
    key_ref[...] = jnp.concatenate([qkv_ref[1, 0], kx_ref[...]], axis=0).T
    total = kx_ref.shape[1]
    state = {}

    def score(place, j):
        here = slice(place * BQ, (place + 1) * BQ)
        if j == 0:
            query_x = jnp.concatenate([qkv_ref[0, 0, :, here], qx_ref[:, here]], axis=0)
            state[place] = [query_x, jnp.full((8, BQ), NEG * 2, jnp.float32)]
        peak8 = state[place][1]
        for rows, columns in parts(j == place):
            found = mm(key_ref[j * BQ + rows.start : j * BQ + rows.stop, :], state[place][0][:, columns])
            if j == place:
                key_row = rows.start + lax.broadcasted_iota(jnp.int32, found.shape, 0)
                query_column = columns.start + lax.broadcasted_iota(jnp.int32, found.shape, 1)
                found = jnp.where(key_row <= query_column, found, NEG)
            scores[place % 2][j * BQ + rows.start : j * BQ + rows.stop, columns] = found
            peak = jnp.max(found.reshape(-1, 8, found.shape[1]), axis=0)
            peak8 = beside(peak8, jnp.maximum(peak8[:, columns], peak), columns)
        state[place][1] = peak8

    def weigh(place, j):
        here = slice(place * BQ, (place + 1) * BQ)
        if j == 0:
            peak = jnp.max(state[place][1], axis=0, keepdims=True)
            state[place] = [peak, jnp.zeros((8, BQ), jnp.float32), jnp.zeros((HEAD, BQ), jnp.float32)]
        peak, sum8, mixed = state[place]
        for rows, columns in parts(j == place):
            at = slice(j * BQ + rows.start, j * BQ + rows.stop)
            share = jnp.exp(scores[place % 2][at, columns] - peak[:, columns])
            total = sum8[:, columns] + jnp.sum(share.reshape(-1, 8, share.shape[1]), axis=0)
            share = low(share)
            share_ref[0, block_at(place, j), rows, columns] = share
            product = mixed[:, columns] + mm(qkv_ref[2, 0, :, at], share)
            sum8 = beside(sum8, total, columns)
            mixed = beside(mixed, product, columns)
        state[place] = [peak, sum8, mixed]
        if j == place:
            inverse = 1.0 / jnp.sum(state[place][1], axis=0, keepdims=True)
            mixed = state[place][2] * inverse
            inverse_ref[0, :, here] = inverse
            full_ref[0, :, here] = mixed
            mixed_ref[0, :, here] = low(mixed)

    places = list(range(total // BQ))
    for j in range(places[0] + 1):
        score(places[0], j)
    for n, place in enumerate(places):
        for j in range(places[-1] + 2):
            if n + 1 < len(places) and j <= places[n + 1]:
                score(places[n + 1], j)
            if j <= place:
                weigh(place, j)


def attend_forward(qkv, kx, qx, first, count, before):
    _, heads, _, total = qkv.shape
    places = total // BQ
    blocks = block_at(places, 0)
    head_rows = lambda rows: pl.BlockSpec((1, rows, total), lambda h: (first + h, 0, 0))
    operands = [qkv, kx, qx]
    in_specs = [
        pl.BlockSpec((3, 1, HEAD, total), lambda h: (0, first + h, 0, 0)),
        pl.BlockSpec((HEAD, total), lambda h: (0, 0)),
        pl.BlockSpec((HEAD, total), lambda h: (0, 0)),
    ]
    aliases = {}
    if before is not None:
        for index, array in enumerate(before):
            aliases[len(operands)] = index
            operands.append(array)
            in_specs.append(pl.BlockSpec(memory_space=pl.ANY))
    return pl.pallas_call(
        partial(forward_kernel, len(aliases)),
        grid=(count,),
        in_specs=in_specs,
        out_specs=[
            head_rows(HEAD),
            head_rows(HEAD),
            head_rows(1),
            pl.BlockSpec((1, blocks, BQ, BQ), lambda h: (first + h, 0, 0, 0)),
        ],
        out_shape=[
            jax.ShapeDtypeStruct((heads, HEAD, total), jnp.bfloat16),
            jax.ShapeDtypeStruct((heads, HEAD, total), jnp.float32),
            jax.ShapeDtypeStruct((heads, 1, total), jnp.float32),
            jax.ShapeDtypeStruct((heads, blocks, BQ, BQ), jnp.bfloat16),
        ],
        scratch_shapes=[pltpu.VMEM((total, 2 * HEAD), jnp.bfloat16)] + [pltpu.VMEM((total, BQ), jnp.float32)] * 2,
        input_output_aliases=aliases,
        compiler_params=pltpu.CompilerParams(vmem_limit_bytes=VMEM),
        cost_estimate=pl.CostEstimate(
            flops=16 * HEAD * count * blocks * BQ * BQ,
            bytes_accessed=2 * count * blocks * BQ * BQ,
            transcendentals=count * blocks * BQ * BQ,
        ),
    )(*operands)


def backward_kernel(qkv_ref, mg_ref, full_ref, inverse_ref, share_ref, cos_ref, sin_ref, jb_ref, value_ref, acc_ref):
    total = cos_ref.shape[1]
    ones = (lax.broadcasted_iota(jnp.int32, (HEAD, total), 0) < 3).astype(jnp.bfloat16)
    value_ref[...] = jnp.concatenate([qkv_ref[2, 0], ones], axis=0).T
    half = ROTARY // 2
    blank = jnp.zeros((HEAD, BQ), jnp.bfloat16)
    row = lax.broadcasted_iota(jnp.int32, (HEAD, BQ), 0)

    def turn_back(rows, at):
        lead, tail = rows[:half], rows[half : 2 * half]
        cosine, sine = cos_ref[:, at], sin_ref[:, at]
        return low(
            jnp.concatenate([lead * cosine + tail * sine, tail * cosine - lead * sine, rows[2 * half :]], axis=0)
        )

    for place in reversed(range(total // BQ)):
        here = slice(place * BQ, (place + 1) * BQ)
        query_t = qkv_ref[0, 0, :, here]
        mg = low(wide(mg_ref[0, :, here]) * inverse_ref[0, :, here])
        delta = -jnp.sum(wide(mg) * full_ref[0, :, here], axis=0, keepdims=True)
        first = low(delta)
        rest = delta - wide(first)
        middle = low(rest)
        final = low(rest - wide(middle))
        extra = jnp.where(
            row == 0, wide(first), jnp.where(row == 1, wide(middle), jnp.where(row == 2, wide(final), 0.0))
        )
        mg_x = jnp.concatenate([mg, low(extra)], axis=0)
        mg_v = jnp.concatenate([blank, mg], axis=0)
        query_k = jnp.concatenate([query_t, blank], axis=0)
        query_grad = jnp.zeros((HEAD, BQ), jnp.float32)
        for j in range(place + 1):
            for rows, columns in parts(j == place):
                at = slice(j * BQ + rows.start, j * BQ + rows.stop)
                share = share_ref[0, block_at(place, j), rows, columns]
                score_grad = low(wide(share) * mm(value_ref[at, :], mg_x[:, columns]))
                pair = mm(share, mg_v[:, columns], NT) + mm(score_grad, query_k[:, columns], NT)
                product = query_grad[:, columns] + mm(qkv_ref[1, 0, :, at], score_grad)
                query_grad = beside(query_grad, product, columns)
                if (place + 1) * BQ < total:
                    pair = pair + acc_ref[at, :]
                if j < place:
                    acc_ref[at, :] = pair
                else:
                    pair_t = pair.T
                    jb_ref[1, 0, :, at] = turn_back(pair_t[:HEAD], at)
                    jb_ref[2, 0, :, at] = low(pair_t[HEAD:])
        jb_ref[0, 0, :, here] = turn_back(query_grad * (HEAD**-0.5), here)


def attend_backward(qkv, mg, full, inverse, shares, tables):
    _, heads, _, total = qkv.shape
    blocks = shares.shape[1]
    head_rows = lambda rows: pl.BlockSpec((1, rows, total), lambda h: (h, 0, 0))
    kinds = pl.BlockSpec((3, 1, HEAD, total), lambda h: (0, h, 0, 0))
    table = pl.BlockSpec((ROTARY // 2, total), lambda h: (0, 0))
    return pl.pallas_call(
        backward_kernel,
        grid=(heads,),
        in_specs=[
            kinds,
            head_rows(HEAD),
            head_rows(HEAD),
            head_rows(1),
            pl.BlockSpec((1, blocks, BQ, BQ), lambda h: (h, 0, 0, 0)),
            table,
            table,
        ],
        out_specs=kinds,
        out_shape=jax.ShapeDtypeStruct((3, heads, HEAD, total), jnp.bfloat16),
        scratch_shapes=[
            pltpu.VMEM((total, 2 * HEAD), jnp.bfloat16),
            pltpu.VMEM((total, 2 * HEAD), jnp.float32),
        ],
        compiler_params=pltpu.CompilerParams(vmem_limit_bytes=VMEM),
        cost_estimate=pl.CostEstimate(
            flops=32 * HEAD * heads * blocks * BQ * BQ,
            bytes_accessed=2 * heads * blocks * BQ * BQ,
            transcendentals=0,
        ),
    )(qkv, mg, full, inverse, shares, *tables)


def chosen(index, options):
    value = options[-1]
    for k in reversed(range(len(options) - 1)):
        value = jnp.where(index == k, options[k], value)
    return value


def token_kernel(slot, count, sub, chunk, spot_ref, *refs):
    sources = refs[:count]
    (wj_ref, bj_ref, we_ref, be_ref, wr_ref, g1_ref, s1_ref, g2_ref, s2_ref, cos_ref, sin_ref) = refs[count : count + 11]
    qkv_ref, unit_ref, second_ref, active_ref, slope_ref, feed_ref = refs[-6:]
    choice = spot_ref[CHOICES + slot + pl.program_id(0)]
    rows = sources[0].shape[0]
    half = ROTARY // 2
    part = wj_ref.shape[0] // 3
    for top in range(0, rows, sub):
        at = slice(top, top + sub)
        x = wide(chosen(choice, [source[at, :] for source in sources]))
        center = x - jnp.mean(x, axis=-1, keepdims=True)
        scale = lax.rsqrt(jnp.mean(center * center, axis=-1, keepdims=True) + EPSILON)
        unit = center * scale
        unit_ref[at, :] = low(unit)
        normed = low(unit * g1_ref[...] + s1_ref[...])
        second = low(unit * g2_ref[...] + s2_ref[...])
        second_ref[at, :] = second
        joint = mm(wj_ref[...], normed, NT) + bj_ref[...]
        cosine, sine = cos_ref[:, at], sin_ref[:, at]
        for kind in range(3):
            for head in range(part // HEAD):
                first = kind * part + head * HEAD
                turned = joint[first : first + HEAD]
                if kind < 2:
                    lead, tail = turned[:half], turned[half : 2 * half]
                    turned = jnp.concatenate(
                        [lead * cosine - tail * sine, tail * cosine + lead * sine, turned[2 * half :]], axis=0
                    )
                if kind == 0:
                    turned = turned * (HEAD**-0.5)
                qkv_ref[first : first + HEAD, at] = low(turned)
        for left in range(0, we_ref.shape[1], chunk):
            over = slice(left, left + chunk)
            hidden = mm(second, we_ref[:, over]) + be_ref[:, over]
            share, bell = gelu_parts(hidden)
            active_ref[at, over] = low(hidden * share)
            slope_ref[at, over] = low(share + hidden * bell * 0.3989422804014327)
    for top in range(0, rows, sub):
        at = slice(top, top + sub)
        feed_ref[at, :] = low(mm(active_ref[at, :], wr_ref[...]))


def run_tokens(slot, steps, spot, data, weights, tables, before, sub=256, chunk=256):
    rows, width = data[0].shape
    total = tables[0].shape[1]
    wj, bj, we, be, wr, g1, s1, g2, s2 = weights
    units = we.shape[1]

    def whole(array):
        return pl.BlockSpec(array.shape, lambda i, spot: (0,) * array.ndim)

    column = lambda height: pl.BlockSpec((height, rows), lambda i, spot: (0, spot[slot + i]))
    placed = pl.BlockSpec((rows, width), lambda i, spot: (spot[slot + i], 0))
    arrived = lambda size: pl.BlockSpec((rows, size), lambda i, spot: (slot + i, 0))
    in_specs = [whole(w) for w in (*data, *weights)] + [column(ROTARY // 2)] * 2
    out_specs = [column(wj.shape[0]), placed, arrived(width), arrived(units), arrived(units), placed]
    shape = lambda *dims: jax.ShapeDtypeStruct(dims, jnp.bfloat16)
    out_shape = [shape(wj.shape[0], total)] + [shape(total, size) for size in (width, width, units, units, width)]
    operands = [spot, *data, *weights, *tables]
    aliases = {}
    if before is not None:
        for index, array in enumerate(before):
            aliases[len(operands)] = index
            operands.append(array)
            in_specs.append(pl.BlockSpec(memory_space=pl.ANY))
    return pl.pallas_call(
        partial(token_kernel, slot, len(data), sub, chunk),
        grid_spec=pltpu.PrefetchScalarGridSpec(
            num_scalar_prefetch=1, grid=(steps,), in_specs=in_specs, out_specs=out_specs
        ),
        out_shape=out_shape,
        input_output_aliases=aliases,
        compiler_params=pltpu.CompilerParams(vmem_limit_bytes=VMEM),
        cost_estimate=pl.CostEstimate(flops=0, bytes_accessed=0, transcendentals=0),
    )(*operands)


def upstream_kernel(chunk, spot_ref, *refs):
    sources, refs = refs[:5], refs[5:]
    (wd_ref, we_ref, wr_ref, g2_ref, unit_ref, slope_ref) = refs[:6]
    (mg_ref, back_ref, up_ref, hg_ref, sums_ref, hsum_ref) = refs[6:12]
    buffer, sems = refs[12:]
    step = pl.program_id(0)
    steps = pl.num_programs(0)
    slot = lax.rem(step, 2)

    def fetch(which, into):
        for k, source in enumerate(sources):

            @pl.when(spot_ref[steps + which] == k)
            def _():
                pltpu.make_async_copy(source, buffer.at[into], sems.at[into]).start()

    @pl.when(step == 0)
    def _():
        fetch(0, 0)
        sums_ref[...] = jnp.zeros_like(sums_ref)
        hsum_ref[...] = jnp.zeros_like(hsum_ref)

    @pl.when(step + 1 < steps)
    def _():
        fetch(step + 1, 1 - slot)

    pltpu.make_async_copy(sources[0], buffer.at[slot], sems.at[slot]).wait()
    up = buffer[slot]
    up_ref[...] = up
    mg_ref[...] = low(mm(wd_ref[...], up, NT))
    for left in range(0, we_ref.shape[1], chunk):
        over = slice(left, left + chunk)
        piece = low(mm(up, wr_ref[over, :], NT) * wide(slope_ref[:, over]))
        hg_ref[:, over] = piece
        hsum_ref[:, over] += fold_rows(wide(piece))
    for left in range(0, we_ref.shape[0], chunk):
        over = slice(left, left + chunk)
        back = mm(hg_ref[...], we_ref[over, :], NT)
        back_ref[:, over] = low(back * g2_ref[:, over])
        sums_ref[0, :, over] += fold_rows(back * wide(unit_ref[:, over]))
        sums_ref[1, :, over] += fold_rows(back)


def run_upstream(spot, sources, weights, unit, slope, chunk=256):
    rows, width = sources[0].shape
    total = unit.shape[0]
    wd, we, wr, g2 = weights
    units = we.shape[1]
    steps = total // rows

    def whole(array):
        return pl.BlockSpec(array.shape, lambda i, spot: (0,) * array.ndim)

    fixed = lambda *dims: pl.BlockSpec(dims, lambda i, spot: (0,) * len(dims))
    column = lambda height: pl.BlockSpec((height, rows), lambda i, spot: (0, spot[i]))
    placed = pl.BlockSpec((rows, width), lambda i, spot: (spot[i], 0))
    arrived = lambda size: pl.BlockSpec((rows, size), lambda i, spot: (i, 0))
    in_specs = [pl.BlockSpec(memory_space=pl.ANY)] * 5 + [whole(w) for w in weights] + [placed, arrived(units)]
    out_specs = [column(wd.shape[0]), placed, arrived(width), arrived(units), fixed(2, 8, width), fixed(8, units)]
    shape = lambda *dims: jax.ShapeDtypeStruct(dims, jnp.bfloat16)
    out_shape = [
        shape(wd.shape[0], total),
        shape(total, width),
        shape(total, width),
        shape(total, units),
        jax.ShapeDtypeStruct((2, 8, width), jnp.float32),
        jax.ShapeDtypeStruct((8, units), jnp.float32),
    ]
    return pl.pallas_call(
        partial(upstream_kernel, chunk),
        grid_spec=pltpu.PrefetchScalarGridSpec(
            num_scalar_prefetch=1,
            grid=(steps,),
            in_specs=in_specs,
            out_specs=out_specs,
            scratch_shapes=[
                pltpu.VMEM((2, rows, width), jnp.bfloat16),
                pltpu.SemaphoreType.DMA((2,)),
            ],
        ),
        out_shape=out_shape,
        compiler_params=pltpu.CompilerParams(vmem_limit_bytes=VMEM),
        cost_estimate=pl.CostEstimate(
            flops=3 * total * width * (wd.shape[0] + 2 * units), bytes_accessed=12 * total * width, transcendentals=0
        ),
    )(spot, *sources, wd, we, wr, g2, unit, slope)


def weight_kernel(spot_ref, second_ref, hg_ref, active_ref, up_ref, mixed_ref, *refs):
    shares, (expand_sum, reduce_sum, dense_sum) = refs[:4], refs[4:]
    step = pl.program_id(0)
    steps = pl.num_programs(0)

    @pl.when(step == 0)
    def _():
        expand_sum[...] = jnp.zeros_like(expand_sum)
        reduce_sum[...] = jnp.zeros_like(reduce_sum)
        dense_sum[...] = jnp.zeros_like(dense_sum)

    up = up_ref[...]
    dense_sum[...] += mm(mixed_ref[...], up)
    expand_sum[...] += mm(second_ref[...], hg_ref[...], TN)
    reduce_sum[...] += mm(active_ref[...], up, TN)

    @pl.when(step == steps - 1)
    def _():
        col = spot_ref[COLUMN]
        large, small = expand_sum.shape[0] // 4, dense_sum.shape[0] // 4
        for k, share in enumerate(shares):
            i = k + col - 2 * (col & k)
            at = pl.ds(pl.multiple_of(i * large, large), large)
            share[:large] = low(expand_sum[at, :])
            share[large : 2 * large] = low(reduce_sum[at, :])
            share[2 * large :] = low(dense_sum[pl.ds(pl.multiple_of(i * small, small), small), :])


def weight_gradients(spot, second, hg, active, ups, mixed):
    total, width = second.shape
    units = hg.shape[1]
    rows = total // N
    height = mixed.shape[0]
    fixed = lambda *dims: pl.BlockSpec(dims, lambda i, spot: (0,) * len(dims))
    arrived = lambda size: pl.BlockSpec((rows, size), lambda i, spot: (i, 0))
    dims = (width // 4 + units // 4 + height // 4, width)
    return pl.pallas_call(
        weight_kernel,
        grid_spec=pltpu.PrefetchScalarGridSpec(
            num_scalar_prefetch=1,
            grid=(N,),
            in_specs=[
                arrived(width),
                arrived(units),
                arrived(units),
                arrived(width),
                pl.BlockSpec((height, rows), lambda i, spot: (0, spot[i])),
            ],
            out_specs=[fixed(*dims)] * 4,
            scratch_shapes=[
                pltpu.VMEM((width, units), jnp.float32),
                pltpu.VMEM((units, width), jnp.float32),
                pltpu.VMEM((height, width), jnp.float32),
            ],
        ),
        out_shape=[jax.ShapeDtypeStruct(dims, jnp.bfloat16)] * 4,
        compiler_params=pltpu.CompilerParams(vmem_limit_bytes=VMEM),
        cost_estimate=pl.CostEstimate(
            flops=3 * total * width * (height + 2 * units), bytes_accessed=8 * total * width, transcendentals=0
        ),
    )(spot, second, hg, active, ups, mixed)


def deliver_kernel(order_ref, left_ref, weight_ref, add_ref, *refs):
    del order_ref
    send_ref, keep_ref = refs[-2:]
    step = pl.program_id(0)
    value = mm(left_ref[...], weight_ref[...], TN)
    if len(refs) > 2:
        value = value * refs[0][...]
    value = low(value + wide(add_ref[...]))

    @pl.when(step < pl.num_programs(0) // 2)
    def _():
        send_ref[...] = value

    @pl.when(step >= pl.num_programs(0) // 2)
    def _():
        keep_ref[...] = value


def deliver(order, left, weight, add, gain=None):
    depth, total = left.shape
    width = weight.shape[1]
    steps = N
    tile = total // N
    rows = pl.BlockSpec((tile, width), lambda s, order: (order[ORDER + s], 0))
    in_specs = [
        pl.BlockSpec((depth, tile), lambda s, order: (0, order[ORDER + s])),
        pl.BlockSpec((depth, width), lambda s, order: (0, 0)),
        rows,
    ]
    operands = [left, weight, add]
    if gain is not None:
        in_specs.append(pl.BlockSpec((1, width), lambda s, order: (0, 0)))
        operands.append(gain)
    return pl.pallas_call(
        deliver_kernel,
        grid_spec=pltpu.PrefetchScalarGridSpec(
            num_scalar_prefetch=1,
            grid=(steps,),
            in_specs=in_specs,
            out_specs=[
                pl.BlockSpec((tile, width), lambda s, order: (jnp.minimum(s, steps // 2 - 1), 0)),
                pl.BlockSpec((tile, width), lambda s, order: (jnp.maximum(s - steps // 2, 0), 0)),
            ],
        ),
        out_shape=[jax.ShapeDtypeStruct((total // 2, width), jnp.bfloat16)] * 2,
        compiler_params=pltpu.CompilerParams(vmem_limit_bytes=VMEM),
        cost_estimate=pl.CostEstimate(
            flops=0, bytes_accessed=0, transcendentals=0
        ),
    )(order, *operands)


def joint_kernel(spot_ref, jb_ref, unit_ref, wj_ref, gain_ref, shift_ref, sums_ref, up_ref, hsum_ref, *refs):
    shares, (vector_ref, total_ref, turned_ref, sum_ref) = refs[:4], refs[4:]
    step = pl.program_id(0)
    jb = jb_ref[...]
    height, tile = jb.shape
    width = unit_ref.shape[1]

    @pl.when(step == 0)
    def _():
        total_ref[...] = jnp.zeros_like(total_ref)
        sum_ref[...] = jnp.zeros_like(sum_ref)

    total_ref[...] += mm(jb, unit_ref[...])
    sum_ref[...] += mm(jb, jnp.ones((tile, 128), jnp.bfloat16))

    @pl.when(step == pl.num_programs(0) - 1)
    def _():
        col, quarter = spot_ref[COLUMN], spot_ref[COLUMN + 1]
        gain = jnp.sum(total_ref[...] * wide(wj_ref[...]), axis=0, keepdims=True)
        turned_ref[...] = (total_ref[...] * gain_ref[...] + sum_ref[:, :1] * shift_ref[...]).T
        part = width // 4
        for k, share in enumerate(shares):
            i = k + col - 2 * (col & k)
            share[:part] = low(turned_ref[pl.ds(pl.multiple_of(i * part, part), part), :])
        jb_sum = sum_ref[...].T[:1]
        first = low(jb_sum)
        rest = jb_sum - wide(first)
        middle = low(rest)
        final = low(rest - wide(middle))
        shift = mm(jnp.concatenate([first, middle, final], axis=0), wj_ref[...])
        rows = [
            gain,
            jnp.sum(shift, axis=0, keepdims=True),
            jnp.sum(sums_ref[0], axis=0, keepdims=True),
            jnp.sum(sums_ref[1], axis=0, keepdims=True),
            jnp.sum(up_ref[...], axis=0, keepdims=True),
        ]
        jb_sum = jnp.concatenate([jb_sum, jnp.zeros((1, width - height), jnp.float32)], axis=1)
        for whole in (jnp.sum(hsum_ref[...], axis=0, keepdims=True), jb_sum):
            rows += [jnp.where(quarter == i, whole, 0.0) for i in range(N)]
        rows.append(jnp.zeros((3, width), jnp.float32))
        vector = jnp.concatenate(rows, axis=0)
        vector_ref[...] = vector
        coarse = low(vector)
        rest = jnp.zeros((16, 2 * height - width), jnp.bfloat16)
        pieces = []
        for piece in (coarse,):
            pieces += [piece[:, :height], jnp.concatenate([piece[:, height:], rest], axis=1)]
        for share in shares[1:]:
            for n, piece in enumerate(pieces):
                share[part + 16 * n : part + 16 * (n + 1)] = piece


def joint_gradient(spot, jb, unit, wj, gain, shift, sums, up_sum, hsum):
    height, total = jb.shape
    width = unit.shape[1]
    tile = total // N
    fixed = lambda *dims: pl.BlockSpec(dims, lambda s, spot: (0,) * len(dims))
    shapes = [(width // 4, height)] + [(width // 4 + 32, height)] * 3
    return pl.pallas_call(
        joint_kernel,
        grid_spec=pltpu.PrefetchScalarGridSpec(
            num_scalar_prefetch=1,
            grid=(N,),
            in_specs=[
                pl.BlockSpec((height, tile), lambda s, spot: (0, s)),
                pl.BlockSpec((tile, width), lambda s, spot: (s, 0)),
                fixed(height, width),
                fixed(1, width),
                fixed(1, width),
                fixed(2, 8, width),
                fixed(8, width),
                fixed(*hsum.shape),
            ],
            out_specs=[fixed(*dims) for dims in shapes] + [fixed(16, width)],
            scratch_shapes=[
                pltpu.VMEM((height, width), jnp.float32),
                pltpu.VMEM((width, height), jnp.float32),
                pltpu.VMEM((height, 128), jnp.float32),
            ],
        ),
        out_shape=[jax.ShapeDtypeStruct(dims, jnp.bfloat16) for dims in shapes]
        + [jax.ShapeDtypeStruct((16, width), jnp.float32)],
        compiler_params=pltpu.CompilerParams(vmem_limit_bytes=VMEM),
        cost_estimate=pl.CostEstimate(
            flops=0, bytes_accessed=0, transcendentals=0
        ),
    )(spot, jb, unit, wj, gain, shift, sums, up_sum, hsum)


def pack(vector, width):
    rest = jnp.zeros((vector.shape[0], 2 * width - vector.shape[1]), jnp.float32)
    return low(jnp.concatenate([vector[:, :width], jnp.concatenate([vector[:, width:], rest], axis=1)], axis=0))


def unpack(rows, size):
    rows = wide(rows).reshape(-1, 2, 16, rows.shape[1]).sum(0)
    return jnp.concatenate([rows[0], rows[1][:, : size - rows.shape[2]]], axis=1)


def hop(value, pairs):
    return lax.ppermute(value, ("core", "blk"), [(a[0] * N + a[1], b[0] * N + b[1]) for a, b in pairs])


PLACES = [(c, z) for c in range(2) for z in range(N)]
MAIN = [(z // 2, z) for z in range(N)]
CORE_SWAP = [((c, z), (1 - c, z)) for c, z in PLACES]
NEAR_SWAP = [((c, z), (c, z ^ 1)) for c, z in PLACES]
FAR_SWAP = [((c, z), (c, z ^ 2)) for c, z in PLACES]
FAR_HOME = [((c, z), (1 - c, z ^ 2)) for c, z in PLACES if c != z // 2]


HOME = [((c, z), (c, z ^ 1)) for c, z in MAIN] + FAR_HOME
OFF_MAIN = [(c, z) for c, z in PLACES if c != z // 2]
NEAR_OFF = [((c, z), (c, z ^ 1)) for c, z in OFF_MAIN]
STAY = [(place, place) for place in MAIN]


def tie(*arrays):
    return lax.optimization_barrier(arrays)


def near_sum(keep, got):
    rows = keep.shape[0] // 2
    return low(wide(keep[rows:]) + wide(got[rows:]))


def home_sum(keep, got, near, got_near, main):
    rows = keep.shape[0] // 2
    return jnp.where(main, near, low(wide(keep[:rows]) + wide(got[:rows]) + wide(got_near)))


def own_sum(keep, got, got_home, main):
    rows = keep.shape[0] // 2
    return jnp.where(main, wide(keep[:rows]) + wide(got[:rows]), 0.0) + wide(got_home)


def pick(value, axis, index):
    return lax.dynamic_index_in_dim(value, index, axis, keepdims=False)


def plane(values):
    return [lax.ppermute(value, "col", [(i, i ^ (k + 1)) for i in range(4)]) for k, value in enumerate(values)]


NEAR = [((c, z), (c, z ^ 1)) for c, z in PLACES]


def first_pieces(value, near):
    return pick(value, 1, 1 - near).reshape(-1, value.shape[-1])


def second_pieces(value, got, core, near):
    got = got.reshape((2,) + value.shape[2:])
    return jnp.concatenate([pick(pick(value, 1, near), 0, 1 - core), pick(got, 0, 1 - core)], axis=0)


def quarters(quarter, line, got, last, core, near):
    size = line.shape[2]
    mine = chosen(2 * core + near, [line[0, 0], line[0, 1], line[1, 0], line[1, 1]])
    pieces = [mine, last[:size], jnp.where(core == 0, got[:size], got[size : 2 * size]), last[size : 2 * size]]
    return [chosen(quarter ^ k, pieces) for k in range(N)]


def finish_kernel(spot_ref, line_ref, got_ref, last_ref, reduce_ref, expand_out, dense_out, reduce_out):
    core, near, half = spot_ref[LINE], spot_ref[LINE + 1], spot_ref[LINE + 2]
    pieces = quarters(2 * near + core, wide(line_ref[...]), wide(got_ref[...]), wide(last_ref[...]), core, near)
    rows = expand_out.shape[0]
    for e in range(pieces[0].shape[1] // 128):
        for slot in range(N):
            piece = pieces[slot ^ (2 * (e % 2))]
            to = (N * e + slot) * 128
            expand_out[:, to : to + 128] = piece[:rows, e * 128 : (e + 1) * 128]
    dense_out[...] = chosen(2 * core + half, [piece[rows:] for piece in pieces])
    reduce_out[...] = wide(reduce_ref[...])


def finish(spot, line, got, last, reduced):
    rows, width = line.shape[2] // 2, line.shape[3]
    return pl.pallas_call(
        finish_kernel,
        in_specs=[pl.BlockSpec(memory_space=pltpu.SMEM)] + [pl.BlockSpec(memory_space=pltpu.VMEM)] * 4,
        out_specs=[pl.BlockSpec(memory_space=pltpu.VMEM)] * 3,
        out_shape=[
            jax.ShapeDtypeStruct((rows, N * width), jnp.float32),
            jax.ShapeDtypeStruct((rows, width), jnp.float32),
            jax.ShapeDtypeStruct(reduced.shape, jnp.float32),
        ],
        compiler_params=pltpu.CompilerParams(vmem_limit_bytes=VMEM),
    )(spot, line, got, last, reduced)


def joint_finish_kernel(spot_ref, line_ref, other_ref, near_ref, last_ref, out_ref):
    core, near = spot_ref[LINE], spot_ref[LINE + 1]
    rows = out_ref.shape[0]
    line = wide(line_ref[...])
    mine = chosen(2 * core + near, [line[0, 0], line[0, 1], line[1, 0], line[1, 1]])
    pieces = [mine] + [wide(ref[:rows]) for ref in (other_ref, near_ref, last_ref)]
    pieces = [chosen((2 * near + core) ^ k, pieces) for k in range(N)]
    for n in range(mine.shape[1] // (2 * HEAD)):
        for slot in range(0, N, 2):
            for other in range(2):
                at = (2 * n + other) * HEAD
                to = ((2 * n + other) * N + slot) * HEAD
                pair = [piece[:, at : at + HEAD] for piece in pieces[slot : slot + 2]]
                out_ref[:, to : to + 2 * HEAD] = jnp.concatenate(pair, axis=1)


def joint_finish(spot, line, got):
    rows, width = line.shape[2:]
    return pl.pallas_call(
        joint_finish_kernel,
        in_specs=[pl.BlockSpec(memory_space=pltpu.SMEM)] + [pl.BlockSpec(memory_space=pltpu.VMEM)] * 4,
        out_specs=pl.BlockSpec(memory_space=pltpu.VMEM),
        out_shape=jax.ShapeDtypeStruct((rows, N * width), jnp.float32),
        compiler_params=pltpu.CompilerParams(vmem_limit_bytes=VMEM),
    )(spot, line, *got)


def split_local(
    tokens,
    lengths,
    first_gain,
    first_shift,
    second_gain,
    second_shift,
    joint_weight,
    joint_bias,
    dense_weight,
    dense_bias,
    expand_weight,
    expand_bias,
    reduce_weight,
    reduce_bias,
    cotangent,
):
    col, core, z = lax.axis_index("col"), lax.axis_index("core"), lax.axis_index("blk")
    half, near = z // 2, z % 2
    quarter = 2 * near + core
    main = core == half
    flag = main.astype(jnp.int32)
    rows, width = tokens.shape[1:]
    total = rows * N
    units = expand_weight.shape[1]
    groups = units // (N * 128)
    heads = HEADS // N
    own_x, own_g = tokens[0], cotangent[0]
    row_of = lambda vector: vector.reshape(1, -1)

    x_other = hop(own_x, CORE_SWAP)
    x_first = hop(own_x, HOME)

    wj, wd, we, wr = prepare(quarter, joint_weight, dense_weight, expand_weight, reduce_weight)
    bj = pick(joint_bias.reshape(3, heads, N, HEAD), 2, quarter).reshape(-1, 1)
    be = expand_bias.reshape(groups // 2, 2, N, 128)
    be = jnp.stack([pick(be[:, 0], 1, quarter), pick(be[:, 1], 1, quarter ^ 2)], axis=1).reshape(1, -1)
    first_row, second_row = row_of(first_gain), row_of(second_gain)

    weights = [wj, bj, we, be, wr, first_row, row_of(first_shift), second_row, row_of(second_shift)]

    sizes = jnp.where(main, lengths, hop(lengths, CORE_SWAP))
    number, offset = doc_tables(sizes, jnp.arange(total, dtype=jnp.int32))
    inverse = 10000.0 ** (-2.0 * jnp.arange(ROTARY // 2, dtype=jnp.float32) / ROTARY)
    phase = inverse[:, None] * offset.astype(jnp.float32)
    tables = [jnp.cos(phase), jnp.sin(phase)]
    docs = lengths.shape[1]
    same = number == jnp.arange(HEAD, dtype=jnp.int32)[:, None]
    used = jnp.arange(HEAD)[:, None] < docs
    qx = low(jnp.where(same & used, 1.0, 0.0))
    kx = low(jnp.where(used & ~same, NEG, 0.0))

    spots = [z, z ^ (2 - flag), z ^ (1 + flag), z ^ 3]
    zero = jnp.int32(0)
    order = z ^ (jnp.arange(N, dtype=jnp.int32) ^ (2 * flag))
    sources = [1 - flag, 3 - flag, 4 - 3 * flag, 2 + 2 * flag]
    line_place = [col, quarter, core, near, half]
    spot = jnp.stack([*spots, *sources, *line_place, *[order[k] for k in range(N)], 1 - flag, zero, zero, 2 - flag])
    up_sum = jnp.sum(wide(own_g).reshape(-1, 8, width), axis=0)
    spot, up_sum = tie(spot, up_sum)
    state = run_tokens(0, 1, spot, [own_x, x_other], weights, tables, None)
    x_first, own_g_late, *state = tie(x_first, own_g, *state)
    g_far = hop(own_g_late, FAR_HOME + STAY)
    x_second = hop(x_first, NEAR_OFF + STAY)
    x_first_other = hop(x_first, CORE_SWAP)
    state = run_tokens(1, 1, spot, [x_first], weights, tables, state)
    x_second, *state = tie(x_second, *state)
    x_second_other = hop(x_second, CORE_SWAP)
    state = run_tokens(2, 2, spot, [x_first_other, x_second_other, x_second], weights, tables, state)
    qkv, unit, second, active, slope, feed = state
    qkv = qkv.reshape(3, heads, HEAD, total)
    g_far, qkv = tie(g_far, qkv)
    g_near = hop(g_far, NEAR)
    g_other = hop(g_far, CORE_SWAP)
    mixed, full, inverse_sum, shares = attend_forward(qkv, kx, qx, 0, heads, None)
    g_near, mixed = tie(g_near, mixed)
    mixed = mixed.reshape(-1, total)
    g_near_other = hop(g_near, CORE_SWAP)
    out_send, out_keep = deliver(spot, mixed, wd, feed)

    spot, out_send, out_keep = tie(spot, out_send, out_keep)
    out_got = hop(out_send, CORE_SWAP)
    gs = (own_g, g_other, g_near, g_far, g_near_other)
    mg, back, ups, hg, sums, hsum = run_upstream(spot, gs, [wd, we, wr, second_row], unit, slope)
    out_near = near_sum(out_keep, out_got)
    out_near, hg = tie(out_near, hg)
    out_got_near = hop(out_near, NEAR_OFF)

    kept_share, *shares_out = weight_gradients(spot, second, hg, active, ups, mixed)
    out_home = home_sum(out_keep, out_got, out_near, out_got_near, main)
    out_home, mg, *shares_out = tie(out_home, mg, *shares_out)
    out_got_home = hop(out_home, HOME)
    shares_got = plane(shares_out)

    jb = attend_backward(qkv, mg.reshape(heads, HEAD, total), full, inverse_sum, shares, tables)
    jb = jb.reshape(-1, total)

    kept_joint, *joint_out, vector = joint_gradient(
        spot, jb, unit, wj, first_row, row_of(first_shift), sums, up_sum, hsum
    )
    jb, *joint_out = tie(jb, *joint_out)
    joint_got = plane(joint_out)

    send, keep = deliver(spot, jb, wj, back, first_row)

    send, out_got_home, *shares_got = tie(send, out_got_home, *shares_got)
    share = wide(kept_share) + sum(wide(piece) for piece in shares_got)
    kept = near ^ half
    part = width // 4
    expand_part = share[:part].reshape(2, 2, 2, part // 8, units // N)
    reduce_part = share[part : part + units // (4 * N)].reshape(2, -1, width)
    dense_part = share[part + units // (4 * N) :]
    far_send = [pick(expand_part, 1, 1 - half).reshape(part // 2, -1), pick(reduce_part, 0, 1 - kept), dense_part]
    far_send = low(jnp.concatenate(far_send, axis=0))
    far_send, send = tie(far_send, send)
    got = hop(send, CORE_SWAP)
    far_got = hop(far_send, FAR_SWAP)
    near_part = near_sum(keep, got)
    out = own_sum(out_keep, out_got, out_got_home, main)
    inputs = wide(own_x)
    result = low(inputs + out + (dense_bias + reduce_bias))
    got_near = hop(near_part, NEAR_OFF)

    got_near, *joint_got = tie(got_near, *joint_got)
    joint_part = wide(kept_joint) + sum(wide(piece[:part]) for piece in joint_got)
    vector = vector + sum(unpack(piece[part:], width) for piece in joint_got)
    joint_width = joint_part.shape[1]
    joint_part = joint_part.reshape(2, 2, 2, part // 8, joint_width)
    joint_far_send = jnp.concatenate(
        [low(pick(joint_part, 1, 1 - half)).reshape(part // 2, joint_width), pack(vector, joint_width)], axis=0
    )
    home = home_sum(keep, got, near_part, got_near, main)
    home, joint_far_send, result = tie(home, joint_far_send, result)
    got_home = hop(home, HOME)
    joint_far = hop(joint_far_send, FAR_SWAP)
    home, far_got = tie(home, far_got)
    far_got = wide(far_got)
    expand_part = low(pick(expand_part, 1, half).reshape(part // 2, -1) + far_got[: part // 2])
    reduce_part = low(pick(reduce_part, 0, kept) + far_got[part // 2 : part // 2 + 128])
    dense_part = low(dense_part + far_got[part // 2 + 128 :]).reshape(2, HEAD // 2, width)
    line = jnp.concatenate(
        [
            expand_part.reshape(2, 2, part // 8, -1),
            jnp.broadcast_to(dense_part[None], (2,) + dense_part.shape),
        ],
        axis=2,
    )
    line_send = first_pieces(line, near)
    line_got = hop(line_send, NEAR)
    reduce_got = hop(reduce_part, [((c, s), ((s % 2) ^ (s // 2), 2 * (s // 2) + c)) for c, s in PLACES])
    scaled = own_sum(keep, got, got_home, main)
    _, unit_rows, inverse_root = normalize(inputs, first_gain, first_shift)
    input_back = inverse_root * (
        scaled
        - jnp.mean(scaled, axis=-1, keepdims=True)
        - unit_rows * jnp.mean(scaled * unit_rows, axis=-1, keepdims=True)
    )
    tokens_gradient = low(wide(own_g) + input_back)
    line_got, tokens_gradient = tie(line_got, tokens_gradient)
    line_send = second_pieces(line, line_got, core, near)
    line_last = hop(line_send, CORE_SWAP)
    joint_far, line_send = tie(joint_far, line_send)
    joint_part = low(pick(joint_part, 1, half).reshape(part // 2, joint_width) + wide(joint_far[: part // 2]))
    vector = vector + unpack(joint_far[part // 2 :], width)
    joint_line = joint_part.reshape(2, 2, part // 8, joint_width)
    vector_rows = pack(vector, joint_width)
    joint_got = []
    for dz, dc in ((0, 1), (1, 0), (1, 1)):
        piece = pick(pick(joint_line, 1, near ^ dz), 0, core ^ dc)
        piece = jnp.concatenate([piece, vector_rows], axis=0)
        joint_got.append(hop(piece, [((c, p), (c ^ dc, p ^ dz)) for c, p in PLACES]))
    expand_mine, dense_mine, reduce_mine = finish(spot, line, line_got, line_last, reduce_got)
    expand_mine, *joint_got = tie(expand_mine, *joint_got)
    vector = vector + sum(unpack(piece[part // 8 :], width) for piece in joint_got)
    joint_mine = joint_finish(spot, joint_line, joint_got)

    device = (2 * col + core) * N + z
    share = width // (8 * N)
    head_row = lambda head: 5 + N + head % N
    cut = lambda row, start, size: lax.dynamic_slice(vector, (row, start), (1, size))[0]
    pieces = [cut(row, device * share, share) for row in range(5)]
    pieces[4:] = [
        cut(head_row(device % HEADS), (device // HEADS * heads + device % HEADS // N) * HEAD, HEAD),
        cut(head_row(device // 2), (2 * heads + device // 2 // N) * HEAD + device % 2 * share, share),
        pieces[4],
        cut(5 + (z ^ (2 * core)), (2 * col + core) * 128, 128),
    ]

    return (
        result[None],
        tokens_gradient[None],
        *pieces[:4],
        joint_mine,
        pieces[4],
        pieces[5],
        dense_mine,
        pieces[6],
        expand_mine,
        pieces[7],
        reduce_mine,
        pieces[6],
    )


def solution(mesh):
    count, blocks = mesh.devices.shape
    split = blocks == N and count == 8
    if split:
        mesh = jax.sharding.Mesh(mesh.devices.reshape(count // 2, 2, blocks), ("col", "core", "blk"))
        batch = ("col", "core")
        every = ("col", "core", "blk")
    else:
        batch, every = "batch", ("batch", "blk")
    by_rows = P(batch, "blk", None)
    placed = (by_rows, P(batch, None)) + (P(),) * 12 + (by_rows,)
    vector, matrix = P(every), P(every, None)
    return jax.shard_map(
        split_local if split else local,
        mesh=mesh,
        in_specs=placed,
        out_specs=(
            by_rows,
            by_rows,
            vector,
            vector,
            vector,
            vector,
            matrix,
            vector,
            vector,
            matrix,
            vector,
            matrix,
            vector,
            matrix,
            vector,
        ),
        check_vma=False,
    )
```

```python
from functools import partial

import jax
import jax.numpy as jnp
from jax import lax
from jax.experimental import pallas as pl
from jax.experimental.pallas import tpu as pltpu
from jax.sharding import PartitionSpec as P

HEADS = 16
HEAD = 64
ROTARY = 16


EPSILON = 1e-05
MASKED = -1e30


def doc_tables(lengths, positions):
    doc_ends = jnp.cumsum(lengths, axis=-1)
    doc_starts = doc_ends - lengths
    doc_number = jnp.sum(
        (positions[None, :, None] >= doc_ends[:, None, :]).astype(jnp.int32), axis=-1
    )
    matches = (
        doc_number[:, :, None] == jnp.arange(lengths.shape[-1], dtype=jnp.int32)[None, None, :]
    )
    begins = jnp.sum(jnp.where(matches, doc_starts[:, None, :], 0), axis=-1)
    return (doc_number, positions[None, :] - begins)


def angles(offsets):
    half_width = ROTARY // 2
    inverse = 10000.0 ** (-2.0 * jnp.arange(half_width, dtype=jnp.float32) / ROTARY)
    phase = offsets.astype(jnp.float32)[..., None] * inverse
    return (jnp.cos(phase), jnp.sin(phase))


def rotate(values, cosine, sine_table, direction):
    half_width = cosine.shape[-1]
    lead_part = values[..., :half_width]
    tail_part = values[..., half_width : 2 * half_width]
    cosine = cosine[:, :, None, :]
    sine_table = sine_table[:, :, None, :] * direction
    return jnp.concatenate(
        [
            lead_part * cosine - tail_part * sine_table,
            tail_part * cosine + lead_part * sine_table,
            values[..., 2 * half_width :],
        ],
        axis=-1,
    )


def normalize(values, gain_row, shift_row):
    center = values - jnp.mean(values, axis=-1, keepdims=True)
    spread = jnp.mean(center * center, axis=-1, keepdims=True)
    inverse_root = lax.rsqrt(spread + EPSILON)
    unit_rows = center * inverse_root
    return (unit_rows * gain_row + shift_row, unit_rows, inverse_root)


def normalize_back(upstream, unit_rows, inverse_root, gain_row):
    scaled_back = upstream * gain_row
    input_back = inverse_root * (
        scaled_back
        - jnp.mean(scaled_back, axis=-1, keepdims=True)
        - unit_rows * jnp.mean(scaled_back * unit_rows, axis=-1, keepdims=True)
    )
    return (input_back, jnp.sum(upstream * unit_rows, axis=0), jnp.sum(upstream, axis=0))


def outer(left_rows, right_rows):
    return lax.dot_general(
        left_rows, right_rows, (((0,), (0,)), ((), ())), preferred_element_type=jnp.float32
    )


def against(left_rows, weight_rows):
    return lax.dot_general(
        left_rows, weight_rows, (((1,), (1,)), ((), ())), preferred_element_type=jnp.float32
    )


def over_piece(stepper, running, segment, stride):
    sub_count = segment.shape[1] // stride

    def one_turn(position, current):
        part_rows = lax.dynamic_slice_in_dim(segment, position * stride, stride, 1)
        return stepper(current, part_rows, position * stride)

    return lax.fori_loop(0, sub_count, one_turn, running)


def local(
    tokens,
    lengths,
    first_gain,
    first_shift,
    second_gain,
    second_shift,
    joint_weight,
    joint_bias,
    dense_weight,
    dense_bias,
    expand_weight,
    expand_bias,
    reduce_weight,
    reduce_bias,
    cotangent,
):
    sequences, stride, model_width = tokens.shape
    cycle_size = lax.axis_size("blk")
    seq_total = stride * cycle_size
    rank_here = lax.axis_index("blk")
    row_count = sequences * stride
    factor = HEAD ** (-0.5)
    head_shape = (sequences, stride, HEADS, HEAD)
    places = jnp.arange(seq_total, dtype=jnp.int32)
    number_all, offset_all = doc_tables(lengths, places)
    first_place = rank_here * stride
    query_number = lax.dynamic_slice_in_dim(number_all, first_place, stride, 1)
    query_offset = lax.dynamic_slice_in_dim(offset_all, first_place, stride, 1)
    query_place = first_place + jnp.arange(stride, dtype=jnp.int32)
    last_place = first_place + stride - 1
    cosine, sine_table = angles(query_offset)
    inputs = tokens.reshape(row_count, model_width).astype(jnp.float32)
    first_norm, first_unit, first_scale = normalize(inputs, first_gain, first_shift)
    normed = first_norm.astype(jnp.bfloat16)
    joint_out = jnp.dot(normed, joint_weight, preferred_element_type=jnp.float32) + joint_bias
    queries = rotate(
        joint_out[:, :model_width].reshape(head_shape), cosine, sine_table, 1.0
    ).astype(jnp.bfloat16)
    key_rows = rotate(
        joint_out[:, model_width : 2 * model_width].reshape(head_shape), cosine, sine_table, 1.0
    ).astype(jnp.bfloat16)
    value_rows = joint_out[:, 2 * model_width :].astype(jnp.bfloat16)
    pair_local = jnp.concatenate(
        [
            key_rows.reshape(sequences, stride, model_width),
            value_rows.reshape(sequences, stride, model_width),
        ],
        axis=-1,
    )

    def masked_scores(key_part, begin_row, row_span):
        key_number = lax.dynamic_slice_in_dim(number_all, begin_row, row_span, 1)
        key_place = begin_row + jnp.arange(row_span, dtype=jnp.int32)
        allowed = (query_number[:, :, None] == key_number[:, None, :]) & (
            key_place[None, None, :] <= query_place[None, :, None]
        )
        allowed = allowed[:, None]
        scores = (
            jnp.einsum("sqhd,skhd->shqk", queries, key_part, preferred_element_type=jnp.float32)
            * factor
        )
        return (jnp.where(allowed, scores, MASKED), allowed)

    def split_piece(segment):
        row_span = segment.shape[1]
        key_part = segment[:, :, :model_width].reshape(sequences, row_span, HEADS, HEAD)
        value_part = segment[:, :, model_width:].reshape(sequences, row_span, HEADS, HEAD)
        return (key_part, value_part, row_span)

    def gated(kernel):

        def stepper(running, segment, begin_row):
            return lax.cond(
                begin_row <= last_place,
                lambda current: kernel(current, segment, begin_row),
                lambda current: current,
                running,
            )

        return stepper

    def forward_kernel(running, segment, begin_row):
        row_peak, row_total, weighted = running
        key_part, value_part, row_span = split_piece(segment)
        scores, allowed = masked_scores(key_part, begin_row, row_span)
        new_peak = jnp.maximum(row_peak, jnp.max(scores, axis=-1))
        shares = jnp.where(allowed, jnp.exp(scores - new_peak[..., None]), 0.0)
        decay_factor = jnp.exp(row_peak - new_peak)
        row_total = row_total * decay_factor + jnp.sum(shares, axis=-1)
        update = jnp.einsum(
            "shqk,skhd->sqhd",
            shares.astype(jnp.bfloat16),
            value_part,
            preferred_element_type=jnp.float32,
        )
        weighted = weighted * jnp.transpose(decay_factor, (0, 2, 1))[..., None] + update
        return (new_peak, row_total, weighted)

    forward_step = gated(forward_kernel)
    initial = (
        jnp.full((sequences, HEADS, stride), MASKED, jnp.float32),
        jnp.zeros((sequences, HEADS, stride), jnp.float32),
        jnp.zeros(head_shape, jnp.float32),
    )
    forward_state = over_piece(
        forward_step, initial, lax.all_gather(pair_local, "blk", axis=1, tiled=True), stride
    )
    row_peak, row_total, weighted = forward_state
    mixed_full = weighted / jnp.transpose(row_total, (0, 2, 1))[..., None]
    log_total = row_peak + jnp.log(row_total)
    mixed = mixed_full.reshape(row_count, model_width).astype(jnp.bfloat16)
    attention_out = jnp.dot(mixed, dense_weight, preferred_element_type=jnp.float32) + dense_bias
    second_norm, second_unit, second_scale = normalize(inputs, second_gain, second_shift)
    second = second_norm.astype(jnp.bfloat16)
    hidden = jnp.dot(second, expand_weight, preferred_element_type=jnp.float32) + expand_bias
    active_full, gelu_pull = jax.vjp(partial(jax.nn.gelu, approximate=False), hidden)
    active = active_full.astype(jnp.bfloat16)
    feed_out = jnp.dot(active, reduce_weight, preferred_element_type=jnp.float32) + reduce_bias
    result = (
        (inputs + attention_out + feed_out)
        .astype(jnp.bfloat16)
        .reshape(sequences, stride, model_width)
    )
    upstream = cotangent.reshape(row_count, model_width)
    dense_grad = outer(mixed, upstream)
    bias_total = jnp.sum(upstream, axis=0, dtype=jnp.float32)
    reduce_grad = outer(active, upstream)
    hidden_grad = gelu_pull(against(upstream, reduce_weight))[0].astype(jnp.bfloat16)
    expand_grad = outer(second, hidden_grad)
    hidden_total = jnp.sum(hidden_grad, axis=0, dtype=jnp.float32)
    input_two, gain_second, shift_second = normalize_back(
        against(hidden_grad, expand_weight), second_unit, second_scale, second_gain
    )
    mixed_grad = against(upstream, dense_weight).astype(jnp.bfloat16)
    out_heads = mixed_grad.reshape(head_shape)
    delta_rows = jnp.transpose(jnp.sum(out_heads * mixed_full, axis=-1), (0, 2, 1))

    def backward_kernel(running, segment, begin_row):
        key_part, value_part, row_span = split_piece(segment)
        scores, allowed = masked_scores(key_part, begin_row, row_span)
        weights_now = jnp.where(allowed, jnp.exp(scores - log_total[..., None]), 0.0)
        weight_grad = jnp.einsum(
            "sqhd,skhd->shqk", out_heads, value_part, preferred_element_type=jnp.float32
        )
        score_grad = (weights_now * (weight_grad - delta_rows[..., None])).astype(jnp.bfloat16)
        query_grad = (
            running[0]
            + jnp.einsum(
                "shqk,skhd->sqhd", score_grad, key_part, preferred_element_type=jnp.float32
            )
            * factor
        )
        value_grad = jnp.einsum(
            "shqk,sqhd->skhd",
            weights_now.astype(jnp.bfloat16),
            out_heads,
            preferred_element_type=jnp.float32,
        )
        key_grad = (
            jnp.einsum("shqk,sqhd->skhd", score_grad, queries, preferred_element_type=jnp.float32)
            * factor
        )
        fresh_rows = jnp.concatenate(
            [
                key_grad.reshape(sequences, row_span, model_width),
                value_grad.reshape(sequences, row_span, model_width),
            ],
            axis=-1,
        )
        pair_grad = lax.dynamic_update_slice_in_dim(running[1], fresh_rows, begin_row, 1)
        return (query_grad, pair_grad)

    backward_step = gated(backward_kernel)
    back_initial = (
        jnp.zeros(head_shape, jnp.float32),
        jnp.zeros((sequences, seq_total, 2 * model_width), jnp.float32),
    )
    back_state = over_piece(
        backward_step, back_initial, lax.all_gather(pair_local, "blk", axis=1, tiled=True), stride
    )
    query_grad = back_state[0]
    pair_mine = lax.psum_scatter(back_state[1], "blk", scatter_dimension=1, tiled=True)
    query_back = rotate(query_grad, cosine, sine_table, -1.0).reshape(row_count, model_width)
    key_back = rotate(
        pair_mine[:, :, :model_width].reshape(head_shape), cosine, sine_table, -1.0
    ).reshape(row_count, model_width)
    value_back = pair_mine[:, :, model_width:].reshape(row_count, model_width)
    joint_back = jnp.concatenate([query_back, key_back, value_back], axis=-1).astype(jnp.bfloat16)
    joint_grad = outer(normed, joint_back)
    joint_total = jnp.sum(joint_back, axis=0, dtype=jnp.float32)
    front_total = joint_total[: 2 * model_width]
    value_total = joint_total[2 * model_width :]
    input_one, gain_first, shift_first = normalize_back(
        against(joint_back, joint_weight), first_unit, first_scale, first_gain
    )
    input_total = (
        (upstream.astype(jnp.float32) + input_one + input_two)
        .astype(jnp.bfloat16)
        .reshape(sequences, stride, model_width)
    )
    summed = (
        lax.psum_scatter(gain_first, ("batch", "blk"), scatter_dimension=0, tiled=True),
        lax.psum_scatter(shift_first, ("batch", "blk"), scatter_dimension=0, tiled=True),
        lax.psum_scatter(gain_second, ("batch", "blk"), scatter_dimension=0, tiled=True),
        lax.psum_scatter(shift_second, ("batch", "blk"), scatter_dimension=0, tiled=True),
        lax.psum_scatter(joint_grad, ("batch", "blk"), scatter_dimension=0, tiled=True),
        lax.psum_scatter(front_total, ("batch", "blk"), scatter_dimension=0, tiled=True),
        lax.psum_scatter(value_total, ("batch", "blk"), scatter_dimension=0, tiled=True),
        lax.psum_scatter(dense_grad, ("batch", "blk"), scatter_dimension=0, tiled=True),
        lax.psum_scatter(bias_total, ("batch", "blk"), scatter_dimension=0, tiled=True),
        lax.psum_scatter(expand_grad, ("batch", "blk"), scatter_dimension=0, tiled=True),
        lax.psum_scatter(hidden_total, ("batch", "blk"), scatter_dimension=0, tiled=True),
        lax.psum_scatter(reduce_grad, ("batch", "blk"), scatter_dimension=0, tiled=True),
    )
    return (
        result,
        input_total,
        summed[0],
        summed[1],
        summed[2],
        summed[3],
        summed[4],
        summed[5],
        summed[6],
        summed[7],
        summed[8],
        summed[9],
        summed[10],
        summed[11],
        summed[8],
    )


BQ = 512
N = 4
TM = 256
VMEM = 56 * 1024 * 1024
NEG = -1e30
NN = (((1,), (0,)), ((), ()))
NT = (((1,), (1,)), ((), ()))
TN = (((0,), (0,)), ((), ()))


def mm(left, right, form=NN):
    return lax.dot_general(left, right, form, preferred_element_type=jnp.float32)


def low(value):
    return value.astype(jnp.bfloat16)


def wide(value):
    return value.astype(jnp.float32)


def gelu_parts(hidden):
    size = jnp.abs(hidden) * (0.5**0.5)
    bell = jnp.exp(-(size * size))
    base = 1.0 + 0.3275911 * size
    guess = pl.reciprocal(base, approx=True)
    t = guess * (2.0 - base * guess)
    series = t * (
        0.5 * 0.254829592
        + t
        * (
            0.5 * -0.284496736
            + t * (0.5 * 1.421413741 + t * (0.5 * -1.453152027 + t * (0.5 * 1.061405429)))
        )
    )
    tail = series * bell
    return (jnp.where(hidden >= 0.0, 1.0 - tail, tail), bell)


def fold_rows(value):
    rows, columns = value.shape
    return jnp.sum(value.reshape(rows // 8, 8, columns), axis=0)


def prepare_kernel(spot_ref, *refs):
    wj_refs, (wd_ref, *refs) = refs[:3], refs[3:]
    we_refs, wr_refs, (wj_out, wd_out, we_out, wr_out) = refs[:2], refs[2:4], refs[4:]
    even = lax.rem(spot_ref[0], 2) == 0
    for kind, wj_ref in enumerate(wj_refs):
        turned = wj_ref[...].T
        wj_out[kind] = jnp.where(even, turned[:HEAD], turned[HEAD:])
    wd_out[...] = wd_ref[...]
    for n in range(2):
        we_out[:, n * 128 : (n + 1) * 128] = we_refs[n][...]
        wr_out[n * 128 : (n + 1) * 128, :] = wr_refs[n][...]


def prepare(quarter, joint_weight, dense_weight, expand_weight, reduce_weight):
    width, units = expand_weight.shape
    heads = HEADS // N
    groups = units // (N * 128)
    group = lambda n, s, spot: N * (2 * s + n) + lax.rem(spot[0] + 2 * n, N)
    pairs = [
        pl.BlockSpec((width, 2 * HEAD), lambda s, spot, k=k: (0, k * (HEADS // 2) + s * (N // 2) + spot[0] // 2))
        for k in range(3)
    ]
    columns = [pl.BlockSpec((width, 128), lambda s, spot, n=n: (0, group(n, s, spot))) for n in range(2)]
    rows = [pl.BlockSpec((128, width), lambda s, spot, n=n: (group(n, s, spot), 0)) for n in range(2)]
    shape = lambda *dims: jax.ShapeDtypeStruct(dims, jnp.bfloat16)
    wj, wd, we, wr = pl.pallas_call(
        prepare_kernel,
        grid_spec=pltpu.PrefetchScalarGridSpec(
            num_scalar_prefetch=1,
            grid=(heads,),
            in_specs=[*pairs, pl.BlockSpec((HEAD, width), lambda s, spot: (N * s + spot[0], 0)), *columns, *rows],
            out_specs=[
                pl.BlockSpec((3, HEAD, width), lambda s, spot: (0, s, 0)),
                pl.BlockSpec((HEAD, width), lambda s, spot: (s, 0)),
                pl.BlockSpec((width, 256), lambda s, spot: (0, s)),
                pl.BlockSpec((256, width), lambda s, spot: (s, 0)),
            ],
        ),
        out_shape=[
            shape(3, heads * HEAD, width),
            shape(heads * HEAD, width),
            shape(width, groups * 128),
            shape(groups * 128, width),
        ],
        compiler_params=pltpu.CompilerParams(vmem_limit_bytes=VMEM),
        cost_estimate=pl.CostEstimate(flops=0, bytes_accessed=14 * width * width, transcendentals=0),
    )(quarter.reshape(1), *[joint_weight] * 3, dense_weight, *[expand_weight] * 2, *[reduce_weight] * 2)
    return wj.reshape(-1, width), wd, we, wr


def parts(diagonal):
    whole, half = slice(0, BQ), slice(BQ // 2, BQ)
    return [(slice(0, BQ // 2), whole), (half, half)] if diagonal else [(whole, whole)]


def beside(value, last, columns):
    return jnp.concatenate([value[:, : columns.start], last], axis=1) if columns.start else last


COLUMN, LINE, ORDER, CHOICES = 8, 10, 13, 17


def block_at(place, j):
    return place * (place + 1) // 2 + j


def forward_kernel(held, qkv_ref, kx_ref, qx_ref, *refs):
    mixed_ref, full_ref, inverse_ref, share_ref, key_ref, *scores = refs[held:]
    key_ref[...] = jnp.concatenate([qkv_ref[1, 0], kx_ref[...]], axis=0).T
    total = kx_ref.shape[1]
    state = {}

    def score(place, j):
        here = slice(place * BQ, (place + 1) * BQ)
        if j == 0:
            query_x = jnp.concatenate([qkv_ref[0, 0, :, here], qx_ref[:, here]], axis=0)
            state[place] = [query_x, jnp.full((8, BQ), NEG * 2, jnp.float32)]
        peak8 = state[place][1]
        for rows, columns in parts(j == place):
            found = mm(key_ref[j * BQ + rows.start : j * BQ + rows.stop, :], state[place][0][:, columns])
            if j == place:
                key_row = rows.start + lax.broadcasted_iota(jnp.int32, found.shape, 0)
                query_column = columns.start + lax.broadcasted_iota(jnp.int32, found.shape, 1)
                found = jnp.where(key_row <= query_column, found, NEG)
            scores[place % 2][j * BQ + rows.start : j * BQ + rows.stop, columns] = found
            peak = jnp.max(found.reshape(-1, 8, found.shape[1]), axis=0)
            peak8 = beside(peak8, jnp.maximum(peak8[:, columns], peak), columns)
        state[place][1] = peak8

    def weigh(place, j):
        here = slice(place * BQ, (place + 1) * BQ)
        if j == 0:
            peak = jnp.max(state[place][1], axis=0, keepdims=True)
            state[place] = [peak, jnp.zeros((8, BQ), jnp.float32), jnp.zeros((HEAD, BQ), jnp.float32)]
        peak, sum8, mixed = state[place]
        for rows, columns in parts(j == place):
            at = slice(j * BQ + rows.start, j * BQ + rows.stop)
            share = jnp.exp(scores[place % 2][at, columns] - peak[:, columns])
            total = sum8[:, columns] + jnp.sum(share.reshape(-1, 8, share.shape[1]), axis=0)
            share = low(share)
            share_ref[0, block_at(place, j), rows, columns] = share
            product = mixed[:, columns] + mm(qkv_ref[2, 0, :, at], share)
            sum8 = beside(sum8, total, columns)
            mixed = beside(mixed, product, columns)
        state[place] = [peak, sum8, mixed]
        if j == place:
            inverse = 1.0 / jnp.sum(state[place][1], axis=0, keepdims=True)
            mixed = state[place][2] * inverse
            inverse_ref[0, :, here] = inverse
            full_ref[0, :, here] = mixed
            mixed_ref[0, :, here] = low(mixed)

    places = list(range(total // BQ))
    for j in range(places[0] + 1):
        score(places[0], j)
    for n, place in enumerate(places):
        for j in range(places[-1] + 2):
            if n + 1 < len(places) and j <= places[n + 1]:
                score(places[n + 1], j)
            if j <= place:
                weigh(place, j)


def attend_forward(qkv, kx, qx, first, count, before):
    _, heads, _, total = qkv.shape
    places = total // BQ
    blocks = block_at(places, 0)
    head_rows = lambda rows: pl.BlockSpec((1, rows, total), lambda h: (first + h, 0, 0))
    operands = [qkv, kx, qx]
    in_specs = [
        pl.BlockSpec((3, 1, HEAD, total), lambda h: (0, first + h, 0, 0)),
        pl.BlockSpec((HEAD, total), lambda h: (0, 0)),
        pl.BlockSpec((HEAD, total), lambda h: (0, 0)),
    ]
    aliases = {}
    if before is not None:
        for index, array in enumerate(before):
            aliases[len(operands)] = index
            operands.append(array)
            in_specs.append(pl.BlockSpec(memory_space=pl.ANY))
    return pl.pallas_call(
        partial(forward_kernel, len(aliases)),
        grid=(count,),
        in_specs=in_specs,
        out_specs=[
            head_rows(HEAD),
            head_rows(HEAD),
            head_rows(1),
            pl.BlockSpec((1, blocks, BQ, BQ), lambda h: (first + h, 0, 0, 0)),
        ],
        out_shape=[
            jax.ShapeDtypeStruct((heads, HEAD, total), jnp.bfloat16),
            jax.ShapeDtypeStruct((heads, HEAD, total), jnp.float32),
            jax.ShapeDtypeStruct((heads, 1, total), jnp.float32),
            jax.ShapeDtypeStruct((heads, blocks, BQ, BQ), jnp.bfloat16),
        ],
        scratch_shapes=[pltpu.VMEM((total, 2 * HEAD), jnp.bfloat16)] + [pltpu.VMEM((total, BQ), jnp.float32)] * 2,
        input_output_aliases=aliases,
        compiler_params=pltpu.CompilerParams(vmem_limit_bytes=VMEM),
        cost_estimate=pl.CostEstimate(
            flops=16 * HEAD * count * blocks * BQ * BQ,
            bytes_accessed=2 * count * blocks * BQ * BQ,
            transcendentals=count * blocks * BQ * BQ,
        ),
    )(*operands)


def backward_kernel(qkv_ref, mg_ref, full_ref, inverse_ref, share_ref, cos_ref, sin_ref, jb_ref, value_ref, acc_ref):
    total = cos_ref.shape[1]
    ones = (lax.broadcasted_iota(jnp.int32, (HEAD, total), 0) < 3).astype(jnp.bfloat16)
    value_ref[...] = jnp.concatenate([qkv_ref[2, 0], ones], axis=0).T
    half = ROTARY // 2
    blank = jnp.zeros((HEAD, BQ), jnp.bfloat16)
    row = lax.broadcasted_iota(jnp.int32, (HEAD, BQ), 0)

    def turn_back(rows, at):
        lead, tail = rows[:half], rows[half : 2 * half]
        cosine, sine = cos_ref[:, at], sin_ref[:, at]
        return low(
            jnp.concatenate([lead * cosine + tail * sine, tail * cosine - lead * sine, rows[2 * half :]], axis=0)
        )

    for place in reversed(range(total // BQ)):
        here = slice(place * BQ, (place + 1) * BQ)
        query_t = qkv_ref[0, 0, :, here]
        mg = low(wide(mg_ref[0, :, here]) * inverse_ref[0, :, here])
        delta = -jnp.sum(wide(mg) * full_ref[0, :, here], axis=0, keepdims=True)
        first = low(delta)
        rest = delta - wide(first)
        middle = low(rest)
        final = low(rest - wide(middle))
        extra = jnp.where(
            row == 0, wide(first), jnp.where(row == 1, wide(middle), jnp.where(row == 2, wide(final), 0.0))
        )
        mg_x = jnp.concatenate([mg, low(extra)], axis=0)
        mg_v = jnp.concatenate([blank, mg], axis=0)
        query_k = jnp.concatenate([query_t, blank], axis=0)
        query_grad = jnp.zeros((HEAD, BQ), jnp.float32)
        for j in range(place + 1):
            for rows, columns in parts(j == place):
                at = slice(j * BQ + rows.start, j * BQ + rows.stop)
                share = share_ref[0, block_at(place, j), rows, columns]
                score_grad = low(wide(share) * mm(value_ref[at, :], mg_x[:, columns]))
                pair = mm(share, mg_v[:, columns], NT) + mm(score_grad, query_k[:, columns], NT)
                product = query_grad[:, columns] + mm(qkv_ref[1, 0, :, at], score_grad)
                query_grad = beside(query_grad, product, columns)
                if (place + 1) * BQ < total:
                    pair = pair + acc_ref[at, :]
                if j < place:
                    acc_ref[at, :] = pair
                else:
                    pair_t = pair.T
                    jb_ref[1, 0, :, at] = turn_back(pair_t[:HEAD], at)
                    jb_ref[2, 0, :, at] = low(pair_t[HEAD:])
        jb_ref[0, 0, :, here] = turn_back(query_grad * (HEAD**-0.5), here)


def attend_backward(qkv, mg, full, inverse, shares, tables):
    _, heads, _, total = qkv.shape
    blocks = shares.shape[1]
    head_rows = lambda rows: pl.BlockSpec((1, rows, total), lambda h: (h, 0, 0))
    kinds = pl.BlockSpec((3, 1, HEAD, total), lambda h: (0, h, 0, 0))
    table = pl.BlockSpec((ROTARY // 2, total), lambda h: (0, 0))
    return pl.pallas_call(
        backward_kernel,
        grid=(heads,),
        in_specs=[
            kinds,
            head_rows(HEAD),
            head_rows(HEAD),
            head_rows(1),
            pl.BlockSpec((1, blocks, BQ, BQ), lambda h: (h, 0, 0, 0)),
            table,
            table,
        ],
        out_specs=kinds,
        out_shape=jax.ShapeDtypeStruct((3, heads, HEAD, total), jnp.bfloat16),
        scratch_shapes=[
            pltpu.VMEM((total, 2 * HEAD), jnp.bfloat16),
            pltpu.VMEM((total, 2 * HEAD), jnp.float32),
        ],
        compiler_params=pltpu.CompilerParams(vmem_limit_bytes=VMEM),
        cost_estimate=pl.CostEstimate(
            flops=32 * HEAD * heads * blocks * BQ * BQ,
            bytes_accessed=2 * heads * blocks * BQ * BQ,
            transcendentals=0,
        ),
    )(qkv, mg, full, inverse, shares, *tables)


def chosen(index, options):
    value = options[-1]
    for k in reversed(range(len(options) - 1)):
        value = jnp.where(index == k, options[k], value)
    return value


def token_kernel(slot, count, sub, chunk, spot_ref, *refs):
    sources = refs[:count]
    (wj_ref, bj_ref, we_ref, be_ref, wr_ref, g1_ref, s1_ref, g2_ref, s2_ref, cos_ref, sin_ref) = refs[count : count + 11]
    qkv_ref, unit_ref, second_ref, active_ref, slope_ref, feed_ref = refs[-6:]
    choice = spot_ref[CHOICES + slot + pl.program_id(0)]
    rows = sources[0].shape[0]
    half = ROTARY // 2
    part = wj_ref.shape[0] // 3
    for top in range(0, rows, sub):
        at = slice(top, top + sub)
        x = wide(chosen(choice, [source[at, :] for source in sources]))
        center = x - jnp.mean(x, axis=-1, keepdims=True)
        scale = lax.rsqrt(jnp.mean(center * center, axis=-1, keepdims=True) + EPSILON)
        unit = center * scale
        unit_ref[at, :] = low(unit)
        normed = low(unit * g1_ref[...] + s1_ref[...])
        second = low(unit * g2_ref[...] + s2_ref[...])
        second_ref[at, :] = second
        joint = mm(wj_ref[...], normed, NT) + bj_ref[...]
        cosine, sine = cos_ref[:, at], sin_ref[:, at]
        for kind in range(3):
            for head in range(part // HEAD):
                first = kind * part + head * HEAD
                turned = joint[first : first + HEAD]
                if kind < 2:
                    lead, tail = turned[:half], turned[half : 2 * half]
                    turned = jnp.concatenate(
                        [lead * cosine - tail * sine, tail * cosine + lead * sine, turned[2 * half :]], axis=0
                    )
                if kind == 0:
                    turned = turned * (HEAD**-0.5)
                qkv_ref[first : first + HEAD, at] = low(turned)
        for left in range(0, we_ref.shape[1], chunk):
            over = slice(left, left + chunk)
            hidden = mm(second, we_ref[:, over]) + be_ref[:, over]
            share, bell = gelu_parts(hidden)
            active_ref[at, over] = low(hidden * share)
            slope_ref[at, over] = low(share + hidden * bell * 0.3989422804014327)
    for top in range(0, rows, sub):
        at = slice(top, top + sub)
        feed_ref[at, :] = low(mm(active_ref[at, :], wr_ref[...]))


def run_tokens(slot, steps, spot, data, weights, tables, before, sub=256, chunk=256):
    rows, width = data[0].shape
    total = tables[0].shape[1]
    wj, bj, we, be, wr, g1, s1, g2, s2 = weights
    units = we.shape[1]

    def whole(array):
        return pl.BlockSpec(array.shape, lambda i, spot: (0,) * array.ndim)

    column = lambda height: pl.BlockSpec((height, rows), lambda i, spot: (0, spot[slot + i]))
    placed = pl.BlockSpec((rows, width), lambda i, spot: (spot[slot + i], 0))
    arrived = lambda size: pl.BlockSpec((rows, size), lambda i, spot: (slot + i, 0))
    in_specs = [whole(w) for w in (*data, *weights)] + [column(ROTARY // 2)] * 2
    out_specs = [column(wj.shape[0]), placed, arrived(width), arrived(units), arrived(units), placed]
    shape = lambda *dims: jax.ShapeDtypeStruct(dims, jnp.bfloat16)
    out_shape = [shape(wj.shape[0], total)] + [shape(total, size) for size in (width, width, units, units, width)]
    operands = [spot, *data, *weights, *tables]
    aliases = {}
    if before is not None:
        for index, array in enumerate(before):
            aliases[len(operands)] = index
            operands.append(array)
            in_specs.append(pl.BlockSpec(memory_space=pl.ANY))
    return pl.pallas_call(
        partial(token_kernel, slot, len(data), sub, chunk),
        grid_spec=pltpu.PrefetchScalarGridSpec(
            num_scalar_prefetch=1, grid=(steps,), in_specs=in_specs, out_specs=out_specs
        ),
        out_shape=out_shape,
        input_output_aliases=aliases,
        compiler_params=pltpu.CompilerParams(vmem_limit_bytes=VMEM),
        cost_estimate=pl.CostEstimate(flops=0, bytes_accessed=0, transcendentals=0),
    )(*operands)


def upstream_kernel(chunk, spot_ref, *refs):
    sources, refs = refs[:5], refs[5:]
    (wd_ref, we_ref, wr_ref, g2_ref, unit_ref, slope_ref) = refs[:6]
    (mg_ref, back_ref, up_ref, hg_ref, sums_ref, hsum_ref) = refs[6:12]
    buffer, sems = refs[12:]
    step = pl.program_id(0)
    steps = pl.num_programs(0)
    slot = lax.rem(step, 2)

    def fetch(which, into):
        for k, source in enumerate(sources):

            @pl.when(spot_ref[steps + which] == k)
            def _():
                pltpu.make_async_copy(source, buffer.at[into], sems.at[into]).start()

    @pl.when(step == 0)
    def _():
        fetch(0, 0)
        sums_ref[...] = jnp.zeros_like(sums_ref)
        hsum_ref[...] = jnp.zeros_like(hsum_ref)

    @pl.when(step + 1 < steps)
    def _():
        fetch(step + 1, 1 - slot)

    pltpu.make_async_copy(sources[0], buffer.at[slot], sems.at[slot]).wait()
    up = buffer[slot]
    up_ref[...] = up
    mg_ref[...] = low(mm(wd_ref[...], up, NT))
    for left in range(0, we_ref.shape[1], chunk):
        over = slice(left, left + chunk)
        piece = low(mm(up, wr_ref[over, :], NT) * wide(slope_ref[:, over]))
        hg_ref[:, over] = piece
        hsum_ref[:, over] += fold_rows(wide(piece))
    for left in range(0, we_ref.shape[0], chunk):
        over = slice(left, left + chunk)
        back = mm(hg_ref[...], we_ref[over, :], NT)
        back_ref[:, over] = low(back * g2_ref[:, over])
        sums_ref[0, :, over] += fold_rows(back * wide(unit_ref[:, over]))
        sums_ref[1, :, over] += fold_rows(back)


def run_upstream(spot, sources, weights, unit, slope, chunk=256):
    rows, width = sources[0].shape
    total = unit.shape[0]
    wd, we, wr, g2 = weights
    units = we.shape[1]
    steps = total // rows

    def whole(array):
        return pl.BlockSpec(array.shape, lambda i, spot: (0,) * array.ndim)

    fixed = lambda *dims: pl.BlockSpec(dims, lambda i, spot: (0,) * len(dims))
    column = lambda height: pl.BlockSpec((height, rows), lambda i, spot: (0, spot[i]))
    placed = pl.BlockSpec((rows, width), lambda i, spot: (spot[i], 0))
    arrived = lambda size: pl.BlockSpec((rows, size), lambda i, spot: (i, 0))
    in_specs = [pl.BlockSpec(memory_space=pl.ANY)] * 5 + [whole(w) for w in weights] + [placed, arrived(units)]
    out_specs = [column(wd.shape[0]), placed, arrived(width), arrived(units), fixed(2, 8, width), fixed(8, units)]
    shape = lambda *dims: jax.ShapeDtypeStruct(dims, jnp.bfloat16)
    out_shape = [
        shape(wd.shape[0], total),
        shape(total, width),
        shape(total, width),
        shape(total, units),
        jax.ShapeDtypeStruct((2, 8, width), jnp.float32),
        jax.ShapeDtypeStruct((8, units), jnp.float32),
    ]
    return pl.pallas_call(
        partial(upstream_kernel, chunk),
        grid_spec=pltpu.PrefetchScalarGridSpec(
            num_scalar_prefetch=1,
            grid=(steps,),
            in_specs=in_specs,
            out_specs=out_specs,
            scratch_shapes=[
                pltpu.VMEM((2, rows, width), jnp.bfloat16),
                pltpu.SemaphoreType.DMA((2,)),
            ],
        ),
        out_shape=out_shape,
        compiler_params=pltpu.CompilerParams(vmem_limit_bytes=VMEM),
        cost_estimate=pl.CostEstimate(
            flops=3 * total * width * (wd.shape[0] + 2 * units), bytes_accessed=12 * total * width, transcendentals=0
        ),
    )(spot, *sources, wd, we, wr, g2, unit, slope)


def weight_kernel(spot_ref, second_ref, hg_ref, active_ref, up_ref, mixed_ref, *refs):
    shares, (expand_sum, reduce_sum, dense_sum) = refs[:4], refs[4:]
    step = pl.program_id(0)
    steps = pl.num_programs(0)

    @pl.when(step == 0)
    def _():
        expand_sum[...] = jnp.zeros_like(expand_sum)
        reduce_sum[...] = jnp.zeros_like(reduce_sum)
        dense_sum[...] = jnp.zeros_like(dense_sum)

    up = up_ref[...]
    dense_sum[...] += mm(mixed_ref[...], up)
    expand_sum[...] += mm(second_ref[...], hg_ref[...], TN)
    reduce_sum[...] += mm(active_ref[...], up, TN)

    @pl.when(step == steps - 1)
    def _():
        col = spot_ref[COLUMN]
        large, small = expand_sum.shape[0] // 4, dense_sum.shape[0] // 4
        for k, share in enumerate(shares):
            i = k + col - 2 * (col & k)
            at = pl.ds(pl.multiple_of(i * large, large), large)
            share[:large] = low(expand_sum[at, :])
            share[large : 2 * large] = low(reduce_sum[at, :])
            share[2 * large :] = low(dense_sum[pl.ds(pl.multiple_of(i * small, small), small), :])


def weight_gradients(spot, second, hg, active, ups, mixed):
    total, width = second.shape
    units = hg.shape[1]
    rows = total // N
    height = mixed.shape[0]
    fixed = lambda *dims: pl.BlockSpec(dims, lambda i, spot: (0,) * len(dims))
    arrived = lambda size: pl.BlockSpec((rows, size), lambda i, spot: (i, 0))
    dims = (width // 4 + units // 4 + height // 4, width)
    return pl.pallas_call(
        weight_kernel,
        grid_spec=pltpu.PrefetchScalarGridSpec(
            num_scalar_prefetch=1,
            grid=(N,),
            in_specs=[
                arrived(width),
                arrived(units),
                arrived(units),
                arrived(width),
                pl.BlockSpec((height, rows), lambda i, spot: (0, spot[i])),
            ],
            out_specs=[fixed(*dims)] * 4,
            scratch_shapes=[
                pltpu.VMEM((width, units), jnp.float32),
                pltpu.VMEM((units, width), jnp.float32),
                pltpu.VMEM((height, width), jnp.float32),
            ],
        ),
        out_shape=[jax.ShapeDtypeStruct(dims, jnp.bfloat16)] * 4,
        compiler_params=pltpu.CompilerParams(vmem_limit_bytes=VMEM),
        cost_estimate=pl.CostEstimate(
            flops=3 * total * width * (height + 2 * units), bytes_accessed=8 * total * width, transcendentals=0
        ),
    )(spot, second, hg, active, ups, mixed)


def deliver_kernel(order_ref, left_ref, weight_ref, add_ref, *refs):
    del order_ref
    send_ref, keep_ref = refs[-2:]
    step = pl.program_id(0)
    value = mm(left_ref[...], weight_ref[...], TN)
    if len(refs) > 2:
        value = value * refs[0][...]
    value = low(value + wide(add_ref[...]))

    @pl.when(step < pl.num_programs(0) // 2)
    def _():
        send_ref[...] = value

    @pl.when(step >= pl.num_programs(0) // 2)
    def _():
        keep_ref[...] = value


def deliver(order, left, weight, add, gain=None):
    depth, total = left.shape
    width = weight.shape[1]
    steps = N
    tile = total // N
    rows = pl.BlockSpec((tile, width), lambda s, order: (order[ORDER + s], 0))
    in_specs = [
        pl.BlockSpec((depth, tile), lambda s, order: (0, order[ORDER + s])),
        pl.BlockSpec((depth, width), lambda s, order: (0, 0)),
        rows,
    ]
    operands = [left, weight, add]
    if gain is not None:
        in_specs.append(pl.BlockSpec((1, width), lambda s, order: (0, 0)))
        operands.append(gain)
    return pl.pallas_call(
        deliver_kernel,
        grid_spec=pltpu.PrefetchScalarGridSpec(
            num_scalar_prefetch=1,
            grid=(steps,),
            in_specs=in_specs,
            out_specs=[
                pl.BlockSpec((tile, width), lambda s, order: (jnp.minimum(s, steps // 2 - 1), 0)),
                pl.BlockSpec((tile, width), lambda s, order: (jnp.maximum(s - steps // 2, 0), 0)),
            ],
        ),
        out_shape=[jax.ShapeDtypeStruct((total // 2, width), jnp.bfloat16)] * 2,
        compiler_params=pltpu.CompilerParams(vmem_limit_bytes=VMEM),
        cost_estimate=pl.CostEstimate(
            flops=0, bytes_accessed=0, transcendentals=0
        ),
    )(order, *operands)


def joint_kernel(spot_ref, jb_ref, unit_ref, wj_ref, gain_ref, shift_ref, sums_ref, up_ref, hsum_ref, *refs):
    shares, (vector_ref, total_ref, turned_ref, sum_ref) = refs[:4], refs[4:]
    step = pl.program_id(0)
    jb = jb_ref[...]
    height, tile = jb.shape
    width = unit_ref.shape[1]

    @pl.when(step == 0)
    def _():
        total_ref[...] = jnp.zeros_like(total_ref)
        sum_ref[...] = jnp.zeros_like(sum_ref)

    total_ref[...] += mm(jb, unit_ref[...])
    sum_ref[...] += mm(jb, jnp.ones((tile, 128), jnp.bfloat16))

    @pl.when(step == pl.num_programs(0) - 1)
    def _():
        col, quarter = spot_ref[COLUMN], spot_ref[COLUMN + 1]
        gain = jnp.sum(total_ref[...] * wide(wj_ref[...]), axis=0, keepdims=True)
        turned_ref[...] = (total_ref[...] * gain_ref[...] + sum_ref[:, :1] * shift_ref[...]).T
        part = width // 4
        for k, share in enumerate(shares):
            i = k + col - 2 * (col & k)
            share[:part] = low(turned_ref[pl.ds(pl.multiple_of(i * part, part), part), :])
        jb_sum = sum_ref[...].T[:1]
        first = low(jb_sum)
        rest = jb_sum - wide(first)
        middle = low(rest)
        final = low(rest - wide(middle))
        shift = mm(jnp.concatenate([first, middle, final], axis=0), wj_ref[...])
        rows = [
            gain,
            jnp.sum(shift, axis=0, keepdims=True),
            jnp.sum(sums_ref[0], axis=0, keepdims=True),
            jnp.sum(sums_ref[1], axis=0, keepdims=True),
            jnp.sum(up_ref[...], axis=0, keepdims=True),
        ]
        jb_sum = jnp.concatenate([jb_sum, jnp.zeros((1, width - height), jnp.float32)], axis=1)
        for whole in (jnp.sum(hsum_ref[...], axis=0, keepdims=True), jb_sum):
            rows += [jnp.where(quarter == i, whole, 0.0) for i in range(N)]
        rows.append(jnp.zeros((3, width), jnp.float32))
        vector = jnp.concatenate(rows, axis=0)
        vector_ref[...] = vector
        coarse = low(vector)
        rest = jnp.zeros((16, 2 * height - width), jnp.bfloat16)
        pieces = []
        for piece in (coarse,):
            pieces += [piece[:, :height], jnp.concatenate([piece[:, height:], rest], axis=1)]
        for share in shares[1:]:
            for n, piece in enumerate(pieces):
                share[part + 16 * n : part + 16 * (n + 1)] = piece


def joint_gradient(spot, jb, unit, wj, gain, shift, sums, up_sum, hsum):
    height, total = jb.shape
    width = unit.shape[1]
    tile = total // N
    fixed = lambda *dims: pl.BlockSpec(dims, lambda s, spot: (0,) * len(dims))
    shapes = [(width // 4, height)] + [(width // 4 + 32, height)] * 3
    return pl.pallas_call(
        joint_kernel,
        grid_spec=pltpu.PrefetchScalarGridSpec(
            num_scalar_prefetch=1,
            grid=(N,),
            in_specs=[
                pl.BlockSpec((height, tile), lambda s, spot: (0, s)),
                pl.BlockSpec((tile, width), lambda s, spot: (s, 0)),
                fixed(height, width),
                fixed(1, width),
                fixed(1, width),
                fixed(2, 8, width),
                fixed(8, width),
                fixed(*hsum.shape),
            ],
            out_specs=[fixed(*dims) for dims in shapes] + [fixed(16, width)],
            scratch_shapes=[
                pltpu.VMEM((height, width), jnp.float32),
                pltpu.VMEM((width, height), jnp.float32),
                pltpu.VMEM((height, 128), jnp.float32),
            ],
        ),
        out_shape=[jax.ShapeDtypeStruct(dims, jnp.bfloat16) for dims in shapes]
        + [jax.ShapeDtypeStruct((16, width), jnp.float32)],
        compiler_params=pltpu.CompilerParams(vmem_limit_bytes=VMEM),
        cost_estimate=pl.CostEstimate(
            flops=0, bytes_accessed=0, transcendentals=0
        ),
    )(spot, jb, unit, wj, gain, shift, sums, up_sum, hsum)


def pack(vector, width):
    rest = jnp.zeros((vector.shape[0], 2 * width - vector.shape[1]), jnp.float32)
    return low(jnp.concatenate([vector[:, :width], jnp.concatenate([vector[:, width:], rest], axis=1)], axis=0))


def unpack(rows, size):
    rows = wide(rows).reshape(-1, 2, 16, rows.shape[1]).sum(0)
    return jnp.concatenate([rows[0], rows[1][:, : size - rows.shape[2]]], axis=1)


def hop(value, pairs):
    return lax.ppermute(value, ("core", "blk"), [(a[0] * N + a[1], b[0] * N + b[1]) for a, b in pairs])


PLACES = [(c, z) for c in range(2) for z in range(N)]
MAIN = [(z // 2, z) for z in range(N)]
CORE_SWAP = [((c, z), (1 - c, z)) for c, z in PLACES]
NEAR_SWAP = [((c, z), (c, z ^ 1)) for c, z in PLACES]
FAR_SWAP = [((c, z), (c, z ^ 2)) for c, z in PLACES]
FAR_HOME = [((c, z), (1 - c, z ^ 2)) for c, z in PLACES if c != z // 2]


HOME = [((c, z), (c, z ^ 1)) for c, z in MAIN] + FAR_HOME
OFF_MAIN = [(c, z) for c, z in PLACES if c != z // 2]
NEAR_OFF = [((c, z), (c, z ^ 1)) for c, z in OFF_MAIN]
STAY = [(place, place) for place in MAIN]


def tie(*arrays):
    return lax.optimization_barrier(arrays)


def near_sum(keep, got):
    rows = keep.shape[0] // 2
    return low(wide(keep[rows:]) + wide(got[rows:]))


def home_sum(keep, got, near, got_near, main):
    rows = keep.shape[0] // 2
    return jnp.where(main, near, low(wide(keep[:rows]) + wide(got[:rows]) + wide(got_near)))


def own_sum(keep, got, got_home, main):
    rows = keep.shape[0] // 2
    return jnp.where(main, wide(keep[:rows]) + wide(got[:rows]), 0.0) + wide(got_home)


def pick(value, axis, index):
    return lax.dynamic_index_in_dim(value, index, axis, keepdims=False)


def plane(values):
    return [lax.ppermute(value, "col", [(i, i ^ (k + 1)) for i in range(4)]) for k, value in enumerate(values)]


NEAR = [((c, z), (c, z ^ 1)) for c, z in PLACES]


def first_pieces(value, near):
    return pick(value, 1, 1 - near).reshape(-1, value.shape[-1])


def second_pieces(value, got, core, near):
    got = got.reshape((2,) + value.shape[2:])
    return jnp.concatenate([pick(pick(value, 1, near), 0, 1 - core), pick(got, 0, 1 - core)], axis=0)


def quarters(quarter, line, got, last, core, near):
    size = line.shape[2]
    mine = chosen(2 * core + near, [line[0, 0], line[0, 1], line[1, 0], line[1, 1]])
    pieces = [mine, last[:size], jnp.where(core == 0, got[:size], got[size : 2 * size]), last[size : 2 * size]]
    return [chosen(quarter ^ k, pieces) for k in range(N)]


def finish_kernel(spot_ref, line_ref, got_ref, last_ref, reduce_ref, expand_out, dense_out, reduce_out):
    core, near, half = spot_ref[LINE], spot_ref[LINE + 1], spot_ref[LINE + 2]
    pieces = quarters(2 * near + core, wide(line_ref[...]), wide(got_ref[...]), wide(last_ref[...]), core, near)
    rows = expand_out.shape[0]
    for e in range(pieces[0].shape[1] // 128):
        for slot in range(N):
            piece = pieces[slot ^ (2 * (e % 2))]
            to = (N * e + slot) * 128
            expand_out[:, to : to + 128] = piece[:rows, e * 128 : (e + 1) * 128]
    dense_out[...] = chosen(2 * core + half, [piece[rows:] for piece in pieces])
    reduce_out[...] = wide(reduce_ref[...])


def finish(spot, line, got, last, reduced):
    rows, width = line.shape[2] // 2, line.shape[3]
    return pl.pallas_call(
        finish_kernel,
        in_specs=[pl.BlockSpec(memory_space=pltpu.SMEM)] + [pl.BlockSpec(memory_space=pltpu.VMEM)] * 4,
        out_specs=[pl.BlockSpec(memory_space=pltpu.VMEM)] * 3,
        out_shape=[
            jax.ShapeDtypeStruct((rows, N * width), jnp.float32),
            jax.ShapeDtypeStruct((rows, width), jnp.float32),
            jax.ShapeDtypeStruct(reduced.shape, jnp.float32),
        ],
        compiler_params=pltpu.CompilerParams(vmem_limit_bytes=VMEM),
    )(spot, line, got, last, reduced)


def joint_finish_kernel(spot_ref, line_ref, other_ref, near_ref, last_ref, out_ref):
    core, near = spot_ref[LINE], spot_ref[LINE + 1]
    rows = out_ref.shape[0]
    line = wide(line_ref[...])
    mine = chosen(2 * core + near, [line[0, 0], line[0, 1], line[1, 0], line[1, 1]])
    pieces = [mine] + [wide(ref[:rows]) for ref in (other_ref, near_ref, last_ref)]
    pieces = [chosen((2 * near + core) ^ k, pieces) for k in range(N)]
    for n in range(mine.shape[1] // (2 * HEAD)):
        for slot in range(0, N, 2):
            for other in range(2):
                at = (2 * n + other) * HEAD
                to = ((2 * n + other) * N + slot) * HEAD
                pair = [piece[:, at : at + HEAD] for piece in pieces[slot : slot + 2]]
                out_ref[:, to : to + 2 * HEAD] = jnp.concatenate(pair, axis=1)


def joint_finish(spot, line, got):
    rows, width = line.shape[2:]
    return pl.pallas_call(
        joint_finish_kernel,
        in_specs=[pl.BlockSpec(memory_space=pltpu.SMEM)] + [pl.BlockSpec(memory_space=pltpu.VMEM)] * 4,
        out_specs=pl.BlockSpec(memory_space=pltpu.VMEM),
        out_shape=jax.ShapeDtypeStruct((rows, N * width), jnp.float32),
        compiler_params=pltpu.CompilerParams(vmem_limit_bytes=VMEM),
    )(spot, line, *got)


def split_local(
    tokens,
    lengths,
    first_gain,
    first_shift,
    second_gain,
    second_shift,
    joint_weight,
    joint_bias,
    dense_weight,
    dense_bias,
    expand_weight,
    expand_bias,
    reduce_weight,
    reduce_bias,
    cotangent,
):
    col, core, z = lax.axis_index("col"), lax.axis_index("core"), lax.axis_index("blk")
    half, near = z // 2, z % 2
    quarter = 2 * near + core
    main = core == half
    flag = main.astype(jnp.int32)
    rows, width = tokens.shape[1:]
    total = rows * N
    units = expand_weight.shape[1]
    groups = units // (N * 128)
    heads = HEADS // N
    own_x, own_g = tokens[0], cotangent[0]
    row_of = lambda vector: vector.reshape(1, -1)

    x_other = hop(own_x, CORE_SWAP)
    x_first = hop(own_x, HOME)

    wj, wd, we, wr = prepare(quarter, joint_weight, dense_weight, expand_weight, reduce_weight)
    bj = pick(joint_bias.reshape(3, heads, N, HEAD), 2, quarter).reshape(-1, 1)
    be = expand_bias.reshape(groups // 2, 2, N, 128)
    be = jnp.stack([pick(be[:, 0], 1, quarter), pick(be[:, 1], 1, quarter ^ 2)], axis=1).reshape(1, -1)
    first_row, second_row = row_of(first_gain), row_of(second_gain)

    weights = [wj, bj, we, be, wr, first_row, row_of(first_shift), second_row, row_of(second_shift)]

    sizes = jnp.where(main, lengths, hop(lengths, CORE_SWAP))
    number, offset = doc_tables(sizes, jnp.arange(total, dtype=jnp.int32))
    inverse = 10000.0 ** (-2.0 * jnp.arange(ROTARY // 2, dtype=jnp.float32) / ROTARY)
    phase = inverse[:, None] * offset.astype(jnp.float32)
    tables = [jnp.cos(phase), jnp.sin(phase)]
    docs = lengths.shape[1]
    same = number == jnp.arange(HEAD, dtype=jnp.int32)[:, None]
    used = jnp.arange(HEAD)[:, None] < docs
    qx = low(jnp.where(same & used, 1.0, 0.0))
    kx = low(jnp.where(used & ~same, NEG, 0.0))

    spots = [z, z ^ (2 - flag), z ^ (1 + flag), z ^ 3]
    zero = jnp.int32(0)
    order = z ^ (jnp.arange(N, dtype=jnp.int32) ^ (2 * flag))
    sources = [1 - flag, 3 - flag, 4 - 3 * flag, 2 + 2 * flag]
    line_place = [col, quarter, core, near, half]
    spot = jnp.stack([*spots, *sources, *line_place, *[order[k] for k in range(N)], 1 - flag, zero, zero, 2 - flag])
    up_sum = jnp.sum(wide(own_g).reshape(-1, 8, width), axis=0)
    spot, up_sum = tie(spot, up_sum)
    state = run_tokens(0, 1, spot, [own_x, x_other], weights, tables, None)
    x_first, own_g_late, *state = tie(x_first, own_g, *state)
    g_far = hop(own_g_late, FAR_HOME + STAY)
    x_second = hop(x_first, NEAR_OFF + STAY)
    x_first_other = hop(x_first, CORE_SWAP)
    state = run_tokens(1, 1, spot, [x_first], weights, tables, state)
    x_second, *state = tie(x_second, *state)
    x_second_other = hop(x_second, CORE_SWAP)
    state = run_tokens(2, 2, spot, [x_first_other, x_second_other, x_second], weights, tables, state)
    qkv, unit, second, active, slope, feed = state
    qkv = qkv.reshape(3, heads, HEAD, total)
    g_far, qkv = tie(g_far, qkv)
    g_near = hop(g_far, NEAR)
    g_other = hop(g_far, CORE_SWAP)
    mixed, full, inverse_sum, shares = attend_forward(qkv, kx, qx, 0, heads, None)
    g_near, mixed = tie(g_near, mixed)
    mixed = mixed.reshape(-1, total)
    g_near_other = hop(g_near, CORE_SWAP)
    out_send, out_keep = deliver(spot, mixed, wd, feed)

    spot, out_send, out_keep = tie(spot, out_send, out_keep)
    out_got = hop(out_send, CORE_SWAP)
    gs = (own_g, g_other, g_near, g_far, g_near_other)
    mg, back, ups, hg, sums, hsum = run_upstream(spot, gs, [wd, we, wr, second_row], unit, slope)
    out_near = near_sum(out_keep, out_got)
    out_near, hg = tie(out_near, hg)
    out_got_near = hop(out_near, NEAR_OFF)

    kept_share, *shares_out = weight_gradients(spot, second, hg, active, ups, mixed)
    out_home = home_sum(out_keep, out_got, out_near, out_got_near, main)
    out_home, mg, *shares_out = tie(out_home, mg, *shares_out)
    out_got_home = hop(out_home, HOME)
    shares_got = plane(shares_out)

    jb = attend_backward(qkv, mg.reshape(heads, HEAD, total), full, inverse_sum, shares, tables)
    jb = jb.reshape(-1, total)

    kept_joint, *joint_out, vector = joint_gradient(
        spot, jb, unit, wj, first_row, row_of(first_shift), sums, up_sum, hsum
    )
    jb, *joint_out = tie(jb, *joint_out)
    joint_got = plane(joint_out)

    send, keep = deliver(spot, jb, wj, back, first_row)

    send, out_got_home, *shares_got = tie(send, out_got_home, *shares_got)
    share = wide(kept_share) + sum(wide(piece) for piece in shares_got)
    kept = near ^ half
    part = width // 4
    expand_part = share[:part].reshape(2, 2, 2, part // 8, units // N)
    reduce_part = share[part : part + units // (4 * N)].reshape(2, -1, width)
    dense_part = share[part + units // (4 * N) :]
    far_send = [pick(expand_part, 1, 1 - half).reshape(part // 2, -1), pick(reduce_part, 0, 1 - kept), dense_part]
    far_send = low(jnp.concatenate(far_send, axis=0))
    far_send, send = tie(far_send, send)
    got = hop(send, CORE_SWAP)
    far_got = hop(far_send, FAR_SWAP)
    near_part = near_sum(keep, got)
    out = own_sum(out_keep, out_got, out_got_home, main)
    inputs = wide(own_x)
    result = low(inputs + out + (dense_bias + reduce_bias))
    got_near = hop(near_part, NEAR_OFF)

    got_near, *joint_got = tie(got_near, *joint_got)
    joint_part = wide(kept_joint) + sum(wide(piece[:part]) for piece in joint_got)
    vector = vector + sum(unpack(piece[part:], width) for piece in joint_got)
    joint_width = joint_part.shape[1]
    joint_part = joint_part.reshape(2, 2, 2, part // 8, joint_width)
    joint_far_send = jnp.concatenate(
        [low(pick(joint_part, 1, 1 - half)).reshape(part // 2, joint_width), pack(vector, joint_width)], axis=0
    )
    home = home_sum(keep, got, near_part, got_near, main)
    home, joint_far_send, result = tie(home, joint_far_send, result)
    got_home = hop(home, HOME)
    joint_far = hop(joint_far_send, FAR_SWAP)
    home, far_got = tie(home, far_got)
    far_got = wide(far_got)
    expand_part = low(pick(expand_part, 1, half).reshape(part // 2, -1) + far_got[: part // 2])
    reduce_part = low(pick(reduce_part, 0, kept) + far_got[part // 2 : part // 2 + 128])
    dense_part = low(dense_part + far_got[part // 2 + 128 :]).reshape(2, HEAD // 2, width)
    line = jnp.concatenate(
        [
            expand_part.reshape(2, 2, part // 8, -1),
            jnp.broadcast_to(dense_part[None], (2,) + dense_part.shape),
        ],
        axis=2,
    )
    line_send = first_pieces(line, near)
    line_got = hop(line_send, NEAR)
    reduce_got = hop(reduce_part, [((c, s), ((s % 2) ^ (s // 2), 2 * (s // 2) + c)) for c, s in PLACES])
    scaled = own_sum(keep, got, got_home, main)
    _, unit_rows, inverse_root = normalize(inputs, first_gain, first_shift)
    input_back = inverse_root * (
        scaled
        - jnp.mean(scaled, axis=-1, keepdims=True)
        - unit_rows * jnp.mean(scaled * unit_rows, axis=-1, keepdims=True)
    )
    tokens_gradient = low(wide(own_g) + input_back)
    line_got, tokens_gradient = tie(line_got, tokens_gradient)
    line_send = second_pieces(line, line_got, core, near)
    line_last = hop(line_send, CORE_SWAP)
    joint_far, line_send = tie(joint_far, line_send)
    joint_part = low(pick(joint_part, 1, half).reshape(part // 2, joint_width) + wide(joint_far[: part // 2]))
    vector = vector + unpack(joint_far[part // 2 :], width)
    joint_line = joint_part.reshape(2, 2, part // 8, joint_width)
    vector_rows = pack(vector, joint_width)
    joint_got = []
    for dz, dc in ((0, 1), (1, 0), (1, 1)):
        piece = pick(pick(joint_line, 1, near ^ dz), 0, core ^ dc)
        piece = jnp.concatenate([piece, vector_rows], axis=0)
        joint_got.append(hop(piece, [((c, p), (c ^ dc, p ^ dz)) for c, p in PLACES]))
    expand_mine, dense_mine, reduce_mine = finish(spot, line, line_got, line_last, reduce_got)
    expand_mine, *joint_got = tie(expand_mine, *joint_got)
    vector = vector + sum(unpack(piece[part // 8 :], width) for piece in joint_got)
    joint_mine = joint_finish(spot, joint_line, joint_got)

    device = (2 * col + core) * N + z
    share = width // (8 * N)
    head_row = lambda head: 5 + N + head % N
    cut = lambda row, start, size: lax.dynamic_slice(vector, (row, start), (1, size))[0]
    pieces = [cut(row, device * share, share) for row in range(5)]
    pieces[4:] = [
        cut(head_row(device % HEADS), (device // HEADS * heads + device % HEADS // N) * HEAD, HEAD),
        cut(head_row(device // 2), (2 * heads + device // 2 // N) * HEAD + device % 2 * share, share),
        pieces[4],
        cut(5 + (z ^ (2 * core)), (2 * col + core) * 128, 128),
    ]

    return (
        result[None],
        tokens_gradient[None],
        *pieces[:4],
        joint_mine,
        pieces[4],
        pieces[5],
        dense_mine,
        pieces[6],
        expand_mine,
        pieces[7],
        reduce_mine,
        pieces[6],
    )


def solution(mesh):
    count, blocks = mesh.devices.shape
    split = blocks == N and count == 8
    if split:
        mesh = jax.sharding.Mesh(mesh.devices.reshape(count // 2, 2, blocks), ("col", "core", "blk"))
        batch = ("col", "core")
        every = ("col", "core", "blk")
    else:
        batch, every = "batch", ("batch", "blk")
    by_rows = P(batch, "blk", None)
    placed = (by_rows, P(batch, None)) + (P(),) * 12 + (by_rows,)
    vector, matrix = P(every), P(every, None)
    return jax.shard_map(
        split_local if split else local,
        mesh=mesh,
        in_specs=placed,
        out_specs=(
            by_rows,
            by_rows,
            vector,
            vector,
            vector,
            vector,
            matrix,
            vector,
            vector,
            matrix,
            vector,
            matrix,
            vector,
            matrix,
            vector,
        ),
        check_vma=False,
    )
```
